32 devices in a mesh: seq: 16 (over z, y, x), span: 2 (over core).
Axes of the slice: x: 2, y: 2, z: 4, core: 2. Of those that a mesh axis runs over, the one named last changes fastest.
Arguments:
- tokens: bfloat16 [32, 1024, 768], P('seq', 'span'), may hold values from -6 to 6
- conditions: bfloat16 [32, 128], P('seq'), may hold values from -6 to 6
- assignment: int32 [32], P('seq'), may hold values from 0 to 31, each once
- lengths: int32 [32], P('seq'), may hold values from 128 to 1024, as said below
- norm1_gain: bfloat16 [768], replicated, may hold values from 0.099609375 to 1.8984375
- ada_weight: bfloat16 [128, 4608], replicated, may hold values from -0.5 to 0.5
- ada_bias: bfloat16 [4608], replicated, may hold values from -4 to 4
- qkv_weight: bfloat16 [768, 2304], replicated, may hold values from -0.21875 to 0.21875
- out_weight: bfloat16 [768, 768], replicated, may hold values from -3.5 to 3.5
- norm2_gain: bfloat16 [768], replicated, may hold values from 0.099609375 to 1.8984375
- up_weight: bfloat16 [768, 3072], replicated, may hold values from -0.21875 to 0.21875
- up_bias: bfloat16 [3072], replicated, may hold values from -6 to 6
- down_weight: bfloat16 [3072, 768], replicated, may hold values from -0.21875 to 0.21875
- down_bias: bfloat16 [768], replicated, may hold values from -4 to 4
- cotangent: bfloat16 [32, 1024, 768], P('seq', 'span'), may hold values from -6 to 6
Outputs:
- out: bfloat16 [32, 1024, 768], P('seq', 'span')
- grad_input: float32 [32, 1024, 768], P('seq', 'span')
- grad_conditions: float32 [32, 128], P('seq')
- grad_norm1_gain: float32 [768], replicated
- grad_ada_weight: float32 [128, 4608], P('seq', 'span')
- grad_ada_bias: float32 [4608], replicated
- grad_qkv_weight: float32 [768, 2304], P('seq', 'span')
- grad_out_weight: float32 [768, 768], P('seq', 'span')
- grad_norm2_gain: float32 [768], replicated
- grad_up_weight: float32 [768, 3072], P('seq', 'span')
- grad_up_bias: float32 [3072], replicated
- grad_down_weight: float32 [3072, 768], P('seq', 'span')
- grad_down_bias: float32 [768], replicated
The draws below stay inside these ranges and needn't reach their ends.
Inputs may be any that keep to these rules, and one draw needn't show every extreme that they name: `assignment`: each sequence is held by exactly one slot. `lengths`: among the 2 slots of each index of seq, one has length 1024 and another has length 128.
All inputs are finite; a program needn't handle non-finite values.
Results may differ from the reference program's by a relative error of at most 0.01.
The reference program's roundings to bfloat16 on the way count: a program that leaves them out, or rounds other values in their place, can miss the bound.
Values may be sent and summed in bfloat16 or wider, within the bound.
A program may use at most 320 MiB of HBM per device.

```python
import jax
import jax.numpy as jnp
from jax import lax

H = 12
HD = 64
D = 768
FF = 3072
COND = 128
LEN = 1024
SD = 2
SLOTS = 32


def draw_lengths(key, part):
    key = jax.random.fold_in(key, 7)
    base_key, order_key = jax.random.split(key)
    group_count = SLOTS // SD
    base_lengths = jax.random.randint(base_key, (group_count, SD), LEN // 8, LEN + 1)
    scores = jax.random.randint(order_key, (group_count, SD), 0, 1 << 20) * SD + jnp.arange(SD, dtype=jnp.int32)[None, :]
    ranking = jnp.argsort(scores, axis=1)
    slot_ids = jnp.arange(SD, dtype=jnp.int32)[None, :]
    longest = slot_ids == ranking[:, :1]
    shortest = slot_ids == ranking[:, 1:2]
    chosen = jnp.where(longest, LEN, jnp.where(shortest, LEN // 8, base_lengths))
    return chosen.reshape(SLOTS).astype(jnp.int32)


def block_scale(own_key, dims, cuts, least, high):
    def one(dim, shards_of):
        steps = jax.random.uniform(jax.random.fold_in(jax.random.fold_in(own_key, 6), dim), (shards_of,), jnp.float32, least / len(cuts), high / len(cuts))
        return jnp.repeat(jnp.exp(steps), dims[dim] // shards_of).reshape((-1,) + (1,) * (len(dims) - dim - 1))

    gain = one(*cuts[0])
    for cut in cuts[1:]:
        gain = gain * one(*cut)
    return gain


def scatter_about(stream_key, extent, scale, most, cuts=(), kind=jnp.bfloat16):
    drawn = jax.random.normal(stream_key, extent, jnp.float32) * scale
    if len(cuts) > 0:
        drawn = block_scale(stream_key, extent, cuts, -0.22, 0.18) * drawn
    return jnp.clip(drawn, min=-most, max=most).astype(kind)


def setup_inputs(seed: int = 0) -> dict:
    keys = jax.random.split(jax.random.key(seed), 16)
    return {
        "tokens": scatter_about(keys[0], (SLOTS, LEN, D), 1.0, 6.0, ((0, 16), (1, 2))),
        "conditions": scatter_about(keys[1], (SLOTS, COND), 1.0, 6.0, ((0, 16),)),
        "assignment": jax.random.permutation(keys[2], SLOTS).astype(jnp.int32),
        "lengths": draw_lengths(jax.random.fold_in(keys[15], 71), 0),
        "norm1_gain": jnp.clip(1.0 + 0.18 * jax.random.normal(keys[4], (D,), jnp.float32), 0.099609375, 1.8984375).astype(jnp.bfloat16),
        "ada_weight": scatter_about(keys[5], (COND, 6 * D), COND ** -0.5, 0.5),
        "ada_bias": scatter_about(keys[6], (6 * D,), 0.3, 4.0),
        "qkv_weight": scatter_about(keys[7], (D, 3 * D), D ** -0.5, 0.21875),
        "out_weight": scatter_about(keys[8], (D, D), (max(D * 4 // LEN, 1)) ** -0.5, 3.5),
        "norm2_gain": jnp.clip(1.0 + 0.18 * jax.random.normal(keys[9], (D,), jnp.float32), 0.099609375, 1.8984375).astype(jnp.bfloat16),
        "up_weight": scatter_about(keys[10], (D, FF), D ** -0.5, 0.21875),
        "up_bias": scatter_about(keys[11], (FF,), 0.5, 6.0),
        "down_weight": scatter_about(keys[12], (FF, D), (FF // 4) ** -0.5, 0.21875),
        "down_bias": scatter_about(keys[13], (D,), 0.3, 4.0),
        "cotangent": scatter_about(keys[14], (SLOTS, LEN, D), 1.0, 6.0, ((0, 16), (1, 2))),
    }


@jax.custom_vjp
def low(v):
    return lax.optimization_barrier(v.astype(jnp.bfloat16)).astype(jnp.float32)

@jax.custom_vjp
def low_back(v):
    return v

def low_keep(v):
    return (low(v), None)

def low_pass(kept, grad):
    return (grad,)

def back_keep(v):
    return (v, None)

def back_low(kept, grad):
    return (low(grad),)
low.defvjp(low_keep, low_pass)
low_back.defvjp(back_keep, back_low)
EPSILON = 1e-05
MASKED = -1e+30
HIGHEST = lax.Precision.HIGHEST

def product(left_in, right_in):
    return jnp.dot(left_in, right_in, precision=HIGHEST, preferred_element_type=jnp.float32)

def layer_norm(inputs, gain_vec):
    center = inputs - lax.optimization_barrier(jnp.mean(inputs, axis=-1, keepdims=True))
    spread = lax.optimization_barrier(jnp.mean(center * center, axis=-1, keepdims=True))
    return center * lax.rsqrt(spread + EPSILON) * gain_vec

def rotary_tables(positions, half_size):
    frequency = jnp.power(10000.0, -jnp.arange(half_size, dtype=jnp.float32) / half_size)
    angles = positions.astype(jnp.float32)[:, None] * frequency[None, :]
    return (jnp.cos(angles), jnp.sin(angles))

def rotate(inputs, cos_table, sine_table):
    half_size = inputs.shape[-1] // 2
    former = inputs[..., :half_size]
    latter = inputs[..., half_size:]
    cos_part = cos_table[:, None, :]
    sine_part = sine_table[:, None, :]
    return jnp.concatenate([former * cos_part - latter * sine_part, latter * cos_part + former * sine_part], axis=-1)

def slot_layer(tokens_row, cond_row, length, norm1_gain, ada_weight, ada_bias, qkv_weight, out_weight, norm2_gain, up_weight, up_bias, down_weight, down_bias):
    seq_len = tokens_row.shape[0]
    model_width = tokens_row.shape[1]
    silu_low = low(jax.nn.silu(cond_row))
    modulation = product(silu_low[None, :], ada_weight)[0] + ada_bias
    shift_one, scale_one, gate_one, shift_two, scale_two, gate_two = jnp.split(modulation, 6)
    hidden_one = low(layer_norm(tokens_row, norm1_gain) * (1.0 + scale_one) + shift_one)
    qkv_all = low_back(product(hidden_one, qkv_weight))
    queries_raw = qkv_all[:, :model_width].reshape(seq_len, H, HD)
    keys_raw = qkv_all[:, model_width:2 * model_width].reshape(seq_len, H, HD)
    values_raw = qkv_all[:, 2 * model_width:].reshape(seq_len, H, HD)
    cos_table, sine_table = rotary_tables(jnp.arange(seq_len, dtype=jnp.int32), HD // 2)
    queries = low(rotate(queries_raw, cos_table, sine_table))
    keys_rot = low(rotate(keys_raw, cos_table, sine_table))
    values_low = low(values_raw)
    scores = low_back(jnp.einsum('qhd,khd->hqk', queries, keys_rot, precision=HIGHEST)) * HD ** (-0.5)
    visible = jnp.arange(seq_len, dtype=jnp.int32) < length
    scores = jnp.where(visible[None, None, :], scores, MASKED)
    maximum = lax.optimization_barrier(jnp.max(scores, axis=-1, keepdims=True))
    exponent = jnp.exp(scores - maximum)
    soft_weights = low(exponent / lax.optimization_barrier(jnp.sum(exponent, axis=-1, keepdims=True)))
    attended = low_back(jnp.einsum('hqk,khd->qhd', soft_weights, values_low, precision=HIGHEST))
    attention = low_back(product(low(attended.reshape(seq_len, model_width)), out_weight))
    middle = tokens_row + gate_one * attention
    hidden_two = low(layer_norm(middle, norm2_gain) * (1.0 + scale_two) + shift_two)
    upper_in = low_back(product(hidden_two, up_weight) + up_bias)
    activation = low(jax.nn.gelu(upper_in, approximate=True))
    lowered = low_back(product(activation, down_weight) + down_bias)
    return middle + gate_two * lowered

def widen(array_in):
    return array_in.astype(jnp.float32)

def reference(tokens, conditions, assignment, lengths, norm1_gain, ada_weight, ada_bias, qkv_weight, out_weight, norm2_gain, up_weight, up_bias, down_weight, down_bias, cotangent):
    params = (widen(norm1_gain), widen(ada_weight), widen(ada_bias), widen(qkv_weight), widen(out_weight), widen(norm2_gain), widen(up_weight), widen(up_bias), widen(down_weight), widen(down_bias))
    slot_step = jax.checkpoint(slot_layer)

    def whole_layer(tokens_f, conditions_f, *weights_f):
        cond_rows = jnp.take(conditions_f, assignment, axis=0)

        def one_slot(inputs):
            return slot_step(inputs[0], inputs[1], inputs[2], *weights_f)
        return lax.map(one_slot, (tokens_f, cond_rows, lengths))
    outputs, pull_back = jax.vjp(whole_layer, widen(tokens), widen(conditions), *params)
    gradients = pull_back(widen(cotangent))
    return (outputs.astype(jnp.bfloat16), gradients[0], gradients[1], gradients[2], gradients[3], gradients[4], gradients[5], gradients[6], gradients[7], gradients[8], gradients[9], gradients[10], gradients[11])
```

```python
from functools import partial

import jax
import jax.numpy as jnp
import numpy as np
from jax import lax
from jax.experimental import pallas as pl
from jax.experimental.pallas import tpu as pltpu
from jax.sharding import PartitionSpec as P

HEADS = 12
HEAD = 64
D = 768
FF = 3072
PAIR = 128
PAIRS = HEADS // 2
LEN = 1024
SHORT = 128
SLOTS = 2
CHUNK = 768
EPSILON = 1e-5
LOG2E = 1.4426950408889634
GELU_C = 0.7978845608028654
BIG = 62 << 20
MESH = pl.DeviceIdType.MESH
F32 = jnp.float32
BF16 = jnp.bfloat16
HIGHEST = lax.Precision.HIGHEST


def nn(a, b):
    return lax.dot_general(a, b, (((1,), (0,)), ((), ())), preferred_element_type=F32)


def nt(a, b):
    return lax.dot_general(a, b, (((1,), (1,)), ((), ())), preferred_element_type=F32)


def tn(a, b):
    return lax.dot_general(a, b, (((0,), (0,)), ((), ())), preferred_element_type=F32)


def whole(shape, buffers=1):
    return pl.BlockSpec(shape, lambda *_: (0,) * len(shape), pipeline_mode=pl.Buffered(buffers))


def cost(flops, bytes_accessed, transcendentals=0):
    return pl.CostEstimate(
        flops=int(flops), bytes_accessed=int(bytes_accessed), transcendentals=int(transcendentals)
    )


def col_sum(x):
    return jnp.sum(x, axis=0, keepdims=True)


def row_mean(x):
    return jnp.mean(x, axis=-1, keepdims=True)


def rotary(length):
    half = HEAD // 2
    freq = np.power(np.float32(10000.0), -np.arange(half, dtype=np.float32) / np.float32(half))
    angles = np.arange(length, dtype=np.float32)[:, None] * freq.astype(np.float32)[None, :]
    cos, sin = np.cos(angles), np.sin(angles)
    return (
        np.concatenate([cos] * 4, axis=1).astype(np.float32),
        np.concatenate([-sin, sin, -sin, sin], axis=1).astype(np.float32),
    )


def swap_halves(x):
    lane = lax.broadcasted_iota(jnp.int32, x.shape, 1)
    first = (lane & 32) == 0
    return jnp.where(first, pltpu.roll(x, x.shape[1] - 32, 1), pltpu.roll(x, 32, 1))


def turn(x, cos, sin):
    return x * cos + swap_halves(x) * sin


def turn_back(x, cos, sin):
    return x * cos - swap_halves(x) * sin


def heads_of(x):
    lane = lax.broadcasted_iota(jnp.int32, x.shape, 1)
    zero = jnp.zeros_like(x)
    return jnp.where(lane < HEAD, x, zero), jnp.where(lane < HEAD, zero, x)


def modulation_kernel(n, own_ref, weight_ref, bias_ref, mod_ref, table_ref, send, recv, local):
    me = lax.axis_index("seq")
    barrier = pltpu.get_barrier_semaphore()
    for step in range(1, n):
        pl.semaphore_signal(
            barrier, inc=1, device_id={"seq": lax.rem(me + step, n)}, device_id_type=MESH
        )
    mine = pltpu.make_async_copy(own_ref, table_ref.at[me], local)
    mine.start()
    pl.semaphore_wait(barrier, n - 1)
    copies = []
    for step in range(1, n):
        copy = pltpu.make_async_remote_copy(
            src_ref=own_ref,
            dst_ref=table_ref.at[me],
            send_sem=send.at[step],
            recv_sem=recv.at[step],
            device_id={"seq": lax.rem(me + step, n)},
            device_id_type=MESH,
        )
        copy.start()
        copies.append(copy)
    mine.wait()
    for copy in copies:
        copy.wait()
    source = lax.broadcasted_iota(jnp.int32, (n, 128), 0).astype(F32) * SLOTS
    rows = []
    for slot in range(SLOTS):
        wanted = own_ref[SLOTS + slot : SLOTS + slot + 1, :]
        row = jnp.zeros((1, 128), F32)
        for k in range(SLOTS):
            row += col_sum(jnp.where(wanted == source + k, table_ref[:, k, :], 0.0))
        rows.append(row)
    cond = jnp.concatenate(rows + [jnp.zeros((8 - SLOTS, 128), F32)], axis=0)
    silu = (cond / (1.0 + jnp.exp(-cond))).astype(BF16)
    mod_ref[...] = nn(silu, weight_ref[...]) + bias_ref[...].astype(F32)


def modulation_call(own, ada_weight, ada_bias, n):
    vmem = pl.BlockSpec(memory_space=pltpu.VMEM)
    return pl.pallas_call(
        partial(modulation_kernel, n),
        name="modulation",
        out_shape=(
            jax.ShapeDtypeStruct((8, 6 * D), F32),
            jax.ShapeDtypeStruct((n, 8, 128), F32),
        ),
        in_specs=[vmem] * 3,
        out_specs=(vmem, vmem),
        scratch_shapes=[
            pltpu.SemaphoreType.DMA((n,)),
            pltpu.SemaphoreType.DMA((n,)),
            pltpu.SemaphoreType.DMA,
        ],
        compiler_params=pltpu.CompilerParams(
            collective_id=0, has_side_effects=True, vmem_limit_bytes=16 << 20
        ),
        cost_estimate=cost(1e7, 2e6),
    )(own, ada_weight, ada_bias)


def project_kernel(
    order, tok_ref, mod_ref, gain_ref, weight_ref, cos_ref, sin_ref,
    q_ref, h_ref, kvl_ref, kvs_ref,
):
    j = pl.program_id(0)
    row = mod_ref[pl.ds(order[j], 1), :]
    shift, scale = row[:, :D], row[:, D : 2 * D]
    x = tok_ref[...].astype(F32)
    center = x - row_mean(x)
    xhat = center * lax.rsqrt(row_mean(center * center) + EPSILON)
    hidden = (xhat * gain_ref[...].astype(F32) * (1.0 + scale) + shift).astype(BF16)
    h_ref[...] = hidden
    cos = jnp.concatenate([cos_ref[...]] * PAIRS, axis=1)
    sin = jnp.concatenate([sin_ref[...]] * PAIRS, axis=1)
    q_ref[...] = turn(nn(hidden, weight_ref[:, :D]), cos, sin).astype(BF16)
    k = turn(nn(hidden, weight_ref[:, D : 2 * D]), cos, sin).astype(BF16)
    v = nn(hidden, weight_ref[:, 2 * D :]).astype(BF16)

    @pl.when(j == 0)
    def _():
        kvl_ref[:, :D] = k
        kvl_ref[:, D:] = v

    @pl.when(j == 1)
    def _():
        kvs_ref[:, :D] = k
        kvs_ref[:, D:] = v


def project_call(place, tokens, mod, gain, weight, cos, sin, rows):
    tile = min(256, rows)
    tiles = rows // tile
    return pl.pallas_call(
        project_kernel,
        name="project",
        out_shape=(
            jax.ShapeDtypeStruct((SLOTS * rows, D), BF16),
            jax.ShapeDtypeStruct((SLOTS * rows, D), BF16),
            jax.ShapeDtypeStruct((rows, 2 * D), BF16),
            jax.ShapeDtypeStruct((rows, 2 * D), BF16),
        ),
        grid_spec=pltpu.PrefetchScalarGridSpec(
            num_scalar_prefetch=1,
            grid=(SLOTS, tiles),
            in_specs=[
                pl.BlockSpec((tile, D), lambda j, t, o: (o[j] * tiles + t, 0)),
                whole((8, 6 * D)),
                whole((1, D)),
                whole((D, 3 * D)),
                pl.BlockSpec((tile, PAIR), lambda j, t, o: (o[2] * tiles + t, 0)),
                pl.BlockSpec((tile, PAIR), lambda j, t, o: (o[2] * tiles + t, 0)),
            ],
            out_specs=[
                pl.BlockSpec((tile, D), lambda j, t, o: (j * tiles + t, 0)),
                pl.BlockSpec((tile, D), lambda j, t, o: (j * tiles + t, 0)),
                pl.BlockSpec((tile, 2 * D), lambda j, t, o: (t + j * (tiles - 1 - t), 0)),
                pl.BlockSpec((tile, 2 * D), lambda j, t, o: (j * t, 0)),
            ],
        ),
        compiler_params=pltpu.CompilerParams(vmem_limit_bytes=BIG),
        cost_estimate=cost(2 * SLOTS * rows * D * 3 * D, 14e6),
    )(place, tokens, mod, gain, weight, cos, sin)


def attend_slot(q, keys, values):
    outs, stats = [], []
    for head, qh in enumerate(heads_of(q)):
        scores = [nt(k, qh) for k in keys]
        top = jnp.max(scores[0], axis=0, keepdims=True)
        for s in scores[1:]:
            top = jnp.maximum(top, jnp.max(s, axis=0, keepdims=True))
        total, out = None, None
        for s, v in zip(scores, values):
            p = jnp.exp2((s - top) * (0.125 * LOG2E))
            part = col_sum(p)
            o = tn(v, p.astype(BF16))
            total = part if total is None else total + part
            out = o if out is None else out + o
        out = out[head * HEAD : (head + 1) * HEAD] / total
        outs.append(out)
        stats.append(top * (0.125 * LOG2E) + jnp.log2(total))
    return jnp.concatenate(outs, axis=0).T.astype(BF16), stats


def attend_kernel(ql, qs, ko, vo, kx, vx, ks, vs, out_ref, lse_ref):
    rows = ql.shape[0]
    out, stats = attend_slot(ql[...], [ko[...], kx[...]], [vo[...], vx[...]])
    out_ref[:rows, :] = out
    lse_ref[0, 0:1, :] = stats[0]
    lse_ref[0, 1:2, :] = stats[1]
    out, stats = attend_slot(qs[...], [ks[...]], [vs[...]])
    out_ref[rows:, :] = out
    lse_ref[0, 2:3, :] = stats[0]
    lse_ref[0, 3:4, :] = stats[1]


def pair_specs(rows):
    def at(n, block, base):
        return pl.BlockSpec((n, PAIR), lambda h: (block, base + h))

    return [
        at(rows, 0, 0),
        at(rows, 1, 0),
        at(rows, 0, 0),
        at(rows, 0, PAIRS),
        at(LEN - rows, 0, 0),
        at(LEN - rows, 0, PAIRS),
        at(SHORT, 0, 0),
        at(SHORT, 0, PAIRS),
    ]


def attend_call(q, kv_own, kv_other, kv_short, rows):
    return pl.pallas_call(
        attend_kernel,
        name="attend",
        grid=(PAIRS,),
        out_shape=(
            jax.ShapeDtypeStruct((SLOTS * rows, D), BF16),
            jax.ShapeDtypeStruct((PAIRS, 4, rows), F32),
        ),
        in_specs=pair_specs(rows),
        out_specs=(
            pl.BlockSpec((SLOTS * rows, PAIR), lambda h: (0, h)),
            pl.BlockSpec((1, 4, rows), lambda h: (h, 0, 0)),
        ),
        compiler_params=pltpu.CompilerParams(vmem_limit_bytes=BIG),
        cost_estimate=cost(16 * D * rows * (LEN + SHORT), 9e6, HEADS * rows * (LEN + SHORT)),
    )(q, q, kv_own, kv_own, kv_other, kv_other, kv_short, kv_short)


def attend_back_slot(q, keys, values, d_out, lse):
    d_keys, d_values = [None] * len(keys), [None] * len(keys)
    d_query = []
    q_heads, d_heads = heads_of(q), heads_of(d_out)
    for head in range(2):
        qh, dh = q_heads[head], d_heads[head]
        probs = [jnp.exp2(nt(k, qh) * (0.125 * LOG2E) - lse[head]) for k in keys]
        d_probs = [nt(v, dh) for v in values]
        inner = None
        for p, dp in zip(probs, d_probs):
            part = col_sum(p * dp)
            inner = part if inner is None else inner + part
        dq = None
        for i in range(len(keys)):
            d_scores = (probs[i] * (d_probs[i] - inner) * 0.125).astype(BF16)
            dv = nn(probs[i].astype(BF16), dh)
            dk = nn(d_scores, qh)
            part = tn(keys[i], d_scores)
            dq = part if dq is None else dq + part
            d_values[i] = dv if head == 0 else d_values[i] + dv
            d_keys[i] = dk if head == 0 else d_keys[i] + dk
        d_query.append(dq[head * HEAD : (head + 1) * HEAD])
    return jnp.concatenate(d_query, axis=0).T, d_keys, d_values


def attend_back_kernel(
    place, ql, qs, ko, vo, kx, vx, ks, vs, dol, dos, lse, cos, sin,
    dq_ref, dko, dvo, dkx, dvx, dks, dvs,
):
    rows = ql.shape[0]
    stats = lse[0]
    dq, dk, dv = attend_back_slot(
        ql[...], [ko[...], kx[...]], [vo[...], vx[...]], dol[...], [stats[0:1], stats[1:2]]
    )
    dq_ref[:rows, :] = turn_back(dq, cos[...], sin[...]).astype(BF16)
    dko[...] = dk[0]
    dvo[...] = dv[0]
    dkx[...] = dk[1].astype(BF16)
    dvx[...] = dv[1].astype(BF16)
    dq, dk, dv = attend_back_slot(
        qs[...], [ks[...]], [vs[...]], dos[...], [stats[2:3], stats[3:4]]
    )
    dq_ref[rows:, :] = turn_back(dq, cos[...], sin[...]).astype(BF16)
    dks[...] = dk[0]
    dvs[...] = dv[0]


def attend_back_call(place, q, kv_own, kv_other, kv_short, d_att, lse, cos, sin, rows):
    specs = [
        pl.BlockSpec(s.block_shape, partial(lambda m, h, o: m(h), s.index_map))
        for s in pair_specs(rows)
    ]
    other = LEN - rows
    return pl.pallas_call(
        attend_back_kernel,
        name="attend_back",
        out_shape=(
            jax.ShapeDtypeStruct((SLOTS * rows, D), BF16),
            jax.ShapeDtypeStruct((rows, D), F32),
            jax.ShapeDtypeStruct((rows, D), F32),
            jax.ShapeDtypeStruct((other, D), BF16),
            jax.ShapeDtypeStruct((other, D), BF16),
            jax.ShapeDtypeStruct((SHORT, D), F32),
            jax.ShapeDtypeStruct((SHORT, D), F32),
        ),
        grid_spec=pltpu.PrefetchScalarGridSpec(
            num_scalar_prefetch=1,
            grid=(PAIRS,),
            in_specs=specs
            + [
                pl.BlockSpec((rows, PAIR), lambda h, o: (0, h)),
                pl.BlockSpec((rows, PAIR), lambda h, o: (1, h)),
                pl.BlockSpec((1, 4, rows), lambda h, o: (h, 0, 0)),
                pl.BlockSpec((rows, PAIR), lambda h, o: (o[2], 0)),
                pl.BlockSpec((rows, PAIR), lambda h, o: (o[2], 0)),
            ],
            out_specs=[
                pl.BlockSpec((SLOTS * rows, PAIR), lambda h, o: (0, h)),
                pl.BlockSpec((rows, PAIR), lambda h, o: (0, h)),
                pl.BlockSpec((rows, PAIR), lambda h, o: (0, h)),
                pl.BlockSpec((other, PAIR), lambda h, o: (0, h)),
                pl.BlockSpec((other, PAIR), lambda h, o: (0, h)),
                pl.BlockSpec((SHORT, PAIR), lambda h, o: (0, h)),
                pl.BlockSpec((SHORT, PAIR), lambda h, o: (0, h)),
            ],
        ),
        compiler_params=pltpu.CompilerParams(vmem_limit_bytes=BIG),
        cost_estimate=cost(40 * D * rows * (LEN + SHORT), 16e6, HEADS * rows * (LEN + SHORT)),
    )(
        place, q, q, kv_own, kv_own, kv_other, kv_other, kv_short, kv_short,
        d_att, d_att, lse, cos, sin,
    )


def add_to(ref, value, first):
    @pl.when(first)
    def _():
        ref[...] = value

    @pl.when(jnp.logical_not(first))
    def _():
        ref[...] += value


def feed_kernel(
    order, tok_ref, att_ref, cot_ref, mod_ref, gain_ref, wo_ref, wu_ref, bu_ref, wd_ref, bd_ref,
    out_ref, dmid_ref, datt_ref, act_ref, dlow_ref, h_ref, dup_ref, dattn_ref,
    dmod_ref, dgain_ref, dbd_ref, dbu_ref,
):
    j, t = pl.program_id(0), pl.program_id(1)
    row = mod_ref[pl.ds(order[j], 1), :]
    gate1, shift2 = row[:, 2 * D : 3 * D], row[:, 3 * D : 4 * D]
    scale2, gate2 = row[:, 4 * D : 5 * D], row[:, 5 * D :]
    gain = gain_ref[...].astype(F32)
    attention = nn(att_ref[...], wo_ref[...])
    middle = tok_ref[...].astype(F32) + gate1 * attention
    center = middle - row_mean(middle)
    r = lax.rsqrt(row_mean(center * center) + EPSILON)
    xhat = center * r
    hidden = (xhat * gain * (1.0 + scale2) + shift2).astype(BF16)
    h_ref[...] = hidden
    dy = cot_ref[...].astype(F32)
    d_low = (gate2 * dy).astype(BF16)
    dlow_ref[...] = d_low
    lowered, d_hidden = None, None
    sums = []
    for f in range(0, FF, CHUNK):
        cols = slice(f, f + CHUNK)
        up = nn(hidden, wu_ref[:, cols]) + bu_ref[:, cols].astype(F32)
        d_act = nt(d_low, wd_ref[cols, :])
        square = up * up
        bend = jnp.tanh(up * (GELU_C + (GELU_C * 0.044715) * square))
        half = 0.5 * (1.0 + bend)
        act = (up * half).astype(BF16)
        slope = half + (0.5 * up) * (1.0 - bend * bend) * (
            GELU_C + (3 * GELU_C * 0.044715) * square
        )
        d_up = (d_act * slope).astype(BF16)
        act_ref[:, cols] = act
        dup_ref[:, cols] = d_up
        sums.append(col_sum(d_up.astype(F32)))
        low = nn(act, wd_ref[cols, :])
        dh = nt(d_up, wu_ref[:, cols])
        lowered = low if lowered is None else lowered + low
        d_hidden = dh if d_hidden is None else d_hidden + dh
    lowered = lowered + bd_ref[...].astype(F32)
    out_ref[...] = (middle + gate2 * lowered).astype(BF16)
    d_gate2 = col_sum(dy * lowered)
    d_shift2 = col_sum(d_hidden)
    hx = col_sum(d_hidden * xhat)
    e = d_hidden * (1.0 + scale2)
    fx = e * gain
    d_mid = dy + r * (fx - row_mean(fx) - xhat * row_mean(fx * xhat))
    dmid_ref[...] = d_mid
    d_gate1 = col_sum(d_mid * attention)
    d_attention = (gate1 * d_mid).astype(BF16)
    dattn_ref[...] = d_attention
    datt_ref[...] = nt(d_attention, wo_ref[...]).astype(BF16)
    first = jnp.logical_and(j == 0, t == 0)
    add_to(
        dmod_ref,
        jnp.concatenate(
            [d_gate1, d_shift2, hx * gain, d_gate2, jnp.zeros((4, D), F32)], axis=0
        )[None],
        t == 0,
    )
    add_to(dgain_ref, hx * (1.0 + scale2), first)
    add_to(dbd_ref, col_sum(d_low.astype(F32)), first)
    add_to(dbu_ref, jnp.concatenate(sums, axis=1), first)


def feed_call(place, tokens, att, cot, mod, gain, wo, wu, bu, wd, bd, rows):
    tile = min(256, rows)
    tiles = rows // tile

    def own(j, t, o):
        return (o[j] * tiles + t, 0)

    def sorted_(j, t, o):
        return (j * tiles + t, 0)

    n = SLOTS * rows
    return pl.pallas_call(
        feed_kernel,
        name="feed",
        out_shape=(
            jax.ShapeDtypeStruct((n, D), BF16),
            jax.ShapeDtypeStruct((n, D), F32),
            jax.ShapeDtypeStruct((n, D), BF16),
            jax.ShapeDtypeStruct((n, FF), BF16),
            jax.ShapeDtypeStruct((n, D), BF16),
            jax.ShapeDtypeStruct((n, D), BF16),
            jax.ShapeDtypeStruct((n, FF), BF16),
            jax.ShapeDtypeStruct((n, D), BF16),
            jax.ShapeDtypeStruct((SLOTS, 8, D), F32),
            jax.ShapeDtypeStruct((1, D), F32),
            jax.ShapeDtypeStruct((1, D), F32),
            jax.ShapeDtypeStruct((1, FF), F32),
        ),
        grid_spec=pltpu.PrefetchScalarGridSpec(
            num_scalar_prefetch=1,
            grid=(SLOTS, tiles),
            in_specs=[
                pl.BlockSpec((tile, D), own),
                pl.BlockSpec((tile, D), sorted_),
                pl.BlockSpec((tile, D), own),
                whole((8, 6 * D)),
                whole((1, D)),
                whole((D, D)),
                whole((D, FF)),
                whole((1, FF)),
                whole((FF, D)),
                whole((1, D)),
            ],
            out_specs=[
                pl.BlockSpec((tile, D), own),
                pl.BlockSpec((tile, D), sorted_),
                pl.BlockSpec((tile, D), sorted_),
                pl.BlockSpec((tile, FF), sorted_),
                pl.BlockSpec((tile, D), sorted_),
                pl.BlockSpec((tile, D), sorted_),
                pl.BlockSpec((tile, FF), sorted_),
                pl.BlockSpec((tile, D), sorted_),
                pl.BlockSpec((1, 8, D), lambda j, t, o: (o[j], 0, 0)),
                pl.BlockSpec((1, D), lambda j, t, o: (0, 0)),
                pl.BlockSpec((1, D), lambda j, t, o: (0, 0)),
                pl.BlockSpec((1, FF), lambda j, t, o: (0, 0)),
            ],
        ),
        compiler_params=pltpu.CompilerParams(vmem_limit_bytes=BIG),
        cost_estimate=cost(2 * n * D * (4 * FF + 2 * D), 40e6, n * FF),
    )(place, tokens, att, cot, mod, gain, wo, wu, bu, wd, bd)


def weight_kernel(place, left_ref, right_ref, other_ref, mine_ref):
    value = tn(left_ref[...], right_ref[...]).astype(BF16)

    @pl.when(pl.program_id(0) == 0)
    def _():
        other_ref[...] = value

    @pl.when(pl.program_id(0) == 1)
    def _():
        mine_ref[...] = value


def weight_call(place, left, right, tile, name):
    n, rows = left.shape
    half = right.shape[1] // 2
    tiles = rows // tile
    return pl.pallas_call(
        weight_kernel,
        name=name,
        out_shape=(jax.ShapeDtypeStruct((rows, half), BF16),) * 2,
        grid_spec=pltpu.PrefetchScalarGridSpec(
            num_scalar_prefetch=1,
            grid=(2, tiles),
            in_specs=[
                pl.BlockSpec((n, tile), lambda c, m, o: (0, m)),
                pl.BlockSpec((n, half), lambda c, m, o: (0, c * o[2] + (1 - c) * (1 - o[2]))),
            ],
            out_specs=[
                pl.BlockSpec((tile, half), lambda c, m, o: (m + c * (tiles - 1 - m), 0)),
                pl.BlockSpec((tile, half), lambda c, m, o: (c * m, 0)),
            ],
        ),
        compiler_params=pltpu.CompilerParams(vmem_limit_bytes=BIG),
        cost_estimate=cost(2 * n * rows * 2 * half, 2 * (n * rows + 2 * (n + rows) * half)),
    )(place, left, right)


def flip(index, bit):
    return index + bit - 2 * bit * ((index // bit) % 2)


def reduce_tiles(other, mine):
    s = lax.axis_index("seq")
    x, y, z = s % 2, (s // 2) % 2, s // 4
    rows, cols = mine.shape
    part = rows // 16
    came = lax.ppermute(other, "span", [(0, 1), (1, 0)])
    pair = (mine.astype(F32) + came.astype(F32)).reshape(2, 2, 2, 2, part, cols)
    along_x = [(i, flip(i, 1)) for i in range(16)]
    along_y = [(i, flip(i, 2)) for i in range(16)]

    def pick(array, axis, index):
        return lax.dynamic_index_in_dim(array, index, axis, keepdims=False)

    first, second = pair[0], pair[1]
    sent_a = lax.ppermute(pick(first, 2, 1 - x).astype(BF16), "seq", along_x)
    sent_b = lax.ppermute(pick(second, 1, 1 - y).astype(BF16), "seq", along_y)
    first = pick(first, 2, x) + sent_a.astype(F32)
    second = pick(second, 1, y) + sent_b.astype(F32)
    sent_a = lax.ppermute(pick(first, 1, 1 - y).astype(BF16), "seq", along_y)
    sent_b = lax.ppermute(pick(second, 1, 1 - x).astype(BF16), "seq", along_x)
    first = pick(first, 1, y) + sent_a.astype(F32)
    second = pick(second, 1, x) + sent_b.astype(F32)
    quarter = jnp.concatenate([first, second], axis=0)
    total = pick(quarter, 0, z)
    for step in range(1, 4):
        came = lax.ppermute(
            pick(quarter, 0, (z + step) % 4).astype(BF16),
            "seq",
            [(i, (i + 4 * step) % 16) for i in range(16)],
        )
        total = total + came.astype(F32)
    return total


def weight_gradient(place, left, right, tile, name):
    seq, span = lax.axis_size("seq"), lax.axis_size("span")
    if seq == 16 and span == 2:
        return reduce_tiles(*weight_call(place, left, right, tile, name))
    grad = tn(left, right)
    rows, cols = grad.shape
    shaped = grad.reshape(seq, rows // seq, span, cols // span).transpose(0, 2, 1, 3)
    return lax.psum_scatter(
        shaped.reshape(seq * span, rows // seq, cols // span),
        ("seq", "span"),
        scatter_dimension=0,
        tiled=True,
    )[0]


def join_kernel(place, dq_ref, dk_ref, dv_ref, ek_ref, ev_ref, sk_ref, sv_ref, cos, sin, out_ref):
    j, t = pl.program_id(0), pl.program_id(1)
    out_ref[:, :D] = dq_ref[...]
    wide_cos = jnp.concatenate([cos[...]] * PAIRS, axis=1)
    wide_sin = jnp.concatenate([sin[...]] * PAIRS, axis=1)

    @pl.when(j == 0)
    def _():
        dk = dk_ref[...] + ek_ref[...].astype(F32)
        out_ref[:, D : 2 * D] = turn_back(dk, wide_cos, wide_sin).astype(BF16)
        out_ref[:, 2 * D :] = (dv_ref[...] + ev_ref[...].astype(F32)).astype(BF16)

    @pl.when(j == 1)
    def _():
        out_ref[:, D:] = jnp.zeros((out_ref.shape[0], 2 * D), BF16)

    @pl.when(jnp.logical_and(j == 1, jnp.logical_and(t == 0, place[2] == 0)))
    def _():
        dk = turn_back(sk_ref[...], wide_cos[:SHORT], wide_sin[:SHORT])
        out_ref[:SHORT, D : 2 * D] = dk.astype(BF16)
        out_ref[:SHORT, 2 * D :] = sv_ref[...].astype(BF16)


def join_call(place, dq, dk, dv, ek, ev, sk, sv, cos, sin, rows):
    tile = min(256, rows)
    tiles = rows // tile

    def long(j, t, o):
        return (t + j * (tiles - 1 - t), 0)

    return pl.pallas_call(
        join_kernel,
        name="join",
        out_shape=jax.ShapeDtypeStruct((SLOTS * rows, 3 * D), BF16),
        grid_spec=pltpu.PrefetchScalarGridSpec(
            num_scalar_prefetch=1,
            grid=(SLOTS, tiles),
            in_specs=[pl.BlockSpec((tile, D), lambda j, t, o: (j * tiles + t, 0))]
            + [pl.BlockSpec((tile, D), long)] * 4
            + [whole((SHORT, D))] * 2
            + [pl.BlockSpec((tile, PAIR), lambda j, t, o: (o[2] * tiles + t, 0))] * 2,
            out_specs=pl.BlockSpec((tile, 3 * D), lambda j, t, o: (j * tiles + t, 0)),
        ),
        compiler_params=pltpu.CompilerParams(vmem_limit_bytes=BIG),
        cost_estimate=cost(1e7, 12e6),
    )(place, dq, dk, dv, ek, ev, sk, sv, cos, sin)


def last_kernel(
    order, tok_ref, dqkv_ref, dmid_ref, mod_ref, gain_ref, weight_ref,
    out_ref, dmod_ref, dgain_ref,
):
    j, t = pl.program_id(0), pl.program_id(1)
    scale = mod_ref[pl.ds(order[j], 1), :][:, D : 2 * D]
    gain = gain_ref[...].astype(F32)
    d_hidden = nt(dqkv_ref[...], weight_ref[...])
    x = tok_ref[...].astype(F32)
    center = x - row_mean(x)
    r = lax.rsqrt(row_mean(center * center) + EPSILON)
    xhat = center * r
    hx = col_sum(d_hidden * xhat)
    fx = d_hidden * (1.0 + scale) * gain
    out_ref[...] = dmid_ref[...] + r * (fx - row_mean(fx) - xhat * row_mean(fx * xhat))
    first = jnp.logical_and(j == 0, t == 0)
    add_to(
        dmod_ref,
        jnp.concatenate([col_sum(d_hidden), hx * gain, jnp.zeros((6, D), F32)], axis=0)[None],
        t == 0,
    )
    add_to(dgain_ref, hx * (1.0 + scale), first)


def last_call(place, tokens, dqkv, dmid, mod, gain, weight, rows):
    tile = min(256, rows)
    tiles = rows // tile

    def own(j, t, o):
        return (o[j] * tiles + t, 0)

    def sorted_(j, t, o):
        return (j * tiles + t, 0)

    n = SLOTS * rows
    return pl.pallas_call(
        last_kernel,
        name="last",
        out_shape=(
            jax.ShapeDtypeStruct((n, D), F32),
            jax.ShapeDtypeStruct((SLOTS, 8, D), F32),
            jax.ShapeDtypeStruct((1, D), F32),
        ),
        grid_spec=pltpu.PrefetchScalarGridSpec(
            num_scalar_prefetch=1,
            grid=(SLOTS, tiles),
            in_specs=[
                pl.BlockSpec((tile, D), own),
                pl.BlockSpec((tile, 3 * D), sorted_),
                pl.BlockSpec((tile, D), sorted_),
                whole((8, 6 * D)),
                whole((1, D)),
                whole((D, 3 * D)),
            ],
            out_specs=[
                pl.BlockSpec((tile, D), own),
                pl.BlockSpec((1, 8, D), lambda j, t, o: (o[j], 0, 0)),
                pl.BlockSpec((1, D), lambda j, t, o: (0, 0)),
            ],
        ),
        compiler_params=pltpu.CompilerParams(vmem_limit_bytes=BIG),
        cost_estimate=cost(2 * n * D * 3 * D, 18e6),
    )(place, tokens, dqkv, dmid, mod, gain, weight)


def from_peers(array, span):
    return [
        lax.ppermute(array, "span", [((i + step) % span, i) for i in range(span)])
        for step in range(1, span)
    ]


def gather_all(flat):
    seq, span = lax.axis_size("seq"), lax.axis_size("span")
    return lax.all_gather(flat, ("seq", "span"), axis=0).reshape(seq, span, flat.shape[0])


def shards(
    tokens, conditions, assignment, lengths, norm1_gain, ada_weight, ada_bias, qkv_weight,
    out_weight, norm2_gain, up_weight, up_bias, down_weight, down_bias, cotangent,
):
    slots, rows, _ = tokens.shape
    seq, span = lax.axis_size("seq"), lax.axis_size("span")
    seq_at, span_at = lax.axis_index("seq"), lax.axis_index("span")
    flat = slots * rows
    longest = (lengths[1] > lengths[0]).astype(jnp.int32)
    place = jnp.stack([longest, 1 - longest, span_at.astype(jnp.int32)])
    cos, sin = (jnp.asarray(table) for table in rotary(LEN))
    cond = conditions.astype(F32)
    asked = jnp.broadcast_to(assignment.astype(F32)[:, None], (slots, 128))
    own = jnp.concatenate([cond, asked, jnp.zeros((8 - 2 * slots, 128), F32)], axis=0)
    mod, table = modulation_call(own, ada_weight, ada_bias[None], seq)

    tokens2 = tokens.reshape(flat, D)
    gain1, gain2 = norm1_gain[None], norm2_gain[None]
    q, hidden1, kv_long, kv_tail = project_call(
        place, tokens2, mod, gain1, qkv_weight, cos, sin, rows
    )
    pieces = from_peers(kv_long, span)
    kv_other = pieces[0] if span == 2 else jnp.concatenate(pieces, axis=0)
    kv_short = kv_tail[:SHORT]
    sent = [lax.ppermute(kv_short, "span", [(0, i)]) for i in range(1, span)]
    kv_short = jnp.where(span_at == 0, kv_short, sum(sent[1:], sent[0]))
    att, lse = attend_call(q, kv_long, kv_other, kv_short, rows)
    (
        out, d_mid, d_att, act, d_low, hidden2, d_up, d_attention, d_mod2, d_gain2, d_bd, d_bu,
    ) = feed_call(
        place, tokens2, att, cotangent.reshape(flat, D), mod, gain2, out_weight, up_weight,
        up_bias[None], down_weight, down_bias[None], rows,
    )
    grad_down = weight_gradient(place, act, d_low, 768, "weight_down")
    grad_up = weight_gradient(place, hidden2, d_up, 256, "weight_up")
    grad_out = weight_gradient(place, att, d_attention, 768, "weight_out")
    early = gather_all(
        jnp.concatenate([d_mod2[:, :4].reshape(-1), d_gain2[0], d_bd[0], d_bu[0]])
    )

    dq, dk, dv, dkx, dvx, dks, dvs = attend_back_call(
        place, q, kv_long, kv_other, kv_short, d_att, lse, cos, sin, rows
    )
    ek = ev = None
    for step in range(1, span):
        back = [((i, (i + step) % span)) for i in range(span)]
        cut = slice((step - 1) * rows, step * rows)
        pk, pv = lax.ppermute((dkx[cut], dvx[cut]), "span", back)
        ek = pk if ek is None else (ek.astype(F32) + pk.astype(F32))
        ev = pv if ev is None else (ev.astype(F32) + pv.astype(F32))
    d_short = jnp.concatenate([dks, dvs], axis=1)
    for step in range(1, span):
        d_short = d_short + lax.ppermute(
            jnp.concatenate([dks, dvs], axis=1), "span", [(step, 0)]
        )
    d_qkv = join_call(
        place, dq, dk, dv, ek, ev, d_short[:, :D], d_short[:, D:], cos, sin, rows
    )
    grad_qkv = weight_gradient(place, hidden1, d_qkv, 384, "weight_qkv")
    grad_in, d_mod1, d_gain1 = last_call(
        place, tokens2, d_qkv, d_mid, mod, gain1, qkv_weight, rows
    )
    late = gather_all(jnp.concatenate([d_mod1[:, :2].reshape(-1), d_gain1[0]]))

    cut = slots * 4 * D
    mods2 = jnp.sum(early[:, :, :cut], axis=1).reshape(seq * slots, 4 * D)
    sums2 = jnp.sum(early[:, :, cut:], axis=(0, 1))
    cut = slots * 2 * D
    mods1 = jnp.sum(late[:, :, :cut], axis=1).reshape(seq * slots, 2 * D)
    gain1_sum = jnp.sum(late[:, :, cut:], axis=(0, 1))
    d_mods = jnp.concatenate([mods1, mods2], axis=1)
    grad_ada_bias = jnp.sum(d_mods, axis=0)
    cond_all = table[:, :slots].reshape(seq * slots, 128)
    assign_all = table[:, slots : 2 * slots, 0].reshape(seq * slots)
    number = jnp.arange(seq * slots, dtype=jnp.int32).astype(F32)
    picker = (assign_all[:, None] == number[None, :]).astype(F32)
    exact = partial(lax.dot_general, precision=HIGHEST, preferred_element_type=F32)
    cond_rows = exact(picker, cond_all, (((1,), (0,)), ((), ())))
    silu_low = jax.nn.silu(cond_rows).astype(BF16).astype(F32)
    ada_rows, ada_cols = 128 // seq, 6 * D // span
    grad_ada = exact(
        lax.dynamic_slice_in_dim(silu_low, seq_at * ada_rows, ada_rows, 1),
        lax.dynamic_slice_in_dim(d_mods, span_at * ada_cols, ada_cols, 1),
        (((0,), (0,)), ((), ())),
    )
    wanted = lax.dynamic_slice_in_dim(picker, seq_at * slots, slots, 1)
    own_mods = exact(wanted, d_mods, (((0,), (0,)), ((), ())))
    d_silu = exact(own_mods, ada_weight.astype(F32), (((1,), (1,)), ((), ())))
    grad_cond = jax.vjp(jax.nn.silu, cond)[1](d_silu)[0]
    return (
        out.reshape(tokens.shape),
        grad_in.reshape(tokens.shape),
        grad_cond,
        gain1_sum,
        grad_ada,
        grad_ada_bias,
        grad_qkv,
        grad_out,
        sums2[:D],
        grad_up,
        sums2[2 * D :],
        grad_down,
        sums2[D : 2 * D],
    )


def solution(mesh):
    data, table, one = P("seq", "span", None), P("seq", None), P("seq")
    tile = P("seq", "span")
    in_specs = (data, table, one, one) + (P(),) * 10 + (data,)
    out_specs = (data, data, table, P(), tile, P(), tile, tile, P(), tile, P(), tile, P())
    return jax.shard_map(shards, mesh=mesh, in_specs=in_specs, out_specs=out_specs, check_vma=False)
```

```python
from functools import partial

import jax
import jax.numpy as jnp
import numpy as np
from jax import lax
from jax.experimental import pallas as pl
from jax.experimental.pallas import tpu as pltpu
from jax.sharding import PartitionSpec as P

HEADS = 12
HEAD = 64
D = 768
FF = 3072
PAIR = 128
PAIRS = HEADS // 2
LEN = 1024
SHORT = 128
SLOTS = 2
CHUNK = 768
EPSILON = 1e-5
LOG2E = 1.4426950408889634
GELU_C = 0.7978845608028654
BIG = 62 << 20
MESH = pl.DeviceIdType.MESH
F32 = jnp.float32
BF16 = jnp.bfloat16
HIGHEST = lax.Precision.HIGHEST


def nn(a, b):
    return lax.dot_general(a, b, (((1,), (0,)), ((), ())), preferred_element_type=F32)


def nt(a, b):
    return lax.dot_general(a, b, (((1,), (1,)), ((), ())), preferred_element_type=F32)


def tn(a, b):
    return lax.dot_general(a, b, (((0,), (0,)), ((), ())), preferred_element_type=F32)


def whole(shape, buffers=1):
    return pl.BlockSpec(shape, lambda *_: (0,) * len(shape), pipeline_mode=pl.Buffered(buffers))


def cost(flops, bytes_accessed, transcendentals=0):
    return pl.CostEstimate(
        flops=int(flops), bytes_accessed=int(bytes_accessed), transcendentals=int(transcendentals)
    )


def col_sum(x):
    return jnp.sum(x, axis=0, keepdims=True)


def row_mean(x):
    return jnp.mean(x, axis=-1, keepdims=True)


def rotary(length):
    half = HEAD // 2
    freq = np.power(np.float32(10000.0), -np.arange(half, dtype=np.float32) / np.float32(half))
    angles = np.arange(length, dtype=np.float32)[:, None] * freq.astype(np.float32)[None, :]
    cos, sin = np.cos(angles), np.sin(angles)
    return (
        np.concatenate([cos] * 4, axis=1).astype(np.float32),
        np.concatenate([-sin, sin, -sin, sin], axis=1).astype(np.float32),
    )


def swap_halves(x):
    lane = lax.broadcasted_iota(jnp.int32, x.shape, 1)
    first = (lane & 32) == 0
    return jnp.where(first, pltpu.roll(x, x.shape[1] - 32, 1), pltpu.roll(x, 32, 1))


def turn(x, cos, sin):
    return x * cos + swap_halves(x) * sin


def turn_back(x, cos, sin):
    return x * cos - swap_halves(x) * sin


def heads_of(x):
    lane = lax.broadcasted_iota(jnp.int32, x.shape, 1)
    zero = jnp.zeros_like(x)
    return jnp.where(lane < HEAD, x, zero), jnp.where(lane < HEAD, zero, x)


def modulation_kernel(
    n, own_ref, weight_ref, bias_ref, mod_ref, table_ref, silu_ref, send, recv, local
):
    me = lax.axis_index("seq")
    barrier = pltpu.get_barrier_semaphore()
    for step in range(1, n):
        pl.semaphore_signal(
            barrier, inc=1, device_id={"seq": lax.rem(me + step, n)}, device_id_type=MESH
        )
    mine = pltpu.make_async_copy(own_ref, table_ref.at[me], local)
    mine.start()
    pl.semaphore_wait(barrier, n - 1)
    copies = []
    for step in range(1, n):
        copy = pltpu.make_async_remote_copy(
            src_ref=own_ref,
            dst_ref=table_ref.at[me],
            send_sem=send.at[step],
            recv_sem=recv.at[step],
            device_id={"seq": lax.rem(me + step, n)},
            device_id_type=MESH,
        )
        copy.start()
        copies.append(copy)
    mine.wait()
    for copy in copies:
        copy.wait()
    source = lax.broadcasted_iota(jnp.int32, (n, 128), 0).astype(F32) * SLOTS
    rows = []
    for slot in range(SLOTS):
        wanted = own_ref[SLOTS + slot : SLOTS + slot + 1, :]
        row = jnp.zeros((1, 128), F32)
        for k in range(SLOTS):
            row += col_sum(jnp.where(wanted == source + k, table_ref[:, k, :], 0.0))
        rows.append(row)
    cond = jnp.concatenate(rows + [jnp.zeros((8 - SLOTS, 128), F32)], axis=0)
    silu = (cond / (1.0 + jnp.exp(-cond))).astype(BF16)
    mod_ref[...] = nn(silu, weight_ref[...]) + bias_ref[...].astype(F32)
    for slot in range(SLOTS):
        wanted = table_ref[:, SLOTS + slot, :]
        rows = jnp.zeros((n, 128), F32)
        for k in range(SLOTS * n):
            row = table_ref[k // SLOTS, k % SLOTS : k % SLOTS + 1, :]
            rows += jnp.where(wanted == k, row, 0.0)
        silu_ref[slot] = (rows / (1.0 + jnp.exp(-rows))).astype(BF16).astype(F32)


def modulation_call(own, ada_weight, ada_bias, n):
    vmem = pl.BlockSpec(memory_space=pltpu.VMEM)
    return pl.pallas_call(
        partial(modulation_kernel, n),
        name="modulation",
        out_shape=(
            jax.ShapeDtypeStruct((8, 6 * D), F32),
            jax.ShapeDtypeStruct((n, 8, 128), F32),
            jax.ShapeDtypeStruct((SLOTS, n, 128), F32),
        ),
        in_specs=[vmem] * 3,
        out_specs=(vmem, vmem, vmem),
        scratch_shapes=[
            pltpu.SemaphoreType.DMA((n,)),
            pltpu.SemaphoreType.DMA((n,)),
            pltpu.SemaphoreType.DMA,
        ],
        compiler_params=pltpu.CompilerParams(
            collective_id=0, has_side_effects=True, vmem_limit_bytes=16 << 20
        ),
        cost_estimate=cost(1e7, 2e6),
    )(own, ada_weight, ada_bias)


def project_kernel(
    order, tok_ref, mod_ref, gain_ref, weight_ref, cos_ref, sin_ref,
    q_ref, h_ref, kvl_ref, kvs_ref, sorted_ref,
):
    j = pl.program_id(0)
    sorted_ref[...] = tok_ref[...]
    row = mod_ref[pl.ds(order[j], 1), :]
    shift, scale = row[:, :D], row[:, D : 2 * D]
    x = tok_ref[...].astype(F32)
    center = x - row_mean(x)
    xhat = center * lax.rsqrt(row_mean(center * center) + EPSILON)
    hidden = (xhat * gain_ref[...].astype(F32) * (1.0 + scale) + shift).astype(BF16)
    h_ref[...] = hidden
    cos = jnp.concatenate([cos_ref[...]] * PAIRS, axis=1)
    sin = jnp.concatenate([sin_ref[...]] * PAIRS, axis=1)
    q_ref[...] = turn(nn(hidden, weight_ref[:, :D]), cos, sin).astype(BF16)
    k = turn(nn(hidden, weight_ref[:, D : 2 * D]), cos, sin).astype(BF16)
    v = nn(hidden, weight_ref[:, 2 * D :]).astype(BF16)

    @pl.when(j == 0)
    def _():
        kvl_ref[:, :D] = k
        kvl_ref[:, D:] = v

    @pl.when(j == 1)
    def _():
        kvs_ref[:, :D] = k
        kvs_ref[:, D:] = v


def project_call(place, tokens, mod, gain, weight, cos, sin, rows):
    tile = min(256, rows)
    tiles = rows // tile
    return pl.pallas_call(
        project_kernel,
        name="project",
        out_shape=(
            jax.ShapeDtypeStruct((SLOTS * rows, D), BF16),
            jax.ShapeDtypeStruct((SLOTS * rows, D), BF16),
            jax.ShapeDtypeStruct((rows, 2 * D), BF16),
            jax.ShapeDtypeStruct((rows, 2 * D), BF16),
            jax.ShapeDtypeStruct((SLOTS * rows, D), BF16),
        ),
        grid_spec=pltpu.PrefetchScalarGridSpec(
            num_scalar_prefetch=1,
            grid=(SLOTS, tiles),
            in_specs=[
                pl.BlockSpec((tile, D), lambda j, t, o: (o[j] * tiles + t, 0)),
                whole((8, 6 * D)),
                whole((1, D)),
                whole((D, 3 * D)),
                pl.BlockSpec((tile, PAIR), lambda j, t, o: (o[2] * tiles + t, 0)),
                pl.BlockSpec((tile, PAIR), lambda j, t, o: (o[2] * tiles + t, 0)),
            ],
            out_specs=[
                pl.BlockSpec((tile, D), lambda j, t, o: (j * tiles + t, 0)),
                pl.BlockSpec((tile, D), lambda j, t, o: (j * tiles + t, 0)),
                pl.BlockSpec((tile, 2 * D), lambda j, t, o: (t + j * (tiles - 1 - t), 0)),
                pl.BlockSpec((tile, 2 * D), lambda j, t, o: (j * t, 0)),
                pl.BlockSpec((tile, D), lambda j, t, o: (j * tiles + t, 0)),
            ],
        ),
        compiler_params=pltpu.CompilerParams(vmem_limit_bytes=BIG),
        cost_estimate=cost(2 * SLOTS * rows * D * 3 * D, 14e6),
    )(place, tokens, mod, gain, weight, cos, sin)


def attend_slot(q, keys, values):
    outs, stats = [], []
    for head, qh in enumerate(heads_of(q)):
        scores = [nt(k, qh) for k in keys]
        top = jnp.max(scores[0], axis=0, keepdims=True)
        for s in scores[1:]:
            top = jnp.maximum(top, jnp.max(s, axis=0, keepdims=True))
        total, out = None, None
        for s, v in zip(scores, values):
            p = jnp.exp2((s - top) * (0.125 * LOG2E))
            part = col_sum(p)
            o = tn(v, p.astype(BF16))
            total = part if total is None else total + part
            out = o if out is None else out + o
        out = out[head * HEAD : (head + 1) * HEAD] / total
        outs.append(out)
        stats.append(top * (0.125 * LOG2E) + jnp.log2(total))
    return jnp.concatenate(outs, axis=0).T.astype(BF16), stats


def attend_kernel(ql, qs, ko, vo, kx, vx, ks, vs, out_ref, lse_ref):
    rows = ql.shape[0]
    out, stats = attend_slot(ql[...], [ko[...], kx[...]], [vo[...], vx[...]])
    out_ref[:rows, :] = out
    lse_ref[0, 0:1, :] = stats[0]
    lse_ref[0, 1:2, :] = stats[1]
    out, stats = attend_slot(qs[...], [ks[...]], [vs[...]])
    out_ref[rows:, :] = out
    lse_ref[0, 2:3, :] = stats[0]
    lse_ref[0, 3:4, :] = stats[1]


def pair_specs(rows):
    def at(n, block, base):
        return pl.BlockSpec((n, PAIR), lambda h: (block, base + h))

    return [
        at(rows, 0, 0),
        at(rows, 1, 0),
        at(rows, 0, 0),
        at(rows, 0, PAIRS),
        at(LEN - rows, 0, 0),
        at(LEN - rows, 0, PAIRS),
        at(SHORT, 0, 0),
        at(SHORT, 0, PAIRS),
    ]


def attend_call(q, kv_own, kv_other, kv_short, rows):
    return pl.pallas_call(
        attend_kernel,
        name="attend",
        grid=(PAIRS,),
        out_shape=(
            jax.ShapeDtypeStruct((SLOTS * rows, D), BF16),
            jax.ShapeDtypeStruct((PAIRS, 4, rows), F32),
        ),
        in_specs=pair_specs(rows),
        out_specs=(
            pl.BlockSpec((SLOTS * rows, PAIR), lambda h: (0, h)),
            pl.BlockSpec((1, 4, rows), lambda h: (h, 0, 0)),
        ),
        compiler_params=pltpu.CompilerParams(vmem_limit_bytes=BIG),
        cost_estimate=cost(16 * D * rows * (LEN + SHORT), 9e6, HEADS * rows * (LEN + SHORT)),
    )(q, q, kv_own, kv_own, kv_other, kv_other, kv_short, kv_short)


def attend_back_slot(q, keys, values, d_out, lse):
    d_keys, d_values = [None] * len(keys), [None] * len(keys)
    d_query = []
    q_heads, d_heads = heads_of(q), heads_of(d_out)
    for head in range(2):
        qh, dh = q_heads[head], d_heads[head]
        probs = [jnp.exp2(nt(k, qh) * (0.125 * LOG2E) - lse[head]) for k in keys]
        d_probs = [nt(v, dh) for v in values]
        inner = None
        for p, dp in zip(probs, d_probs):
            part = col_sum(p * dp)
            inner = part if inner is None else inner + part
        dq = None
        for i in range(len(keys)):
            d_scores = (probs[i] * (d_probs[i] - inner) * 0.125).astype(BF16)
            dv = nn(probs[i].astype(BF16), dh)
            dk = nn(d_scores, qh)
            part = tn(keys[i], d_scores)
            dq = part if dq is None else dq + part
            d_values[i] = dv if head == 0 else d_values[i] + dv
            d_keys[i] = dk if head == 0 else d_keys[i] + dk
        d_query.append(dq[head * HEAD : (head + 1) * HEAD])
    return jnp.concatenate(d_query, axis=0).T, d_keys, d_values


def attend_back_kernel(
    place, ql, qs, ko, vo, kx, vx, ks, vs, dol, dos, lse, cos, sin,
    dq_ref, dko, dvo, dkx, dvx, dks, dvs,
):
    rows = ql.shape[0]
    stats = lse[0]
    dq, dk, dv = attend_back_slot(
        ql[...], [ko[...], kx[...]], [vo[...], vx[...]], dol[...], [stats[0:1], stats[1:2]]
    )
    dq_ref[:rows, :] = turn_back(dq, cos[...], sin[...]).astype(BF16)
    dko[...] = dk[0]
    dvo[...] = dv[0]
    dkx[...] = dk[1].astype(BF16)
    dvx[...] = dv[1].astype(BF16)
    dq, dk, dv = attend_back_slot(
        qs[...], [ks[...]], [vs[...]], dos[...], [stats[2:3], stats[3:4]]
    )
    dq_ref[rows:, :] = turn_back(dq, cos[...], sin[...]).astype(BF16)
    dks[...] = dk[0]
    dvs[...] = dv[0]


def attend_back_call(place, q, kv_own, kv_other, kv_short, d_att, lse, cos, sin, rows):
    specs = [
        pl.BlockSpec(s.block_shape, partial(lambda m, h, o: m(h), s.index_map))
        for s in pair_specs(rows)
    ]
    other = LEN - rows
    return pl.pallas_call(
        attend_back_kernel,
        name="attend_back",
        out_shape=(
            jax.ShapeDtypeStruct((SLOTS * rows, D), BF16),
            jax.ShapeDtypeStruct((rows, D), F32),
            jax.ShapeDtypeStruct((rows, D), F32),
            jax.ShapeDtypeStruct((other, D), BF16),
            jax.ShapeDtypeStruct((other, D), BF16),
            jax.ShapeDtypeStruct((SHORT, D), F32),
            jax.ShapeDtypeStruct((SHORT, D), F32),
        ),
        grid_spec=pltpu.PrefetchScalarGridSpec(
            num_scalar_prefetch=1,
            grid=(PAIRS,),
            in_specs=specs
            + [
                pl.BlockSpec((rows, PAIR), lambda h, o: (0, h)),
                pl.BlockSpec((rows, PAIR), lambda h, o: (1, h)),
                pl.BlockSpec((1, 4, rows), lambda h, o: (h, 0, 0)),
                pl.BlockSpec((rows, PAIR), lambda h, o: (o[2], 0)),
                pl.BlockSpec((rows, PAIR), lambda h, o: (o[2], 0)),
            ],
            out_specs=[
                pl.BlockSpec((SLOTS * rows, PAIR), lambda h, o: (0, h)),
                pl.BlockSpec((rows, PAIR), lambda h, o: (0, h)),
                pl.BlockSpec((rows, PAIR), lambda h, o: (0, h)),
                pl.BlockSpec((other, PAIR), lambda h, o: (0, h)),
                pl.BlockSpec((other, PAIR), lambda h, o: (0, h)),
                pl.BlockSpec((SHORT, PAIR), lambda h, o: (0, h)),
                pl.BlockSpec((SHORT, PAIR), lambda h, o: (0, h)),
            ],
        ),
        compiler_params=pltpu.CompilerParams(vmem_limit_bytes=BIG),
        cost_estimate=cost(40 * D * rows * (LEN + SHORT), 16e6, HEADS * rows * (LEN + SHORT)),
    )(
        place, q, q, kv_own, kv_own, kv_other, kv_other, kv_short, kv_short,
        d_att, d_att, lse, cos, sin,
    )


def part_of(index, size):
    if isinstance(index, int):
        return pl.ds(index * size, size)
    return pl.ds(pl.multiple_of(index * size, size), size)


def add_to(ref, value, first):
    @pl.when(first)
    def _():
        ref[...] = value

    @pl.when(jnp.logical_not(first))
    def _():
        ref[...] += value


def feed_kernel(
    halves, order, tok_ref, att_ref, cot_ref, mod_ref, gain_ref, wo_ref, wu_ref, bu_ref, wd_ref, bd_ref,
    out_ref, dmid_ref, datt_ref, act_ref, dlow_ref, h_ref, dup_ref, dattn_ref,
    dmod_ref, dgain_ref, dbd_ref, dbu_ref,
):
    j, t = pl.program_id(0), pl.program_id(1)
    row = mod_ref[pl.ds(order[j], 1), :]
    gate1, shift2 = row[:, 2 * D : 3 * D], row[:, 3 * D : 4 * D]
    scale2, gate2 = row[:, 4 * D : 5 * D], row[:, 5 * D :]
    gain = gain_ref[...].astype(F32)
    attention = nn(att_ref[...], wo_ref[...])
    middle = tok_ref[...].astype(F32) + gate1 * attention
    center = middle - row_mean(middle)
    r = lax.rsqrt(row_mean(center * center) + EPSILON)
    xhat = center * r
    hidden = (xhat * gain * (1.0 + scale2) + shift2).astype(BF16)
    h_ref[...] = hidden
    dy = cot_ref[...].astype(F32)
    d_low = (gate2 * dy).astype(BF16)
    at = [h * order[2] + (1 - h) * (1 - order[2]) if halves else h for h in range(2)]
    for h in range(2):
        dlow_ref[:, part_of(at[h], D // 2)] = d_low[:, h * (D // 2) : (h + 1) * (D // 2)]
    lowered, d_hidden = None, None
    sums = []
    for f in range(0, FF, CHUNK):
        cols = slice(f, f + CHUNK)
        up = nn(hidden, wu_ref[:, cols]) + bu_ref[:, cols].astype(F32)
        d_act = nt(d_low, wd_ref[cols, :])
        square = up * up
        bend = jnp.tanh(up * (GELU_C + (GELU_C * 0.044715) * square))
        half = 0.5 * (1.0 + bend)
        act = (up * half).astype(BF16)
        slope = half + (0.5 * up) * (1.0 - bend * bend) * (
            GELU_C + (3 * GELU_C * 0.044715) * square
        )
        d_up = (d_act * slope).astype(BF16)
        act_ref[:, cols] = act
        place = at[f // (FF // 2)] * (FF // 2) + f % (FF // 2)
        dup_ref[:, pl.ds(pl.multiple_of(place, CHUNK) if halves else place, CHUNK)] = d_up
        sums.append(col_sum(d_up.astype(F32)))
        low = nn(act, wd_ref[cols, :])
        dh = nt(d_up, wu_ref[:, cols])
        lowered = low if lowered is None else lowered + low
        d_hidden = dh if d_hidden is None else d_hidden + dh
    lowered = lowered + bd_ref[...].astype(F32)
    out_ref[...] = (middle + gate2 * lowered).astype(BF16)
    d_gate2 = col_sum(dy * lowered)
    d_shift2 = col_sum(d_hidden)
    hx = col_sum(d_hidden * xhat)
    e = d_hidden * (1.0 + scale2)
    fx = e * gain
    d_mid = dy + r * (fx - row_mean(fx) - xhat * row_mean(fx * xhat))
    dmid_ref[...] = d_mid
    d_gate1 = col_sum(d_mid * attention)
    d_attention = (gate1 * d_mid).astype(BF16)
    for h in range(2):
        dattn_ref[:, part_of(at[h], D // 2)] = d_attention[:, h * (D // 2) : (h + 1) * (D // 2)]
    datt_ref[...] = nt(d_attention, wo_ref[...]).astype(BF16)
    first = jnp.logical_and(j == 0, t == 0)
    add_to(
        dmod_ref,
        jnp.concatenate(
            [d_gate1, d_shift2, hx * gain, d_gate2, jnp.zeros((4, D), F32)], axis=0
        )[None],
        t == 0,
    )
    add_to(dgain_ref, hx * (1.0 + scale2), first)
    add_to(dbd_ref, col_sum(d_low.astype(F32)), first)
    add_to(dbu_ref, jnp.concatenate(sums, axis=1), first)


def feed_call(halves, place, tokens, att, cot, mod, gain, wo, wu, bu, wd, bd, rows):
    tile = min(256, rows)
    tiles = rows // tile

    def own(j, t, o):
        return (o[j] * tiles + t, 0)

    def sorted_(j, t, o):
        return (j * tiles + t, 0)

    n = SLOTS * rows
    return pl.pallas_call(
        partial(feed_kernel, halves),
        name="feed",
        out_shape=(
            jax.ShapeDtypeStruct((n, D), BF16),
            jax.ShapeDtypeStruct((n, D), F32),
            jax.ShapeDtypeStruct((n, D), BF16),
            jax.ShapeDtypeStruct((n, FF), BF16),
            jax.ShapeDtypeStruct((n, D), BF16),
            jax.ShapeDtypeStruct((n, D), BF16),
            jax.ShapeDtypeStruct((n, FF), BF16),
            jax.ShapeDtypeStruct((n, D), BF16),
            jax.ShapeDtypeStruct((SLOTS, 8, D), F32),
            jax.ShapeDtypeStruct((1, D), F32),
            jax.ShapeDtypeStruct((1, D), F32),
            jax.ShapeDtypeStruct((1, FF), F32),
        ),
        grid_spec=pltpu.PrefetchScalarGridSpec(
            num_scalar_prefetch=1,
            grid=(SLOTS, tiles),
            in_specs=[
                pl.BlockSpec((tile, D), own),
                pl.BlockSpec((tile, D), sorted_),
                pl.BlockSpec((tile, D), own),
                whole((8, 6 * D)),
                whole((1, D)),
                whole((D, D)),
                whole((D, FF)),
                whole((1, FF)),
                whole((FF, D)),
                whole((1, D)),
            ],
            out_specs=[
                pl.BlockSpec((tile, D), own),
                pl.BlockSpec((tile, D), sorted_),
                pl.BlockSpec((tile, D), sorted_),
                pl.BlockSpec((tile, FF), sorted_),
                pl.BlockSpec((tile, D), sorted_),
                pl.BlockSpec((tile, D), sorted_),
                pl.BlockSpec((tile, FF), sorted_),
                pl.BlockSpec((tile, D), sorted_),
                pl.BlockSpec((1, 8, D), lambda j, t, o: (o[j], 0, 0)),
                pl.BlockSpec((1, D), lambda j, t, o: (0, 0)),
                pl.BlockSpec((1, D), lambda j, t, o: (0, 0)),
                pl.BlockSpec((1, FF), lambda j, t, o: (0, 0)),
            ],
        ),
        compiler_params=pltpu.CompilerParams(vmem_limit_bytes=BIG),
        cost_estimate=cost(2 * n * D * (4 * FF + 2 * D), 40e6, n * FF),
    )(place, tokens, att, cot, mod, gain, wo, wu, bu, wd, bd)


def weight_kernel(place, left_ref, right_ref, other_ref, mine_ref):
    value = tn(left_ref[...], right_ref[...]).astype(BF16)

    @pl.when(pl.program_id(0) == 0)
    def _():
        other_ref[...] = value

    @pl.when(pl.program_id(0) == 1)
    def _():
        mine_ref[...] = value


def weight_call(place, left, right, tile, name):
    n, rows = left.shape
    half = right.shape[1] // 2
    tiles = rows // tile
    return pl.pallas_call(
        weight_kernel,
        name=name,
        out_shape=(jax.ShapeDtypeStruct((rows, half), BF16),) * 2,
        grid_spec=pltpu.PrefetchScalarGridSpec(
            num_scalar_prefetch=1,
            grid=(2, tiles),
            in_specs=[
                pl.BlockSpec((n, tile), lambda c, m, o: (0, m)),
                pl.BlockSpec((n, half), lambda c, m, o: (0, c)),
            ],
            out_specs=[
                pl.BlockSpec((tile, half), lambda c, m, o: (m + c * (tiles - 1 - m), 0)),
                pl.BlockSpec((tile, half), lambda c, m, o: (c * m, 0)),
            ],
        ),
        compiler_params=pltpu.CompilerParams(vmem_limit_bytes=BIG),
        cost_estimate=cost(2 * n * rows * 2 * half, 2 * (n * rows + 2 * (n + rows) * half)),
    )(place, left, right)


def weight_gradient(left, right):
    seq, span = lax.axis_size("seq"), lax.axis_size("span")
    grad = tn(left, right)
    rows, cols = grad.shape
    shaped = grad.reshape(seq, rows // seq, span, cols // span).transpose(0, 2, 1, 3)
    return lax.psum_scatter(
        shaped.reshape(seq * span, rows // seq, cols // span),
        ("seq", "span"),
        scatter_dimension=0,
        tiled=True,
    )[0]


def join_kernel(place, dq_ref, dk_ref, dv_ref, ek_ref, ev_ref, sk_ref, sv_ref, cos, sin, out_ref):
    j, t = pl.program_id(0), pl.program_id(1)
    out_ref[:, :D] = dq_ref[...]
    wide_cos = jnp.concatenate([cos[...]] * PAIRS, axis=1)
    wide_sin = jnp.concatenate([sin[...]] * PAIRS, axis=1)

    @pl.when(j == 0)
    def _():
        dk = dk_ref[...] + ek_ref[...].astype(F32)
        out_ref[:, D : 2 * D] = turn_back(dk, wide_cos, wide_sin).astype(BF16)
        out_ref[:, 2 * D :] = (dv_ref[...] + ev_ref[...].astype(F32)).astype(BF16)

    @pl.when(j == 1)
    def _():
        out_ref[:, D:] = jnp.zeros((out_ref.shape[0], 2 * D), BF16)

    @pl.when(jnp.logical_and(j == 1, jnp.logical_and(t == 0, place[2] == 0)))
    def _():
        dk = turn_back(sk_ref[...], wide_cos[:SHORT], wide_sin[:SHORT])
        out_ref[:SHORT, D : 2 * D] = dk.astype(BF16)
        out_ref[:SHORT, 2 * D :] = sv_ref[...].astype(BF16)


def join_call(place, dq, dk, dv, ek, ev, sk, sv, cos, sin, rows):
    tile = min(256, rows)
    tiles = rows // tile

    def long(j, t, o):
        return (t + j * (tiles - 1 - t), 0)

    return pl.pallas_call(
        join_kernel,
        name="join",
        out_shape=jax.ShapeDtypeStruct((SLOTS * rows, 3 * D), BF16),
        grid_spec=pltpu.PrefetchScalarGridSpec(
            num_scalar_prefetch=1,
            grid=(SLOTS, tiles),
            in_specs=[pl.BlockSpec((tile, D), lambda j, t, o: (j * tiles + t, 0))]
            + [pl.BlockSpec((tile, D), long)] * 4
            + [whole((SHORT, D))] * 2
            + [pl.BlockSpec((tile, PAIR), lambda j, t, o: (o[2] * tiles + t, 0))] * 2,
            out_specs=pl.BlockSpec((tile, 3 * D), lambda j, t, o: (j * tiles + t, 0)),
        ),
        compiler_params=pltpu.CompilerParams(vmem_limit_bytes=BIG),
        cost_estimate=cost(1e7, 12e6),
    )(place, dq, dk, dv, ek, ev, sk, sv, cos, sin)


def last_kernel(
    order, tok_ref, dqkv_ref, dmid_ref, mod_ref, gain_ref, weight_ref,
    out_ref, dmod_ref, dgain_ref,
):
    j, t = pl.program_id(0), pl.program_id(1)
    scale = mod_ref[pl.ds(order[j], 1), :][:, D : 2 * D]
    gain = gain_ref[...].astype(F32)
    d_hidden = nt(dqkv_ref[...], weight_ref[...])
    x = tok_ref[...].astype(F32)
    center = x - row_mean(x)
    r = lax.rsqrt(row_mean(center * center) + EPSILON)
    xhat = center * r
    hx = col_sum(d_hidden * xhat)
    fx = d_hidden * (1.0 + scale) * gain
    out_ref[...] = dmid_ref[...] + r * (fx - row_mean(fx) - xhat * row_mean(fx * xhat))
    first = jnp.logical_and(j == 0, t == 0)
    add_to(
        dmod_ref,
        jnp.concatenate([col_sum(d_hidden), hx * gain, jnp.zeros((6, D), F32)], axis=0)[None],
        t == 0,
    )
    add_to(dgain_ref, hx * (1.0 + scale), first)


def last_call(place, tokens, dqkv, dmid, mod, gain, weight, rows):
    tile = min(256, rows)
    tiles = rows // tile

    def own(j, t, o):
        return (o[j] * tiles + t, 0)

    def sorted_(j, t, o):
        return (j * tiles + t, 0)

    n = SLOTS * rows
    return pl.pallas_call(
        last_kernel,
        name="last",
        out_shape=(
            jax.ShapeDtypeStruct((n, D), F32),
            jax.ShapeDtypeStruct((SLOTS, 8, D), F32),
            jax.ShapeDtypeStruct((1, D), F32),
        ),
        grid_spec=pltpu.PrefetchScalarGridSpec(
            num_scalar_prefetch=1,
            grid=(SLOTS, tiles),
            in_specs=[
                pl.BlockSpec((tile, D), own),
                pl.BlockSpec((tile, 3 * D), sorted_),
                pl.BlockSpec((tile, D), sorted_),
                whole((8, 6 * D)),
                whole((1, D)),
                whole((D, 3 * D)),
            ],
            out_specs=[
                pl.BlockSpec((tile, D), own),
                pl.BlockSpec((1, 8, D), lambda j, t, o: (o[j], 0, 0)),
                pl.BlockSpec((1, D), lambda j, t, o: (0, 0)),
            ],
        ),
        compiler_params=pltpu.CompilerParams(vmem_limit_bytes=BIG),
        cost_estimate=cost(2 * n * D * 3 * D, 18e6),
    )(place, tokens, dqkv, dmid, mod, gain, weight)


def flip(index, bit):
    return index + bit - 2 * bit * ((index // bit) % 2)


def add_low(a, b):
    return (a.astype(F32) + b.astype(F32)).astype(BF16)


def plane_peers():
    s, c = lax.axis_index("seq"), lax.axis_index("span")
    return [{"span": 1 - c}, {"seq": flip(s, 1)}, {"seq": flip(s, 2)}]


def line_peers():
    s = lax.axis_index("seq")
    return [{"seq": lax.rem(s + 4 * step, 16)} for step in range(1, 4)]


def greet(peers):
    barrier = pltpu.get_barrier_semaphore()
    for peer in peers:
        pl.semaphore_signal(barrier, inc=1, device_id=peer, device_id_type=MESH)
    pl.semaphore_wait(barrier, len(peers))


class Scatter:
    def __init__(self, send, recv, base, other=None, own=None, came0=None, a1=None, b1=None,
                 came2=None, came3=None):
        self.send, self.recv, self.base = send, recv, base
        self.other, self.own, self.came0 = other, own, came0
        self.a1, self.b1, self.came2, self.came3 = a1, b1, came2, came3
        s = lax.axis_index("seq")
        self.x, self.y, self.z = lax.rem(s, 2), lax.rem(s // 2, 2), s // 4
        self.core_peer, self.x_peer, self.y_peer = plane_peers()
        self.z_peers = line_peers()

    def copy(self, i):
        x, y, z = self.x, self.y, self.z
        if i == 0:
            src, dst, peer = self.other, self.came0, self.core_peer
        elif i == 1:
            src, dst, peer = self.own.at[0:2, :, 1 - x], self.a1, self.x_peer
        elif i == 2:
            src, dst, peer = self.own.at[2:4, 1 - y], self.b1, self.y_peer
        elif i == 3:
            src, dst, peer = self.a1.at[:, 1 - y], self.came2.at[0:2], self.y_peer
        elif i == 4:
            src, dst, peer = self.b1.at[:, 1 - x], self.came2.at[2:4], self.x_peer
        else:
            step = i - 4
            src, dst = self.came2.at[lax.rem(z + step, 4)], self.came3.at[step - 1]
            peer = self.z_peers[step - 1]
        return pltpu.make_async_remote_copy(
            src_ref=src,
            dst_ref=dst,
            send_sem=self.send.at[self.base + i],
            recv_sem=self.recv.at[self.base + i],
            device_id=peer,
            device_id_type=MESH,
        )

    def start(self, *which):
        for i in which:
            self.copy(i).start()

    def arrive(self, *which):
        for i in which:
            self.copy(i).wait_recv()

    def drain(self, *which):
        for i in which:
            self.copy(i).wait_send()

    def add0(self):
        self.arrive(0)

        def body(i, _):
            z, y, x = i // 4, lax.rem(i // 2, 2), lax.rem(i, 2)
            self.own[z, y, x] = add_low(self.own[z, y, x], self.came0[z, y, x])
            return 0

        lax.fori_loop(0, 16, body, 0)

    def add1(self, a_ref, b_ref):
        self.arrive(1, 2)

        def body(i, _):
            z, k = i // 2, lax.rem(i, 2)
            a_ref[z, k] = add_low(self.own[z, k, self.x], self.a1[z, k])
            b_ref[z, k] = add_low(self.own[2 + z, self.y, k], self.b1[z, k])
            return 0

        lax.fori_loop(0, 4, body, 0)

    def add2(self, out_ref):
        self.arrive(3, 4)

        def body(z, _):
            out_ref[z] = add_low(self.a1[z, self.y], self.came2[z])
            out_ref[2 + z] = add_low(self.b1[z, self.x], self.came2[2 + z])
            return 0

        lax.fori_loop(0, 2, body, 0)

    def total(self):
        self.arrive(5, 6, 7)
        total = self.came2[self.z].astype(F32)
        for step in range(3):
            total = total + self.came3[step].astype(F32)
        return total

    def scatter0(self):
        self.start(0)

    def scatter1(self):
        self.add0()
        self.start(1, 2)

    def scatter2(self):
        self.add1(self.a1, self.b1)
        self.start(3, 4)

    def scatter3(self):
        self.add2(self.came2)
        self.start(5, 6, 7)


def half_shape(rows, cols):
    return (4, 2, 2, rows, cols)


def scatter_scratch(rows, cols, first=True, middle=True, last=True):
    shapes = []
    if first:
        shapes += [half_shape(rows, cols)] * 2
    if first or middle:
        shapes += [(2, 2, rows, cols)] * 2
    if middle or last:
        shapes += [(4, rows, cols)]
    if last:
        shapes += [(3, rows, cols)]
    return [pltpu.VMEM(shape, BF16) for shape in shapes]


ANY = pl.BlockSpec(memory_space=pl.ANY)
DMA = pltpu.SemaphoreType.DMA


def weights_kernel(
    h_ref, dup_ref, att_ref, dattn_ref, other_ref, mine_ref,
    up_other, up_mine, out_other, out_mine, a_ref, b_ref,
    own, came0, a1, b1, send, recv, local,
):
    step = pl.program_id(0)
    down = Scatter(send, recv, 0, other=other_ref, own=own, came0=came0, a1=a1, b1=b1)
    load = pltpu.make_async_copy(mine_ref, own, local)

    @pl.when(step == 0)
    def _():
        load.start()
        greet(plane_peers())
        down.scatter0()

    @pl.when(step == 2)
    def _():
        load.wait()
        down.scatter1()

    @pl.when(step < 6)
    def _():
        value = tn(h_ref[...], dup_ref[...]).astype(BF16)

        @pl.when(step < 3)
        def _():
            up_other[...] = value

        @pl.when(step >= 3)
        def _():
            up_mine[...] = value

    @pl.when(step >= 6)
    def _():
        value = tn(att_ref[...], dattn_ref[...]).astype(BF16)

        @pl.when(step == 6)
        def _():
            out_other[...] = value

        @pl.when(step == 7)
        def _():
            out_mine[...] = value
            down.add1(a_ref, b_ref)
            down.drain(0, 1, 2)


def weights_call(hidden, d_up, att, d_attention, other, mine):
    n = hidden.shape[0]
    half = FF // 2
    rows, cols = D * 4 // 16, D // 2

    def clamp(s, low, high):
        return jnp.minimum(jnp.maximum(s, low), high)

    def fixed(shape):
        return pl.BlockSpec(shape, lambda s: (0,) * len(shape))

    handed = (2, 2, rows, cols)
    return pl.pallas_call(
        weights_kernel,
        name="weights",
        grid=(8,),
        out_shape=(
            jax.ShapeDtypeStruct((D, half), BF16),
            jax.ShapeDtypeStruct((D, half), BF16),
            jax.ShapeDtypeStruct((D, D // 2), BF16),
            jax.ShapeDtypeStruct((D, D // 2), BF16),
            jax.ShapeDtypeStruct(handed, BF16),
            jax.ShapeDtypeStruct(handed, BF16),
        ),
        in_specs=[
            pl.BlockSpec((n, 256), lambda s: (0, jnp.where(s < 6, lax.rem(s, 3), 2))),
            pl.BlockSpec((n, half), lambda s: (0, jnp.where(s < 3, 0, 1))),
            whole((n, D)),
            pl.BlockSpec((n, D // 2), lambda s: (0, jnp.where(s < 7, 0, 1))),
            ANY,
            ANY,
        ],
        out_specs=(
            pl.BlockSpec((256, half), lambda s: (clamp(s, 0, 2), 0)),
            pl.BlockSpec((256, half), lambda s: (clamp(s - 3, 0, 2), 0)),
            fixed((D, D // 2)),
            fixed((D, D // 2)),
            fixed(handed),
            fixed(handed),
        ),
        scratch_shapes=scatter_scratch(rows, cols, middle=False, last=False)
        + [DMA((3,)), DMA((3,)), DMA],
        compiler_params=pltpu.CompilerParams(
            collective_id=1, has_side_effects=True, vmem_limit_bytes=BIG
        ),
        cost_estimate=cost(2 * n * D * (FF + D), 30e6),
    )(
        hidden, d_up, att, d_attention,
        other.reshape(half_shape(rows, cols)), mine.reshape(half_shape(rows, cols)),
    )


def back_kernel(
    ql, qs, ko, vo, kx, vx, ks, vs, dol, dos, lse, cos_ref, sin_ref,
    a_in, b_in, up_other, up_mine, out_other, out_mine,
    dq_ref, dk_ref, dv_ref, down_ref, up_ref, out_ref,
    down_a, down_b, down2, down3,
    up_own, up_came, up_a, up_b, up2,
    out_own, out_came, out_a, out_b, out2,
    leave, come, keep_k, keep_v, keep_sk, keep_sv,
    send, recv, send_kv, recv_kv, local,
):
    step = pl.program_id(0)
    me = lax.axis_index("span")
    rows = ql.shape[0]
    down = Scatter(send, recv, 0, a1=down_a, b1=down_b, came2=down2, came3=down3)
    up = Scatter(
        send, recv, 8, other=up_other, own=up_own, came0=up_came, a1=up_a, b1=up_b, came2=up2
    )
    out = Scatter(
        send, recv, 13, other=out_other, own=out_own, came0=out_came, a1=out_a, b1=out_b,
        came2=out2,
    )
    loads = [
        pltpu.make_async_copy(src, dst, local.at[i])
        for i, (src, dst) in enumerate(
            [(a_in, down_a), (b_in, down_b), (up_mine, up_own), (out_mine, out_own)]
        )
    ]
    cos = cos_ref[pl.ds(pl.multiple_of(me * rows, rows), rows), :]
    sin = sin_ref[pl.ds(pl.multiple_of(me * rows, rows), rows), :]

    def kv_copy(pair):
        return pltpu.make_async_remote_copy(
            src_ref=leave.at[pair],
            dst_ref=come.at[pair],
            send_sem=send_kv.at[pair],
            recv_sem=recv_kv.at[pair],
            device_id={"span": 1 - me},
            device_id_type=MESH,
        )

    @pl.when(step == 0)
    def _():
        for load in loads:
            load.start()
        greet(plane_peers() + line_peers())
        up.scatter0()
        out.scatter0()
        loads[0].wait()
        loads[1].wait()
        down.start(3, 4)

    @pl.when(step == 1)
    def _():
        loads[2].wait()
        loads[3].wait()
        up.scatter1()
        out.scatter1()

    @pl.when(step == 3)
    def _():
        down.scatter3()

    @pl.when(step == 5)
    def _():
        up.scatter2()
        out.scatter2()

    @pl.when(step > 0)
    def _():
        pair = step - 1
        kv_copy(pair).wait_recv()
        dk = keep_k[...] + come[pair, :rows, :PAIR].astype(F32)
        dk_ref[:rows, :] = turn_back(dk, cos, sin).astype(BF16)
        dv = keep_v[...] + come[pair, :rows, PAIR:].astype(F32)
        dv_ref[:rows, :] = dv.astype(BF16)
        zero = jnp.zeros((SHORT, PAIR), F32)
        sk = keep_sk[...] + come[pair, rows:, :PAIR].astype(F32)
        sk = jnp.where(me == 0, turn_back(sk, cos[:SHORT], sin[:SHORT]), zero)
        sv = jnp.where(me == 0, keep_sv[...] + come[pair, rows:, PAIR:].astype(F32), zero)
        dk_ref[rows : rows + SHORT, :] = sk.astype(BF16)
        dv_ref[rows : rows + SHORT, :] = sv.astype(BF16)
        rest = jnp.zeros((rows - SHORT, PAIR), BF16)
        dk_ref[rows + SHORT :, :] = rest
        dv_ref[rows + SHORT :, :] = rest

    @pl.when(step < PAIRS)
    def _():
        stats = lse[0]
        dq, dk, dv = attend_back_slot(
            ql[...], [ko[...], kx[...]], [vo[...], vx[...]], dol[...], [stats[0:1], stats[1:2]]
        )
        dq_ref[:rows, :] = turn_back(dq, cos, sin).astype(BF16)
        keep_k[...] = dk[0]
        keep_v[...] = dv[0]
        leave[step, :rows, :PAIR] = dk[1].astype(BF16)
        leave[step, :rows, PAIR:] = dv[1].astype(BF16)
        dq, dk, dv = attend_back_slot(
            qs[...], [ks[...]], [vs[...]], dos[...], [stats[2:3], stats[3:4]]
        )
        dq_ref[rows:, :] = turn_back(dq, cos, sin).astype(BF16)
        keep_sk[...] = dk[0]
        keep_sv[...] = dv[0]
        leave[step, rows:, :PAIR] = dk[0].astype(BF16)
        leave[step, rows:, PAIR:] = dv[0].astype(BF16)
        kv_copy(step).start()

    @pl.when(step == PAIRS)
    def _():
        down_ref[...] = down.total()
        up.add2(up_ref)
        out.add2(out_ref)
        down.drain(3, 4, 5, 6, 7)
        up.drain(0, 1, 2, 3, 4)
        out.drain(0, 1, 2, 3, 4)
        for pair in range(PAIRS):
            kv_copy(pair).wait_send()


def back_call(q, kv_own, kv_other, kv_short, d_att, lse, cos, sin, handed, up, out, rows):
    last = PAIRS - 1

    def late(s):
        return jnp.minimum(s, last)

    def early(s):
        return jnp.maximum(s - 1, 0)

    def fixed(shape):
        return pl.BlockSpec(shape, lambda s: (0,) * len(shape))

    specs = [
        pl.BlockSpec(s.block_shape, partial(lambda m, h: m(late(h)), s.index_map))
        for s in pair_specs(rows)
    ]
    n = SLOTS * rows
    dr, dc = FF // 16, D // 2
    ur, uc = D // 16, FF // 2
    wr, wc = D // 16, D // 2
    return pl.pallas_call(
        back_kernel,
        name="attend_back",
        grid=(PAIRS + 1,),
        out_shape=(
            jax.ShapeDtypeStruct((n, D), BF16),
            jax.ShapeDtypeStruct((n, D), BF16),
            jax.ShapeDtypeStruct((n, D), BF16),
            jax.ShapeDtypeStruct((dr, dc), F32),
            jax.ShapeDtypeStruct((4, ur, uc), BF16),
            jax.ShapeDtypeStruct((4, wr, wc), BF16),
        ),
        in_specs=specs
        + [
            pl.BlockSpec((rows, PAIR), lambda s: (0, late(s))),
            pl.BlockSpec((rows, PAIR), lambda s: (1, late(s))),
            pl.BlockSpec((1, 4, rows), lambda s: (late(s), 0, 0)),
            whole((LEN, PAIR)),
            whole((LEN, PAIR)),
        ]
        + [ANY] * 6,
        out_specs=(
            pl.BlockSpec((n, PAIR), lambda s: (0, late(s))),
            pl.BlockSpec((n, PAIR), lambda s: (0, early(s))),
            pl.BlockSpec((n, PAIR), lambda s: (0, early(s))),
            fixed((dr, dc)),
            fixed((4, ur, uc)),
            fixed((4, wr, wc)),
        ),
        scratch_shapes=[
            pltpu.VMEM((2, 2, dr, dc), BF16),
            pltpu.VMEM((2, 2, dr, dc), BF16),
            pltpu.VMEM((4, dr, dc), BF16),
            pltpu.VMEM((3, dr, dc), BF16),
        ]
        + scatter_scratch(ur, uc, last=False)
        + scatter_scratch(wr, wc, last=False)
        + [
            pltpu.VMEM((PAIRS, rows + SHORT, 2 * PAIR), BF16),
            pltpu.VMEM((PAIRS, rows + SHORT, 2 * PAIR), BF16),
            pltpu.VMEM((rows, PAIR), F32),
            pltpu.VMEM((rows, PAIR), F32),
            pltpu.VMEM((SHORT, PAIR), F32),
            pltpu.VMEM((SHORT, PAIR), F32),
            DMA((18,)),
            DMA((18,)),
            DMA((PAIRS,)),
            DMA((PAIRS,)),
            DMA((4,)),
        ],
        compiler_params=pltpu.CompilerParams(
            collective_id=2, has_side_effects=True, vmem_limit_bytes=BIG
        ),
        cost_estimate=cost(40 * D * rows * (LEN + SHORT), 30e6, HEADS * rows * (LEN + SHORT)),
    )(
        q, q, kv_own, kv_own, kv_other, kv_other, kv_short, kv_short, d_att, d_att, lse, cos, sin,
        *handed, *(w.reshape(half_shape(ur, uc)) for w in up),
        *(w.reshape(half_shape(wr, wc)) for w in out),
    )


BLOCKS = 3
TILES = 4


def end_kernel(
    tok_ref, dmid_ref, hidden_ref, mod_ref, gain_ref, weight_ref, flag_ref,
    dq_any, dk_any, dv_any, up_any, out_any,
    grad_ref, gqkv_ref, gup_ref, gout_ref, late_ref,
    dqkv, hidden_t,
    up2, up3, out2, out3,
    other, own, came0, a1, b1, came2, came3,
    sums, sums_came, sums_all, late_came,
    send, recv, send_late, recv_late, local,
):
    step = pl.program_id(0)
    s, me = lax.axis_index("seq"), lax.axis_index("span")
    up = Scatter(send, recv, 0, came2=up2, came3=up3)
    out = Scatter(send, recv, 8, came2=out2, came3=out3)
    blocks = [
        Scatter(
            send, recv, 16 + 8 * b, other=other.at[b], own=own.at[b], came0=came0.at[b],
            a1=a1.at[b], b1=b1.at[b], came2=came2.at[b], came3=came3.at[b],
        )
        for b in range(BLOCKS)
    ]
    loads = [
        pltpu.make_async_copy(src, dst, local.at[i])
        for i, (src, dst) in enumerate(
            [(up_any, up2), (out_any, out2)]
            + [
                (a, dqkv.at[:, pl.ds(k * D, D)])
                for k, a in enumerate([dq_any, dk_any, dv_any])
            ]
        )
    ]
    wide = 3 * D // 2 // BLOCKS

    def product(core, b):
        start = pl.multiple_of(core * (3 * D // 2) + b * wide, 128)
        value = nn(hidden_t[...], dqkv[:, pl.ds(start, wide)]).astype(BF16)
        return value.reshape(half_shape(D // 16, wide))

    def late_copy(k):
        if k == 0:
            src, dst, peer = sums, sums_came, {"span": 1 - me}
        else:
            src, dst, peer = sums_all, late_came.at[s], {"seq": lax.rem(s + k, 16)}
        return pltpu.make_async_remote_copy(
            src_ref=src,
            dst_ref=dst,
            send_sem=send_late.at[k],
            recv_sem=recv_late.at[k],
            device_id=peer,
            device_id_type=MESH,
        )

    @pl.when(step == 0)
    def _():
        for load in loads:
            load.start()
        hidden_t[...] = hidden_ref[...].T
        greet([{"span": 1 - me}] + [{"seq": lax.rem(s + k, 16)} for k in range(1, 16)])
        loads[0].wait()
        loads[1].wait()
        up.start(5, 6, 7)
        out.start(5, 6, 7)
        for load in loads[2:]:
            load.wait()
        sums[...] = jnp.zeros_like(sums)

    for b in range(BLOCKS):
        @pl.when(step == b)
        def _():
            other[b] = product(1 - me, b)
            blocks[b].scatter0()
            if b > 0:
                blocks[b - 1].scatter1()
            own[b] = product(me, b)

    @pl.when(step == 3)
    def _():
        blocks[2].scatter1()
        blocks[0].scatter2()

    @pl.when(step == 4)
    def _():
        blocks[1].scatter2()

    @pl.when(step == 5)
    def _():
        blocks[2].scatter2()
        blocks[0].scatter3()

    @pl.when(step == 6)
    def _():
        blocks[1].scatter3()

    @pl.when(step >= BLOCKS)
    def _():
        t = step - BLOCKS
        j = t // 2
        size = tok_ref.shape[0]
        scale = mod_ref[pl.ds(j, 1), :][:, D : 2 * D]
        gain = gain_ref[...].astype(F32)
        start = pl.multiple_of(t * size, size)
        d_hidden = nt(dqkv[pl.ds(start, size), :], weight_ref[...])
        x = tok_ref[...].astype(F32)
        center = x - row_mean(x)
        r = lax.rsqrt(row_mean(center * center) + EPSILON)
        xhat = center * r
        hx = col_sum(d_hidden * xhat)
        fx = d_hidden * (1.0 + scale) * gain
        grad_ref[...] = dmid_ref[...] + r * (fx - row_mean(fx) - xhat * row_mean(fx * xhat))
        flag = flag_ref[...]
        mine = jnp.where(j == 0, flag, 1.0 - flag)
        shift = col_sum(d_hidden)
        none = jnp.zeros((3, D), F32)
        first, second = mine == 0.0, mine != 0.0
        zero = jnp.zeros((1, D), F32)
        sums[...] += jnp.concatenate(
            [
                jnp.where(first, shift, zero), jnp.where(first, hx * gain, zero),
                jnp.where(second, shift, zero), jnp.where(second, hx * gain, zero),
                hx * (1.0 + scale), none,
            ],
            axis=0,
        )

    @pl.when(step == BLOCKS + TILES - 1)
    def _():
        late_copy(0).start()
        blocks[2].scatter3()
        late_copy(0).wait_recv()
        sums_all[...] = sums[...] + sums_came[...]
        for k in range(1, 16):
            late_copy(k).start()
        late_came[s] = sums_all[...]
        gup_ref[...] = up.total()
        gout_ref[...] = out.total()
        for b in range(BLOCKS):
            gqkv_ref[:, b * wide : (b + 1) * wide] = blocks[b].total()
        up.drain(5, 6, 7)
        out.drain(5, 6, 7)
        for block in blocks:
            block.drain(*range(8))
        for k in range(16):
            if k > 0:
                late_copy(k).wait_recv()
            late_copy(k).wait_send()
        late_ref[...] = late_came[...]


def end_call(tokens, d_mid, hidden, mods, gain, weight, flag, dq, dk, dv, up2, out2, rows):
    n = SLOTS * rows
    size = n // TILES
    r = D // 16
    wide = 3 * D // 2 // BLOCKS

    def tile(s):
        return (jnp.maximum(s - BLOCKS, 0), 0)

    def fixed(shape):
        return pl.BlockSpec(shape, lambda s: (0,) * len(shape))

    def each(shape):
        return pltpu.VMEM((BLOCKS,) + shape, BF16)

    return pl.pallas_call(
        end_kernel,
        name="end",
        grid=(BLOCKS + TILES,),
        out_shape=(
            jax.ShapeDtypeStruct((n, D), F32),
            jax.ShapeDtypeStruct((r, 3 * D // 2), F32),
            jax.ShapeDtypeStruct((r, FF // 2), F32),
            jax.ShapeDtypeStruct((r, D // 2), F32),
            jax.ShapeDtypeStruct((16, 8, D), F32),
        ),
        in_specs=[
            pl.BlockSpec((size, D), tile),
            pl.BlockSpec((size, D), tile),
            whole((n, D)),
            whole((8, 6 * D)),
            whole((1, D)),
            whole((D, 3 * D)),
            whole((1, D)),
        ]
        + [ANY] * 5,
        out_specs=(
            pl.BlockSpec((size, D), tile),
            fixed((r, 3 * D // 2)),
            fixed((r, FF // 2)),
            fixed((r, D // 2)),
            fixed((16, 8, D)),
        ),
        scratch_shapes=[
            pltpu.VMEM((n, 3 * D), BF16),
            pltpu.VMEM((D, n), BF16),
            pltpu.VMEM((4, r, FF // 2), BF16),
            pltpu.VMEM((3, r, FF // 2), BF16),
            pltpu.VMEM((4, r, D // 2), BF16),
            pltpu.VMEM((3, r, D // 2), BF16),
            each(half_shape(r, wide)),
            each(half_shape(r, wide)),
            each(half_shape(r, wide)),
            each((2, 2, r, wide)),
            each((2, 2, r, wide)),
            each((4, r, wide)),
            each((3, r, wide)),
            pltpu.VMEM((8, D), F32),
            pltpu.VMEM((8, D), F32),
            pltpu.VMEM((8, D), F32),
            pltpu.VMEM((16, 8, D), F32),
            DMA((16 + 8 * BLOCKS,)),
            DMA((16 + 8 * BLOCKS,)),
            DMA((16,)),
            DMA((16,)),
            DMA((5,)),
        ],
        compiler_params=pltpu.CompilerParams(
            collective_id=3, has_side_effects=True, vmem_limit_bytes=BIG
        ),
        cost_estimate=cost(4 * n * D * 3 * D, 30e6),
    )(tokens, d_mid, hidden, mods, gain, weight, flag, dq, dk, dv, up2, out2)


def exact(left, right, over):
    return lax.dot_general(
        left, right, (over, ((), ())), precision=HIGHEST, preferred_element_type=F32
    )


def condition_kernel(
    place, early_ref, late_ref, table_ref, silu_ref, weight_ref, cond_ref,
    ada_ref, bias_ref, gcond_ref, gain1_ref, gain2_ref, bd_ref, bu_ref,
):
    seq = late_ref.shape[0]
    me, s = place[2], place[3]
    early = early_ref[...].reshape(seq, 2, 16, D)
    early = early[:, 0] + early[:, 1]
    late = late_ref[...]
    mods = []
    for k in range(SLOTS):
        mods.append(
            [late[:, 2 * k], late[:, 2 * k + 1]] + [early[:, 4 * k + b] for b in range(4)]
        )
    gain1_ref[...] = col_sum(late[:, 4])
    gain2_ref[...] = col_sum(early[:, 8])
    bd_ref[...] = col_sum(early[:, 9])
    for f in range(4):
        bu_ref[:, f * D : (f + 1) * D] = col_sum(early[:, 10 + f])
    own = [jnp.zeros((8, D), F32)] * 6
    row = lax.broadcasted_iota(jnp.int32, (8, seq), 0)
    wanted = (s * SLOTS + row).astype(F32)
    for k in range(SLOTS):
        asked = table_ref[:, SLOTS + k, :].T[:8]
        chosen = jnp.where(jnp.logical_and(asked == wanted, row < SLOTS), 1.0, 0.0)
        for b in range(6):
            own[b] = own[b] + exact(chosen, mods[k][b], ((1,), (0,)))
    d_silu = jnp.zeros((8, 128), F32)
    for b in range(6):
        cols = slice(b * D, (b + 1) * D)
        bias_ref[:, cols] = col_sum(mods[0][b]) + col_sum(mods[1][b])
        d_silu += exact(own[b], weight_ref[:, cols].astype(F32), ((1,), (1,)))
    v = cond_ref[...]
    sig = 1.0 / (1.0 + jnp.exp(-v))
    gcond_ref[...] = d_silu * (sig * (1.0 + v * (1.0 - sig)))
    rows = 128 // seq
    pick = lax.broadcasted_iota(jnp.int32, (rows, 128), 1) == (
        s * rows + lax.broadcasted_iota(jnp.int32, (rows, 128), 0)
    )
    pick = jnp.where(pick, 1.0, 0.0)
    silu = [exact(pick, silu_ref[k], ((1,), (1,))) for k in range(SLOTS)]
    for b in range(3):
        total = jnp.zeros((rows, D), F32)
        for k in range(SLOTS):
            block = jnp.where(me == 0, mods[k][b], mods[k][3 + b])
            total += exact(silu[k], block, ((1,), (0,)))
        ada_ref[:, b * D : (b + 1) * D] = total


def condition_call(place, early, late, table, silu, ada_weight, cond):
    seq = late.shape[0]

    def all_of(a):
        return whole(a.shape)

    outs = ((128 // seq, 3 * D), (1, 6 * D), (8, 128), (1, D), (1, D), (1, D), (1, FF))
    return pl.pallas_call(
        condition_kernel,
        name="condition",
        out_shape=tuple(jax.ShapeDtypeStruct(o, F32) for o in outs),
        grid_spec=pltpu.PrefetchScalarGridSpec(
            num_scalar_prefetch=1,
            grid=(1,),
            in_specs=[all_of(a) for a in (early, late, table, silu, ada_weight, cond)],
            out_specs=[pl.BlockSpec(o, lambda i, p: (0, 0)) for o in outs],
        ),
        compiler_params=pltpu.CompilerParams(vmem_limit_bytes=32 << 20),
        cost_estimate=cost(1e7, 4e6),
    )(place, early, late, table, silu, ada_weight, cond)


def from_peers(array, span):
    return [
        lax.ppermute(array, "span", [((i + step) % span, i) for i in range(span)])
        for step in range(1, span)
    ]


def gather_all(flat):
    seq, span = lax.axis_size("seq"), lax.axis_size("span")
    return lax.all_gather(flat, ("seq", "span"), axis=0).reshape(seq, span, flat.shape[0])


def shards(
    tokens, conditions, assignment, lengths, norm1_gain, ada_weight, ada_bias, qkv_weight,
    out_weight, norm2_gain, up_weight, up_bias, down_weight, down_bias, cotangent,
):
    slots, rows, _ = tokens.shape
    seq, span = lax.axis_size("seq"), lax.axis_size("span")
    seq_at, span_at = lax.axis_index("seq"), lax.axis_index("span")
    flat = slots * rows
    longest = (lengths[1] > lengths[0]).astype(jnp.int32)
    place = jnp.stack(
        [longest, 1 - longest, span_at.astype(jnp.int32), seq_at.astype(jnp.int32)]
    )
    fast = seq == 16 and span == 2
    cos, sin = (jnp.asarray(table) for table in rotary(LEN))
    cond = conditions.astype(F32)
    asked = jnp.broadcast_to(assignment.astype(F32)[:, None], (slots, 128))
    own = jnp.concatenate([cond, asked, jnp.zeros((8 - 2 * slots, 128), F32)], axis=0)
    mod, table, silu_all = modulation_call(own, ada_weight, ada_bias[None], seq)

    tokens2 = tokens.reshape(flat, D)
    gain1, gain2 = norm1_gain[None], norm2_gain[None]
    q, hidden1, kv_long, kv_tail, tokens_sorted = project_call(
        place, tokens2, mod, gain1, qkv_weight, cos, sin, rows
    )
    pieces = from_peers(kv_long, span)
    kv_other = pieces[0] if span == 2 else jnp.concatenate(pieces, axis=0)
    kv_short = kv_tail[:SHORT]
    sent = [lax.ppermute(kv_short, "span", [(0, i)]) for i in range(1, span)]
    kv_short = jnp.where(span_at == 0, kv_short, sum(sent[1:], sent[0]))
    att, lse = attend_call(q, kv_long, kv_other, kv_short, rows)
    (
        out, d_mid, d_att, act, d_low, hidden2, d_up, d_attention, d_mod2, d_gain2, d_bd, d_bu,
    ) = feed_call(
        fast, place, tokens2, att, cotangent.reshape(flat, D), mod, gain2, out_weight, up_weight,
        up_bias[None], down_weight, down_bias[None], rows,
    )
    if fast:
        payload = jnp.concatenate(
            [
                d_mod2[:, :4].reshape(8, D), d_gain2, d_bd, d_bu.reshape(4, D),
                jnp.zeros((2, D), F32),
            ],
            axis=0,
        )
        early = lax.all_gather(payload, ("seq", "span"), axis=0)
        down = weight_call(place, act, d_low, 768, "weight_down")
        uo, um, wo, wm, *handed = weights_call(hidden2, d_up, att, d_attention, *down)
        dq, dk, dv, grad_down, up2, out2 = back_call(
            q, kv_long, kv_other, kv_short, d_att, lse, cos, sin, handed, (uo, um), (wo, wm), rows
        )
        swapped = longest == 1
        mods = jnp.where(swapped, mod[jnp.array([1, 0, 2, 3, 4, 5, 6, 7])], mod)
        flag = jnp.broadcast_to(longest.astype(F32), (1, D))
        grad_in, grad_qkv, grad_up, grad_out, late = end_call(
            tokens_sorted, d_mid, hidden1, mods, gain1, qkv_weight, flag, dq, dk, dv, up2, out2,
            rows,
        )
        grad_in = grad_in.reshape(tokens.shape)
        grad_in = jnp.where(swapped, grad_in[::-1], grad_in)
        padded = jnp.concatenate([cond, jnp.zeros((8 - slots, 128), F32)], axis=0)
        grad_ada, ada_bias_sum, grad_cond, gain1_sum, gain2_sum, bd_sum, bu_sum = condition_call(
            place, early, late, table, silu_all, ada_weight, padded
        )
        return (
            out.reshape(tokens.shape), grad_in, grad_cond[:slots], gain1_sum[0], grad_ada,
            ada_bias_sum[0], grad_qkv, grad_out, gain2_sum[0], grad_up, bu_sum[0], grad_down,
            bd_sum[0],
        )
    grad_down = weight_gradient(act, d_low)
    grad_up = weight_gradient(hidden2, d_up)
    grad_out = weight_gradient(att, d_attention)
    early = gather_all(
        jnp.concatenate([d_mod2[:, :4].reshape(-1), d_gain2[0], d_bd[0], d_bu[0]])
    )

    dq, dk, dv, dkx, dvx, dks, dvs = attend_back_call(
        place, q, kv_long, kv_other, kv_short, d_att, lse, cos, sin, rows
    )
    ek = ev = None
    for step in range(1, span):
        back = [((i, (i + step) % span)) for i in range(span)]
        cut = slice((step - 1) * rows, step * rows)
        pk, pv = lax.ppermute((dkx[cut], dvx[cut]), "span", back)
        ek = pk if ek is None else (ek.astype(F32) + pk.astype(F32))
        ev = pv if ev is None else (ev.astype(F32) + pv.astype(F32))
    d_short = jnp.concatenate([dks, dvs], axis=1)
    for step in range(1, span):
        d_short = d_short + lax.ppermute(
            jnp.concatenate([dks, dvs], axis=1), "span", [(step, 0)]
        )
    d_qkv = join_call(
        place, dq, dk, dv, ek, ev, d_short[:, :D], d_short[:, D:], cos, sin, rows
    )
    grad_qkv = weight_gradient(hidden1, d_qkv)
    grad_in, d_mod1, d_gain1 = last_call(
        place, tokens2, d_qkv, d_mid, mod, gain1, qkv_weight, rows
    )
    late = gather_all(jnp.concatenate([d_mod1[:, :2].reshape(-1), d_gain1[0]]))

    cut = slots * 4 * D
    mods2 = jnp.sum(early[:, :, :cut], axis=1).reshape(seq * slots, 4 * D)
    sums2 = jnp.sum(early[:, :, cut:], axis=(0, 1))
    cut = slots * 2 * D
    mods1 = jnp.sum(late[:, :, :cut], axis=1).reshape(seq * slots, 2 * D)
    gain1_sum = jnp.sum(late[:, :, cut:], axis=(0, 1))
    d_mods = jnp.concatenate([mods1, mods2], axis=1)
    grad_ada_bias = jnp.sum(d_mods, axis=0)
    cond_all = table[:, :slots].reshape(seq * slots, 128)
    assign_all = table[:, slots : 2 * slots, 0].reshape(seq * slots)
    number = jnp.arange(seq * slots, dtype=jnp.int32).astype(F32)
    picker = (assign_all[:, None] == number[None, :]).astype(F32)
    exact = partial(lax.dot_general, precision=HIGHEST, preferred_element_type=F32)
    cond_rows = exact(picker, cond_all, (((1,), (0,)), ((), ())))
    silu_low = jax.nn.silu(cond_rows).astype(BF16).astype(F32)
    ada_rows, ada_cols = 128 // seq, 6 * D // span
    grad_ada = exact(
        lax.dynamic_slice_in_dim(silu_low, seq_at * ada_rows, ada_rows, 1),
        lax.dynamic_slice_in_dim(d_mods, span_at * ada_cols, ada_cols, 1),
        (((0,), (0,)), ((), ())),
    )
    wanted = lax.dynamic_slice_in_dim(picker, seq_at * slots, slots, 1)
    own_mods = exact(wanted, d_mods, (((0,), (0,)), ((), ())))
    d_silu = exact(own_mods, ada_weight.astype(F32), (((1,), (1,)), ((), ())))
    grad_cond = jax.vjp(jax.nn.silu, cond)[1](d_silu)[0]
    return (
        out.reshape(tokens.shape),
        grad_in.reshape(tokens.shape),
        grad_cond,
        gain1_sum,
        grad_ada,
        grad_ada_bias,
        grad_qkv,
        grad_out,
        sums2[:D],
        grad_up,
        sums2[2 * D :],
        grad_down,
        sums2[D : 2 * D],
    )


def solution(mesh):
    data, table, one = P("seq", "span", None), P("seq", None), P("seq")
    tile = P("seq", "span")
    in_specs = (data, table, one, one) + (P(),) * 10 + (data,)
    out_specs = (data, data, table, P(), tile, P(), tile, tile, P(), tile, P(), tile, P())
    return jax.shard_map(shards, mesh=mesh, in_specs=in_specs, out_specs=out_specs, check_vma=False)
```

```python
from functools import partial

import jax
import jax.numpy as jnp
import numpy as np
from jax import lax
from jax.experimental import pallas as pl
from jax.experimental.pallas import tpu as pltpu
from jax.sharding import PartitionSpec as P

HEADS = 12
HEAD = 64
D = 768
FF = 3072
PAIR = 128
PAIRS = HEADS // 2
LEN = 1024
SHORT = 128
SLOTS = 2
CHUNK = 768
EPSILON = 1e-5
LOG2E = 1.4426950408889634
GELU_C = 0.7978845608028654
BIG = 62 << 20
MESH = pl.DeviceIdType.MESH
F32 = jnp.float32
BF16 = jnp.bfloat16
HIGHEST = lax.Precision.HIGHEST


def nn(a, b):
    return lax.dot_general(a, b, (((1,), (0,)), ((), ())), preferred_element_type=F32)


def nt(a, b):
    return lax.dot_general(a, b, (((1,), (1,)), ((), ())), preferred_element_type=F32)


def tn(a, b):
    return lax.dot_general(a, b, (((0,), (0,)), ((), ())), preferred_element_type=F32)


def whole(shape, buffers=1):
    return pl.BlockSpec(shape, lambda *_: (0,) * len(shape), pipeline_mode=pl.Buffered(buffers))


def cost(flops, bytes_accessed, transcendentals=0):
    return pl.CostEstimate(
        flops=int(flops), bytes_accessed=int(bytes_accessed), transcendentals=int(transcendentals)
    )


def col_sum(x):
    return jnp.sum(x, axis=0, keepdims=True)


def wide_row(ref):
    return ref[...].astype(F32).reshape(1, ref.shape[0])


def row_mean(x):
    return jnp.mean(x, axis=-1, keepdims=True)


def rotary(length):
    half = HEAD // 2
    freq = np.power(np.float32(10000.0), -np.arange(half, dtype=np.float32) / np.float32(half))
    angles = np.arange(length, dtype=np.float32)[:, None] * freq.astype(np.float32)[None, :]
    cos, sin = np.cos(angles), np.sin(angles)
    return (
        np.concatenate([cos] * 4, axis=1).astype(np.float32),
        np.concatenate([-sin, sin, -sin, sin], axis=1).astype(np.float32),
    )


def swap_halves(x):
    lane = lax.broadcasted_iota(jnp.int32, x.shape, 1)
    first = (lane & 32) == 0
    return jnp.where(first, pltpu.roll(x, x.shape[1] - 32, 1), pltpu.roll(x, 32, 1))


def turn(x, cos, sin):
    return x * cos + swap_halves(x) * sin


def turn_back(x, cos, sin):
    return x * cos - swap_halves(x) * sin


def slot_of(lengths, j):
    long = jnp.where(lengths[1] > lengths[0], 1, 0)
    return j + long - 2 * j * long


def heads_of(x):
    lane = lax.broadcasted_iota(jnp.int32, x.shape, 1)
    zero = jnp.zeros_like(x)
    return jnp.where(lane < HEAD, x, zero), jnp.where(lane < HEAD, zero, x)


def modulation_kernel(
    n, cond_ref, assign_ref, weight_ref, bias_ref, mod_ref, table_ref, silu_ref,
    own_ref, send, recv, local,
):
    me = lax.axis_index("seq")
    asked = [jnp.full((1, 128), assign_ref[k].astype(F32)) for k in range(SLOTS)]
    own_ref[...] = jnp.concatenate(
        [cond_ref[...].astype(F32)] + asked + [jnp.zeros((8 - 2 * SLOTS, 128), F32)], axis=0
    )
    barrier = pltpu.get_barrier_semaphore()
    for step in range(1, n):
        pl.semaphore_signal(
            barrier, inc=1, device_id={"seq": lax.rem(me + step, n)}, device_id_type=MESH
        )
    mine = pltpu.make_async_copy(own_ref, table_ref.at[me], local)
    mine.start()
    pl.semaphore_wait(barrier, n - 1)
    copies = []
    for step in range(1, n):
        copy = pltpu.make_async_remote_copy(
            src_ref=own_ref,
            dst_ref=table_ref.at[me],
            send_sem=send.at[step],
            recv_sem=recv.at[step],
            device_id={"seq": lax.rem(me + step, n)},
            device_id_type=MESH,
        )
        copy.start()
        copies.append(copy)
    mine.wait()
    for copy in copies:
        copy.wait()
    source = lax.broadcasted_iota(jnp.int32, (n, 128), 0).astype(F32) * SLOTS
    rows = []
    for slot in range(SLOTS):
        wanted = own_ref[SLOTS + slot : SLOTS + slot + 1, :]
        row = jnp.zeros((1, 128), F32)
        for k in range(SLOTS):
            row += col_sum(jnp.where(wanted == source + k, table_ref[:, k, :], 0.0))
        rows.append(row)
    cond = jnp.concatenate(rows + [jnp.zeros((8 - SLOTS, 128), F32)], axis=0)
    silu = (cond / (1.0 + jnp.exp(-cond))).astype(BF16)
    mod_ref[...] = nn(silu, weight_ref[...]) + bias_ref[...].astype(F32).reshape(1, 6 * D)
    for slot in range(SLOTS):
        wanted = table_ref[:, SLOTS + slot, :]
        rows = jnp.zeros((n, 128), F32)
        for k in range(SLOTS * n):
            row = table_ref[k // SLOTS, k % SLOTS : k % SLOTS + 1, :]
            rows += jnp.where(wanted == k, row, 0.0)
        silu_ref[slot] = (rows / (1.0 + jnp.exp(-rows))).astype(BF16).astype(F32)


def modulation_call(cond, assignment, ada_weight, ada_bias, n):
    vmem = pl.BlockSpec(memory_space=pltpu.VMEM)
    return pl.pallas_call(
        partial(modulation_kernel, n),
        name="modulation",
        out_shape=(
            jax.ShapeDtypeStruct((8, 6 * D), F32),
            jax.ShapeDtypeStruct((n, 8, 128), F32),
            jax.ShapeDtypeStruct((SLOTS, n, 128), F32),
        ),
        in_specs=[vmem, pl.BlockSpec(memory_space=pltpu.SMEM), vmem, vmem],
        out_specs=(vmem, vmem, vmem),
        scratch_shapes=[
            pltpu.VMEM((8, 128), F32),
            pltpu.SemaphoreType.DMA((n,)),
            pltpu.SemaphoreType.DMA((n,)),
            pltpu.SemaphoreType.DMA,
        ],
        compiler_params=pltpu.CompilerParams(
            collective_id=0, has_side_effects=True, vmem_limit_bytes=16 << 20
        ),
        cost_estimate=cost(1e7, 2e6),
    )(cond, assignment, ada_weight, ada_bias)


def project_kernel(
    order, tok_ref, mod_ref, gain_ref, weight_ref, cos_ref, sin_ref,
    q_ref, h_ref, kvl_ref, kvs_ref,
):
    j = pl.program_id(0)
    row = mod_ref[pl.ds(slot_of(order, j), 1), :]
    shift, scale = row[:, :D], row[:, D : 2 * D]
    x = tok_ref[...].astype(F32)
    center = x - row_mean(x)
    xhat = center * lax.rsqrt(row_mean(center * center) + EPSILON)
    hidden = (xhat * wide_row(gain_ref) * (1.0 + scale) + shift).astype(BF16)
    h_ref[...] = hidden
    cos = jnp.concatenate([cos_ref[...]] * PAIRS, axis=1)
    sin = jnp.concatenate([sin_ref[...]] * PAIRS, axis=1)
    q_ref[...] = turn(nn(hidden, weight_ref[:, :D]), cos, sin).astype(BF16)
    k = turn(nn(hidden, weight_ref[:, D : 2 * D]), cos, sin).astype(BF16)
    v = nn(hidden, weight_ref[:, 2 * D :]).astype(BF16)

    @pl.when(j == 0)
    def _():
        kvl_ref[:, :D] = k
        kvl_ref[:, D:] = v

    @pl.when(j == 1)
    def _():
        kvs_ref[:, :D] = k
        kvs_ref[:, D:] = v


def project_call(place, tokens, mod, gain, weight, cos, sin, rows):
    tile = min(256, rows)
    tiles = rows // tile
    return pl.pallas_call(
        project_kernel,
        name="project",
        out_shape=(
            jax.ShapeDtypeStruct((SLOTS * rows, D), BF16),
            jax.ShapeDtypeStruct((SLOTS * rows, D), BF16),
            jax.ShapeDtypeStruct((rows, 2 * D), BF16),
            jax.ShapeDtypeStruct((rows, 2 * D), BF16),
        ),
        grid_spec=pltpu.PrefetchScalarGridSpec(
            num_scalar_prefetch=1,
            grid=(SLOTS, tiles),
            in_specs=[
                pl.BlockSpec((tile, D), lambda j, t, o: (slot_of(o, j) * tiles + t, 0)),
                whole((8, 6 * D)),
                whole((D,)),
                whole((D, 3 * D)),
                pl.BlockSpec((tile, PAIR), lambda j, t, o: (o[2] * tiles + t, 0)),
                pl.BlockSpec((tile, PAIR), lambda j, t, o: (o[2] * tiles + t, 0)),
            ],
            out_specs=[
                pl.BlockSpec((tile, D), lambda j, t, o: (j * tiles + t, 0)),
                pl.BlockSpec((tile, D), lambda j, t, o: (j * tiles + t, 0)),
                pl.BlockSpec((tile, 2 * D), lambda j, t, o: (t + j * (tiles - 1 - t), 0)),
                pl.BlockSpec((tile, 2 * D), lambda j, t, o: (j * t, 0)),
            ],
        ),
        compiler_params=pltpu.CompilerParams(vmem_limit_bytes=BIG),
        cost_estimate=cost(2 * SLOTS * rows * D * 3 * D, 14e6),
    )(place, tokens, mod, gain, weight, cos, sin)


def attend_slot(q, keys, values):
    outs, stats = [], []
    for head, qh in enumerate(heads_of(q)):
        scores = [nt(k, qh) for k in keys]
        top = jnp.max(scores[0], axis=0, keepdims=True)
        for s in scores[1:]:
            top = jnp.maximum(top, jnp.max(s, axis=0, keepdims=True))
        total, out = None, None
        for s, v in zip(scores, values):
            p = jnp.exp2((s - top) * (0.125 * LOG2E))
            part = col_sum(p)
            o = tn(v, p.astype(BF16))
            total = part if total is None else total + part
            out = o if out is None else out + o
        out = out[head * HEAD : (head + 1) * HEAD] / total
        outs.append(out)
        stats.append(top * (0.125 * LOG2E) + jnp.log2(total))
    return jnp.concatenate(outs, axis=0).T.astype(BF16), stats


def attend_kernel(ql, qs, ko, vo, kx, vx, ks, vs, out_ref, lse_ref):
    rows = ql.shape[0]
    out, stats = attend_slot(ql[...], [ko[...], kx[...]], [vo[...], vx[...]])
    out_ref[:rows, :] = out
    lse_ref[0, 0:1, :] = stats[0]
    lse_ref[0, 1:2, :] = stats[1]
    out, stats = attend_slot(qs[...], [ks[...]], [vs[...]])
    out_ref[rows:, :] = out
    lse_ref[0, 2:3, :] = stats[0]
    lse_ref[0, 3:4, :] = stats[1]


def pair_specs(rows):
    def at(n, block, base):
        return pl.BlockSpec((n, PAIR), lambda h: (block, base + h))

    return [
        at(rows, 0, 0),
        at(rows, 1, 0),
        at(rows, 0, 0),
        at(rows, 0, PAIRS),
        at(LEN - rows, 0, 0),
        at(LEN - rows, 0, PAIRS),
        at(SHORT, 0, 0),
        at(SHORT, 0, PAIRS),
    ]


def attend_call(q, kv_own, kv_other, kv_short, rows):
    return pl.pallas_call(
        attend_kernel,
        name="attend",
        grid=(PAIRS,),
        out_shape=(
            jax.ShapeDtypeStruct((SLOTS * rows, D), BF16),
            jax.ShapeDtypeStruct((PAIRS, 4, rows), F32),
        ),
        in_specs=pair_specs(rows),
        out_specs=(
            pl.BlockSpec((SLOTS * rows, PAIR), lambda h: (0, h)),
            pl.BlockSpec((1, 4, rows), lambda h: (h, 0, 0)),
        ),
        compiler_params=pltpu.CompilerParams(vmem_limit_bytes=BIG),
        cost_estimate=cost(16 * D * rows * (LEN + SHORT), 9e6, HEADS * rows * (LEN + SHORT)),
    )(q, q, kv_own, kv_own, kv_other, kv_other, kv_short, kv_short)


def attend_back_slot(q, keys, values, d_out, lse):
    d_keys, d_values = [None] * len(keys), [None] * len(keys)
    d_query = []
    q_heads, d_heads = heads_of(q), heads_of(d_out)
    for head in range(2):
        qh, dh = q_heads[head], d_heads[head]
        probs = [jnp.exp2(nt(k, qh) * (0.125 * LOG2E) - lse[head]) for k in keys]
        d_probs = [nt(v, dh) for v in values]
        inner = None
        for p, dp in zip(probs, d_probs):
            part = col_sum(p * dp)
            inner = part if inner is None else inner + part
        dq = None
        for i in range(len(keys)):
            d_scores = (probs[i] * (d_probs[i] - inner) * 0.125).astype(BF16)
            dv = nn(probs[i].astype(BF16), dh)
            dk = nn(d_scores, qh)
            part = tn(keys[i], d_scores)
            dq = part if dq is None else dq + part
            d_values[i] = dv if head == 0 else d_values[i] + dv
            d_keys[i] = dk if head == 0 else d_keys[i] + dk
        d_query.append(dq[head * HEAD : (head + 1) * HEAD])
    return jnp.concatenate(d_query, axis=0).T, d_keys, d_values


def attend_back_kernel(
    place, ql, qs, ko, vo, kx, vx, ks, vs, dol, dos, lse, cos, sin,
    dq_ref, dko, dvo, dkx, dvx, dks, dvs,
):
    rows = ql.shape[0]
    stats = lse[0]
    dq, dk, dv = attend_back_slot(
        ql[...], [ko[...], kx[...]], [vo[...], vx[...]], dol[...], [stats[0:1], stats[1:2]]
    )
    dq_ref[:rows, :] = turn_back(dq, cos[...], sin[...]).astype(BF16)
    dko[...] = dk[0]
    dvo[...] = dv[0]
    dkx[...] = dk[1].astype(BF16)
    dvx[...] = dv[1].astype(BF16)
    dq, dk, dv = attend_back_slot(
        qs[...], [ks[...]], [vs[...]], dos[...], [stats[2:3], stats[3:4]]
    )
    dq_ref[rows:, :] = turn_back(dq, cos[...], sin[...]).astype(BF16)
    dks[...] = dk[0]
    dvs[...] = dv[0]


def attend_back_call(place, q, kv_own, kv_other, kv_short, d_att, lse, cos, sin, rows):
    specs = [
        pl.BlockSpec(s.block_shape, partial(lambda m, h, o: m(h), s.index_map))
        for s in pair_specs(rows)
    ]
    other = LEN - rows
    return pl.pallas_call(
        attend_back_kernel,
        name="attend_back",
        out_shape=(
            jax.ShapeDtypeStruct((SLOTS * rows, D), BF16),
            jax.ShapeDtypeStruct((rows, D), F32),
            jax.ShapeDtypeStruct((rows, D), F32),
            jax.ShapeDtypeStruct((other, D), BF16),
            jax.ShapeDtypeStruct((other, D), BF16),
            jax.ShapeDtypeStruct((SHORT, D), F32),
            jax.ShapeDtypeStruct((SHORT, D), F32),
        ),
        grid_spec=pltpu.PrefetchScalarGridSpec(
            num_scalar_prefetch=1,
            grid=(PAIRS,),
            in_specs=specs
            + [
                pl.BlockSpec((rows, PAIR), lambda h, o: (0, h)),
                pl.BlockSpec((rows, PAIR), lambda h, o: (1, h)),
                pl.BlockSpec((1, 4, rows), lambda h, o: (h, 0, 0)),
                pl.BlockSpec((rows, PAIR), lambda h, o: (o[2], 0)),
                pl.BlockSpec((rows, PAIR), lambda h, o: (o[2], 0)),
            ],
            out_specs=[
                pl.BlockSpec((SLOTS * rows, PAIR), lambda h, o: (0, h)),
                pl.BlockSpec((rows, PAIR), lambda h, o: (0, h)),
                pl.BlockSpec((rows, PAIR), lambda h, o: (0, h)),
                pl.BlockSpec((other, PAIR), lambda h, o: (0, h)),
                pl.BlockSpec((other, PAIR), lambda h, o: (0, h)),
                pl.BlockSpec((SHORT, PAIR), lambda h, o: (0, h)),
                pl.BlockSpec((SHORT, PAIR), lambda h, o: (0, h)),
            ],
        ),
        compiler_params=pltpu.CompilerParams(vmem_limit_bytes=BIG),
        cost_estimate=cost(40 * D * rows * (LEN + SHORT), 16e6, HEADS * rows * (LEN + SHORT)),
    )(
        place, q, q, kv_own, kv_own, kv_other, kv_other, kv_short, kv_short,
        d_att, d_att, lse, cos, sin,
    )


def part_of(index, size):
    if isinstance(index, int):
        return pl.ds(index * size, size)
    return pl.ds(pl.multiple_of(index * size, size), size)


def add_to(ref, value, first):
    @pl.when(first)
    def _():
        ref[...] = value

    @pl.when(jnp.logical_not(first))
    def _():
        ref[...] += value


def feed_kernel(
    halves, order, tok_ref, att_ref, cot_ref, hid1_ref, mod_ref, gain_ref, wo_ref, wu_ref, bu_ref, wd_ref, bd_ref,
    out_ref, dmid_ref, datt_ref, act_ref, dlow_ref, h_ref, dup_ref, dattn_ref,
    payload_ref, toks_ref, hid1s_ref,
):
    j, t = pl.program_id(0), pl.program_id(1)
    toks_ref[...] = tok_ref[...]
    hid1s_ref[...] = hid1_ref[...]
    row = mod_ref[pl.ds(slot_of(order, j), 1), :]
    gate1, shift2 = row[:, 2 * D : 3 * D], row[:, 3 * D : 4 * D]
    scale2, gate2 = row[:, 4 * D : 5 * D], row[:, 5 * D :]
    gain, up_bias = wide_row(gain_ref), wide_row(bu_ref)
    attention = nn(att_ref[...], wo_ref[...])
    middle = tok_ref[...].astype(F32) + gate1 * attention
    center = middle - row_mean(middle)
    r = lax.rsqrt(row_mean(center * center) + EPSILON)
    xhat = center * r
    hidden = (xhat * gain * (1.0 + scale2) + shift2).astype(BF16)
    h_ref[...] = hidden
    dy = cot_ref[...].astype(F32)
    d_low = (gate2 * dy).astype(BF16)
    me = lax.axis_index("span")
    at = [h * me + (1 - h) * (1 - me) if halves else h for h in range(2)]
    for h in range(2):
        dlow_ref[:, part_of(at[h], D // 2)] = d_low[:, h * (D // 2) : (h + 1) * (D // 2)]
    lowered, d_hidden = None, None
    sums = []
    for f in range(0, FF, CHUNK):
        cols = slice(f, f + CHUNK)
        up = nn(hidden, wu_ref[:, cols]) + up_bias[:, cols]
        d_act = nt(d_low, wd_ref[cols, :])
        square = up * up
        bend = jnp.tanh(up * (GELU_C + (GELU_C * 0.044715) * square))
        half = 0.5 * (1.0 + bend)
        act = (up * half).astype(BF16)
        slope = half + (0.5 * up) * (1.0 - bend * bend) * (
            GELU_C + (3 * GELU_C * 0.044715) * square
        )
        d_up = (d_act * slope).astype(BF16)
        act_ref[:, cols] = act
        place = at[f // (FF // 2)] * (FF // 2) + f % (FF // 2)
        dup_ref[:, pl.ds(pl.multiple_of(place, CHUNK) if halves else place, CHUNK)] = d_up
        sums.append(col_sum(d_up.astype(F32)))
        low = nn(act, wd_ref[cols, :])
        dh = nt(d_up, wu_ref[:, cols])
        lowered = low if lowered is None else lowered + low
        d_hidden = dh if d_hidden is None else d_hidden + dh
    lowered = lowered + wide_row(bd_ref)
    out_ref[...] = (middle + gate2 * lowered).astype(BF16)
    d_gate2 = col_sum(dy * lowered)
    d_shift2 = col_sum(d_hidden)
    hx = col_sum(d_hidden * xhat)
    e = d_hidden * (1.0 + scale2)
    fx = e * gain
    d_mid = dy + r * (fx - row_mean(fx) - xhat * row_mean(fx * xhat))
    dmid_ref[...] = d_mid
    d_gate1 = col_sum(d_mid * attention)
    d_attention = (gate1 * d_mid).astype(BF16)
    for h in range(2):
        dattn_ref[:, part_of(at[h], D // 2)] = d_attention[:, h * (D // 2) : (h + 1) * (D // 2)]
    datt_ref[...] = nt(d_attention, wo_ref[...]).astype(BF16)
    first = jnp.logical_and(j == 0, t == 0)
    slot = slot_of(order, j)
    four = jnp.concatenate([d_gate1, d_shift2, hx * gain, d_gate2], axis=0)
    none = jnp.zeros((4, D), F32)
    add_to(
        payload_ref,
        jnp.concatenate(
            [
                jnp.where(slot == 0, four, none), jnp.where(slot == 0, none, four),
                hx * (1.0 + scale2), col_sum(d_low.astype(F32)), *sums, jnp.zeros((2, D), F32),
            ],
            axis=0,
        ),
        first,
    )


def feed_call(halves, place, tokens, att, cot, hidden1, mod, gain, wo, wu, bu, wd, bd, rows):
    tile = min(256, rows)
    tiles = rows // tile

    def own(j, t, o):
        return (slot_of(o, j) * tiles + t, 0)

    def sorted_(j, t, o):
        return (j * tiles + t, 0)

    n = SLOTS * rows
    return pl.pallas_call(
        partial(feed_kernel, halves),
        name="feed",
        out_shape=(
            jax.ShapeDtypeStruct((n, D), BF16),
            jax.ShapeDtypeStruct((n, D), F32),
            jax.ShapeDtypeStruct((n, D), BF16),
            jax.ShapeDtypeStruct((n, FF), BF16),
            jax.ShapeDtypeStruct((n, D), BF16),
            jax.ShapeDtypeStruct((n, D), BF16),
            jax.ShapeDtypeStruct((n, FF), BF16),
            jax.ShapeDtypeStruct((n, D), BF16),
            jax.ShapeDtypeStruct((16, D), F32),
            jax.ShapeDtypeStruct((n, D), BF16),
            jax.ShapeDtypeStruct((n, D), BF16),
        ),
        grid_spec=pltpu.PrefetchScalarGridSpec(
            num_scalar_prefetch=1,
            grid=(SLOTS, tiles),
            in_specs=[
                pl.BlockSpec((tile, D), own),
                pl.BlockSpec((tile, D), sorted_),
                pl.BlockSpec((tile, D), own),
                pl.BlockSpec((tile, D), own if halves else sorted_),
                whole((8, 6 * D)),
                whole((D,)),
                whole((D, D)),
                whole((D, FF)),
                whole((FF,)),
                whole((FF, D)),
                whole((D,)),
            ],
            out_specs=[
                pl.BlockSpec((tile, D), own),
                pl.BlockSpec((tile, D), sorted_),
                pl.BlockSpec((tile, D), sorted_),
                pl.BlockSpec((tile, FF), sorted_),
                pl.BlockSpec((tile, D), sorted_),
                pl.BlockSpec((tile, D), sorted_),
                pl.BlockSpec((tile, FF), sorted_),
                pl.BlockSpec((tile, D), sorted_),
                pl.BlockSpec((16, D), lambda j, t, o: (0, 0)),
                pl.BlockSpec((tile, D), sorted_),
                pl.BlockSpec((tile, D), sorted_),
            ],
        ),
        compiler_params=pltpu.CompilerParams(vmem_limit_bytes=BIG),
        cost_estimate=cost(2 * n * D * (4 * FF + 2 * D), 40e6, n * FF),
    )(place, tokens, att, cot, hidden1, mod, gain, wo, wu, bu, wd, bd)


def weight_gradient(left, right):
    seq, span = lax.axis_size("seq"), lax.axis_size("span")
    grad = tn(left, right)
    rows, cols = grad.shape
    shaped = grad.reshape(seq, rows // seq, span, cols // span).transpose(0, 2, 1, 3)
    return lax.psum_scatter(
        shaped.reshape(seq * span, rows // seq, cols // span),
        ("seq", "span"),
        scatter_dimension=0,
        tiled=True,
    )[0]


def join_kernel(place, dq_ref, dk_ref, dv_ref, ek_ref, ev_ref, sk_ref, sv_ref, cos, sin, out_ref):
    j, t = pl.program_id(0), pl.program_id(1)
    out_ref[:, :D] = dq_ref[...]
    wide_cos = jnp.concatenate([cos[...]] * PAIRS, axis=1)
    wide_sin = jnp.concatenate([sin[...]] * PAIRS, axis=1)

    @pl.when(j == 0)
    def _():
        dk = dk_ref[...] + ek_ref[...].astype(F32)
        out_ref[:, D : 2 * D] = turn_back(dk, wide_cos, wide_sin).astype(BF16)
        out_ref[:, 2 * D :] = (dv_ref[...] + ev_ref[...].astype(F32)).astype(BF16)

    @pl.when(j == 1)
    def _():
        out_ref[:, D:] = jnp.zeros((out_ref.shape[0], 2 * D), BF16)

    @pl.when(jnp.logical_and(j == 1, jnp.logical_and(t == 0, place[2] == 0)))
    def _():
        dk = turn_back(sk_ref[...], wide_cos[:SHORT], wide_sin[:SHORT])
        out_ref[:SHORT, D : 2 * D] = dk.astype(BF16)
        out_ref[:SHORT, 2 * D :] = sv_ref[...].astype(BF16)


def join_call(place, dq, dk, dv, ek, ev, sk, sv, cos, sin, rows):
    tile = min(256, rows)
    tiles = rows // tile

    def long(j, t, o):
        return (t + j * (tiles - 1 - t), 0)

    return pl.pallas_call(
        join_kernel,
        name="join",
        out_shape=jax.ShapeDtypeStruct((SLOTS * rows, 3 * D), BF16),
        grid_spec=pltpu.PrefetchScalarGridSpec(
            num_scalar_prefetch=1,
            grid=(SLOTS, tiles),
            in_specs=[pl.BlockSpec((tile, D), lambda j, t, o: (j * tiles + t, 0))]
            + [pl.BlockSpec((tile, D), long)] * 4
            + [whole((SHORT, D))] * 2
            + [pl.BlockSpec((tile, PAIR), lambda j, t, o: (o[2] * tiles + t, 0))] * 2,
            out_specs=pl.BlockSpec((tile, 3 * D), lambda j, t, o: (j * tiles + t, 0)),
        ),
        compiler_params=pltpu.CompilerParams(vmem_limit_bytes=BIG),
        cost_estimate=cost(1e7, 12e6),
    )(place, dq, dk, dv, ek, ev, sk, sv, cos, sin)


def last_kernel(
    order, tok_ref, dqkv_ref, dmid_ref, mod_ref, gain_ref, weight_ref,
    out_ref, dmod_ref, dgain_ref,
):
    j, t = pl.program_id(0), pl.program_id(1)
    scale = mod_ref[pl.ds(slot_of(order, j), 1), :][:, D : 2 * D]
    gain = wide_row(gain_ref)
    d_hidden = nt(dqkv_ref[...], weight_ref[...])
    x = tok_ref[...].astype(F32)
    center = x - row_mean(x)
    r = lax.rsqrt(row_mean(center * center) + EPSILON)
    xhat = center * r
    hx = col_sum(d_hidden * xhat)
    fx = d_hidden * (1.0 + scale) * gain
    out_ref[...] = dmid_ref[...] + r * (fx - row_mean(fx) - xhat * row_mean(fx * xhat))
    first = jnp.logical_and(j == 0, t == 0)
    add_to(
        dmod_ref,
        jnp.concatenate([col_sum(d_hidden), hx * gain, jnp.zeros((6, D), F32)], axis=0)[None],
        t == 0,
    )
    add_to(dgain_ref, hx * (1.0 + scale), first)


def last_call(place, tokens, dqkv, dmid, mod, gain, weight, rows):
    tile = min(256, rows)
    tiles = rows // tile

    def own(j, t, o):
        return (slot_of(o, j) * tiles + t, 0)

    def sorted_(j, t, o):
        return (j * tiles + t, 0)

    n = SLOTS * rows
    return pl.pallas_call(
        last_kernel,
        name="last",
        out_shape=(
            jax.ShapeDtypeStruct((n, D), F32),
            jax.ShapeDtypeStruct((SLOTS, 8, D), F32),
            jax.ShapeDtypeStruct((1, D), F32),
        ),
        grid_spec=pltpu.PrefetchScalarGridSpec(
            num_scalar_prefetch=1,
            grid=(SLOTS, tiles),
            in_specs=[
                pl.BlockSpec((tile, D), own),
                pl.BlockSpec((tile, 3 * D), sorted_),
                pl.BlockSpec((tile, D), sorted_),
                whole((8, 6 * D)),
                whole((D,)),
                whole((D, 3 * D)),
            ],
            out_specs=[
                pl.BlockSpec((tile, D), own),
                pl.BlockSpec((1, 8, D), lambda j, t, o: (slot_of(o, j), 0, 0)),
                pl.BlockSpec((1, D), lambda j, t, o: (0, 0)),
            ],
        ),
        compiler_params=pltpu.CompilerParams(vmem_limit_bytes=BIG),
        cost_estimate=cost(2 * n * D * 3 * D, 18e6),
    )(place, tokens, dqkv, dmid, mod, gain, weight)


def share_kernel(
    tok_ref, mod_ref, gain_ref, weight_ref, cos_ref, sin_ref,
    q_ref, h_ref, kv_ref, kvx_any, stage, send, recv,
):
    step = pl.program_id(0)
    steps = stage.shape[0]
    tile = tok_ref.shape[0]
    me = lax.axis_index("span")

    def copy(i):
        return pltpu.make_async_remote_copy(
            src_ref=stage.at[i],
            dst_ref=kvx_any.at[pl.ds(pl.multiple_of(i * tile, tile), tile)],
            send_sem=send.at[i],
            recv_sem=recv.at[i],
            device_id={"span": 1 - me},
            device_id_type=MESH,
        )

    row = mod_ref[pl.ds(step // (steps // SLOTS), 1), :]
    shift, scale = row[:, :D], row[:, D : 2 * D]
    x = tok_ref[...].astype(F32)
    center = x - row_mean(x)
    xhat = center * lax.rsqrt(row_mean(center * center) + EPSILON)
    hidden = (xhat * wide_row(gain_ref) * (1.0 + scale) + shift).astype(BF16)
    h_ref[...] = hidden
    start = (me * (steps // SLOTS) + lax.rem(step, steps // SLOTS)) * tile
    start = pl.multiple_of(start, tile)
    cos = jnp.concatenate([cos_ref[pl.ds(start, tile), :]] * PAIRS, axis=1)
    sin = jnp.concatenate([sin_ref[pl.ds(start, tile), :]] * PAIRS, axis=1)
    k = turn(nn(hidden, weight_ref[:, D : 2 * D]), cos, sin).astype(BF16)
    v = nn(hidden, weight_ref[:, 2 * D :]).astype(BF16)
    kv_ref[:, :D] = k
    kv_ref[:, D:] = v
    stage[step, :, :D] = k
    stage[step, :, D:] = v

    @pl.when(step == 0)
    def _():
        greet([{"span": 1 - me}])

    copy(step).start()
    q_ref[...] = turn(nn(hidden, weight_ref[:, :D]), cos, sin).astype(BF16)

    @pl.when(step == steps - 1)
    def _():
        for i in range(steps):
            copy(i).wait()


def share_call(tokens, mod, gain, weight, cos, sin, rows):
    tile = 256
    n = SLOTS * rows
    steps = n // tile

    def at(width):
        return pl.BlockSpec((tile, width), lambda s: (s, 0))

    return pl.pallas_call(
        share_kernel,
        name="project",
        grid=(steps,),
        out_shape=(
            jax.ShapeDtypeStruct((n, D), BF16),
            jax.ShapeDtypeStruct((n, D), BF16),
            jax.ShapeDtypeStruct((n, 2 * D), BF16),
            jax.ShapeDtypeStruct((n, 2 * D), BF16),
        ),
        in_specs=[
            at(D),
            whole((8, 6 * D)),
            whole((D,)),
            whole((D, 3 * D)),
            whole((LEN, PAIR)),
            whole((LEN, PAIR)),
        ],
        out_specs=(at(D), at(D), at(2 * D), pl.BlockSpec(memory_space=pl.ANY)),
        scratch_shapes=[
            pltpu.VMEM((steps, tile, 2 * D), BF16),
            pltpu.SemaphoreType.DMA((steps,)),
            pltpu.SemaphoreType.DMA((steps,)),
        ],
        compiler_params=pltpu.CompilerParams(
            collective_id=4, has_side_effects=True, vmem_limit_bytes=BIG
        ),
        cost_estimate=cost(2 * n * D * 3 * D, 14e6),
    )(tokens, mod, gain, weight, cos, sin)


def attend_sorted_kernel(
    lengths, ql, qs, ko, vo, kx, vx, ks_own, vs_own, ks_other, vs_other,
    out_ref, lse_ref, q_ref, ko_ref, vo_ref, kx_ref, vx_ref, ks_ref, vs_ref,
):
    rows = ql.shape[0]
    first = lax.axis_index("span") == 0
    ks = jnp.where(first, ks_own[...], ks_other[...])
    vs = jnp.where(first, vs_own[...], vs_other[...])
    q_ref[:rows, :] = ql[...]
    q_ref[rows:, :] = qs[...]
    ks_ref[...] = ks
    vs_ref[...] = vs
    for ref, given in ((ko_ref, ko), (vo_ref, vo), (kx_ref, kx), (vx_ref, vx)):
        ref[...] = given[...]
    out, stats = attend_slot(ql[...], [ko[...], kx[...]], [vo[...], vx[...]])
    out_ref[:rows, :] = out
    lse_ref[0, 0:1, :] = stats[0]
    lse_ref[0, 1:2, :] = stats[1]
    out, stats = attend_slot(qs[...], [ks], [vs])
    out_ref[rows:, :] = out
    lse_ref[0, 2:3, :] = stats[0]
    lse_ref[0, 3:4, :] = stats[1]


def attend_sorted_call(lengths, q, kv, kvx, rows):
    n = SLOTS * rows
    per = rows // SHORT

    def long(base):
        return pl.BlockSpec((rows, PAIR), lambda h, o: (slot_of(o, 0), base + h))

    def short(base):
        return pl.BlockSpec((SHORT, PAIR), lambda h, o: (slot_of(o, 1) * per, base + h))

    def out(size):
        return pl.BlockSpec((size, PAIR), lambda h, o: (0, h))

    return pl.pallas_call(
        attend_sorted_kernel,
        name="attend",
        out_shape=(
            jax.ShapeDtypeStruct((n, D), BF16),
            jax.ShapeDtypeStruct((PAIRS, 4, rows), F32),
            jax.ShapeDtypeStruct((n, D), BF16),
        )
        + (jax.ShapeDtypeStruct((rows, D), BF16),) * 4
        + (jax.ShapeDtypeStruct((SHORT, D), BF16),) * 2,
        grid_spec=pltpu.PrefetchScalarGridSpec(
            num_scalar_prefetch=1,
            grid=(PAIRS,),
            in_specs=[
                long(0),
                pl.BlockSpec((rows, PAIR), lambda h, o: (slot_of(o, 1), h)),
                long(0), long(PAIRS), long(0), long(PAIRS),
                short(0), short(PAIRS), short(0), short(PAIRS),
            ],
            out_specs=[out(n), pl.BlockSpec((1, 4, rows), lambda h, o: (h, 0, 0)), out(n)]
            + [out(rows)] * 4
            + [out(SHORT)] * 2,
        ),
        compiler_params=pltpu.CompilerParams(vmem_limit_bytes=BIG),
        cost_estimate=cost(16 * D * rows * (LEN + SHORT), 16e6, HEADS * rows * (LEN + SHORT)),
    )(lengths, q, q, kv, kv, kvx, kvx, kv, kv, kvx, kvx)


def flip(index, bit):
    return index + bit - 2 * bit * ((index // bit) % 2)


def add_low(a, b):
    return (a.astype(F32) + b.astype(F32)).astype(BF16)


def plane_peers():
    s, c = lax.axis_index("seq"), lax.axis_index("span")
    return [{"span": 1 - c}, {"seq": flip(s, 1)}, {"seq": flip(s, 2)}]


def line_peers():
    s = lax.axis_index("seq")
    return [{"seq": lax.rem(s + 4 * step, 16)} for step in range(1, 4)]


def greet(peers):
    barrier = pltpu.get_barrier_semaphore()
    for peer in peers:
        pl.semaphore_signal(barrier, inc=1, device_id=peer, device_id_type=MESH)
    pl.semaphore_wait(barrier, len(peers))


class Scatter:
    def __init__(self, send, recv, base, other=None, own=None, came0=None, a1=None, b1=None,
                 came2=None, came3=None):
        self.send, self.recv, self.base = send, recv, base
        self.other, self.own, self.came0 = other, own, came0
        self.a1, self.b1, self.came2, self.came3 = a1, b1, came2, came3
        s = lax.axis_index("seq")
        self.x, self.y, self.z = lax.rem(s, 2), lax.rem(s // 2, 2), s // 4
        self.core_peer, self.x_peer, self.y_peer = plane_peers()
        self.z_peers = line_peers()

    def copy(self, i):
        x, y, z = self.x, self.y, self.z
        if i == 0:
            src, dst, peer = self.other, self.came0, self.core_peer
        elif i == 1:
            src, dst, peer = self.own.at[0:2, :, 1 - x], self.a1, self.x_peer
        elif i == 2:
            src, dst, peer = self.own.at[2:4, 1 - y], self.b1, self.y_peer
        elif i == 3:
            src, dst, peer = self.a1.at[:, 1 - y], self.came2.at[0:2], self.y_peer
        elif i == 4:
            src, dst, peer = self.b1.at[:, 1 - x], self.came2.at[2:4], self.x_peer
        else:
            step = i - 4
            src, dst = self.came2.at[lax.rem(z + step, 4)], self.came3.at[step - 1]
            peer = self.z_peers[step - 1]
        return pltpu.make_async_remote_copy(
            src_ref=src,
            dst_ref=dst,
            send_sem=self.send.at[self.base + i],
            recv_sem=self.recv.at[self.base + i],
            device_id=peer,
            device_id_type=MESH,
        )

    def start(self, *which):
        for i in which:
            self.copy(i).start()

    def arrive(self, *which):
        for i in which:
            self.copy(i).wait_recv()

    def drain(self, *which):
        for i in which:
            self.copy(i).wait_send()

    def add0(self):
        self.arrive(0)

        def body(i, _):
            z, y, x = i // 4, lax.rem(i // 2, 2), lax.rem(i, 2)
            self.own[z, y, x] = add_low(self.own[z, y, x], self.came0[z, y, x])
            return 0

        lax.fori_loop(0, 16, body, 0)

    def add1(self, a_ref, b_ref):
        self.arrive(1, 2)

        def body(i, _):
            z, k = i // 2, lax.rem(i, 2)
            a_ref[z, k] = add_low(self.own[z, k, self.x], self.a1[z, k])
            b_ref[z, k] = add_low(self.own[2 + z, self.y, k], self.b1[z, k])
            return 0

        lax.fori_loop(0, 4, body, 0)

    def add2(self, out_ref):
        self.arrive(3, 4)

        def body(z, _):
            out_ref[z] = add_low(self.a1[z, self.y], self.came2[z])
            out_ref[2 + z] = add_low(self.b1[z, self.x], self.came2[2 + z])
            return 0

        lax.fori_loop(0, 2, body, 0)

    def total(self):
        self.arrive(5, 6, 7)
        total = self.came2[self.z].astype(F32)
        for step in range(3):
            total = total + self.came3[step].astype(F32)
        return total

    def scatter0(self):
        self.start(0)

    def scatter1(self):
        self.add0()
        self.start(1, 2)

    def scatter2(self):
        self.add1(self.a1, self.b1)
        self.start(3, 4)

    def scatter3(self):
        self.add2(self.came2)
        self.start(5, 6, 7)


def half_shape(rows, cols):
    return (4, 2, 2, rows, cols)


def scatter_scratch(rows, cols, first=True, middle=True, last=True):
    shapes = []
    if first:
        shapes += [half_shape(rows, cols)] * 2
    if first or middle:
        shapes += [(2, 2, rows, cols)] * 2
    if middle or last:
        shapes += [(4, rows, cols)]
    if last:
        shapes += [(3, rows, cols)]
    return [pltpu.VMEM(shape, BF16) for shape in shapes]


ANY = pl.BlockSpec(memory_space=pl.ANY)
DMA = pltpu.SemaphoreType.DMA


def weights_kernel(
    act_ref, dlow_ref, att_ref, dattn_ref, h_ref, dup_ref,
    a_ref, b_ref, out_ref, up_ref,
    other, own, came0, a1, b1, out_other, out_came, up_other, up_came, send, recv,
):
    step = pl.program_id(0)
    down = Scatter(send, recv, 0, other=other, own=own, came0=came0, a1=a1, b1=b1)
    out = Scatter(send, recv, 3, other=out_other, own=out_ref, came0=out_came)
    up = Scatter(send, recv, 4, other=up_other, own=up_ref, came0=up_came)

    @pl.when(step == 0)
    def _():
        greet(plane_peers())

    @pl.when(step == 8)
    def _():
        down.scatter1()

    @pl.when(step == 10)
    def _():
        out.add0()

    @pl.when(step < 8)
    def _():
        value = tn(act_ref[...], dlow_ref[...]).astype(BF16)
        value = value.reshape((2, 2) + own.shape[3:])

        @pl.when(step < 4)
        def _():
            other[step] = value

        @pl.when(step >= 4)
        def _():
            own[step - 4] = value

    @pl.when(step == 3)
    def _():
        down.scatter0()

    @pl.when(jnp.logical_and(step >= 8, step < 10))
    def _():
        value = tn(att_ref[...], dattn_ref[...]).astype(BF16).reshape(out_ref.shape)

        @pl.when(step == 8)
        def _():
            out_other[...] = value
            out.scatter0()

        @pl.when(step == 9)
        def _():
            out_ref[...] = value

    @pl.when(step >= 10)
    def _():
        value = tn(h_ref[...], dup_ref[...]).astype(BF16)
        value = value.reshape((2,) + up_ref.shape[1:])
        z = lax.rem(step, 2) * 2

        @pl.when(step < 12)
        def _():
            up_other[pl.ds(z, 2)] = value

        @pl.when(step >= 12)
        def _():
            up_ref[pl.ds(z, 2)] = value

    @pl.when(step == 11)
    def _():
        up.scatter0()

    @pl.when(step == 13)
    def _():
        up.add0()
        down.add1(a_ref, b_ref)
        down.drain(0, 1, 2)
        out.drain(0)
        up.drain(0)


def weights_call(act, d_low, att, d_attention, hidden, d_up):
    n = hidden.shape[0]
    half = FF // 2
    dr, dc = FF // 16, D // 2
    ur, wr = D // 16, D // 16
    down, up, out = half_shape(dr, dc), half_shape(ur, half), half_shape(wr, dc)

    def clamp(s, low, high):
        return jnp.minimum(jnp.maximum(s, low), high)

    def fixed(shape):
        return whole(shape)

    handed = (2, 2, dr, dc)
    shapes = (handed, handed, out, up)
    return pl.pallas_call(
        weights_kernel,
        name="weights",
        grid=(14,),
        out_shape=tuple(jax.ShapeDtypeStruct(o, BF16) for o in shapes),
        in_specs=[
            pl.BlockSpec((n, D), lambda s: (0, jnp.where(s < 8, lax.rem(s, 4), 3))),
            pl.BlockSpec((n, dc), lambda s: (0, jnp.where(s < 4, 0, 1))),
            fixed((n, D)),
            pl.BlockSpec((n, dc), lambda s: (0, jnp.where(s < 9, 0, 1))),
            pl.BlockSpec((n, dc), lambda s: (0, jnp.where(s < 10, 0, lax.rem(s, 2)))),
            pl.BlockSpec((n, half), lambda s: (0, jnp.where(s < 12, 0, 1))),
        ],
        out_specs=tuple(fixed(o) for o in shapes),
        scratch_shapes=[
            pltpu.VMEM(down, BF16),
            pltpu.VMEM(down, BF16),
            pltpu.VMEM(down, BF16),
            pltpu.VMEM(handed, BF16),
            pltpu.VMEM(handed, BF16),
            pltpu.VMEM(out, BF16),
            pltpu.VMEM(out, BF16),
            pltpu.VMEM(up, BF16),
            pltpu.VMEM(up, BF16),
            DMA((5,)),
            DMA((5,)),
        ],
        compiler_params=pltpu.CompilerParams(
            collective_id=1, has_side_effects=True, vmem_limit_bytes=BIG
        ),
        cost_estimate=cost(2 * n * D * (2 * FF + D), 30e6),
    )(act, d_low, att, d_attention, hidden, d_up)


def back_kernel(
    ql, qs, ko, vo, kx, vx, ks, vs, dol, dos, lse, cos_ref, sin_ref,
    a_in, b_in, up_in, out_in,
    dq_ref, dk_ref, dv_ref, down_ref, up_ref, out_ref,
    down_a, down_b, down2, down3,
    up_own, up_a, up_b, up2,
    out_own, out_a, out_b, out2,
    leave, come, keep_k, keep_v, keep_sk, keep_sv,
    send, recv, send_kv, recv_kv, local,
):
    step = pl.program_id(0)
    me = lax.axis_index("span")
    rows = ql.shape[0]
    down = Scatter(send, recv, 0, a1=down_a, b1=down_b, came2=down2, came3=down3)
    up = Scatter(send, recv, 8, own=up_own, a1=up_a, b1=up_b, came2=up2)
    out = Scatter(send, recv, 13, own=out_own, a1=out_a, b1=out_b, came2=out2)
    loads = [
        pltpu.make_async_copy(src, dst, local.at[i])
        for i, (src, dst) in enumerate(
            [(a_in, down_a), (b_in, down_b), (up_in, up_own), (out_in, out_own)]
        )
    ]
    cos = cos_ref[pl.ds(pl.multiple_of(me * rows, rows), rows), :]
    sin = sin_ref[pl.ds(pl.multiple_of(me * rows, rows), rows), :]

    def kv_copy(pair):
        return pltpu.make_async_remote_copy(
            src_ref=leave.at[pair],
            dst_ref=come.at[pair],
            send_sem=send_kv.at[pair],
            recv_sem=recv_kv.at[pair],
            device_id={"span": 1 - me},
            device_id_type=MESH,
        )

    @pl.when(step == 0)
    def _():
        for load in loads:
            load.start()
        greet(plane_peers() + line_peers())
        loads[0].wait()
        loads[1].wait()
        down.start(3, 4)

    @pl.when(step == 1)
    def _():
        loads[2].wait()
        loads[3].wait()
        out.start(1, 2)
        up.start(1, 2)

    @pl.when(step == 2)
    def _():
        down.scatter3()

    @pl.when(step == 5)
    def _():
        up.scatter2()
        out.scatter2()

    @pl.when(step < PAIRS)
    def _():
        stats = lse[0]
        dq, dk, dv = attend_back_slot(
            ql[...], [ko[...], kx[...]], [vo[...], vx[...]], dol[...], [stats[0:1], stats[1:2]]
        )
        dq_ref[:rows, :] = turn_back(dq, cos, sin).astype(BF16)
        keep_k[lax.rem(step, 2)] = dk[0]
        keep_v[lax.rem(step, 2)] = dv[0]
        leave[step, :rows, :PAIR] = dk[1].astype(BF16)
        leave[step, :rows, PAIR:] = dv[1].astype(BF16)
        dq, dk, dv = attend_back_slot(
            qs[...], [ks[...]], [vs[...]], dos[...], [stats[2:3], stats[3:4]]
        )
        dq_ref[rows:, :] = turn_back(dq, cos, sin).astype(BF16)
        keep_sk[lax.rem(step, 2)] = dk[0]
        keep_sv[lax.rem(step, 2)] = dv[0]
        leave[step, rows:, :PAIR] = dk[0].astype(BF16)
        leave[step, rows:, PAIR:] = dv[0].astype(BF16)
        kv_copy(step).start()

    @pl.when(step > 0)
    def _():
        pair = step - 1
        kv_copy(pair).wait_recv()
        dk = keep_k[lax.rem(pair, 2)] + come[pair, :rows, :PAIR].astype(F32)
        dk_ref[:rows, :] = turn_back(dk, cos, sin).astype(BF16)
        dv = keep_v[lax.rem(pair, 2)] + come[pair, :rows, PAIR:].astype(F32)
        dv_ref[:rows, :] = dv.astype(BF16)
        zero = jnp.zeros((SHORT, PAIR), F32)
        sk = keep_sk[lax.rem(pair, 2)] + come[pair, rows:, :PAIR].astype(F32)
        sk = jnp.where(me == 0, turn_back(sk, cos[:SHORT], sin[:SHORT]), zero)
        sv = jnp.where(me == 0, keep_sv[lax.rem(pair, 2)] + come[pair, rows:, PAIR:].astype(F32), zero)
        dk_ref[rows : rows + SHORT, :] = sk.astype(BF16)
        dv_ref[rows : rows + SHORT, :] = sv.astype(BF16)
        rest = jnp.zeros((rows - SHORT, PAIR), BF16)
        dk_ref[rows + SHORT :, :] = rest
        dv_ref[rows + SHORT :, :] = rest

    @pl.when(step == PAIRS)
    def _():
        down_ref[...] = down.total()
        up.add2(up_ref)
        out.add2(out_ref)
        down.drain(3, 4, 5, 6, 7)
        up.drain(1, 2, 3, 4)
        out.drain(1, 2, 3, 4)
        for pair in range(PAIRS):
            kv_copy(pair).wait_send()


def back_call(q, kv, d_att, lse, cos, sin, handed, rows):
    last = PAIRS - 1

    def late(s):
        return jnp.minimum(s, last)

    def early(s):
        return jnp.maximum(s - 1, 0)

    def fixed(shape):
        return pl.BlockSpec(shape, lambda s: (0,) * len(shape))

    specs = [
        pl.BlockSpec((rows, PAIR), lambda s: (0, late(s))),
        pl.BlockSpec((rows, PAIR), lambda s: (1, late(s))),
    ]
    specs += [pl.BlockSpec((rows, PAIR), lambda s: (0, late(s)))] * 4
    specs += [pl.BlockSpec((SHORT, PAIR), lambda s: (0, late(s)))] * 2
    n = SLOTS * rows
    dr, dc = FF // 16, D // 2
    ur, uc = D // 16, FF // 2
    wr, wc = D // 16, D // 2
    return pl.pallas_call(
        back_kernel,
        name="attend_back",
        grid=(PAIRS + 1,),
        out_shape=(
            jax.ShapeDtypeStruct((n, D), BF16),
            jax.ShapeDtypeStruct((n, D), BF16),
            jax.ShapeDtypeStruct((n, D), BF16),
            jax.ShapeDtypeStruct((dr, dc), F32),
            jax.ShapeDtypeStruct((4, ur, uc), BF16),
            jax.ShapeDtypeStruct((4, wr, wc), BF16),
        ),
        in_specs=specs
        + [
            pl.BlockSpec((rows, PAIR), lambda s: (0, late(s))),
            pl.BlockSpec((rows, PAIR), lambda s: (1, late(s))),
            pl.BlockSpec((1, 4, rows), lambda s: (late(s), 0, 0)),
            whole((LEN, PAIR)),
            whole((LEN, PAIR)),
        ]
        + [ANY] * 4,
        out_specs=(
            pl.BlockSpec((n, PAIR), lambda s: (0, late(s))),
            pl.BlockSpec((n, PAIR), lambda s: (0, early(s))),
            pl.BlockSpec((n, PAIR), lambda s: (0, early(s))),
            fixed((dr, dc)),
            fixed((4, ur, uc)),
            fixed((4, wr, wc)),
        ),
        scratch_shapes=[
            pltpu.VMEM((2, 2, dr, dc), BF16),
            pltpu.VMEM((2, 2, dr, dc), BF16),
            pltpu.VMEM((4, dr, dc), BF16),
            pltpu.VMEM((3, dr, dc), BF16),
        ]
        + [pltpu.VMEM(half_shape(ur, uc), BF16)]
        + scatter_scratch(ur, uc, first=False, last=False)
        + [pltpu.VMEM(half_shape(wr, wc), BF16)]
        + scatter_scratch(wr, wc, first=False, last=False)
        + [
            pltpu.VMEM((PAIRS, rows + SHORT, 2 * PAIR), BF16),
            pltpu.VMEM((PAIRS, rows + SHORT, 2 * PAIR), BF16),
            pltpu.VMEM((2,) + (rows, PAIR), F32),
            pltpu.VMEM((2,) + (rows, PAIR), F32),
            pltpu.VMEM((2,) + (SHORT, PAIR), F32),
            pltpu.VMEM((2,) + (SHORT, PAIR), F32),
            DMA((18,)),
            DMA((18,)),
            DMA((PAIRS,)),
            DMA((PAIRS,)),
            DMA((4,)),
        ],
        compiler_params=pltpu.CompilerParams(
            collective_id=2, has_side_effects=True, vmem_limit_bytes=BIG
        ),
        cost_estimate=cost(40 * D * rows * (LEN + SHORT), 30e6, HEADS * rows * (LEN + SHORT)),
    )(q, q, *kv, d_att, d_att, lse, cos, sin, *handed)


BLOCKS = 3
TILES = 4


def end_kernel(
    tok_ref, dmid_ref, hidden_ref, mod_ref, gain_ref, weight_ref, lengths,
    dq_any, dk_any, dv_any, up_any, out_any,
    grad_ref, gqkv_ref, gup_ref, gout_ref, late_ref,
    dqkv, hidden_t,
    up2, up3, out2, out3,
    other, own, came0, a1, b1, came2, came3,
    sums, sums_came, sums_all, late_came,
    send, recv, send_late, recv_late, local,
):
    step = pl.program_id(0)
    s, me = lax.axis_index("seq"), lax.axis_index("span")
    up = Scatter(send, recv, 0, came2=up2, came3=up3)
    out = Scatter(send, recv, 8, came2=out2, came3=out3)
    blocks = [
        Scatter(
            send, recv, 16 + 8 * b, other=other.at[b], own=own.at[b], came0=came0.at[b],
            a1=a1.at[b], b1=b1.at[b], came2=came2.at[b], came3=came3.at[b],
        )
        for b in range(BLOCKS)
    ]
    loads = [
        pltpu.make_async_copy(src, dst, local.at[i])
        for i, (src, dst) in enumerate(
            [(up_any, up2), (out_any, out2)]
            + [
                (a, dqkv.at[:, pl.ds(k * D, D)])
                for k, a in enumerate([dq_any, dk_any, dv_any])
            ]
        )
    ]
    wide = 3 * D // 2 // BLOCKS

    def product(core, b):
        start = pl.multiple_of(core * (3 * D // 2) + b * wide, 128)
        value = nn(hidden_t[...], dqkv[:, pl.ds(start, wide)]).astype(BF16)
        return value.reshape(half_shape(D // 16, wide))

    def late_copy(k):
        if k == 0:
            src, dst, peer = sums, sums_came, {"span": 1 - me}
        else:
            src, dst, peer = sums_all, late_came.at[s], {"seq": lax.rem(s + k, 16)}
        return pltpu.make_async_remote_copy(
            src_ref=src,
            dst_ref=dst,
            send_sem=send_late.at[k],
            recv_sem=recv_late.at[k],
            device_id=peer,
            device_id_type=MESH,
        )

    @pl.when(step == 0)
    def _():
        for load in loads:
            load.start()
        hidden_t[...] = hidden_ref[...].T
        greet([{"span": 1 - me}] + [{"seq": lax.rem(s + k, 16)} for k in range(1, 16)])
        loads[0].wait()
        loads[1].wait()
        up.start(5, 6, 7)
        out.start(5, 6, 7)
        for load in loads[2:]:
            load.wait()
        sums[...] = jnp.zeros_like(sums)

    for b in range(BLOCKS):
        @pl.when(step == b)
        def _():
            other[b] = product(1 - me, b)
            blocks[b].scatter0()
            if b > 0:
                blocks[b - 1].scatter1()
            own[b] = product(me, b)

    @pl.when(step == 3)
    def _():
        blocks[2].scatter1()
        blocks[0].scatter2()

    @pl.when(step == 4)
    def _():
        blocks[1].scatter2()

    @pl.when(step == 5)
    def _():
        blocks[2].scatter2()
        blocks[0].scatter3()

    @pl.when(step == 6)
    def _():
        blocks[1].scatter3()

    @pl.when(step >= BLOCKS)
    def _():
        t = step - BLOCKS
        j = t // 2
        size = tok_ref.shape[0]
        swapped = jnp.full((1, D), jnp.where(lengths[1] > lengths[0], 1.0, 0.0))
        mine = jnp.where(j == 0, swapped, 1.0 - swapped)
        scale = jnp.where(mine == 0.0, mod_ref[0:1, D : 2 * D], mod_ref[1:2, D : 2 * D])
        gain = wide_row(gain_ref)
        start = pl.multiple_of(t * size, size)
        d_hidden = nt(dqkv[pl.ds(start, size), :], weight_ref[...])
        x = tok_ref[...].astype(F32)
        center = x - row_mean(x)
        r = lax.rsqrt(row_mean(center * center) + EPSILON)
        xhat = center * r
        hx = col_sum(d_hidden * xhat)
        fx = d_hidden * (1.0 + scale) * gain
        grad_ref[...] = dmid_ref[...] + r * (fx - row_mean(fx) - xhat * row_mean(fx * xhat))
        shift = col_sum(d_hidden)
        none = jnp.zeros((3, D), F32)
        first, second = mine == 0.0, mine != 0.0
        zero = jnp.zeros((1, D), F32)
        sums[...] += jnp.concatenate(
            [
                jnp.where(first, shift, zero), jnp.where(first, hx * gain, zero),
                jnp.where(second, shift, zero), jnp.where(second, hx * gain, zero),
                hx * (1.0 + scale), none,
            ],
            axis=0,
        )

    @pl.when(step == BLOCKS + TILES - 1)
    def _():
        late_copy(0).start()
        blocks[2].scatter3()
        late_copy(0).wait_recv()
        sums_all[...] = sums[...] + sums_came[...]
        for k in range(1, 16):
            late_copy(k).start()
        late_came[s] = sums_all[...]
        gup_ref[...] = up.total()
        gout_ref[...] = out.total()
        for b in range(BLOCKS):
            gqkv_ref[:, b * wide : (b + 1) * wide] = blocks[b].total()
        up.drain(5, 6, 7)
        out.drain(5, 6, 7)
        for block in blocks:
            block.drain(*range(8))
        for k in range(16):
            if k > 0:
                late_copy(k).wait_recv()
            late_copy(k).wait_send()
        late_ref[...] = late_came[...]


def end_call(tokens, d_mid, hidden, mod, gain, weight, lengths, dq, dk, dv, up2, out2, rows):
    n = SLOTS * rows
    size = n // TILES
    r = D // 16
    wide = 3 * D // 2 // BLOCKS

    def tile(s):
        return (jnp.maximum(s - BLOCKS, 0), 0)

    def fixed(shape):
        return pl.BlockSpec(shape, lambda s: (0,) * len(shape))

    def each(shape):
        return pltpu.VMEM((BLOCKS,) + shape, BF16)

    return pl.pallas_call(
        end_kernel,
        name="end",
        grid=(BLOCKS + TILES,),
        out_shape=(
            jax.ShapeDtypeStruct((n, D), F32),
            jax.ShapeDtypeStruct((r, 3 * D // 2), F32),
            jax.ShapeDtypeStruct((r, FF // 2), F32),
            jax.ShapeDtypeStruct((r, D // 2), F32),
            jax.ShapeDtypeStruct((16, 8, D), F32),
        ),
        in_specs=[
            pl.BlockSpec((size, D), tile),
            pl.BlockSpec((size, D), tile),
            whole((n, D)),
            whole((8, 6 * D)),
            whole((D,)),
            whole((D, 3 * D)),
            pl.BlockSpec(memory_space=pltpu.SMEM),
        ]
        + [ANY] * 5,
        out_specs=(
            pl.BlockSpec((size, D), tile),
            fixed((r, 3 * D // 2)),
            fixed((r, FF // 2)),
            fixed((r, D // 2)),
            fixed((16, 8, D)),
        ),
        scratch_shapes=[
            pltpu.VMEM((n, 3 * D), BF16),
            pltpu.VMEM((D, n), BF16),
            pltpu.VMEM((4, r, FF // 2), BF16),
            pltpu.VMEM((3, r, FF // 2), BF16),
            pltpu.VMEM((4, r, D // 2), BF16),
            pltpu.VMEM((3, r, D // 2), BF16),
            each(half_shape(r, wide)),
            each(half_shape(r, wide)),
            each(half_shape(r, wide)),
            each((2, 2, r, wide)),
            each((2, 2, r, wide)),
            each((4, r, wide)),
            each((3, r, wide)),
            pltpu.VMEM((8, D), F32),
            pltpu.VMEM((8, D), F32),
            pltpu.VMEM((8, D), F32),
            pltpu.VMEM((16, 8, D), F32),
            DMA((16 + 8 * BLOCKS,)),
            DMA((16 + 8 * BLOCKS,)),
            DMA((16,)),
            DMA((16,)),
            DMA((5,)),
        ],
        compiler_params=pltpu.CompilerParams(
            collective_id=3, has_side_effects=True, vmem_limit_bytes=BIG
        ),
        cost_estimate=cost(4 * n * D * 3 * D, 30e6),
    )(tokens, d_mid, hidden, mod, gain, weight, lengths, dq, dk, dv, up2, out2)


def exact(left, right, over):
    return lax.dot_general(
        left, right, (over, ((), ())), precision=HIGHEST, preferred_element_type=F32
    )


def exact(left, right, over):
    return lax.dot_general(
        left, right, (over, ((), ())), precision=HIGHEST, preferred_element_type=F32
    )


def condition_kernel(
    lengths, early_ref, late_ref, table_ref, silu_ref, weight_ref,
    qkv_in, out_in, up_in, down_in, sorted_any,
    ada_ref, bias_ref, gcond_ref, gain1_ref, gain2_ref, bd_ref, bu_ref,
    qkv_ref, out_ref, up_ref, down_ref, natural_any, moved,
):
    seq = late_ref.shape[0]
    me, s = lax.axis_index("span"), lax.axis_index("seq")
    half = sorted_any.shape[0] // SLOTS
    moves = [
        pltpu.make_async_copy(
            sorted_any.at[pl.ds(j * half, half)],
            natural_any.at[pl.ds(pl.multiple_of(slot_of(lengths, j) * half, half), half)],
            moved.at[j],
        )
        for j in range(SLOTS)
    ]
    for move in moves:
        move.start()
    qkv_ref[...] = qkv_in[...]
    out_ref[...] = out_in[...]
    up_ref[...] = up_in[...]
    down_ref[...] = down_in[...]
    early = early_ref[...].reshape(seq, 2, 16, D)
    early = early[:, 0] + early[:, 1]
    late = late_ref[...]
    mods = []
    for k in range(SLOTS):
        mods.append(
            [late[:, 2 * k], late[:, 2 * k + 1]] + [early[:, 4 * k + b] for b in range(4)]
        )
    gain1_ref[...] = jnp.sum(late[:, 4], axis=0)
    gain2_ref[...] = jnp.sum(early[:, 8], axis=0)
    bd_ref[...] = jnp.sum(early[:, 9], axis=0)
    for f in range(4):
        bu_ref[f * D : (f + 1) * D] = jnp.sum(early[:, 10 + f], axis=0)
    own = [jnp.zeros((8, D), F32)] * 6
    row = lax.broadcasted_iota(jnp.int32, (8, seq), 0)
    wanted = (s * SLOTS + row).astype(F32)
    for k in range(SLOTS):
        asked = table_ref[:, SLOTS + k, :].T[:8]
        chosen = jnp.where(jnp.logical_and(asked == wanted, row < SLOTS), 1.0, 0.0)
        for b in range(6):
            own[b] = own[b] + exact(chosen, mods[k][b], ((1,), (0,)))
    d_silu = jnp.zeros((8, 128), F32)
    for b in range(6):
        cols = slice(b * D, (b + 1) * D)
        bias_ref[cols] = jnp.sum(mods[0][b] + mods[1][b], axis=0)
        d_silu += exact(own[b], weight_ref[:, cols].astype(F32), ((1,), (1,)))
    v = table_ref[s]
    sig = 1.0 / (1.0 + jnp.exp(-v))
    gcond_ref[...] = (d_silu * (sig * (1.0 + v * (1.0 - sig))))[:SLOTS]
    rows = 128 // seq
    pick = lax.broadcasted_iota(jnp.int32, (rows, 128), 1) == (
        s * rows + lax.broadcasted_iota(jnp.int32, (rows, 128), 0)
    )
    pick = jnp.where(pick, 1.0, 0.0)
    silu = [exact(pick, silu_ref[k], ((1,), (1,))) for k in range(SLOTS)]
    for b in range(3):
        total = jnp.zeros((rows, D), F32)
        for k in range(SLOTS):
            block = jnp.where(me == 0, mods[k][b], mods[k][3 + b])
            total += exact(silu[k], block, ((1,), (0,)))
        ada_ref[:, b * D : (b + 1) * D] = total
    for move in moves:
        move.wait()


def condition_call(lengths, early, late, table, silu, ada_weight, tiles, grad_in):
    seq = late.shape[0]

    def all_of(shape):
        return pl.BlockSpec(shape, lambda i, p: (0,) * len(shape))

    given = (early, late, table, silu, ada_weight) + tiles
    outs = ((128 // seq, 3 * D), (6 * D,), (SLOTS, 128), (D,), (D,), (D,), (FF,))
    outs += tuple(t.shape for t in tiles)
    return pl.pallas_call(
        condition_kernel,
        name="condition",
        out_shape=tuple(jax.ShapeDtypeStruct(o, F32) for o in outs + (grad_in.shape,)),
        grid_spec=pltpu.PrefetchScalarGridSpec(
            num_scalar_prefetch=1,
            grid=(1,),
            in_specs=[whole(a.shape) for a in given] + [ANY],
            out_specs=[all_of(o) for o in outs] + [ANY],
            scratch_shapes=[DMA((SLOTS,))],
        ),
        compiler_params=pltpu.CompilerParams(vmem_limit_bytes=32 << 20),
        cost_estimate=cost(1e7, 12e6),
    )(lengths, *given, grad_in)


def from_peers(array, span):
    return [
        lax.ppermute(array, "span", [((i + step) % span, i) for i in range(span)])
        for step in range(1, span)
    ]


def gather_all(flat):
    seq, span = lax.axis_size("seq"), lax.axis_size("span")
    return lax.all_gather(flat, ("seq", "span"), axis=0).reshape(seq, span, flat.shape[0])


def shards(
    tokens, conditions, assignment, lengths, norm1_gain, ada_weight, ada_bias, qkv_weight,
    out_weight, norm2_gain, up_weight, up_bias, down_weight, down_bias, cotangent,
):
    slots, rows, _ = tokens.shape
    seq, span = lax.axis_size("seq"), lax.axis_size("span")
    seq_at, span_at = lax.axis_index("seq"), lax.axis_index("span")
    flat = slots * rows
    place = jnp.concatenate(
        [lengths, jnp.stack([span_at.astype(jnp.int32), seq_at.astype(jnp.int32)])]
    )
    fast = seq == 16 and span == 2
    cos, sin = (jnp.asarray(table) for table in rotary(LEN))
    mod, table, silu_all = modulation_call(conditions, assignment, ada_weight, ada_bias, seq)

    tokens2 = tokens.reshape(flat, D)
    gain1, gain2 = norm1_gain, norm2_gain
    if fast:
        q, hidden1, kv, kvx = share_call(tokens2, mod, gain1, qkv_weight, cos, sin, rows)
        att, lse, q, *kv = attend_sorted_call(lengths, q, kv, kvx, rows)
    else:
        q, hidden1, kv_long, kv_tail = project_call(
            place, tokens2, mod, gain1, qkv_weight, cos, sin, rows
        )
        kv_other = jnp.concatenate(from_peers(kv_long, span), axis=0)
        kv_short = kv_tail[:SHORT]
        sent = [lax.ppermute(kv_short, "span", [(0, i)]) for i in range(1, span)]
        kv_short = jnp.where(span_at == 0, kv_short, sum(sent[1:], sent[0]))
        att, lse = attend_call(q, kv_long, kv_other, kv_short, rows)
    (
        out, d_mid, d_att, act, d_low, hidden2, d_up, d_attention, payload, tokens_sorted,
        hidden1_sorted,
    ) = feed_call(
        fast, lengths, tokens2, att, cotangent.reshape(flat, D), hidden1, mod, gain2, out_weight,
        up_weight, up_bias, down_weight, down_bias, rows,
    )
    if fast:
        early = lax.all_gather(payload, ("seq", "span"), axis=0)
        a1, b1, out0, up0 = weights_call(act, d_low, att, d_attention, hidden2, d_up)
        dq, dk, dv, grad_down, up2, out2 = back_call(
            q, kv, d_att, lse, cos, sin, (a1, b1, up0, out0), rows
        )
        grad_in, grad_qkv, grad_up, grad_out, late = end_call(
            tokens_sorted, d_mid, hidden1_sorted, mod, gain1, qkv_weight, lengths, dq, dk, dv,
            up2, out2, rows,
        )
        (
            grad_ada, ada_bias_sum, grad_cond, gain1_sum, gain2_sum, bd_sum, bu_sum,
            grad_qkv, grad_out, grad_up, grad_down, grad_in,
        ) = condition_call(
            lengths, early, late, table, silu_all, ada_weight,
            (grad_qkv, grad_out, grad_up, grad_down), grad_in,
        )
        return (
            out.reshape(tokens.shape), grad_in.reshape(tokens.shape), grad_cond, gain1_sum,
            grad_ada, ada_bias_sum, grad_qkv, grad_out, gain2_sum, grad_up, bu_sum, grad_down,
            bd_sum,
        )
    grad_down = weight_gradient(act, d_low)
    grad_up = weight_gradient(hidden2, d_up)
    grad_out = weight_gradient(att, d_attention)
    early = gather_all(payload[:14].reshape(-1))

    dq, dk, dv, dkx, dvx, dks, dvs = attend_back_call(
        place, q, kv_long, kv_other, kv_short, d_att, lse, cos, sin, rows
    )
    ek = ev = None
    for step in range(1, span):
        back = [((i, (i + step) % span)) for i in range(span)]
        cut = slice((step - 1) * rows, step * rows)
        pk, pv = lax.ppermute((dkx[cut], dvx[cut]), "span", back)
        ek = pk if ek is None else (ek.astype(F32) + pk.astype(F32))
        ev = pv if ev is None else (ev.astype(F32) + pv.astype(F32))
    d_short = jnp.concatenate([dks, dvs], axis=1)
    for step in range(1, span):
        d_short = d_short + lax.ppermute(
            jnp.concatenate([dks, dvs], axis=1), "span", [(step, 0)]
        )
    d_qkv = join_call(
        place, dq, dk, dv, ek, ev, d_short[:, :D], d_short[:, D:], cos, sin, rows
    )
    grad_qkv = weight_gradient(hidden1, d_qkv)
    grad_in, d_mod1, d_gain1 = last_call(
        place, tokens2, d_qkv, d_mid, mod, gain1, qkv_weight, rows
    )
    late = gather_all(jnp.concatenate([d_mod1[:, :2].reshape(-1), d_gain1[0]]))

    cut = slots * 4 * D
    mods2 = jnp.sum(early[:, :, :cut], axis=1).reshape(seq * slots, 4 * D)
    sums2 = jnp.sum(early[:, :, cut:], axis=(0, 1))
    cut = slots * 2 * D
    mods1 = jnp.sum(late[:, :, :cut], axis=1).reshape(seq * slots, 2 * D)
    gain1_sum = jnp.sum(late[:, :, cut:], axis=(0, 1))
    d_mods = jnp.concatenate([mods1, mods2], axis=1)
    grad_ada_bias = jnp.sum(d_mods, axis=0)
    cond_all = table[:, :slots].reshape(seq * slots, 128)
    assign_all = table[:, slots : 2 * slots, 0].reshape(seq * slots)
    number = jnp.arange(seq * slots, dtype=jnp.int32).astype(F32)
    picker = (assign_all[:, None] == number[None, :]).astype(F32)
    exact = partial(lax.dot_general, precision=HIGHEST, preferred_element_type=F32)
    cond_rows = exact(picker, cond_all, (((1,), (0,)), ((), ())))
    silu_low = jax.nn.silu(cond_rows).astype(BF16).astype(F32)
    ada_rows, ada_cols = 128 // seq, 6 * D // span
    grad_ada = exact(
        lax.dynamic_slice_in_dim(silu_low, seq_at * ada_rows, ada_rows, 1),
        lax.dynamic_slice_in_dim(d_mods, span_at * ada_cols, ada_cols, 1),
        (((0,), (0,)), ((), ())),
    )
    wanted = lax.dynamic_slice_in_dim(picker, seq_at * slots, slots, 1)
    own_mods = exact(wanted, d_mods, (((0,), (0,)), ((), ())))
    d_silu = exact(own_mods, ada_weight.astype(F32), (((1,), (1,)), ((), ())))
    grad_cond = jax.vjp(jax.nn.silu, conditions.astype(F32))[1](d_silu)[0]
    return (
        out.reshape(tokens.shape),
        grad_in.reshape(tokens.shape),
        grad_cond,
        gain1_sum,
        grad_ada,
        grad_ada_bias,
        grad_qkv,
        grad_out,
        sums2[:D],
        grad_up,
        sums2[2 * D :],
        grad_down,
        sums2[D : 2 * D],
    )


def solution(mesh):
    data, table, one = P("seq", "span", None), P("seq", None), P("seq")
    tile = P("seq", "span")
    in_specs = (data, table, one, one) + (P(),) * 10 + (data,)
    out_specs = (data, data, table, P(), tile, P(), tile, tile, P(), tile, P(), tile, P())
    return jax.shard_map(shards, mesh=mesh, in_specs=in_specs, out_specs=out_specs, check_vma=False)
```

```python
from functools import partial

import jax
import jax.numpy as jnp
import numpy as np
from jax import lax
from jax.experimental import pallas as pl
from jax.experimental.pallas import tpu as pltpu
from jax.sharding import PartitionSpec as P

HEADS = 12
HEAD = 64
D = 768
FF = 3072
PAIR = 128
PAIRS = HEADS // 2
LEN = 1024
SHORT = 128
SLOTS = 2
CHUNK = 768
EPSILON = 1e-5
LOG2E = 1.4426950408889634
GELU_C = 0.7978845608028654
BIG = 62 << 20
MESH = pl.DeviceIdType.MESH
F32 = jnp.float32
BF16 = jnp.bfloat16
HIGHEST = lax.Precision.HIGHEST


def nn(a, b):
    return lax.dot_general(a, b, (((1,), (0,)), ((), ())), preferred_element_type=F32)


def nt(a, b):
    return lax.dot_general(a, b, (((1,), (1,)), ((), ())), preferred_element_type=F32)


def tn(a, b):
    return lax.dot_general(a, b, (((0,), (0,)), ((), ())), preferred_element_type=F32)


def whole(shape, buffers=1):
    return pl.BlockSpec(shape, lambda *_: (0,) * len(shape), pipeline_mode=pl.Buffered(buffers))


def cost(flops, bytes_accessed, transcendentals=0):
    return pl.CostEstimate(
        flops=int(flops), bytes_accessed=int(bytes_accessed), transcendentals=int(transcendentals)
    )


def col_sum(x):
    return jnp.sum(x, axis=0, keepdims=True)


def wide_row(ref):
    return ref[...].astype(F32).reshape(1, ref.shape[0])


def row_mean(x):
    return jnp.mean(x, axis=-1, keepdims=True)


def rotary(length):
    half = HEAD // 2
    freq = np.power(np.float32(10000.0), -np.arange(half, dtype=np.float32) / np.float32(half))
    angles = np.arange(length, dtype=np.float32)[:, None] * freq.astype(np.float32)[None, :]
    cos, sin = np.cos(angles), np.sin(angles)
    return (
        np.concatenate([cos] * 4, axis=1).astype(np.float32),
        np.concatenate([-sin, sin, -sin, sin], axis=1).astype(np.float32),
    )


def swap_halves(x):
    lane = lax.broadcasted_iota(jnp.int32, x.shape, 1)
    first = (lane & 32) == 0
    return jnp.where(first, pltpu.roll(x, x.shape[1] - 32, 1), pltpu.roll(x, 32, 1))


def turn(x, cos, sin):
    return x * cos + swap_halves(x) * sin


def turn_back(x, cos, sin):
    return x * cos - swap_halves(x) * sin


def slot_of(lengths, j):
    long = jnp.where(lengths[1] > lengths[0], 1, 0)
    return j + long - 2 * j * long


def heads_of(x):
    lane = lax.broadcasted_iota(jnp.int32, x.shape, 1)
    zero = jnp.zeros_like(x)
    return jnp.where(lane < HEAD, x, zero), jnp.where(lane < HEAD, zero, x)


def modulation_kernel(
    n, cond_ref, assign_ref, weight_ref, bias_ref, mod_ref, table_ref, silu_ref,
    own_ref, send, recv, local,
):
    me = lax.axis_index("seq")
    asked = [jnp.full((1, 128), assign_ref[k].astype(F32)) for k in range(SLOTS)]
    own_ref[...] = jnp.concatenate(
        [cond_ref[...].astype(F32)] + asked + [jnp.zeros((8 - 2 * SLOTS, 128), F32)], axis=0
    )
    barrier = pltpu.get_barrier_semaphore()
    for step in range(1, n):
        pl.semaphore_signal(
            barrier, inc=1, device_id={"seq": lax.rem(me + step, n)}, device_id_type=MESH
        )
    mine = pltpu.make_async_copy(own_ref, table_ref.at[me], local)
    mine.start()
    pl.semaphore_wait(barrier, n - 1)
    copies = []
    for step in range(1, n):
        copy = pltpu.make_async_remote_copy(
            src_ref=own_ref,
            dst_ref=table_ref.at[me],
            send_sem=send.at[step],
            recv_sem=recv.at[step],
            device_id={"seq": lax.rem(me + step, n)},
            device_id_type=MESH,
        )
        copy.start()
        copies.append(copy)
    mine.wait()
    for copy in copies:
        copy.wait()
    source = lax.broadcasted_iota(jnp.int32, (n, 128), 0).astype(F32) * SLOTS
    rows = []
    for slot in range(SLOTS):
        wanted = own_ref[SLOTS + slot : SLOTS + slot + 1, :]
        row = jnp.zeros((1, 128), F32)
        for k in range(SLOTS):
            row += col_sum(jnp.where(wanted == source + k, table_ref[:, k, :], 0.0))
        rows.append(row)
    cond = jnp.concatenate(rows + [jnp.zeros((8 - SLOTS, 128), F32)], axis=0)
    silu = (cond / (1.0 + jnp.exp(-cond))).astype(BF16)
    mod_ref[...] = nn(silu, weight_ref[...]) + bias_ref[...].astype(F32).reshape(1, 6 * D)
    for slot in range(SLOTS):
        wanted = table_ref[:, SLOTS + slot, :]
        rows = jnp.zeros((n, 128), F32)
        for k in range(SLOTS * n):
            row = table_ref[k // SLOTS, k % SLOTS : k % SLOTS + 1, :]
            rows += jnp.where(wanted == k, row, 0.0)
        silu_ref[slot] = (rows / (1.0 + jnp.exp(-rows))).astype(BF16).astype(F32)


def modulation_call(cond, assignment, ada_weight, ada_bias, n):
    vmem = pl.BlockSpec(memory_space=pltpu.VMEM)
    return pl.pallas_call(
        partial(modulation_kernel, n),
        name="modulation",
        out_shape=(
            jax.ShapeDtypeStruct((8, 6 * D), F32),
            jax.ShapeDtypeStruct((n, 8, 128), F32),
            jax.ShapeDtypeStruct((SLOTS, n, 128), F32),
        ),
        in_specs=[vmem, pl.BlockSpec(memory_space=pltpu.SMEM), vmem, vmem],
        out_specs=(vmem, vmem, vmem),
        scratch_shapes=[
            pltpu.VMEM((8, 128), F32),
            pltpu.SemaphoreType.DMA((n,)),
            pltpu.SemaphoreType.DMA((n,)),
            pltpu.SemaphoreType.DMA,
        ],
        compiler_params=pltpu.CompilerParams(
            collective_id=0, has_side_effects=True, vmem_limit_bytes=BIG
        ),
        cost_estimate=cost(1e7, 2e6),
    )(cond, assignment, ada_weight, ada_bias)


def project_kernel(
    order, tok_ref, mod_ref, gain_ref, weight_ref, cos_ref, sin_ref,
    q_ref, h_ref, kvl_ref, kvs_ref,
):
    j = pl.program_id(0)
    row = mod_ref[pl.ds(slot_of(order, j), 1), :]
    shift, scale = row[:, :D], row[:, D : 2 * D]
    x = tok_ref[...].astype(F32)
    center = x - row_mean(x)
    xhat = center * lax.rsqrt(row_mean(center * center) + EPSILON)
    hidden = (xhat * wide_row(gain_ref) * (1.0 + scale) + shift).astype(BF16)
    h_ref[...] = hidden
    cos = jnp.concatenate([cos_ref[...]] * PAIRS, axis=1)
    sin = jnp.concatenate([sin_ref[...]] * PAIRS, axis=1)
    q_ref[...] = turn(nn(hidden, weight_ref[:, :D]), cos, sin).astype(BF16)
    k = turn(nn(hidden, weight_ref[:, D : 2 * D]), cos, sin).astype(BF16)
    v = nn(hidden, weight_ref[:, 2 * D :]).astype(BF16)

    @pl.when(j == 0)
    def _():
        kvl_ref[:, :D] = k
        kvl_ref[:, D:] = v

    @pl.when(j == 1)
    def _():
        kvs_ref[:, :D] = k
        kvs_ref[:, D:] = v


def project_call(place, tokens, mod, gain, weight, cos, sin, rows):
    tile = min(256, rows)
    tiles = rows // tile
    return pl.pallas_call(
        project_kernel,
        name="project",
        out_shape=(
            jax.ShapeDtypeStruct((SLOTS * rows, D), BF16),
            jax.ShapeDtypeStruct((SLOTS * rows, D), BF16),
            jax.ShapeDtypeStruct((rows, 2 * D), BF16),
            jax.ShapeDtypeStruct((rows, 2 * D), BF16),
        ),
        grid_spec=pltpu.PrefetchScalarGridSpec(
            num_scalar_prefetch=1,
            grid=(SLOTS, tiles),
            in_specs=[
                pl.BlockSpec((tile, D), lambda j, t, o: (slot_of(o, j) * tiles + t, 0)),
                whole((8, 6 * D)),
                whole((D,)),
                whole((D, 3 * D)),
                pl.BlockSpec((tile, PAIR), lambda j, t, o: (o[2] * tiles + t, 0)),
                pl.BlockSpec((tile, PAIR), lambda j, t, o: (o[2] * tiles + t, 0)),
            ],
            out_specs=[
                pl.BlockSpec((tile, D), lambda j, t, o: (j * tiles + t, 0)),
                pl.BlockSpec((tile, D), lambda j, t, o: (j * tiles + t, 0)),
                pl.BlockSpec((tile, 2 * D), lambda j, t, o: (t + j * (tiles - 1 - t), 0)),
                pl.BlockSpec((tile, 2 * D), lambda j, t, o: (j * t, 0)),
            ],
        ),
        compiler_params=pltpu.CompilerParams(vmem_limit_bytes=BIG),
        cost_estimate=cost(2 * SLOTS * rows * D * 3 * D, 14e6),
    )(place, tokens, mod, gain, weight, cos, sin)


def attend_slot(q, keys, values):
    outs, stats = [], []
    all_scores = [[nt(k, qh) for k in keys] for qh in heads_of(q)]
    for head, scores in enumerate(all_scores):
        top = jnp.max(scores[0], axis=0, keepdims=True)
        for s in scores[1:]:
            top = jnp.maximum(top, jnp.max(s, axis=0, keepdims=True))
        total, out = None, None
        for s, v in zip(scores, values):
            p = jnp.exp2((s - top) * (0.125 * LOG2E))
            part = col_sum(p)
            o = tn(v, p.astype(BF16))
            total = part if total is None else total + part
            out = o if out is None else out + o
        out = out[head * HEAD : (head + 1) * HEAD] / total
        outs.append(out)
        stats.append(top * (0.125 * LOG2E) + jnp.log2(total))
    return jnp.concatenate(outs, axis=0).T.astype(BF16), stats


def attend_kernel(ql, qs, ko, vo, kx, vx, ks, vs, out_ref, lse_ref):
    rows = ql.shape[0]
    out, stats = attend_slot(ql[...], [ko[...], kx[...]], [vo[...], vx[...]])
    out_ref[:rows, :] = out
    lse_ref[0, 0:1, :] = stats[0]
    lse_ref[0, 1:2, :] = stats[1]
    out, stats = attend_slot(qs[...], [ks[...]], [vs[...]])
    out_ref[rows:, :] = out
    lse_ref[0, 2:3, :] = stats[0]
    lse_ref[0, 3:4, :] = stats[1]


def pair_specs(rows):
    def at(n, block, base):
        return pl.BlockSpec((n, PAIR), lambda h: (block, base + h))

    return [
        at(rows, 0, 0),
        at(rows, 1, 0),
        at(rows, 0, 0),
        at(rows, 0, PAIRS),
        at(LEN - rows, 0, 0),
        at(LEN - rows, 0, PAIRS),
        at(SHORT, 0, 0),
        at(SHORT, 0, PAIRS),
    ]


def attend_call(q, kv_own, kv_other, kv_short, rows):
    return pl.pallas_call(
        attend_kernel,
        name="attend",
        grid=(PAIRS,),
        out_shape=(
            jax.ShapeDtypeStruct((SLOTS * rows, D), BF16),
            jax.ShapeDtypeStruct((PAIRS, 4, rows), F32),
        ),
        in_specs=pair_specs(rows),
        out_specs=(
            pl.BlockSpec((SLOTS * rows, PAIR), lambda h: (0, h)),
            pl.BlockSpec((1, 4, rows), lambda h: (h, 0, 0)),
        ),
        compiler_params=pltpu.CompilerParams(vmem_limit_bytes=BIG),
        cost_estimate=cost(16 * D * rows * (LEN + SHORT), 9e6, HEADS * rows * (LEN + SHORT)),
    )(q, q, kv_own, kv_own, kv_other, kv_other, kv_short, kv_short)


def attend_back_slot(q, keys, values, d_out, out, lse, between=None):
    count = len(keys)
    d_keys, d_values = [None] * count, [None] * count
    d_query = []
    q_heads, d_heads = heads_of(q), heads_of(d_out)
    inner = (d_out.astype(F32) * out.astype(F32)).T
    all_scores = [[nt(k, qh) for k in keys] for qh in q_heads]
    all_d_probs = [[nt(v, dh) for v in values] for dh in d_heads]
    for head in range(2):
        if head == 1 and between is not None:
            between()
        qh, dh = q_heads[head], d_heads[head]
        delta = col_sum(inner[head * HEAD : (head + 1) * HEAD])
        scores, d_probs = all_scores[head], all_d_probs[head]
        dq = None
        for i in range(count):
            probs = jnp.exp2(scores[i] * (0.125 * LOG2E) - lse[head])
            d_scores = (probs * (d_probs[i] - delta)).astype(BF16)
            dv = nn(probs.astype(BF16), dh)
            dk = nn(d_scores, qh)
            part = tn(keys[i], d_scores)
            dq = part if dq is None else dq + part
            d_values[i] = dv if head == 0 else d_values[i] + dv
            d_keys[i] = dk if head == 0 else d_keys[i] + dk
        d_query.append(dq[head * HEAD : (head + 1) * HEAD])
    d_keys = [dk * 0.125 for dk in d_keys]
    return (jnp.concatenate(d_query, axis=0) * 0.125).T, d_keys, d_values


def attend_back_kernel(
    place, ql, qs, ko, vo, kx, vx, ks, vs, dol, dos, al, as_, lse, cos, sin,
    dq_ref, dko, dvo, dkx, dvx, dks, dvs,
):
    rows = ql.shape[0]
    stats = lse[0]
    dq, dk, dv = attend_back_slot(
        ql[...], [ko[...], kx[...]], [vo[...], vx[...]], dol[...], al[...],
        [stats[0:1], stats[1:2]],
    )
    dq_ref[:rows, :] = turn_back(dq, cos[...], sin[...]).astype(BF16)
    dko[...] = dk[0]
    dvo[...] = dv[0]
    dkx[...] = dk[1].astype(BF16)
    dvx[...] = dv[1].astype(BF16)
    dq, dk, dv = attend_back_slot(
        qs[...], [ks[...]], [vs[...]], dos[...], as_[...], [stats[2:3], stats[3:4]]
    )
    dq_ref[rows:, :] = turn_back(dq, cos[...], sin[...]).astype(BF16)
    dks[...] = dk[0]
    dvs[...] = dv[0]


def attend_back_call(place, q, kv_own, kv_other, kv_short, d_att, att, lse, cos, sin, rows):
    specs = [
        pl.BlockSpec(s.block_shape, partial(lambda m, h, o: m(h), s.index_map))
        for s in pair_specs(rows)
    ]
    other = LEN - rows
    return pl.pallas_call(
        attend_back_kernel,
        name="attend_back",
        out_shape=(
            jax.ShapeDtypeStruct((SLOTS * rows, D), BF16),
            jax.ShapeDtypeStruct((rows, D), F32),
            jax.ShapeDtypeStruct((rows, D), F32),
            jax.ShapeDtypeStruct((other, D), BF16),
            jax.ShapeDtypeStruct((other, D), BF16),
            jax.ShapeDtypeStruct((SHORT, D), F32),
            jax.ShapeDtypeStruct((SHORT, D), F32),
        ),
        grid_spec=pltpu.PrefetchScalarGridSpec(
            num_scalar_prefetch=1,
            grid=(PAIRS,),
            in_specs=specs
            + [
                pl.BlockSpec((rows, PAIR), lambda h, o: (0, h)),
                pl.BlockSpec((rows, PAIR), lambda h, o: (1, h)),
                pl.BlockSpec((rows, PAIR), lambda h, o: (0, h)),
                pl.BlockSpec((rows, PAIR), lambda h, o: (1, h)),
                pl.BlockSpec((1, 4, rows), lambda h, o: (h, 0, 0)),
                pl.BlockSpec((rows, PAIR), lambda h, o: (o[2], 0)),
                pl.BlockSpec((rows, PAIR), lambda h, o: (o[2], 0)),
            ],
            out_specs=[
                pl.BlockSpec((SLOTS * rows, PAIR), lambda h, o: (0, h)),
                pl.BlockSpec((rows, PAIR), lambda h, o: (0, h)),
                pl.BlockSpec((rows, PAIR), lambda h, o: (0, h)),
                pl.BlockSpec((other, PAIR), lambda h, o: (0, h)),
                pl.BlockSpec((other, PAIR), lambda h, o: (0, h)),
                pl.BlockSpec((SHORT, PAIR), lambda h, o: (0, h)),
                pl.BlockSpec((SHORT, PAIR), lambda h, o: (0, h)),
            ],
        ),
        compiler_params=pltpu.CompilerParams(vmem_limit_bytes=BIG),
        cost_estimate=cost(40 * D * rows * (LEN + SHORT), 16e6, HEADS * rows * (LEN + SHORT)),
    )(
        place, q, q, kv_own, kv_own, kv_other, kv_other, kv_short, kv_short,
        d_att, d_att, att, att, lse, cos, sin,
    )


def part_of(index, size):
    if isinstance(index, int):
        return pl.ds(index * size, size)
    return pl.ds(pl.multiple_of(index * size, size), size)


def add_to(ref, value, first):
    @pl.when(first)
    def _():
        ref[...] = value

    @pl.when(jnp.logical_not(first))
    def _():
        ref[...] += value


def feed_kernel(
    halves, order, tok_ref, att_ref, cot_ref, hid1_ref, mod_ref, gain_ref, wo_ref, wu_ref, bu_ref, wd_ref, bd_ref,
    out_ref, dmid_ref, datt_ref, act_ref, dlow_ref, h_ref, dup_ref, dattn_ref,
    payload_ref, toks_ref, hid1s_ref,
):
    j, t = pl.program_id(0), pl.program_id(1)
    toks_ref[...] = tok_ref[...]
    hid1s_ref[...] = hid1_ref[...]
    row = mod_ref[pl.ds(slot_of(order, j), 1), :]
    gate1, shift2 = row[:, 2 * D : 3 * D], row[:, 3 * D : 4 * D]
    scale2, gate2 = row[:, 4 * D : 5 * D], row[:, 5 * D :]
    gain, up_bias = wide_row(gain_ref), wide_row(bu_ref)
    attention = nn(att_ref[...], wo_ref[...])
    middle = tok_ref[...].astype(F32) + gate1 * attention
    center = middle - row_mean(middle)
    r = lax.rsqrt(row_mean(center * center) + EPSILON)
    xhat = center * r
    hidden = (xhat * gain * (1.0 + scale2) + shift2).astype(BF16)
    h_ref[...] = hidden
    dy = cot_ref[...].astype(F32)
    d_low = (gate2 * dy).astype(BF16)
    me = lax.axis_index("span")
    at = [h * me + (1 - h) * (1 - me) if halves else h for h in range(2)]
    for h in range(2):
        dlow_ref[:, part_of(at[h], D // 2)] = d_low[:, h * (D // 2) : (h + 1) * (D // 2)]
    lowered, d_hidden = None, None
    sums = []
    for f in range(0, FF, CHUNK):
        cols = slice(f, f + CHUNK)
        up = nn(hidden, wu_ref[:, cols]) + up_bias[:, cols]
        d_act = nt(d_low, wd_ref[cols, :])
        square = up * up
        bend = jnp.tanh(up * (GELU_C + (GELU_C * 0.044715) * square))
        half = 0.5 * (1.0 + bend)
        act = (up * half).astype(BF16)
        slope = half + (0.5 * up) * (1.0 - bend * bend) * (
            GELU_C + (3 * GELU_C * 0.044715) * square
        )
        d_up = (d_act * slope).astype(BF16)
        act_ref[:, cols] = act
        place = at[f // (FF // 2)] * (FF // 2) + f % (FF // 2)
        dup_ref[:, pl.ds(pl.multiple_of(place, CHUNK) if halves else place, CHUNK)] = d_up
        sums.append(col_sum(d_up.astype(F32)))
        low = nn(act, wd_ref[cols, :])
        dh = nt(d_up, wu_ref[:, cols])
        lowered = low if lowered is None else lowered + low
        d_hidden = dh if d_hidden is None else d_hidden + dh
    lowered = lowered + wide_row(bd_ref)
    out_ref[...] = (middle + gate2 * lowered).astype(BF16)
    d_gate2 = col_sum(dy * lowered)
    d_shift2 = col_sum(d_hidden)
    hx = col_sum(d_hidden * xhat)
    e = d_hidden * (1.0 + scale2)
    fx = e * gain
    d_mid = dy + r * (fx - row_mean(fx) - xhat * row_mean(fx * xhat))
    dmid_ref[...] = d_mid
    d_gate1 = col_sum(d_mid * attention)
    d_attention = (gate1 * d_mid).astype(BF16)
    for h in range(2):
        dattn_ref[:, part_of(at[h], D // 2)] = d_attention[:, h * (D // 2) : (h + 1) * (D // 2)]
    datt_ref[...] = nt(d_attention, wo_ref[...]).astype(BF16)
    first = jnp.logical_and(j == 0, t == 0)
    slot = slot_of(order, j)
    four = jnp.concatenate([d_gate1, d_shift2, hx * gain, d_gate2], axis=0)
    none = jnp.zeros((4, D), F32)
    add_to(
        payload_ref,
        jnp.concatenate(
            [
                jnp.where(slot == 0, four, none), jnp.where(slot == 0, none, four),
                hx * (1.0 + scale2), col_sum(d_low.astype(F32)), *sums, jnp.zeros((2, D), F32),
            ],
            axis=0,
        ),
        first,
    )


def feed_call(halves, place, tokens, att, cot, hidden1, mod, gain, wo, wu, bu, wd, bd, rows):
    tile = min(256, rows)
    tiles = rows // tile

    def own(j, t, o):
        return (slot_of(o, j) * tiles + t, 0)

    def sorted_(j, t, o):
        return (j * tiles + t, 0)

    n = SLOTS * rows
    return pl.pallas_call(
        partial(feed_kernel, halves),
        name="feed",
        out_shape=(
            jax.ShapeDtypeStruct((n, D), BF16),
            jax.ShapeDtypeStruct((n, D), F32),
            jax.ShapeDtypeStruct((n, D), BF16),
            jax.ShapeDtypeStruct((n, FF), BF16),
            jax.ShapeDtypeStruct((n, D), BF16),
            jax.ShapeDtypeStruct((n, D), BF16),
            jax.ShapeDtypeStruct((n, FF), BF16),
            jax.ShapeDtypeStruct((n, D), BF16),
            jax.ShapeDtypeStruct((16, D), F32),
            jax.ShapeDtypeStruct((n, D), BF16),
            jax.ShapeDtypeStruct((n, D), BF16),
        ),
        grid_spec=pltpu.PrefetchScalarGridSpec(
            num_scalar_prefetch=1,
            grid=(SLOTS, tiles),
            in_specs=[
                pl.BlockSpec((tile, D), own),
                pl.BlockSpec((tile, D), sorted_),
                pl.BlockSpec((tile, D), own),
                pl.BlockSpec((tile, D), own if halves else sorted_),
                whole((8, 6 * D)),
                whole((D,)),
                whole((D, D)),
                whole((D, FF)),
                whole((FF,)),
                whole((FF, D)),
                whole((D,)),
            ],
            out_specs=[
                pl.BlockSpec((tile, D), own),
                pl.BlockSpec((tile, D), sorted_),
                pl.BlockSpec((tile, D), sorted_),
                pl.BlockSpec((tile, FF), sorted_),
                pl.BlockSpec((tile, D), sorted_),
                pl.BlockSpec((tile, D), sorted_),
                pl.BlockSpec((tile, FF), sorted_),
                pl.BlockSpec((tile, D), sorted_),
                pl.BlockSpec((16, D), lambda j, t, o: (0, 0)),
                pl.BlockSpec((tile, D), sorted_),
                pl.BlockSpec((tile, D), sorted_),
            ],
        ),
        compiler_params=pltpu.CompilerParams(vmem_limit_bytes=BIG),
        cost_estimate=cost(2 * n * D * (4 * FF + 2 * D), 40e6, n * FF),
    )(place, tokens, att, cot, hidden1, mod, gain, wo, wu, bu, wd, bd)


def weight_gradient(left, right):
    seq, span = lax.axis_size("seq"), lax.axis_size("span")
    grad = tn(left, right)
    rows, cols = grad.shape
    shaped = grad.reshape(seq, rows // seq, span, cols // span).transpose(0, 2, 1, 3)
    return lax.psum_scatter(
        shaped.reshape(seq * span, rows // seq, cols // span),
        ("seq", "span"),
        scatter_dimension=0,
        tiled=True,
    )[0]


def join_kernel(place, dq_ref, dk_ref, dv_ref, ek_ref, ev_ref, sk_ref, sv_ref, cos, sin, out_ref):
    j, t = pl.program_id(0), pl.program_id(1)
    out_ref[:, :D] = dq_ref[...]
    wide_cos = jnp.concatenate([cos[...]] * PAIRS, axis=1)
    wide_sin = jnp.concatenate([sin[...]] * PAIRS, axis=1)

    @pl.when(j == 0)
    def _():
        dk = dk_ref[...] + ek_ref[...].astype(F32)
        out_ref[:, D : 2 * D] = turn_back(dk, wide_cos, wide_sin).astype(BF16)
        out_ref[:, 2 * D :] = (dv_ref[...] + ev_ref[...].astype(F32)).astype(BF16)

    @pl.when(j == 1)
    def _():
        out_ref[:, D:] = jnp.zeros((out_ref.shape[0], 2 * D), BF16)

    @pl.when(jnp.logical_and(j == 1, jnp.logical_and(t == 0, place[2] == 0)))
    def _():
        dk = turn_back(sk_ref[...], wide_cos[:SHORT], wide_sin[:SHORT])
        out_ref[:SHORT, D : 2 * D] = dk.astype(BF16)
        out_ref[:SHORT, 2 * D :] = sv_ref[...].astype(BF16)


def join_call(place, dq, dk, dv, ek, ev, sk, sv, cos, sin, rows):
    tile = min(256, rows)
    tiles = rows // tile

    def long(j, t, o):
        return (t + j * (tiles - 1 - t), 0)

    return pl.pallas_call(
        join_kernel,
        name="join",
        out_shape=jax.ShapeDtypeStruct((SLOTS * rows, 3 * D), BF16),
        grid_spec=pltpu.PrefetchScalarGridSpec(
            num_scalar_prefetch=1,
            grid=(SLOTS, tiles),
            in_specs=[pl.BlockSpec((tile, D), lambda j, t, o: (j * tiles + t, 0))]
            + [pl.BlockSpec((tile, D), long)] * 4
            + [whole((SHORT, D))] * 2
            + [pl.BlockSpec((tile, PAIR), lambda j, t, o: (o[2] * tiles + t, 0))] * 2,
            out_specs=pl.BlockSpec((tile, 3 * D), lambda j, t, o: (j * tiles + t, 0)),
        ),
        compiler_params=pltpu.CompilerParams(vmem_limit_bytes=BIG),
        cost_estimate=cost(1e7, 12e6),
    )(place, dq, dk, dv, ek, ev, sk, sv, cos, sin)


def last_kernel(
    order, tok_ref, dqkv_ref, dmid_ref, mod_ref, gain_ref, weight_ref,
    out_ref, dmod_ref, dgain_ref,
):
    j, t = pl.program_id(0), pl.program_id(1)
    scale = mod_ref[pl.ds(slot_of(order, j), 1), :][:, D : 2 * D]
    gain = wide_row(gain_ref)
    d_hidden = nt(dqkv_ref[...], weight_ref[...])
    x = tok_ref[...].astype(F32)
    center = x - row_mean(x)
    r = lax.rsqrt(row_mean(center * center) + EPSILON)
    xhat = center * r
    hx = col_sum(d_hidden * xhat)
    fx = d_hidden * (1.0 + scale) * gain
    out_ref[...] = dmid_ref[...] + r * (fx - row_mean(fx) - xhat * row_mean(fx * xhat))
    first = jnp.logical_and(j == 0, t == 0)
    add_to(
        dmod_ref,
        jnp.concatenate([col_sum(d_hidden), hx * gain, jnp.zeros((6, D), F32)], axis=0)[None],
        t == 0,
    )
    add_to(dgain_ref, hx * (1.0 + scale), first)


def last_call(place, tokens, dqkv, dmid, mod, gain, weight, rows):
    tile = min(256, rows)
    tiles = rows // tile

    def own(j, t, o):
        return (slot_of(o, j) * tiles + t, 0)

    def sorted_(j, t, o):
        return (j * tiles + t, 0)

    n = SLOTS * rows
    return pl.pallas_call(
        last_kernel,
        name="last",
        out_shape=(
            jax.ShapeDtypeStruct((n, D), F32),
            jax.ShapeDtypeStruct((SLOTS, 8, D), F32),
            jax.ShapeDtypeStruct((1, D), F32),
        ),
        grid_spec=pltpu.PrefetchScalarGridSpec(
            num_scalar_prefetch=1,
            grid=(SLOTS, tiles),
            in_specs=[
                pl.BlockSpec((tile, D), own),
                pl.BlockSpec((tile, 3 * D), sorted_),
                pl.BlockSpec((tile, D), sorted_),
                whole((8, 6 * D)),
                whole((D,)),
                whole((D, 3 * D)),
            ],
            out_specs=[
                pl.BlockSpec((tile, D), own),
                pl.BlockSpec((1, 8, D), lambda j, t, o: (slot_of(o, j), 0, 0)),
                pl.BlockSpec((1, D), lambda j, t, o: (0, 0)),
            ],
        ),
        compiler_params=pltpu.CompilerParams(vmem_limit_bytes=BIG),
        cost_estimate=cost(2 * n * D * 3 * D, 18e6),
    )(place, tokens, dqkv, dmid, mod, gain, weight)


def share_kernel(
    tok_ref, mod_ref, gain_ref, weight_ref, cos_ref, sin_ref,
    q_ref, h_ref, kv_ref, kvx_any, stage, send, recv,
):
    step = pl.program_id(0)
    steps = stage.shape[0]
    tile = tok_ref.shape[0]
    me = lax.axis_index("span")

    def copy(i):
        return pltpu.make_async_remote_copy(
            src_ref=stage.at[i],
            dst_ref=kvx_any.at[pl.ds(pl.multiple_of(i * tile, tile), tile)],
            send_sem=send.at[i],
            recv_sem=recv.at[i],
            device_id={"span": 1 - me},
            device_id_type=MESH,
        )

    row = mod_ref[pl.ds(step // (steps // SLOTS), 1), :]
    shift, scale = row[:, :D], row[:, D : 2 * D]
    x = tok_ref[...].astype(F32)
    center = x - row_mean(x)
    xhat = center * lax.rsqrt(row_mean(center * center) + EPSILON)
    hidden = (xhat * wide_row(gain_ref) * (1.0 + scale) + shift).astype(BF16)
    h_ref[...] = hidden
    start = (me * (steps // SLOTS) + lax.rem(step, steps // SLOTS)) * tile
    start = pl.multiple_of(start, tile)
    cos = jnp.concatenate([cos_ref[pl.ds(start, tile), :]] * PAIRS, axis=1)
    sin = jnp.concatenate([sin_ref[pl.ds(start, tile), :]] * PAIRS, axis=1)
    k = turn(nn(hidden, weight_ref[:, D : 2 * D]), cos, sin).astype(BF16)
    v = nn(hidden, weight_ref[:, 2 * D :]).astype(BF16)
    kv_ref[:, :D] = k
    kv_ref[:, D:] = v
    stage[step, :, :D] = k
    stage[step, :, D:] = v

    @pl.when(step == 0)
    def _():
        greet([{"span": 1 - me}])

    copy(step).start()
    q_ref[...] = turn(nn(hidden, weight_ref[:, :D]), cos, sin).astype(BF16)

    @pl.when(step == steps - 1)
    def _():
        for i in range(steps):
            copy(i).wait()


def share_call(tokens, mod, gain, weight, cos, sin, rows):
    tile = 256
    n = SLOTS * rows
    steps = n // tile

    def at(width):
        return pl.BlockSpec((tile, width), lambda s: (s, 0))

    return pl.pallas_call(
        share_kernel,
        name="project",
        grid=(steps,),
        out_shape=(
            jax.ShapeDtypeStruct((n, D), BF16),
            jax.ShapeDtypeStruct((n, D), BF16),
            jax.ShapeDtypeStruct((n, 2 * D), BF16),
            jax.ShapeDtypeStruct((n, 2 * D), BF16),
        ),
        in_specs=[
            at(D),
            whole((8, 6 * D)),
            whole((D,)),
            whole((D, 3 * D)),
            whole((LEN, PAIR)),
            whole((LEN, PAIR)),
        ],
        out_specs=(at(D), at(D), at(2 * D), pl.BlockSpec(memory_space=pl.ANY)),
        scratch_shapes=[
            pltpu.VMEM((steps, tile, 2 * D), BF16),
            pltpu.SemaphoreType.DMA((steps,)),
            pltpu.SemaphoreType.DMA((steps,)),
        ],
        compiler_params=pltpu.CompilerParams(
            collective_id=4, has_side_effects=True, vmem_limit_bytes=BIG
        ),
        cost_estimate=cost(2 * n * D * 3 * D, 14e6),
    )(tokens, mod, gain, weight, cos, sin)


def attend_sorted_kernel(
    lengths, ql, qs, ko, vo, kx, vx, ks_own, vs_own, ks_other, vs_other,
    out_ref, lse_ref, q_ref, ko_ref, vo_ref, kx_ref, vx_ref, ks_ref, vs_ref,
):
    rows = ql.shape[0]
    first = lax.axis_index("span") == 0
    ks = jnp.where(first, ks_own[...], ks_other[...])
    vs = jnp.where(first, vs_own[...], vs_other[...])
    q_ref[:rows, :] = ql[...]
    q_ref[rows:, :] = qs[...]
    ks_ref[...] = ks
    vs_ref[...] = vs
    for ref, given in ((ko_ref, ko), (vo_ref, vo), (kx_ref, kx), (vx_ref, vx)):
        ref[...] = given[...]
    out, stats = attend_slot(ql[...], [ko[...], kx[...]], [vo[...], vx[...]])
    out_ref[:rows, :] = out
    lse_ref[0, 0:1, :] = stats[0]
    lse_ref[0, 1:2, :] = stats[1]
    out, stats = attend_slot(qs[...], [ks], [vs])
    out_ref[rows:, :] = out
    lse_ref[0, 2:3, :] = stats[0]
    lse_ref[0, 3:4, :] = stats[1]


def attend_sorted_call(lengths, q, kv, kvx, rows):
    n = SLOTS * rows
    per = rows // SHORT

    def long(base):
        return pl.BlockSpec((rows, PAIR), lambda h, o: (slot_of(o, 0), base + h))

    def short(base):
        return pl.BlockSpec((SHORT, PAIR), lambda h, o: (slot_of(o, 1) * per, base + h))

    def out(size):
        return pl.BlockSpec((size, PAIR), lambda h, o: (0, h))

    return pl.pallas_call(
        attend_sorted_kernel,
        name="attend",
        out_shape=(
            jax.ShapeDtypeStruct((n, D), BF16),
            jax.ShapeDtypeStruct((PAIRS, 4, rows), F32),
            jax.ShapeDtypeStruct((n, D), BF16),
        )
        + (jax.ShapeDtypeStruct((rows, D), BF16),) * 4
        + (jax.ShapeDtypeStruct((SHORT, D), BF16),) * 2,
        grid_spec=pltpu.PrefetchScalarGridSpec(
            num_scalar_prefetch=1,
            grid=(PAIRS,),
            in_specs=[
                long(0),
                pl.BlockSpec((rows, PAIR), lambda h, o: (slot_of(o, 1), h)),
                long(0), long(PAIRS), long(0), long(PAIRS),
                short(0), short(PAIRS), short(0), short(PAIRS),
            ],
            out_specs=[out(n), pl.BlockSpec((1, 4, rows), lambda h, o: (h, 0, 0)), out(n)]
            + [out(rows)] * 4
            + [out(SHORT)] * 2,
        ),
        compiler_params=pltpu.CompilerParams(vmem_limit_bytes=BIG),
        cost_estimate=cost(16 * D * rows * (LEN + SHORT), 16e6, HEADS * rows * (LEN + SHORT)),
    )(lengths, q, q, kv, kv, kvx, kvx, kv, kv, kvx, kvx)


def flip(index, bit):
    return index + bit - 2 * bit * ((index // bit) % 2)


def add_low(a, b):
    return (a.astype(F32) + b.astype(F32)).astype(BF16)


def plane_peers():
    s, c = lax.axis_index("seq"), lax.axis_index("span")
    return [{"span": 1 - c}, {"seq": flip(s, 1)}, {"seq": flip(s, 2)}]


def line_peers():
    s = lax.axis_index("seq")
    return [{"seq": lax.rem(s + 4 * step, 16)} for step in range(1, 4)]


def greet(peers):
    barrier = pltpu.get_barrier_semaphore()
    for peer in peers:
        pl.semaphore_signal(barrier, inc=1, device_id=peer, device_id_type=MESH)
    pl.semaphore_wait(barrier, len(peers))


class Scatter:
    def __init__(self, send, recv, base, other=None, own=None, came0=None, a1=None, b1=None,
                 came2=None, came3=None):
        self.send, self.recv, self.base = send, recv, base
        self.other, self.own, self.came0 = other, own, came0
        self.a1, self.b1, self.came2, self.came3 = a1, b1, came2, came3
        s = lax.axis_index("seq")
        self.x, self.y, self.z = lax.rem(s, 2), lax.rem(s // 2, 2), s // 4
        self.core_peer, self.x_peer, self.y_peer = plane_peers()
        self.z_peers = line_peers()

    def copy(self, i):
        x, y, z = self.x, self.y, self.z
        if i == 0:
            src, dst, peer = self.other, self.came0, self.core_peer
        elif i >= 8:
            src, dst, peer = self.other.at[i - 8], self.came0.at[i - 8], self.core_peer
        elif i == 1:
            src, dst, peer = self.own.at[0:2, :, 1 - x], self.a1, self.x_peer
        elif i == 2:
            src, dst, peer = self.own.at[2:4, 1 - y], self.b1, self.y_peer
        elif i == 3:
            src, dst, peer = self.a1.at[:, 1 - y], self.came2.at[0:2], self.y_peer
        elif i == 4:
            src, dst, peer = self.b1.at[:, 1 - x], self.came2.at[2:4], self.x_peer
        else:
            step = i - 4
            src, dst = self.came2.at[lax.rem(z + step, 4)], self.came3.at[step - 1]
            peer = self.z_peers[step - 1]
        return pltpu.make_async_remote_copy(
            src_ref=src,
            dst_ref=dst,
            send_sem=self.send.at[self.base + i],
            recv_sem=self.recv.at[self.base + i],
            device_id=peer,
            device_id_type=MESH,
        )

    def start(self, *which):
        for i in which:
            self.copy(i).start()

    def arrive(self, *which):
        for i in which:
            self.copy(i).wait_recv()

    def drain(self, *which):
        for i in which:
            self.copy(i).wait_send()

    def merge0(self):
        def body(i, _):
            z, y, x = i // 4, lax.rem(i // 2, 2), lax.rem(i, 2)
            self.own[z, y, x] = add_low(self.own[z, y, x], self.came0[z, y, x])
            return 0

        lax.fori_loop(0, 16, body, 0)

    def add1(self, a_ref, b_ref):
        self.arrive(1, 2)

        def body(i, _):
            z, k = i // 2, lax.rem(i, 2)
            a_ref[z, k] = add_low(self.own[z, k, self.x], self.a1[z, k])
            b_ref[z, k] = add_low(self.own[2 + z, self.y, k], self.b1[z, k])
            return 0

        lax.fori_loop(0, 4, body, 0)

    def add2(self, out_ref):
        self.arrive(3, 4)

        def body(z, _):
            out_ref[z] = add_low(self.a1[z, self.y], self.came2[z])
            out_ref[2 + z] = add_low(self.b1[z, self.x], self.came2[2 + z])
            return 0

        lax.fori_loop(0, 2, body, 0)

    def total(self):
        self.arrive(5, 6, 7)
        total = self.came2[self.z].astype(F32)
        for step in range(3):
            total = total + self.came3[step].astype(F32)
        return total

    def scatter0(self):
        self.start(0)

    def scatter1(self):
        self.arrive(0)
        self.merge0()
        self.start(1, 2)

    def scatter2(self):
        self.add1(self.a1, self.b1)
        self.start(3, 4)

    def scatter3(self):
        self.add2(self.came2)
        self.start(5, 6, 7)


def half_shape(rows, cols):
    return (4, 2, 2, rows, cols)


ANY = pl.BlockSpec(memory_space=pl.ANY)
DMA = pltpu.SemaphoreType.DMA


FIRST = 9
ROUNDS = PAIRS // 2
WIDE = 3 * PAIR


def middle_kernel(
    act_ref, dlow_ref, att_ref, dattn_ref, h_ref, dup_ref, hid1_ref, payload_ref,
    ql, qs, ko, vo, kx, vx, ks, vs, dol, dos, al, as_, lse, cos_ref, sin_ref,
    dq_ref, dk_ref, dv_ref, down_ref, out_ref, up_ref, ra_ref, rb_ref, rown_ref, early_ref,
    down_other, down_own, down_came, down_a, down_b, down2, down3,
    out_other, out_own, out_came, out_a, out_b, out2, out3,
    up_other, up_own, up_came, up_a, up_b, up2,
    round_came, round_a, round_b, d_round, keep_q,
    leave, come, keep_k, keep_v, keep_sk, keep_sv, early_came, early_sum, early_all,
    send, recv, send_kv, recv_kv, send_early, recv_early,
):
    step = pl.program_id(0)
    s, me = lax.axis_index("seq"), lax.axis_index("span")
    rows = ql.shape[0]
    down = Scatter(
        send, recv, 0, other=down_other, own=down_own, came0=down_came, a1=down_a, b1=down_b,
        came2=down2, came3=down3,
    )
    out = Scatter(
        send, recv, 12, other=out_other, own=out_own, came0=out_came, a1=out_a, b1=out_b,
        came2=out2, came3=out3,
    )
    up = Scatter(
        send, recv, 20, other=up_other, own=up_own, came0=up_came, a1=up_a, b1=up_b, came2=up2,
    )
    part, wide = hid1_ref.shape[1] // 16, WIDE
    rounds = [
        Scatter(
            send, recv, 28 + 3 * k,
            other=down_other.at[:, :, :, k * part : (k + 1) * part],
            own=rown_ref.at[k - 1] if k else up_other.at[:, :, :, :, :wide],
            came0=round_came.at[k],
            a1=round_a,
            b1=round_b,
        )
        for k in range(ROUNDS)
    ]
    cos = cos_ref[pl.ds(pl.multiple_of(me * rows, rows), rows), :]
    sin = sin_ref[pl.ds(pl.multiple_of(me * rows, rows), rows), :]

    def kv_copy(pair):
        return pltpu.make_async_remote_copy(
            src_ref=leave.at[pair],
            dst_ref=come.at[pair],
            send_sem=send_kv.at[pair],
            recv_sem=recv_kv.at[pair],
            device_id={"span": 1 - me},
            device_id_type=MESH,
        )

    def early_copy(k):
        if k == 0:
            src, dst, peer = payload_ref, early_came, {"span": 1 - me}
        else:
            src, dst, peer = early_sum, early_all.at[s], {"seq": lax.rem(s + k, 16)}
        return pltpu.make_async_remote_copy(
            src_ref=src,
            dst_ref=dst,
            send_sem=send_early.at[k],
            recv_sem=recv_early.at[k],
            device_id=peer,
            device_id_type=MESH,
        )

    def at(number):
        return pl.when(step == number)

    @at(0)
    def _():
        greet([{"span": 1 - me}] + [{"seq": lax.rem(s + k, 16)} for k in range(1, 16)])
        early_copy(0).start()

    @at(3)
    def _():
        early_copy(0).wait_recv()
        early_sum[...] = (payload_ref[...] + early_came[...]).astype(BF16)
        for k in range(1, 16):
            early_copy(k).start()
        early_all[s] = early_sum[...]

    @at(2)
    def _():
        out.scatter1()

    @at(4)
    def _():
        out.scatter2()

    @at(6)
    def _():
        down.arrive(8, 9, 10, 11)
        down.merge0()
        down.start(1, 2)
        out.scatter3()

    @at(FIRST + 1)
    def _():
        up.scatter1()

    @at(FIRST + 2)
    def _():
        down.drain(8, 9, 10, 11)
        up.drain(0)
        down.scatter2()

    @at(FIRST + 5)
    def _():
        rounds[0].scatter1()

    def between():
        @at(FIRST + 4)
        def _():
            down.scatter3()

        @at(FIRST + 5)
        def _():
            up.scatter2()

    @at(0)
    def _():
        value = tn(att_ref[...], dattn_ref[...]).astype(BF16)
        out_other[...] = value[:, : D // 2].reshape(out_own.shape)
        out_own[...] = value[:, D // 2 :].reshape(out_own.shape)
        out.scatter0()

    @pl.when(jnp.logical_and(step >= 1, step < 5))
    def _():
        value = tn(act_ref[...], dlow_ref[...]).astype(BF16)
        shape = down_own.shape[1:]
        down_other[step - 1] = value[:, : D // 2].reshape(shape)
        down_own[step - 1] = value[:, D // 2 :].reshape(shape)

        for m in range(4):
            @at(m + 1)
            def _():
                down.start(8 + m)

    @pl.when(jnp.logical_and(step >= 5, step < FIRST))
    def _():
        value = tn(h_ref[...], dup_ref[...]).astype(BF16)
        value = value.reshape(up_own.shape[:4] + (CHUNK,))
        cols = pl.ds(pl.multiple_of(lax.rem(step - 5, 2) * CHUNK, CHUNK), CHUNK)

        @pl.when(step < 7)
        def _():
            up_other[:, :, :, :, cols] = value

        @pl.when(step >= 7)
        def _():
            up_own[:, :, :, :, cols] = value

    @at(6)
    def _():
        up.scatter0()

    @pl.when(jnp.logical_and(step >= FIRST, step < FIRST + PAIRS))
    def _():
        pair = step - FIRST
        stats = lse[0]
        dq, dk, dv = attend_back_slot(
            ql[...], [ko[...], kx[...]], [vo[...], vx[...]], dol[...], al[...],
            [stats[0:1], stats[1:2]], between,
        )
        dq = turn_back(dq, cos, sin).astype(BF16)
        dq_ref[:rows, :] = dq
        keep_q[lax.rem(pair, 2), :rows, :] = dq
        keep_k[lax.rem(pair, 2)] = dk[0]
        keep_v[lax.rem(pair, 2)] = dv[0]
        leave[pair, :rows, :PAIR] = dk[1].astype(BF16)
        leave[pair, :rows, PAIR:] = dv[1].astype(BF16)
        dq, dk, dv = attend_back_slot(
            qs[...], [ks[...]], [vs[...]], dos[...], as_[...], [stats[2:3], stats[3:4]]
        )
        dq = turn_back(dq, cos, sin).astype(BF16)
        dq_ref[rows:, :] = dq
        keep_q[lax.rem(pair, 2), rows:, :] = dq
        keep_sk[lax.rem(pair, 2)] = dk[0]
        keep_sv[lax.rem(pair, 2)] = dv[0]
        leave[pair, rows:, :PAIR] = dk[0].astype(BF16)
        leave[pair, rows:, PAIR:] = dv[0].astype(BF16)
        kv_copy(pair).start()

    @pl.when(step > FIRST)
    def _():
        pair = step - FIRST - 1
        kv_copy(pair).wait_recv()
        dk = keep_k[lax.rem(pair, 2)] + come[pair, :rows, :PAIR].astype(F32)
        dk_ref[:rows, :] = turn_back(dk, cos, sin).astype(BF16)
        dv = keep_v[lax.rem(pair, 2)] + come[pair, :rows, PAIR:].astype(F32)
        dv_ref[:rows, :] = dv.astype(BF16)
        zero = jnp.zeros((SHORT, PAIR), F32)
        sk = keep_sk[lax.rem(pair, 2)] + come[pair, rows:, :PAIR].astype(F32)
        sk = jnp.where(me == 0, turn_back(sk, cos[:SHORT], sin[:SHORT]), zero)
        sv = keep_sv[lax.rem(pair, 2)] + come[pair, rows:, PAIR:].astype(F32)
        dk_ref[rows : rows + SHORT, :] = sk.astype(BF16)
        dv_ref[rows : rows + SHORT, :] = jnp.where(me == 0, sv, zero).astype(BF16)
        rest = jnp.zeros((rows - SHORT, PAIR), BF16)
        dk_ref[rows + SHORT :, :] = rest
        dv_ref[rows + SHORT :, :] = rest
        later = lax.rem(pair, 2)
        first, second = wide * (1 - me), wide * me
        q_at = first + later * PAIR
        k_at = (first + 2 * PAIR) * (1 - later) + second * later
        v_at = second + PAIR + later * PAIR
        d_round[:, pl.ds(pl.multiple_of(q_at, PAIR), PAIR)] = keep_q[later]
        d_round[:, pl.ds(pl.multiple_of(k_at, PAIR), PAIR)] = dk_ref[...]
        d_round[:, pl.ds(pl.multiple_of(v_at, PAIR), PAIR)] = dv_ref[...]

    for k in range(ROUNDS):
        @at(FIRST + 2 * k + 2)
        def _():
            value = tn(hid1_ref[...], d_round[...]).astype(BF16)
            rounds[k].other[...] = value[:, :wide].reshape(half_shape(part, wide))
            rounds[k].start(0)
            rounds[k].own[...] = value[:, wide:].reshape(half_shape(part, wide))

    @at(FIRST + PAIRS)
    def _():
        out_ref[...] = out.total()
        for k in (1, 2):
            rounds[k].arrive(0)
            rounds[k].merge0()
        rounds[0].add1(ra_ref, rb_ref)
        down_ref[...] = down.total()
        up.add2(up_ref)
        down.drain(*range(1, 8))
        out.drain(*range(8))
        up.drain(*range(1, 5))
        rounds[0].drain(0, 1, 2)
        rounds[1].drain(0)
        rounds[2].drain(0)
        for pair in range(PAIRS):
            kv_copy(pair).wait_send()
        for k in range(16):
            if k > 0:
                early_copy(k).wait_recv()
            early_copy(k).wait_send()
        early_ref[...] = early_all[...]


def middle_call(
    act, d_low, att, d_attention, hidden, d_up, hidden1, payload, q, kv, d_att, lse, cos, sin, rows,
):
    n = SLOTS * rows
    half = FF // 2
    dr, dc = FF // 16, D // 2
    ur, wr = D // 16, D // 16

    def clamp(s, low, high):
        return jnp.minimum(jnp.maximum(s, low), high)

    def order_of(k):
        return k // 2 + lax.rem(k, 2) * ROUNDS

    def now(s):
        return order_of(clamp(s - FIRST, 0, PAIRS - 1))

    def before(s):
        return order_of(clamp(s - FIRST - 1, 0, PAIRS - 1))

    def long():
        return pl.BlockSpec((rows, PAIR), lambda s: (0, now(s)))

    def second():
        return pl.BlockSpec((rows, PAIR), lambda s: (1, now(s)))

    def short():
        return pl.BlockSpec((SHORT, PAIR), lambda s: (0, now(s)))

    def low(shape):
        return pltpu.VMEM(shape, BF16)

    handed = ((4, ur, half), (2, 2, ur, WIDE), (2, 2, ur, WIDE), (2,) + half_shape(ur, WIDE))

    return pl.pallas_call(
        middle_kernel,
        name="middle",
        grid=(FIRST + PAIRS + 1,),
        out_shape=(
            jax.ShapeDtypeStruct((n, D), BF16),
            jax.ShapeDtypeStruct((n, D), BF16),
            jax.ShapeDtypeStruct((n, D), BF16),
            jax.ShapeDtypeStruct((dr, dc), F32),
            jax.ShapeDtypeStruct((wr, dc), F32),
        )
        + tuple(jax.ShapeDtypeStruct(o, BF16) for o in handed + ((16, 16, D),)),
        in_specs=[
            pl.BlockSpec((n, D), lambda s: (0, clamp(s - 1, 0, 3))),
            whole((n, D)),
            whole((n, D)),
            whole((n, D)),
            whole((n, D)),
            pl.BlockSpec((n, CHUNK), lambda s: (0, clamp(s - 5, 0, 3))),
            whole((n, D)),
            whole((16, D)),
            long(), second(), long(), long(), long(), long(), short(), short(), long(), second(),
            long(), second(),
            pl.BlockSpec((1, 4, rows), lambda s: (now(s), 0, 0)),
            whole((LEN, PAIR)),
            whole((LEN, PAIR)),
        ],
        out_specs=(
            pl.BlockSpec((n, PAIR), lambda s: (0, now(s))),
            pl.BlockSpec((n, PAIR), lambda s: (0, before(s))),
            pl.BlockSpec((n, PAIR), lambda s: (0, before(s))),
            whole((dr, dc)),
            whole((wr, dc)),
        )
        + tuple(whole(o) for o in handed + ((16, 16, D),)),
        scratch_shapes=[low(half_shape(dr, dc))] * 3
        + [low((2, 2, dr, dc))] * 2
        + [low((4, dr, dc)), low((3, dr, dc))]
        + [low(half_shape(wr, dc))] * 3
        + [low((2, 2, wr, dc))] * 2
        + [low((4, wr, dc)), low((3, wr, dc))]
        + [low(half_shape(ur, half))] * 3
        + [low((2, 2, ur, half))] * 2
        + [low((4, ur, half))]
        + [low((ROUNDS,) + half_shape(ur, WIDE))]
        + [low((2, 2, ur, WIDE))] * 2
        + [low((n, 2 * WIDE)), low((2, n, PAIR))]
        + [low((PAIRS, rows + SHORT, 2 * PAIR))] * 2
        + [pltpu.VMEM((2, rows, PAIR), F32)] * 2
        + [pltpu.VMEM((2, SHORT, PAIR), F32)] * 2
        + [pltpu.VMEM((16, D), F32), low((16, D)), low((16, 16, D))]
        + [DMA((37,)), DMA((37,)), DMA((PAIRS,)), DMA((PAIRS,)), DMA((16,)), DMA((16,))],
        compiler_params=pltpu.CompilerParams(
            collective_id=1, has_side_effects=True, vmem_limit_bytes=BIG
        ),
        cost_estimate=cost(2 * n * D * (2 * FF + D) + 40 * D * rows * (LEN + SHORT), 50e6),
    )(
        act, d_low, att, d_attention, hidden, d_up, hidden1, payload, q, q, *kv, d_att, d_att,
        att, att, lse, cos, sin,
    )


TILES = 4


def pack_rows(rows):
    parts = [rows[r : r + 1, c : c + 128] for r in range(5) for c in range(0, D, 128)]
    return jnp.concatenate(parts + [jnp.zeros((2, 128), F32)], axis=0).astype(BF16)


def end_kernel(
    tok_ref, dmid_ref, dq_ref, dk_ref, dv_ref, mod_ref, gain_ref, weight_ref, lengths,
    up_in, ra, rb, rown,
    grad_ref, gqkv_ref, gup_ref, late_ref,
    up2, up3, r2, r3, last_a, last_b, sums, sums_came, sums_all, late_came,
    send, recv, send_late, recv_late,
):
    step = pl.program_id(0)
    s, me = lax.axis_index("seq"), lax.axis_index("span")
    up = Scatter(send, recv, 0, came2=up2, came3=up3)
    rounds = [
        Scatter(
            send, recv, 8 * (k + 1), own=rown.at[k - 1] if k else None,
            a1=last_a.at[k - 1] if k else ra,
            b1=last_b.at[k - 1] if k else rb,
            came2=r2.at[k], came3=r3.at[k],
        )
        for k in range(ROUNDS)
    ]

    def late_copy(k):
        if k == 0:
            src, dst, peer = sums, sums_came, {"span": 1 - me}
        else:
            src, dst, peer = sums_all, late_came.at[s], {"seq": lax.rem(s + k, 16)}
        return pltpu.make_async_remote_copy(
            src_ref=src,
            dst_ref=dst,
            send_sem=send_late.at[k],
            recv_sem=recv_late.at[k],
            device_id=peer,
            device_id_type=MESH,
        )

    def at(number):
        return pl.when(step == number)

    @at(0)
    def _():
        up2[...] = up_in[...]
        sums[...] = jnp.zeros_like(sums)
        greet([{"span": 1 - me}] + [{"seq": lax.rem(s + k, 16)} for k in range(1, 16)])
        up.start(5, 6, 7)
        rounds[0].start(3, 4)
        rounds[1].start(1, 2)
        rounds[2].start(1, 2)

    size = tok_ref.shape[0]
    j = step // 2
    swapped = jnp.full((1, D), jnp.where(lengths[1] > lengths[0], 1.0, 0.0))
    mine = jnp.where(j == 0, swapped, 1.0 - swapped)
    scale = jnp.where(mine == 0.0, mod_ref[0:1, D : 2 * D], mod_ref[1:2, D : 2 * D])
    gain = wide_row(gain_ref)
    d_hidden = (
        nt(dq_ref[...], weight_ref[:, :D])
        + nt(dk_ref[...], weight_ref[:, D : 2 * D])
        + nt(dv_ref[...], weight_ref[:, 2 * D :])
    )
    x = tok_ref[...].astype(F32)
    center = x - row_mean(x)
    r = lax.rsqrt(row_mean(center * center) + EPSILON)
    xhat = center * r
    hx = col_sum(d_hidden * xhat)
    fx = d_hidden * (1.0 + scale) * gain
    grad_ref[...] = dmid_ref[...] + r * (fx - row_mean(fx) - xhat * row_mean(fx * xhat))
    shift = col_sum(d_hidden)
    first, second = mine == 0.0, mine != 0.0
    zero = jnp.zeros((1, D), F32)
    sums[...] += jnp.concatenate(
        [
            jnp.where(first, shift, zero), jnp.where(first, hx * gain, zero),
            jnp.where(second, shift, zero), jnp.where(second, hx * gain, zero),
            hx * (1.0 + scale), jnp.zeros((3, D), F32),
        ],
        axis=0,
    )

    @at(TILES - 1)
    def _():
        late_copy(0).start()
        rounds[0].scatter3()
        late_copy(0).wait_recv()
        sums_all[...] = pack_rows(sums[...] + sums_came[...])
        for k in range(1, 16):
            late_copy(k).start()
        rounds[1].scatter2()
        rounds[2].scatter2()
        rounds[1].scatter3()
        late_came[s] = sums_all[...]
        rounds[2].scatter3()
        gup_ref[...] = up.total()
        for k in range(ROUNDS):
            total = rounds[k].total()
            for c in range(3):
                cols = slice((c * ROUNDS + k) * PAIR, (c * ROUNDS + k + 1) * PAIR)
                gqkv_ref[:, cols] = total[:, c * PAIR : (c + 1) * PAIR]
        up.drain(5, 6, 7)
        rounds[0].drain(*range(3, 8))
        rounds[1].drain(*range(1, 8))
        rounds[2].drain(*range(1, 8))
        for k in range(16):
            if k > 0:
                late_copy(k).wait_recv()
            late_copy(k).wait_send()
        late_ref[...] = late_came[...]


def end_call(tokens, d_mid, dq, dk, dv, mod, gain, weight, lengths, handed, rows):
    n = SLOTS * rows
    size = n // TILES
    r = D // 16

    def tile():
        return pl.BlockSpec((size, D), lambda s: (s, 0))

    return pl.pallas_call(
        end_kernel,
        name="end",
        grid=(TILES,),
        out_shape=(
            jax.ShapeDtypeStruct((n, D), F32),
            jax.ShapeDtypeStruct((r, 3 * D // 2), F32),
            jax.ShapeDtypeStruct((r, FF // 2), F32),
            jax.ShapeDtypeStruct((16, 32, 128), BF16),
        ),
        in_specs=[tile()] * 5
        + [
            whole((8, 6 * D)),
            whole((D,)),
            whole((D, 3 * D)),
            pl.BlockSpec(memory_space=pltpu.SMEM),
        ]
        + [whole(a.shape) for a in handed],
        out_specs=(
            tile(),
            whole((r, 3 * D // 2)),
            whole((r, FF // 2)),
            whole((16, 32, 128)),
        ),
        scratch_shapes=[
            pltpu.VMEM((4, r, FF // 2), BF16),
            pltpu.VMEM((3, r, FF // 2), BF16),
            pltpu.VMEM((ROUNDS, 4, r, WIDE), BF16),
            pltpu.VMEM((ROUNDS, 3, r, WIDE), BF16),
            pltpu.VMEM((2, 2, 2, r, WIDE), BF16),
            pltpu.VMEM((2, 2, 2, r, WIDE), BF16),
            pltpu.VMEM((8, D), F32),
            pltpu.VMEM((8, D), F32),
            pltpu.VMEM((32, 128), BF16),
            pltpu.VMEM((16, 32, 128), BF16),
            DMA((8 * (ROUNDS + 1),)),
            DMA((8 * (ROUNDS + 1),)),
            DMA((16,)),
            DMA((16,)),
        ],
        compiler_params=pltpu.CompilerParams(
            collective_id=3, has_side_effects=True, vmem_limit_bytes=BIG
        ),
        cost_estimate=cost(2 * n * D * 3 * D, 22e6),
    )(tokens, d_mid, dq, dk, dv, mod, gain, weight, lengths, *handed)


def exact(left, right, over):
    return lax.dot_general(
        left, right, (over, ((), ())), precision=HIGHEST, preferred_element_type=F32
    )


def exact(left, right, over):
    return lax.dot_general(
        left, right, (over, ((), ())), precision=HIGHEST, preferred_element_type=F32
    )


def condition_kernel(
    lengths, early_ref, late_ref, table_ref, silu_ref, weight_ref,
    qkv_in, out_in, up_in, down_in, sorted_any,
    ada_ref, bias_ref, gcond_ref, gain1_ref, gain2_ref, bd_ref, bu_ref,
    qkv_ref, out_ref, up_ref, down_ref, natural_any, stage, read, moved,
):
    seq = late_ref.shape[0]
    me, s = lax.axis_index("span"), lax.axis_index("seq")
    half = sorted_any.shape[0] // SLOTS
    reads = [
        pltpu.make_async_copy(sorted_any.at[pl.ds(j * half, half)], stage.at[j], read.at[j])
        for j in range(SLOTS)
    ]
    moves = [
        pltpu.make_async_copy(
            stage.at[j],
            natural_any.at[pl.ds(pl.multiple_of(slot_of(lengths, j) * half, half), half)],
            moved.at[j],
        )
        for j in range(SLOTS)
    ]
    for copy in reads:
        copy.start()
    qkv_ref[...] = qkv_in[...]
    out_ref[...] = out_in[...]
    up_ref[...] = up_in[...]
    down_ref[...] = down_in[...]
    for j in range(SLOTS):
        reads[j].wait()
        moves[j].start()
    early = early_ref[...].astype(F32)
    packed = late_ref[...].astype(F32)
    late = [
        jnp.concatenate([packed[:, 6 * r + c] for c in range(6)], axis=1) for r in range(5)
    ]
    mods = []
    for k in range(SLOTS):
        mods.append(
            [late[2 * k], late[2 * k + 1]] + [early[:, 4 * k + b] for b in range(4)]
        )
    gain1_ref[...] = jnp.sum(late[4], axis=0)
    gain2_ref[...] = jnp.sum(early[:, 8], axis=0)
    bd_ref[...] = jnp.sum(early[:, 9], axis=0)
    for f in range(4):
        bu_ref[f * D : (f + 1) * D] = jnp.sum(early[:, 10 + f], axis=0)
    own = [jnp.zeros((8, D), F32)] * 6
    row = lax.broadcasted_iota(jnp.int32, (8, seq), 0)
    wanted = (s * SLOTS + row).astype(F32)
    for k in range(SLOTS):
        asked = table_ref[:, SLOTS + k, :].T[:8]
        chosen = jnp.where(jnp.logical_and(asked == wanted, row < SLOTS), 1.0, 0.0)
        for b in range(6):
            own[b] = own[b] + exact(chosen, mods[k][b], ((1,), (0,)))
    d_silu = jnp.zeros((8, 128), F32)
    for b in range(6):
        cols = slice(b * D, (b + 1) * D)
        bias_ref[cols] = jnp.sum(mods[0][b] + mods[1][b], axis=0)
        d_silu += exact(own[b], weight_ref[:, cols].astype(F32), ((1,), (1,)))
    v = table_ref[s]
    sig = 1.0 / (1.0 + jnp.exp(-v))
    gcond_ref[...] = (d_silu * (sig * (1.0 + v * (1.0 - sig))))[:SLOTS]
    rows = 128 // seq
    pick = lax.broadcasted_iota(jnp.int32, (rows, 128), 1) == (
        s * rows + lax.broadcasted_iota(jnp.int32, (rows, 128), 0)
    )
    pick = jnp.where(pick, 1.0, 0.0)
    silu = [exact(pick, silu_ref[k], ((1,), (1,))) for k in range(SLOTS)]
    for b in range(3):
        total = jnp.zeros((rows, D), F32)
        for k in range(SLOTS):
            block = jnp.where(me == 0, mods[k][b], mods[k][3 + b])
            total += exact(silu[k], block, ((1,), (0,)))
        ada_ref[:, b * D : (b + 1) * D] = total
    for move in moves:
        move.wait()


def condition_call(lengths, early, late, table, silu, ada_weight, tiles, grad_in):
    seq = late.shape[0]

    def all_of(shape):
        return pl.BlockSpec(shape, lambda i, p: (0,) * len(shape))

    given = (early, late, table, silu, ada_weight) + tiles
    outs = ((128 // seq, 3 * D), (6 * D,), (SLOTS, 128), (D,), (D,), (D,), (FF,))
    outs += tuple(t.shape for t in tiles)
    return pl.pallas_call(
        condition_kernel,
        name="condition",
        out_shape=tuple(jax.ShapeDtypeStruct(o, F32) for o in outs + (grad_in.shape,)),
        grid_spec=pltpu.PrefetchScalarGridSpec(
            num_scalar_prefetch=1,
            grid=(1,),
            in_specs=[whole(a.shape) for a in given] + [ANY],
            out_specs=[all_of(o) for o in outs] + [ANY],
            scratch_shapes=[
                pltpu.VMEM((SLOTS, grad_in.shape[0] // SLOTS, D), F32), DMA((SLOTS,)), DMA((SLOTS,)),
            ],
        ),
        compiler_params=pltpu.CompilerParams(vmem_limit_bytes=BIG),
        cost_estimate=cost(1e7, 12e6),
    )(lengths, *given, grad_in)


def from_peers(array, span):
    return [
        lax.ppermute(array, "span", [((i + step) % span, i) for i in range(span)])
        for step in range(1, span)
    ]


def gather_all(flat):
    seq, span = lax.axis_size("seq"), lax.axis_size("span")
    return lax.all_gather(flat, ("seq", "span"), axis=0).reshape(seq, span, flat.shape[0])


def shards(
    tokens, conditions, assignment, lengths, norm1_gain, ada_weight, ada_bias, qkv_weight,
    out_weight, norm2_gain, up_weight, up_bias, down_weight, down_bias, cotangent,
):
    slots, rows, _ = tokens.shape
    seq, span = lax.axis_size("seq"), lax.axis_size("span")
    seq_at, span_at = lax.axis_index("seq"), lax.axis_index("span")
    flat = slots * rows
    place = jnp.concatenate(
        [lengths, jnp.stack([span_at.astype(jnp.int32), seq_at.astype(jnp.int32)])]
    )
    fast = seq == 16 and span == 2
    cos, sin = (jnp.asarray(table) for table in rotary(LEN))
    mod, table, silu_all = modulation_call(conditions, assignment, ada_weight, ada_bias, seq)

    tokens2 = tokens.reshape(flat, D)
    gain1, gain2 = norm1_gain, norm2_gain
    if fast:
        q, hidden1, kv, kvx = share_call(tokens2, mod, gain1, qkv_weight, cos, sin, rows)
        att, lse, q, *kv = attend_sorted_call(lengths, q, kv, kvx, rows)
    else:
        q, hidden1, kv_long, kv_tail = project_call(
            place, tokens2, mod, gain1, qkv_weight, cos, sin, rows
        )
        kv_other = jnp.concatenate(from_peers(kv_long, span), axis=0)
        kv_short = kv_tail[:SHORT]
        sent = [lax.ppermute(kv_short, "span", [(0, i)]) for i in range(1, span)]
        kv_short = jnp.where(span_at == 0, kv_short, sum(sent[1:], sent[0]))
        att, lse = attend_call(q, kv_long, kv_other, kv_short, rows)
    (
        out, d_mid, d_att, act, d_low, hidden2, d_up, d_attention, payload, tokens_sorted,
        hidden1_sorted,
    ) = feed_call(
        fast, lengths, tokens2, att, cotangent.reshape(flat, D), hidden1, mod, gain2, out_weight,
        up_weight, up_bias, down_weight, down_bias, rows,
    )
    if fast:
        dq, dk, dv, grad_down, grad_out, *handed, early = middle_call(
            act, d_low, att, d_attention, hidden2, d_up, hidden1_sorted, payload, q, kv, d_att,
            lse, cos, sin, rows,
        )
        grad_in, grad_qkv, grad_up, late = end_call(
            tokens_sorted, d_mid, dq, dk, dv, mod, gain1, qkv_weight, lengths, handed, rows
        )
        (
            grad_ada, ada_bias_sum, grad_cond, gain1_sum, gain2_sum, bd_sum, bu_sum,
            grad_qkv, grad_out, grad_up, grad_down, grad_in,
        ) = condition_call(
            lengths, early, late, table, silu_all, ada_weight,
            (grad_qkv, grad_out, grad_up, grad_down), grad_in,
        )
        return (
            out.reshape(tokens.shape), grad_in.reshape(tokens.shape), grad_cond, gain1_sum,
            grad_ada, ada_bias_sum, grad_qkv, grad_out, gain2_sum, grad_up, bu_sum, grad_down,
            bd_sum,
        )
    grad_down = weight_gradient(act, d_low)
    grad_up = weight_gradient(hidden2, d_up)
    grad_out = weight_gradient(att, d_attention)
    early = gather_all(payload[:14].reshape(-1))

    dq, dk, dv, dkx, dvx, dks, dvs = attend_back_call(
        place, q, kv_long, kv_other, kv_short, d_att, att, lse, cos, sin, rows
    )
    ek = ev = None
    for step in range(1, span):
        back = [((i, (i + step) % span)) for i in range(span)]
        cut = slice((step - 1) * rows, step * rows)
        pk, pv = lax.ppermute((dkx[cut], dvx[cut]), "span", back)
        ek = pk if ek is None else (ek.astype(F32) + pk.astype(F32))
        ev = pv if ev is None else (ev.astype(F32) + pv.astype(F32))
    d_short = jnp.concatenate([dks, dvs], axis=1)
    for step in range(1, span):
        d_short = d_short + lax.ppermute(
            jnp.concatenate([dks, dvs], axis=1), "span", [(step, 0)]
        )
    d_qkv = join_call(
        place, dq, dk, dv, ek, ev, d_short[:, :D], d_short[:, D:], cos, sin, rows
    )
    grad_qkv = weight_gradient(hidden1, d_qkv)
    grad_in, d_mod1, d_gain1 = last_call(
        place, tokens2, d_qkv, d_mid, mod, gain1, qkv_weight, rows
    )
    late = gather_all(jnp.concatenate([d_mod1[:, :2].reshape(-1), d_gain1[0]]))

    cut = slots * 4 * D
    mods2 = jnp.sum(early[:, :, :cut], axis=1).reshape(seq * slots, 4 * D)
    sums2 = jnp.sum(early[:, :, cut:], axis=(0, 1))
    cut = slots * 2 * D
    mods1 = jnp.sum(late[:, :, :cut], axis=1).reshape(seq * slots, 2 * D)
    gain1_sum = jnp.sum(late[:, :, cut:], axis=(0, 1))
    d_mods = jnp.concatenate([mods1, mods2], axis=1)
    grad_ada_bias = jnp.sum(d_mods, axis=0)
    cond_all = table[:, :slots].reshape(seq * slots, 128)
    assign_all = table[:, slots : 2 * slots, 0].reshape(seq * slots)
    number = jnp.arange(seq * slots, dtype=jnp.int32).astype(F32)
    picker = (assign_all[:, None] == number[None, :]).astype(F32)
    exact = partial(lax.dot_general, precision=HIGHEST, preferred_element_type=F32)
    cond_rows = exact(picker, cond_all, (((1,), (0,)), ((), ())))
    silu_low = jax.nn.silu(cond_rows).astype(BF16).astype(F32)
    ada_rows, ada_cols = 128 // seq, 6 * D // span
    grad_ada = exact(
        lax.dynamic_slice_in_dim(silu_low, seq_at * ada_rows, ada_rows, 1),
        lax.dynamic_slice_in_dim(d_mods, span_at * ada_cols, ada_cols, 1),
        (((0,), (0,)), ((), ())),
    )
    wanted = lax.dynamic_slice_in_dim(picker, seq_at * slots, slots, 1)
    own_mods = exact(wanted, d_mods, (((0,), (0,)), ((), ())))
    d_silu = exact(own_mods, ada_weight.astype(F32), (((1,), (1,)), ((), ())))
    grad_cond = jax.vjp(jax.nn.silu, conditions.astype(F32))[1](d_silu)[0]
    return (
        out.reshape(tokens.shape),
        grad_in.reshape(tokens.shape),
        grad_cond,
        gain1_sum,
        grad_ada,
        grad_ada_bias,
        grad_qkv,
        grad_out,
        sums2[:D],
        grad_up,
        sums2[2 * D :],
        grad_down,
        sums2[D : 2 * D],
    )


def solution(mesh):
    data, table, one = P("seq", "span", None), P("seq", None), P("seq")
    tile = P("seq", "span")
    in_specs = (data, table, one, one) + (P(),) * 10 + (data,)
    out_specs = (data, data, table, P(), tile, P(), tile, tile, P(), tile, P(), tile, P())
    return jax.shard_map(shards, mesh=mesh, in_specs=in_specs, out_specs=out_specs, check_vma=False)
```

```python
from functools import partial

import jax
import jax.numpy as jnp
import numpy as np
from jax import lax
from jax.experimental import pallas as pl
from jax.experimental.pallas import tpu as pltpu
from jax.sharding import PartitionSpec as P

HEADS = 12
HEAD = 64
D = 768
FF = 3072
PAIR = 128
PAIRS = HEADS // 2
LEN = 1024
SHORT = 128
SLOTS = 2
CHUNK = 768
EPSILON = 1e-5
LOG2E = 1.4426950408889634
GELU_C = 0.7978845608028654
BIG = 62 << 20
MESH = pl.DeviceIdType.MESH
F32 = jnp.float32
BF16 = jnp.bfloat16
HIGHEST = lax.Precision.HIGHEST


def nn(a, b):
    return lax.dot_general(a, b, (((1,), (0,)), ((), ())), preferred_element_type=F32)


def nt(a, b):
    return lax.dot_general(a, b, (((1,), (1,)), ((), ())), preferred_element_type=F32)


def tn(a, b):
    return lax.dot_general(a, b, (((0,), (0,)), ((), ())), preferred_element_type=F32)


def whole(shape, buffers=1):
    return pl.BlockSpec(shape, lambda *_: (0,) * len(shape), pipeline_mode=pl.Buffered(buffers))


def cost(flops, bytes_accessed, transcendentals=0):
    return pl.CostEstimate(
        flops=int(flops), bytes_accessed=int(bytes_accessed), transcendentals=int(transcendentals)
    )


def col_sum(x):
    return jnp.sum(x, axis=0, keepdims=True)


def wide_row(ref):
    return ref[...].astype(F32).reshape(1, ref.shape[0])


def row_mean(x):
    return jnp.mean(x, axis=-1, keepdims=True)


def rotary(length):
    half = HEAD // 2
    freq = np.power(np.float32(10000.0), -np.arange(half, dtype=np.float32) / np.float32(half))
    angles = np.arange(length, dtype=np.float32)[:, None] * freq.astype(np.float32)[None, :]
    cos, sin = np.cos(angles), np.sin(angles)
    return (
        np.concatenate([cos] * 4, axis=1).astype(np.float32),
        np.concatenate([-sin, sin, -sin, sin], axis=1).astype(np.float32),
    )


def swap_halves(x):
    lane = lax.broadcasted_iota(jnp.int32, x.shape, 1)
    first = (lane & 32) == 0
    return jnp.where(first, pltpu.roll(x, x.shape[1] - 32, 1), pltpu.roll(x, 32, 1))


def turn(x, cos, sin):
    return x * cos + swap_halves(x) * sin


def turn_back(x, cos, sin):
    return x * cos - swap_halves(x) * sin


def slot_of(lengths, j):
    long = jnp.where(lengths[1] > lengths[0], 1, 0)
    return j + long - 2 * j * long


def heads_of(x):
    lane = lax.broadcasted_iota(jnp.int32, x.shape, 1)
    zero = jnp.zeros_like(x)
    return jnp.where(lane < HEAD, x, zero), jnp.where(lane < HEAD, zero, x)


def modulation_kernel(
    n, cond_ref, assign_ref, weight_ref, bias_ref, mod_ref, table_ref, silu_ref,
    own_ref, send, recv, local, extra=(),
):
    me = lax.axis_index("seq")
    asked = [jnp.full((1, 128), assign_ref[k].astype(F32)) for k in range(SLOTS)]
    own_ref[...] = jnp.concatenate(
        [cond_ref[...].astype(F32)] + asked + [jnp.zeros((8 - 2 * SLOTS, 128), F32)], axis=0
    )
    barrier = pltpu.get_barrier_semaphore()
    for step in range(1, n):
        pl.semaphore_signal(
            barrier, inc=1, device_id={"seq": lax.rem(me + step, n)}, device_id_type=MESH
        )
    for peer in extra:
        pl.semaphore_signal(barrier, inc=1, device_id=peer, device_id_type=MESH)
    mine = pltpu.make_async_copy(own_ref, table_ref.at[me], local)
    mine.start()
    pl.semaphore_wait(barrier, n - 1 + len(extra))
    copies = []
    for step in range(1, n):
        copy = pltpu.make_async_remote_copy(
            src_ref=own_ref,
            dst_ref=table_ref.at[me],
            send_sem=send.at[step],
            recv_sem=recv.at[step],
            device_id={"seq": lax.rem(me + step, n)},
            device_id_type=MESH,
        )
        copy.start()
        copies.append(copy)
    mine.wait()
    for copy in copies:
        copy.wait()
    source = lax.broadcasted_iota(jnp.int32, (n, 128), 0).astype(F32) * SLOTS
    rows = []
    for slot in range(SLOTS):
        wanted = own_ref[SLOTS + slot : SLOTS + slot + 1, :]
        row = jnp.zeros((1, 128), F32)
        for k in range(SLOTS):
            row += col_sum(jnp.where(wanted == source + k, table_ref[:, k, :], 0.0))
        rows.append(row)
    cond = jnp.concatenate(rows + [jnp.zeros((8 - SLOTS, 128), F32)], axis=0)
    silu = (cond / (1.0 + jnp.exp(-cond))).astype(BF16)
    mod_ref[...] = nn(silu, weight_ref[...]) + bias_ref[...].astype(F32).reshape(1, 6 * D)
    for slot in range(SLOTS):
        wanted = table_ref[:, SLOTS + slot, :][:, :n]
        lane = lax.broadcasted_iota(jnp.int32, (n, n), 1).astype(F32) * SLOTS
        rows = jnp.zeros((n, 128), F32)
        for k in range(SLOTS):
            chosen = jnp.where(wanted == lane + k, 1.0, 0.0).astype(BF16)
            rows += nn(chosen, table_ref[:, k, :].astype(BF16))
        silu_ref[slot] = (rows / (1.0 + jnp.exp(-rows))).astype(BF16).astype(F32)


def modulation_call(cond, assignment, ada_weight, ada_bias, n):
    vmem = pl.BlockSpec(memory_space=pltpu.VMEM)
    return pl.pallas_call(
        partial(modulation_kernel, n),
        name="modulation",
        out_shape=(
            jax.ShapeDtypeStruct((8, 6 * D), F32),
            jax.ShapeDtypeStruct((n, 8, 128), F32),
            jax.ShapeDtypeStruct((SLOTS, n, 128), F32),
        ),
        in_specs=[vmem, pl.BlockSpec(memory_space=pltpu.SMEM), vmem, vmem],
        out_specs=(vmem, vmem, vmem),
        scratch_shapes=[
            pltpu.VMEM((8, 128), F32),
            pltpu.SemaphoreType.DMA((n,)),
            pltpu.SemaphoreType.DMA((n,)),
            pltpu.SemaphoreType.DMA,
        ],
        compiler_params=pltpu.CompilerParams(
            collective_id=0, has_side_effects=True, vmem_limit_bytes=BIG
        ),
        cost_estimate=cost(1e7, 2e6),
    )(cond, assignment, ada_weight, ada_bias)


def project_kernel(
    order, tok_ref, mod_ref, gain_ref, weight_ref, cos_ref, sin_ref,
    q_ref, h_ref, kvl_ref, kvs_ref,
):
    j = pl.program_id(0)
    row = mod_ref[pl.ds(slot_of(order, j), 1), :]
    shift, scale = row[:, :D], row[:, D : 2 * D]
    x = tok_ref[...].astype(F32)
    center = x - row_mean(x)
    xhat = center * lax.rsqrt(row_mean(center * center) + EPSILON)
    hidden = (xhat * wide_row(gain_ref) * (1.0 + scale) + shift).astype(BF16)
    h_ref[...] = hidden
    cos = jnp.concatenate([cos_ref[...]] * PAIRS, axis=1)
    sin = jnp.concatenate([sin_ref[...]] * PAIRS, axis=1)
    q_ref[...] = turn(nn(hidden, weight_ref[:, :D]), cos, sin).astype(BF16)
    k = turn(nn(hidden, weight_ref[:, D : 2 * D]), cos, sin).astype(BF16)
    v = nn(hidden, weight_ref[:, 2 * D :]).astype(BF16)

    @pl.when(j == 0)
    def _():
        kvl_ref[:, :D] = k
        kvl_ref[:, D:] = v

    @pl.when(j == 1)
    def _():
        kvs_ref[:, :D] = k
        kvs_ref[:, D:] = v


def project_call(place, tokens, mod, gain, weight, cos, sin, rows):
    tile = min(256, rows)
    tiles = rows // tile
    return pl.pallas_call(
        project_kernel,
        name="project",
        out_shape=(
            jax.ShapeDtypeStruct((SLOTS * rows, D), BF16),
            jax.ShapeDtypeStruct((SLOTS * rows, D), BF16),
            jax.ShapeDtypeStruct((rows, 2 * D), BF16),
            jax.ShapeDtypeStruct((rows, 2 * D), BF16),
        ),
        grid_spec=pltpu.PrefetchScalarGridSpec(
            num_scalar_prefetch=1,
            grid=(SLOTS, tiles),
            in_specs=[
                pl.BlockSpec((tile, D), lambda j, t, o: (slot_of(o, j) * tiles + t, 0)),
                whole((8, 6 * D)),
                whole((D,)),
                whole((D, 3 * D)),
                pl.BlockSpec((tile, PAIR), lambda j, t, o: (o[2] * tiles + t, 0)),
                pl.BlockSpec((tile, PAIR), lambda j, t, o: (o[2] * tiles + t, 0)),
            ],
            out_specs=[
                pl.BlockSpec((tile, D), lambda j, t, o: (j * tiles + t, 0)),
                pl.BlockSpec((tile, D), lambda j, t, o: (j * tiles + t, 0)),
                pl.BlockSpec((tile, 2 * D), lambda j, t, o: (t + j * (tiles - 1 - t), 0)),
                pl.BlockSpec((tile, 2 * D), lambda j, t, o: (j * t, 0)),
            ],
        ),
        compiler_params=pltpu.CompilerParams(vmem_limit_bytes=BIG),
        cost_estimate=cost(2 * SLOTS * rows * D * 3 * D, 14e6),
    )(place, tokens, mod, gain, weight, cos, sin)


def attend_slot(q, keys, values):
    outs, stats = [], []
    all_scores = [[nt(k, qh) for k in keys] for qh in heads_of(q)]
    for head, scores in enumerate(all_scores):
        top = jnp.max(scores[0], axis=0, keepdims=True)
        for s in scores[1:]:
            top = jnp.maximum(top, jnp.max(s, axis=0, keepdims=True))
        total, out = None, None
        for s, v in zip(scores, values):
            p = jnp.exp2((s - top) * (0.125 * LOG2E))
            part = col_sum(p)
            o = tn(v, p.astype(BF16))
            total = part if total is None else total + part
            out = o if out is None else out + o
        out = out[head * HEAD : (head + 1) * HEAD] / total
        outs.append(out)
        stats.append(top * (0.125 * LOG2E) + jnp.log2(total))
    return jnp.concatenate(outs, axis=0).T.astype(BF16), stats


def attend_kernel(ql, qs, ko, vo, kx, vx, ks, vs, out_ref, lse_ref):
    rows = ql.shape[0]
    out, stats = attend_slot(ql[...], [ko[...], kx[...]], [vo[...], vx[...]])
    out_ref[:rows, :] = out
    lse_ref[0, 0:1, :] = stats[0]
    lse_ref[0, 1:2, :] = stats[1]
    out, stats = attend_slot(qs[...], [ks[...]], [vs[...]])
    out_ref[rows:, :] = out
    lse_ref[0, 2:3, :] = stats[0]
    lse_ref[0, 3:4, :] = stats[1]


def pair_specs(rows):
    def at(n, block, base):
        return pl.BlockSpec((n, PAIR), lambda h: (block, base + h))

    return [
        at(rows, 0, 0),
        at(rows, 1, 0),
        at(rows, 0, 0),
        at(rows, 0, PAIRS),
        at(LEN - rows, 0, 0),
        at(LEN - rows, 0, PAIRS),
        at(SHORT, 0, 0),
        at(SHORT, 0, PAIRS),
    ]


def attend_call(q, kv_own, kv_other, kv_short, rows):
    return pl.pallas_call(
        attend_kernel,
        name="attend",
        grid=(PAIRS,),
        out_shape=(
            jax.ShapeDtypeStruct((SLOTS * rows, D), BF16),
            jax.ShapeDtypeStruct((PAIRS, 4, rows), F32),
        ),
        in_specs=pair_specs(rows),
        out_specs=(
            pl.BlockSpec((SLOTS * rows, PAIR), lambda h: (0, h)),
            pl.BlockSpec((1, 4, rows), lambda h: (h, 0, 0)),
        ),
        compiler_params=pltpu.CompilerParams(vmem_limit_bytes=BIG),
        cost_estimate=cost(16 * D * rows * (LEN + SHORT), 9e6, HEADS * rows * (LEN + SHORT)),
    )(q, q, kv_own, kv_own, kv_other, kv_other, kv_short, kv_short)


def attend_back_slot(q, keys, values, d_out, out, lse, between=None):
    count = len(keys)
    d_keys, d_values = [None] * count, [None] * count
    d_query = []
    q_heads, d_heads = heads_of(q), heads_of(d_out)
    inner = (d_out.astype(F32) * out.astype(F32)).T
    all_scores = [[nt(k, qh) for k in keys] for qh in q_heads]
    all_d_probs = [[nt(v, dh) for v in values] for dh in d_heads]
    for head in range(2):
        if head == 1 and between is not None:
            between()
        qh, dh = q_heads[head], d_heads[head]
        delta = col_sum(inner[head * HEAD : (head + 1) * HEAD])
        scores, d_probs = all_scores[head], all_d_probs[head]
        dq = None
        for i in range(count):
            probs = jnp.exp2(scores[i] * (0.125 * LOG2E) - lse[head])
            d_scores = (probs * (d_probs[i] - delta)).astype(BF16)
            dv = nn(probs.astype(BF16), dh)
            dk = nn(d_scores, qh)
            part = tn(keys[i], d_scores)
            dq = part if dq is None else dq + part
            d_values[i] = dv if head == 0 else d_values[i] + dv
            d_keys[i] = dk if head == 0 else d_keys[i] + dk
        d_query.append(dq[head * HEAD : (head + 1) * HEAD])
    d_keys = [dk * 0.125 for dk in d_keys]
    return (jnp.concatenate(d_query, axis=0) * 0.125).T, d_keys, d_values


def attend_back_kernel(
    place, ql, qs, ko, vo, kx, vx, ks, vs, dol, dos, al, as_, lse, cos, sin,
    dq_ref, dko, dvo, dkx, dvx, dks, dvs,
):
    rows = ql.shape[0]
    stats = lse[0]
    dq, dk, dv = attend_back_slot(
        ql[...], [ko[...], kx[...]], [vo[...], vx[...]], dol[...], al[...],
        [stats[0:1], stats[1:2]],
    )
    dq_ref[:rows, :] = turn_back(dq, cos[...], sin[...]).astype(BF16)
    dko[...] = dk[0]
    dvo[...] = dv[0]
    dkx[...] = dk[1].astype(BF16)
    dvx[...] = dv[1].astype(BF16)
    dq, dk, dv = attend_back_slot(
        qs[...], [ks[...]], [vs[...]], dos[...], as_[...], [stats[2:3], stats[3:4]]
    )
    dq_ref[rows:, :] = turn_back(dq, cos[...], sin[...]).astype(BF16)
    dks[...] = dk[0]
    dvs[...] = dv[0]


def attend_back_call(place, q, kv_own, kv_other, kv_short, d_att, att, lse, cos, sin, rows):
    specs = [
        pl.BlockSpec(s.block_shape, partial(lambda m, h, o: m(h), s.index_map))
        for s in pair_specs(rows)
    ]
    other = LEN - rows
    return pl.pallas_call(
        attend_back_kernel,
        name="attend_back",
        out_shape=(
            jax.ShapeDtypeStruct((SLOTS * rows, D), BF16),
            jax.ShapeDtypeStruct((rows, D), F32),
            jax.ShapeDtypeStruct((rows, D), F32),
            jax.ShapeDtypeStruct((other, D), BF16),
            jax.ShapeDtypeStruct((other, D), BF16),
            jax.ShapeDtypeStruct((SHORT, D), F32),
            jax.ShapeDtypeStruct((SHORT, D), F32),
        ),
        grid_spec=pltpu.PrefetchScalarGridSpec(
            num_scalar_prefetch=1,
            grid=(PAIRS,),
            in_specs=specs
            + [
                pl.BlockSpec((rows, PAIR), lambda h, o: (0, h)),
                pl.BlockSpec((rows, PAIR), lambda h, o: (1, h)),
                pl.BlockSpec((rows, PAIR), lambda h, o: (0, h)),
                pl.BlockSpec((rows, PAIR), lambda h, o: (1, h)),
                pl.BlockSpec((1, 4, rows), lambda h, o: (h, 0, 0)),
                pl.BlockSpec((rows, PAIR), lambda h, o: (o[2], 0)),
                pl.BlockSpec((rows, PAIR), lambda h, o: (o[2], 0)),
            ],
            out_specs=[
                pl.BlockSpec((SLOTS * rows, PAIR), lambda h, o: (0, h)),
                pl.BlockSpec((rows, PAIR), lambda h, o: (0, h)),
                pl.BlockSpec((rows, PAIR), lambda h, o: (0, h)),
                pl.BlockSpec((other, PAIR), lambda h, o: (0, h)),
                pl.BlockSpec((other, PAIR), lambda h, o: (0, h)),
                pl.BlockSpec((SHORT, PAIR), lambda h, o: (0, h)),
                pl.BlockSpec((SHORT, PAIR), lambda h, o: (0, h)),
            ],
        ),
        compiler_params=pltpu.CompilerParams(vmem_limit_bytes=BIG),
        cost_estimate=cost(40 * D * rows * (LEN + SHORT), 16e6, HEADS * rows * (LEN + SHORT)),
    )(
        place, q, q, kv_own, kv_own, kv_other, kv_other, kv_short, kv_short,
        d_att, d_att, att, att, lse, cos, sin,
    )


def part_of(index, size):
    if isinstance(index, int):
        return pl.ds(index * size, size)
    return pl.ds(pl.multiple_of(index * size, size), size)


def add_to(ref, value, first):
    @pl.when(first)
    def _():
        ref[...] = value

    @pl.when(jnp.logical_not(first))
    def _():
        ref[...] += value


def feed_kernel(
    halves, order, tok_ref, att_ref, cot_ref, hid1_ref, mod_ref, gain_ref, wo_ref, wu_ref, bu_ref, wd_ref, bd_ref,
    out_ref, dmid_ref, datt_ref, act_ref, dlow_ref, h_ref, dup_ref, dattn_ref,
    payload_ref, toks_ref, hid1s_ref,
):
    j, t = pl.program_id(0), pl.program_id(1)
    toks_ref[...] = tok_ref[...]
    hid1s_ref[...] = hid1_ref[...]
    row = mod_ref[pl.ds(slot_of(order, j), 1), :]
    gate1, shift2 = row[:, 2 * D : 3 * D], row[:, 3 * D : 4 * D]
    scale2, gate2 = row[:, 4 * D : 5 * D], row[:, 5 * D :]
    gain, up_bias = wide_row(gain_ref), wide_row(bu_ref)
    attention = nn(att_ref[...], wo_ref[...])
    middle = tok_ref[...].astype(F32) + gate1 * attention
    center = middle - row_mean(middle)
    r = lax.rsqrt(row_mean(center * center) + EPSILON)
    xhat = center * r
    hidden = (xhat * gain * (1.0 + scale2) + shift2).astype(BF16)
    h_ref[...] = hidden
    dy = cot_ref[...].astype(F32)
    d_low = (gate2 * dy).astype(BF16)
    me = lax.axis_index("span")
    at = [h * me + (1 - h) * (1 - me) if halves else h for h in range(2)]
    for h in range(2):
        dlow_ref[:, part_of(at[h], D // 2)] = d_low[:, h * (D // 2) : (h + 1) * (D // 2)]
    lowered, d_hidden = None, None
    sums = []
    for f in range(0, FF, CHUNK):
        cols = slice(f, f + CHUNK)
        up = nn(hidden, wu_ref[:, cols]) + up_bias[:, cols]
        d_act = nt(d_low, wd_ref[cols, :])
        square = up * up
        bend = jnp.tanh(up * (GELU_C + (GELU_C * 0.044715) * square))
        half = 0.5 * (1.0 + bend)
        act = (up * half).astype(BF16)
        slope = half + (0.5 * up) * (1.0 - bend * bend) * (
            GELU_C + (3 * GELU_C * 0.044715) * square
        )
        d_up = (d_act * slope).astype(BF16)
        act_ref[:, cols] = act
        place = at[f // (FF // 2)] * (FF // 2) + f % (FF // 2)
        dup_ref[:, pl.ds(pl.multiple_of(place, CHUNK) if halves else place, CHUNK)] = d_up
        sums.append(col_sum(d_up.astype(F32)))
        low = nn(act, wd_ref[cols, :])
        dh = nt(d_up, wu_ref[:, cols])
        lowered = low if lowered is None else lowered + low
        d_hidden = dh if d_hidden is None else d_hidden + dh
    lowered = lowered + wide_row(bd_ref)
    out_ref[...] = (middle + gate2 * lowered).astype(BF16)
    d_gate2 = col_sum(dy * lowered)
    d_shift2 = col_sum(d_hidden)
    hx = col_sum(d_hidden * xhat)
    e = d_hidden * (1.0 + scale2)
    fx = e * gain
    d_mid = dy + r * (fx - row_mean(fx) - xhat * row_mean(fx * xhat))
    dmid_ref[...] = d_mid
    d_gate1 = col_sum(d_mid * attention)
    d_attention = (gate1 * d_mid).astype(BF16)
    for h in range(2):
        dattn_ref[:, part_of(at[h], D // 2)] = d_attention[:, h * (D // 2) : (h + 1) * (D // 2)]
    datt_ref[...] = nt(d_attention, wo_ref[...]).astype(BF16)
    first = jnp.logical_and(j == 0, t == 0)
    slot = slot_of(order, j)
    four = jnp.concatenate([d_gate1, d_shift2, hx * gain, d_gate2], axis=0)
    none = jnp.zeros((4, D), F32)
    add_to(
        payload_ref,
        jnp.concatenate(
            [
                jnp.where(slot == 0, four, none), jnp.where(slot == 0, none, four),
                hx * (1.0 + scale2), col_sum(d_low.astype(F32)), *sums, jnp.zeros((2, D), F32),
            ],
            axis=0,
        ),
        first,
    )


def feed_call(halves, place, tokens, att, cot, hidden1, mod, gain, wo, wu, bu, wd, bd, rows):
    tile = min(256, rows)
    tiles = rows // tile

    def own(j, t, o):
        return (slot_of(o, j) * tiles + t, 0)

    def sorted_(j, t, o):
        return (j * tiles + t, 0)

    n = SLOTS * rows
    return pl.pallas_call(
        partial(feed_kernel, halves),
        name="feed",
        out_shape=(
            jax.ShapeDtypeStruct((n, D), BF16),
            jax.ShapeDtypeStruct((n, D), F32),
            jax.ShapeDtypeStruct((n, D), BF16),
            jax.ShapeDtypeStruct((n, FF), BF16),
            jax.ShapeDtypeStruct((n, D), BF16),
            jax.ShapeDtypeStruct((n, D), BF16),
            jax.ShapeDtypeStruct((n, FF), BF16),
            jax.ShapeDtypeStruct((n, D), BF16),
            jax.ShapeDtypeStruct((16, D), F32),
            jax.ShapeDtypeStruct((n, D), BF16),
            jax.ShapeDtypeStruct((n, D), BF16),
        ),
        grid_spec=pltpu.PrefetchScalarGridSpec(
            num_scalar_prefetch=1,
            grid=(SLOTS, tiles),
            in_specs=[
                pl.BlockSpec((tile, D), own),
                pl.BlockSpec((tile, D), sorted_),
                pl.BlockSpec((tile, D), own),
                pl.BlockSpec((tile, D), own if halves else sorted_),
                whole((8, 6 * D)),
                whole((D,)),
                whole((D, D)),
                whole((D, FF)),
                whole((FF,)),
                whole((FF, D)),
                whole((D,)),
            ],
            out_specs=[
                pl.BlockSpec((tile, D), own),
                pl.BlockSpec((tile, D), sorted_),
                pl.BlockSpec((tile, D), sorted_),
                pl.BlockSpec((tile, FF), sorted_),
                pl.BlockSpec((tile, D), sorted_),
                pl.BlockSpec((tile, D), sorted_),
                pl.BlockSpec((tile, FF), sorted_),
                pl.BlockSpec((tile, D), sorted_),
                pl.BlockSpec((16, D), lambda j, t, o: (0, 0)),
                pl.BlockSpec((tile, D), sorted_),
                pl.BlockSpec((tile, D), sorted_),
            ],
        ),
        compiler_params=pltpu.CompilerParams(vmem_limit_bytes=BIG),
        cost_estimate=cost(2 * n * D * (4 * FF + 2 * D), 40e6, n * FF),
    )(place, tokens, att, cot, hidden1, mod, gain, wo, wu, bu, wd, bd)


def weight_gradient(left, right):
    seq, span = lax.axis_size("seq"), lax.axis_size("span")
    grad = tn(left, right)
    rows, cols = grad.shape
    shaped = grad.reshape(seq, rows // seq, span, cols // span).transpose(0, 2, 1, 3)
    return lax.psum_scatter(
        shaped.reshape(seq * span, rows // seq, cols // span),
        ("seq", "span"),
        scatter_dimension=0,
        tiled=True,
    )[0]


def join_kernel(place, dq_ref, dk_ref, dv_ref, ek_ref, ev_ref, sk_ref, sv_ref, cos, sin, out_ref):
    j, t = pl.program_id(0), pl.program_id(1)
    out_ref[:, :D] = dq_ref[...]
    wide_cos = jnp.concatenate([cos[...]] * PAIRS, axis=1)
    wide_sin = jnp.concatenate([sin[...]] * PAIRS, axis=1)

    @pl.when(j == 0)
    def _():
        dk = dk_ref[...] + ek_ref[...].astype(F32)
        out_ref[:, D : 2 * D] = turn_back(dk, wide_cos, wide_sin).astype(BF16)
        out_ref[:, 2 * D :] = (dv_ref[...] + ev_ref[...].astype(F32)).astype(BF16)

    @pl.when(j == 1)
    def _():
        out_ref[:, D:] = jnp.zeros((out_ref.shape[0], 2 * D), BF16)

    @pl.when(jnp.logical_and(j == 1, jnp.logical_and(t == 0, place[2] == 0)))
    def _():
        dk = turn_back(sk_ref[...], wide_cos[:SHORT], wide_sin[:SHORT])
        out_ref[:SHORT, D : 2 * D] = dk.astype(BF16)
        out_ref[:SHORT, 2 * D :] = sv_ref[...].astype(BF16)


def join_call(place, dq, dk, dv, ek, ev, sk, sv, cos, sin, rows):
    tile = min(256, rows)
    tiles = rows // tile

    def long(j, t, o):
        return (t + j * (tiles - 1 - t), 0)

    return pl.pallas_call(
        join_kernel,
        name="join",
        out_shape=jax.ShapeDtypeStruct((SLOTS * rows, 3 * D), BF16),
        grid_spec=pltpu.PrefetchScalarGridSpec(
            num_scalar_prefetch=1,
            grid=(SLOTS, tiles),
            in_specs=[pl.BlockSpec((tile, D), lambda j, t, o: (j * tiles + t, 0))]
            + [pl.BlockSpec((tile, D), long)] * 4
            + [whole((SHORT, D))] * 2
            + [pl.BlockSpec((tile, PAIR), lambda j, t, o: (o[2] * tiles + t, 0))] * 2,
            out_specs=pl.BlockSpec((tile, 3 * D), lambda j, t, o: (j * tiles + t, 0)),
        ),
        compiler_params=pltpu.CompilerParams(vmem_limit_bytes=BIG),
        cost_estimate=cost(1e7, 12e6),
    )(place, dq, dk, dv, ek, ev, sk, sv, cos, sin)


def last_kernel(
    order, tok_ref, dqkv_ref, dmid_ref, mod_ref, gain_ref, weight_ref,
    out_ref, dmod_ref, dgain_ref,
):
    j, t = pl.program_id(0), pl.program_id(1)
    scale = mod_ref[pl.ds(slot_of(order, j), 1), :][:, D : 2 * D]
    gain = wide_row(gain_ref)
    d_hidden = nt(dqkv_ref[...], weight_ref[...])
    x = tok_ref[...].astype(F32)
    center = x - row_mean(x)
    r = lax.rsqrt(row_mean(center * center) + EPSILON)
    xhat = center * r
    hx = col_sum(d_hidden * xhat)
    fx = d_hidden * (1.0 + scale) * gain
    out_ref[...] = dmid_ref[...] + r * (fx - row_mean(fx) - xhat * row_mean(fx * xhat))
    first = jnp.logical_and(j == 0, t == 0)
    add_to(
        dmod_ref,
        jnp.concatenate([col_sum(d_hidden), hx * gain, jnp.zeros((6, D), F32)], axis=0)[None],
        t == 0,
    )
    add_to(dgain_ref, hx * (1.0 + scale), first)


def last_call(place, tokens, dqkv, dmid, mod, gain, weight, rows):
    tile = min(256, rows)
    tiles = rows // tile

    def own(j, t, o):
        return (slot_of(o, j) * tiles + t, 0)

    def sorted_(j, t, o):
        return (j * tiles + t, 0)

    n = SLOTS * rows
    return pl.pallas_call(
        last_kernel,
        name="last",
        out_shape=(
            jax.ShapeDtypeStruct((n, D), F32),
            jax.ShapeDtypeStruct((SLOTS, 8, D), F32),
            jax.ShapeDtypeStruct((1, D), F32),
        ),
        grid_spec=pltpu.PrefetchScalarGridSpec(
            num_scalar_prefetch=1,
            grid=(SLOTS, tiles),
            in_specs=[
                pl.BlockSpec((tile, D), own),
                pl.BlockSpec((tile, 3 * D), sorted_),
                pl.BlockSpec((tile, D), sorted_),
                whole((8, 6 * D)),
                whole((D,)),
                whole((D, 3 * D)),
            ],
            out_specs=[
                pl.BlockSpec((tile, D), own),
                pl.BlockSpec((1, 8, D), lambda j, t, o: (slot_of(o, j), 0, 0)),
                pl.BlockSpec((1, D), lambda j, t, o: (0, 0)),
            ],
        ),
        compiler_params=pltpu.CompilerParams(vmem_limit_bytes=BIG),
        cost_estimate=cost(2 * n * D * 3 * D, 18e6),
    )(place, tokens, dqkv, dmid, mod, gain, weight)


def share_kernel(
    cond_ref, assign_ref, ada_ref, bias_ref, tok_ref, gain_ref, weight_ref, cos_ref, sin_ref,
    q_ref, h_ref, kv_ref, mod_ref, table_out, silu_ref, kvx_any,
    stage, table_ref, send, recv, own_ref, send_cond, recv_cond, local,
):
    step = pl.program_id(0)
    steps = stage.shape[0]
    tile = tok_ref.shape[0]
    me = lax.axis_index("span")

    def copy(i):
        return pltpu.make_async_remote_copy(
            src_ref=stage.at[i],
            dst_ref=kvx_any.at[pl.ds(pl.multiple_of(i * tile, tile), tile)],
            send_sem=send.at[i],
            recv_sem=recv.at[i],
            device_id={"span": 1 - me},
            device_id_type=MESH,
        )

    @pl.when(step == 0)
    def _():
        modulation_kernel(
            table_ref.shape[0], cond_ref, assign_ref, ada_ref, bias_ref, mod_ref, table_ref,
            silu_ref, own_ref, send_cond, recv_cond, local, ({"span": 1 - me},),
        )
        table_out[...] = table_ref[...]

    row = mod_ref[pl.ds(step // (steps // SLOTS), 1), :]
    shift, scale = row[:, :D], row[:, D : 2 * D]
    x = tok_ref[...].astype(F32)
    center = x - row_mean(x)
    xhat = center * lax.rsqrt(row_mean(center * center) + EPSILON)
    hidden = (xhat * wide_row(gain_ref) * (1.0 + scale) + shift).astype(BF16)
    h_ref[...] = hidden
    start = (me * (steps // SLOTS) + lax.rem(step, steps // SLOTS)) * tile
    start = pl.multiple_of(start, tile)
    cos, sin = cos_ref[pl.ds(start, tile), :], sin_ref[pl.ds(start, tile), :]
    k = nn(hidden, weight_ref[:, D : 2 * D])
    k = [turn(k[:, p : p + PAIR], cos, sin).astype(BF16) for p in range(0, D, PAIR)]
    k = jnp.concatenate(k, axis=1)
    v = nn(hidden, weight_ref[:, 2 * D :]).astype(BF16)
    kv_ref[:, :D] = k
    kv_ref[:, D:] = v
    stage[step, :, :D] = k
    stage[step, :, D:] = v

    q = nn(hidden, weight_ref[:, :D])
    for p in range(0, D, PAIR):
        q_ref[:, p : p + PAIR] = turn(q[:, p : p + PAIR], cos, sin).astype(BF16)

    copy(step).start()

    @pl.when(step == steps - 1)
    def _():
        for i in range(steps):
            copy(i).wait()


def share_call(cond, assignment, ada_weight, ada_bias, tokens, gain, weight, cos, sin, rows):
    tile = 256
    n = SLOTS * rows
    steps = n // tile

    def at(width):
        return pl.BlockSpec((tile, width), lambda s: (s, 0))

    return pl.pallas_call(
        share_kernel,
        name="project",
        grid=(steps,),
        out_shape=(
            jax.ShapeDtypeStruct((n, D), BF16),
            jax.ShapeDtypeStruct((n, D), BF16),
            jax.ShapeDtypeStruct((n, 2 * D), BF16),
            jax.ShapeDtypeStruct((8, 6 * D), F32),
            jax.ShapeDtypeStruct((16, 8, 128), F32),
            jax.ShapeDtypeStruct((SLOTS, 16, 128), F32),
            jax.ShapeDtypeStruct((n, 2 * D), BF16),
        ),
        in_specs=[
            whole((SLOTS, 128)),
            pl.BlockSpec(memory_space=pltpu.SMEM),
            whole((128, 6 * D)),
            whole((6 * D,)),
            at(D),
            whole((D,)),
            whole((D, 3 * D)),
            whole((LEN, PAIR)),
            whole((LEN, PAIR)),
        ],
        out_specs=(
            at(D), at(D), at(2 * D), whole((8, 6 * D)), whole((16, 8, 128)),
            whole((SLOTS, 16, 128)), pl.BlockSpec(memory_space=pl.ANY),
        ),
        scratch_shapes=[
            pltpu.VMEM((steps, tile, 2 * D), BF16),
            pltpu.VMEM((16, 8, 128), F32),
            pltpu.SemaphoreType.DMA((steps,)),
            pltpu.SemaphoreType.DMA((steps,)),
            pltpu.VMEM((8, 128), F32),
            pltpu.SemaphoreType.DMA((16,)),
            pltpu.SemaphoreType.DMA((16,)),
            pltpu.SemaphoreType.DMA,
        ],
        compiler_params=pltpu.CompilerParams(
            collective_id=4, has_side_effects=True, vmem_limit_bytes=BIG
        ),
        cost_estimate=cost(2 * n * D * 3 * D, 14e6),
    )(cond, assignment, ada_weight, ada_bias, tokens, gain, weight, cos, sin)


def attend_sorted_kernel(
    lengths, ql, qs, ko, vo, kx, vx, ks_own, vs_own, ks_other, vs_other,
    tl, ts, cl, cs, hl, hs,
    out_ref, lse_ref, q_ref, ko_ref, vo_ref, kx_ref, vx_ref, ks_ref, vs_ref,
    t_ref, c_ref, h_ref,
):
    rows = ql.shape[0]
    first = lax.axis_index("span") == 0
    ks = jnp.where(first, ks_own[...], ks_other[...])
    vs = jnp.where(first, vs_own[...], vs_other[...])
    for ref, long, short in ((q_ref, ql, qs), (t_ref, tl, ts), (c_ref, cl, cs), (h_ref, hl, hs)):
        ref[:rows, :] = long[...]
        ref[rows:, :] = short[...]
    ks_ref[...] = ks
    vs_ref[...] = vs
    for ref, given in ((ko_ref, ko), (vo_ref, vo), (kx_ref, kx), (vx_ref, vx)):
        ref[...] = given[...]
    out, stats = attend_slot(ql[...], [ko[...], kx[...]], [vo[...], vx[...]])
    out_ref[:rows, :] = out
    lse_ref[0, 0:1, :] = stats[0]
    lse_ref[0, 1:2, :] = stats[1]
    out, stats = attend_slot(qs[...], [ks], [vs])
    out_ref[rows:, :] = out
    lse_ref[0, 2:3, :] = stats[0]
    lse_ref[0, 3:4, :] = stats[1]


def attend_sorted_call(lengths, q, kv, kvx, tokens, cot, hidden, rows):
    n = SLOTS * rows
    per = rows // SHORT

    def long(base):
        return pl.BlockSpec((rows, PAIR), lambda h, o: (slot_of(o, 0), base + h))

    def second():
        return pl.BlockSpec((rows, PAIR), lambda h, o: (slot_of(o, 1), h))

    def short(base):
        return pl.BlockSpec((SHORT, PAIR), lambda h, o: (slot_of(o, 1) * per, base + h))

    def out(size):
        return pl.BlockSpec((size, PAIR), lambda h, o: (0, h))

    return pl.pallas_call(
        attend_sorted_kernel,
        name="attend",
        out_shape=(
            jax.ShapeDtypeStruct((n, D), BF16),
            jax.ShapeDtypeStruct((PAIRS, 4, rows), F32),
            jax.ShapeDtypeStruct((n, D), BF16),
        )
        + (jax.ShapeDtypeStruct((rows, D), BF16),) * 4
        + (jax.ShapeDtypeStruct((SHORT, D), BF16),) * 2
        + (jax.ShapeDtypeStruct((n, D), BF16),) * 3,
        grid_spec=pltpu.PrefetchScalarGridSpec(
            num_scalar_prefetch=1,
            grid=(PAIRS,),
            in_specs=[
                long(0),
                second(),
                long(0), long(PAIRS), long(0), long(PAIRS),
                short(0), short(PAIRS), short(0), short(PAIRS),
            ]
            + [long(0), second()] * 3,
            out_specs=[out(n), pl.BlockSpec((1, 4, rows), lambda h, o: (h, 0, 0)), out(n)]
            + [out(rows)] * 4
            + [out(SHORT)] * 2
            + [out(n)] * 3,
        ),
        compiler_params=pltpu.CompilerParams(vmem_limit_bytes=BIG),
        cost_estimate=cost(16 * D * rows * (LEN + SHORT), 16e6, HEADS * rows * (LEN + SHORT)),
    )(
        lengths, q, q, kv, kv, kvx, kvx, kv, kv, kvx, kvx, tokens, tokens, cot, cot, hidden, hidden
    )


def flip(index, bit):
    return index + bit - 2 * bit * ((index // bit) % 2)


def add_low(a, b):
    return (a.astype(F32) + b.astype(F32)).astype(BF16)


def plane_peers():
    s, c = lax.axis_index("seq"), lax.axis_index("span")
    return [{"span": 1 - c}, {"seq": flip(s, 1)}, {"seq": flip(s, 2)}]


def line_peers():
    s = lax.axis_index("seq")
    return [{"seq": lax.rem(s + 4 * step, 16)} for step in range(1, 4)]


def greet(peers):
    barrier = pltpu.get_barrier_semaphore()
    for peer in peers:
        pl.semaphore_signal(barrier, inc=1, device_id=peer, device_id_type=MESH)
    pl.semaphore_wait(barrier, len(peers))


class Scatter:
    def __init__(self, send, recv, base, other=None, own=None, came0=None, a1=None, b1=None,
                 came2=None, came3=None):
        self.send, self.recv, self.base = send, recv, base
        self.other, self.own, self.came0 = other, own, came0
        self.a1, self.b1, self.came2, self.came3 = a1, b1, came2, came3
        s = lax.axis_index("seq")
        self.x, self.y, self.z = lax.rem(s, 2), lax.rem(s // 2, 2), s // 4
        self.core_peer, self.x_peer, self.y_peer = plane_peers()
        self.z_peers = line_peers()

    def copy(self, i):
        x, y, z = self.x, self.y, self.z
        if i == 0:
            src, dst, peer = self.other, self.came0, self.core_peer
        elif i >= 8:
            src, dst, peer = self.other.at[i - 8], self.came0.at[i - 8], self.core_peer
        elif i == 1:
            src, dst, peer = self.own.at[0:2, :, 1 - x], self.a1, self.x_peer
        elif i == 2:
            src, dst, peer = self.own.at[2:4, 1 - y], self.b1, self.y_peer
        elif i == 3:
            src, dst, peer = self.a1.at[:, 1 - y], self.came2.at[0:2], self.y_peer
        elif i == 4:
            src, dst, peer = self.b1.at[:, 1 - x], self.came2.at[2:4], self.x_peer
        else:
            step = i - 4
            src, dst = self.came2.at[lax.rem(z + step, 4)], self.came3.at[step - 1]
            peer = self.z_peers[step - 1]
        return pltpu.make_async_remote_copy(
            src_ref=src,
            dst_ref=dst,
            send_sem=self.send.at[self.base + i],
            recv_sem=self.recv.at[self.base + i],
            device_id=peer,
            device_id_type=MESH,
        )

    def start(self, *which):
        for i in which:
            self.copy(i).start()

    def arrive(self, *which):
        for i in which:
            self.copy(i).wait_recv()

    def drain(self, *which):
        for i in which:
            self.copy(i).wait_send()

    def merge0(self):
        def body(i, _):
            z, y, x = i // 4, lax.rem(i // 2, 2), lax.rem(i, 2)
            self.own[z, y, x] = add_low(self.own[z, y, x], self.came0[z, y, x])
            return 0

        lax.fori_loop(0, 16, body, 0)

    def add1(self, a_ref, b_ref):
        self.arrive(1, 2)

        def body(i, _):
            z, k = i // 2, lax.rem(i, 2)
            a_ref[z, k] = add_low(self.own[z, k, self.x], self.a1[z, k])
            b_ref[z, k] = add_low(self.own[2 + z, self.y, k], self.b1[z, k])
            return 0

        lax.fori_loop(0, 4, body, 0)

    def add2(self, out_ref):
        self.arrive(3, 4)

        def body(z, _):
            out_ref[z] = add_low(self.a1[z, self.y], self.came2[z])
            out_ref[2 + z] = add_low(self.b1[z, self.x], self.came2[2 + z])
            return 0

        lax.fori_loop(0, 2, body, 0)

    def total(self):
        self.arrive(5, 6, 7)
        total = self.came2[self.z].astype(F32)
        for step in range(3):
            total = total + self.came3[step].astype(F32)
        return total

    def scatter0(self):
        self.start(0)

    def scatter1(self):
        self.arrive(0)
        self.merge0()
        self.start(1, 2)

    def scatter2(self):
        self.add1(self.a1, self.b1)
        self.start(3, 4)

    def scatter3(self):
        self.add2(self.came2)
        self.start(5, 6, 7)


def half_shape(rows, cols):
    return (4, 2, 2, rows, cols)


ANY = pl.BlockSpec(memory_space=pl.ANY)
DMA = pltpu.SemaphoreType.DMA


def both_kernel(
    tok_ref, att_ref, cot_ref, mod_ref, gain_ref, wo_ref, wu_ref, bu_ref, wd_any, bd_ref, lengths,
    out_ref, dmid_ref, datt_ref, h_ref, dup_ref, dattn_ref, payload_ref, a_ref, b_ref,
    act_all, slope_all, dlow_all, mid_all, attention_all,
    wd_ref, other, own, came0, a1, b1, send, recv, loaded,
):
    step = pl.program_id(0)
    me = lax.axis_index("span")
    down = Scatter(send, recv, 0, other=other, own=own, came0=came0, a1=a1, b1=b1)
    load = pltpu.make_async_copy(wd_any, wd_ref, loaded)
    tiles = act_all.shape[0] // tok_ref.shape[0]
    tile = tok_ref.shape[0]
    t = lax.rem(step, tiles)
    at_rows = pl.ds(pl.multiple_of(t * tile, tile), tile)
    halves = [h * me + (1 - h) * (1 - me) for h in range(2)]
    swapped = jnp.full((1, D), jnp.where(lengths[1] > lengths[0], 1.0, 0.0))
    mine = jnp.where(t // (tiles // SLOTS) == 0, swapped, 1.0 - swapped)

    def modulation(b):
        cols = slice(b * D, (b + 1) * D)
        return jnp.where(mine == 0.0, mod_ref[0:1, cols], mod_ref[1:2, cols])

    @pl.when(step == 0)
    def _():
        load.start()
        greet(plane_peers())

    @pl.when(step == 2 * tiles)
    def _():
        load.wait()
        down.arrive(8, 9, 10, 11)
        down.merge0()
        down.start(1, 2)

    @pl.when(step < tiles)
    def _():
        attention = nn(att_ref[...], wo_ref[...])
        middle = tok_ref[...].astype(F32) + modulation(2) * attention
        attention_all[at_rows, :] = attention
        mid_all[at_rows, :] = middle
        center = middle - row_mean(middle)
        xhat = center * lax.rsqrt(row_mean(center * center) + EPSILON)
        hidden = xhat * wide_row(gain_ref) * (1.0 + modulation(4)) + modulation(3)
        hidden = hidden.astype(BF16)
        h_ref[...] = hidden
        d_low = (modulation(5) * cot_ref[...].astype(F32)).astype(BF16)
        for h in range(2):
            half = d_low[:, h * (D // 2) : (h + 1) * (D // 2)]
            dlow_all[at_rows, part_of(halves[h], D // 2)] = half
        up_bias = wide_row(bu_ref)
        for f in range(0, FF, CHUNK):
            cols = slice(f, f + CHUNK)
            up = nn(hidden, wu_ref[:, cols]) + up_bias[:, cols]
            square = up * up
            bend = jnp.tanh(up * (GELU_C + (GELU_C * 0.044715) * square))
            half = 0.5 * (1.0 + bend)
            slope = half + (0.5 * up) * (1.0 - bend * bend) * (
                GELU_C + (3 * GELU_C * 0.044715) * square
            )
            act_all[at_rows, cols] = (up * half).astype(BF16)
            slope_all[at_rows, cols] = slope.astype(BF16)

    @pl.when(jnp.logical_and(step >= tiles, step < 2 * tiles))
    def _():
        cols = pl.ds(pl.multiple_of(t * CHUNK, CHUNK), CHUNK)
        value = tn(act_all[:, cols], dlow_all[...]).astype(BF16)
        shape = own.shape[1:]
        other[t] = value[:, : D // 2].reshape(shape)
        own[t] = value[:, D // 2 :].reshape(shape)

        for m in range(4):
            @pl.when(t == m)
            def _():
                down.start(8 + m)

    @pl.when(step >= 2 * tiles)
    def _():
        middle, attention = mid_all[at_rows, :], attention_all[at_rows, :]
        gain = wide_row(gain_ref)
        gate1, scale2, gate2 = modulation(2), modulation(4), modulation(5)
        dy = cot_ref[...].astype(F32)
        d_low = (gate2 * dy).astype(BF16)
        lowered, d_hidden = None, None
        sums = []
        for f in range(0, FF, CHUNK):
            cols = slice(f, f + CHUNK)
            d_act = nt(d_low, wd_ref[cols, :])
            d_up = (d_act * slope_all[at_rows, cols].astype(F32)).astype(BF16)
            place = halves[f // (FF // 2)] * (FF // 2) + f % (FF // 2)
            dup_ref[:, pl.ds(pl.multiple_of(place, CHUNK), CHUNK)] = d_up
            sums.append(col_sum(d_up.astype(F32)))
            low = nn(act_all[at_rows, cols], wd_ref[cols, :])
            dh = nt(d_up, wu_ref[:, cols])
            lowered = low if lowered is None else lowered + low
            d_hidden = dh if d_hidden is None else d_hidden + dh
        center = middle - row_mean(middle)
        r = lax.rsqrt(row_mean(center * center) + EPSILON)
        xhat = center * r
        lowered = lowered + wide_row(bd_ref)
        out_ref[...] = (middle + gate2 * lowered).astype(BF16)
        hx = col_sum(d_hidden * xhat)
        fx = d_hidden * (1.0 + scale2) * gain
        d_mid = dy + r * (fx - row_mean(fx) - xhat * row_mean(fx * xhat))
        dmid_ref[...] = d_mid
        d_attention = (gate1 * d_mid).astype(BF16)
        for h in range(2):
            half = d_attention[:, h * (D // 2) : (h + 1) * (D // 2)]
            dattn_ref[:, part_of(halves[h], D // 2)] = half
        datt_ref[...] = nt(d_attention, wo_ref[...]).astype(BF16)
        four = jnp.concatenate(
            [
                col_sum(d_mid * attention), col_sum(d_hidden), hx * gain,
                col_sum(dy * lowered),
            ],
            axis=0,
        )
        is_second = jnp.concatenate([mine] * 4, axis=0) != 0.0
        none = jnp.zeros((4, D), F32)
        add_to(
            payload_ref,
            jnp.concatenate(
                [
                    jnp.where(is_second, none, four), jnp.where(is_second, four, none),
                    hx * (1.0 + scale2), col_sum(d_low.astype(F32)), *sums,
                    jnp.zeros((2, D), F32),
                ],
                axis=0,
            ),
            step == 2 * tiles,
        )

    @pl.when(step == 3 * tiles - 1)
    def _():
        down.add1(a_ref, b_ref)
        down.drain(1, 2, 8, 9, 10, 11)


def both_call(tokens, att, cot, mod, gain, wo, wu, bu, wd, bd, lengths, rows):
    n = SLOTS * rows
    tile = 256
    tiles = n // tile
    dr, dc = FF // 16, D // 2

    def first():
        return pl.BlockSpec((tile, D), lambda s: (jnp.minimum(s, tiles - 1), 0))

    def last(width):
        return pl.BlockSpec((tile, width), lambda s: (jnp.maximum(s - 2 * tiles, 0), 0))

    def low(*shape):
        return pltpu.VMEM(shape, BF16)

    return pl.pallas_call(
        both_kernel,
        name="feed",
        grid=(3 * tiles,),
        out_shape=(
            jax.ShapeDtypeStruct((n, D), BF16),
            jax.ShapeDtypeStruct((n, D), F32),
            jax.ShapeDtypeStruct((n, D), BF16),
            jax.ShapeDtypeStruct((n, D), BF16),
            jax.ShapeDtypeStruct((n, FF), BF16),
            jax.ShapeDtypeStruct((n, D), BF16),
            jax.ShapeDtypeStruct((16, D), F32),
            jax.ShapeDtypeStruct((2, 2, dr, dc), BF16),
            jax.ShapeDtypeStruct((2, 2, dr, dc), BF16),
        ),
        in_specs=[
            first(),
            first(),
            pl.BlockSpec((tile, D), lambda s: (lax.rem(s, tiles), 0)),
            whole((8, 6 * D)),
            whole((D,)),
            whole((D, D)),
            whole((D, FF)),
            whole((FF,)),
            ANY,
            whole((D,)),
            pl.BlockSpec(memory_space=pltpu.SMEM),
        ],
        out_specs=(
            last(D), last(D), last(D), first(), last(FF), last(D), whole((16, D)),
            whole((2, 2, dr, dc)),
            whole((2, 2, dr, dc)),
        ),
        scratch_shapes=[
            low(n, FF), low(n, FF), low(n, D),
            pltpu.VMEM((n, D), F32),
            pltpu.VMEM((n, D), F32),
        ]
        + [low(FF, D)]
        + [low(*half_shape(dr, dc))] * 3
        + [low(2, 2, dr, dc)] * 2
        + [DMA((12,)), DMA((12,)), DMA],
        compiler_params=pltpu.CompilerParams(
            collective_id=2, has_side_effects=True, vmem_limit_bytes=BIG
        ),
        cost_estimate=cost(2 * n * D * (5 * FF + 2 * D), 40e6, n * FF),
    )(tokens, att, cot, mod, gain, wo, wu, bu, wd, bd, lengths)


def pack_rows(rows, count):
    parts = [rows[r : r + 1, c : c + 128] for r in range(count) for c in range(0, D, 128)]
    rest = -len(parts) % 16
    if rest:
        parts.append(jnp.zeros((rest, 128), F32))
    return jnp.concatenate(parts, axis=0).astype(BF16)


FIRST = 5
ROUNDS = PAIRS // 2
WIDE = 3 * PAIR


def middle_kernel(
    att_ref, dattn_ref, h_ref, dup_ref, hid1_ref, payload_ref, down_a, down_b,
    ql, qs, ko, vo, kx, vx, ks, vs, dol, dos, al, as_, lse, cos_ref, sin_ref,
    dq_ref, dk_ref, dv_ref, down_ref, out_ref, up_ref, r_ref, ra_ref, rb_ref, rown_ref, early_ref,
    down2, down3,
    out_other, out_own, out_came, out_a, out_b, out2, out3,
    up_other, up_own, up_came, up_a, up_b, up2, up3,
    round_other, round_came, round_a, round_b, round2, d_round, keep_q,
    leave, come, keep_k, keep_v, keep_sk, keep_sv, early_came, early_sum, early_all,
    send, recv, send_kv, recv_kv, send_early, recv_early,
):
    step = pl.program_id(0)
    s, me = lax.axis_index("seq"), lax.axis_index("span")
    rows = ql.shape[0]
    down = Scatter(send, recv, 0, a1=down_a, b1=down_b, came2=down2, came3=down3)
    out = Scatter(
        send, recv, 12, other=out_other, own=out_own, came0=out_came, a1=out_a, b1=out_b,
        came2=out2, came3=out3,
    )
    up = Scatter(
        send, recv, 20, other=up_other, own=up_own, came0=up_came, a1=up_a, b1=up_b, came2=up2,
        came3=up3,
    )
    part, wide = hid1_ref.shape[1] // 16, WIDE
    rounds = [
        Scatter(
            send, recv, 28 + 5 * k,
            other=round_other.at[k],
            own=(up_other.at[:, :, :, :, :wide], up_other.at[:, :, :, :, wide : 2 * wide], rown_ref)[k],
            came0=round_came.at[k],
            a1=round_a.at[k] if k < 2 else None,
            b1=round_b.at[k] if k < 2 else None,
            came2=round2,
        )
        for k in range(ROUNDS)
    ]
    cos = cos_ref[pl.ds(pl.multiple_of(me * rows, rows), rows), :]
    sin = sin_ref[pl.ds(pl.multiple_of(me * rows, rows), rows), :]

    def kv_copy(pair):
        return pltpu.make_async_remote_copy(
            src_ref=leave.at[pair],
            dst_ref=come.at[pair],
            send_sem=send_kv.at[pair],
            recv_sem=recv_kv.at[pair],
            device_id={"span": 1 - me},
            device_id_type=MESH,
        )

    def early_copy(k):
        half = pl.ds(pl.multiple_of(me * 48, 16), 48)
        if k == 0:
            src, dst, peer = payload_ref, early_came, {"span": 1 - me}
        elif k == 16:
            src, dst, peer = early_all.at[:, half], early_all.at[:, half], {"span": 1 - me}
        else:
            src, dst = early_sum.at[half], early_all.at[s, half]
            peer = {"seq": lax.rem(s + k, 16)}
        return pltpu.make_async_remote_copy(
            src_ref=src,
            dst_ref=dst,
            send_sem=send_early.at[k],
            recv_sem=recv_early.at[k],
            device_id=peer,
            device_id_type=MESH,
        )

    def at(number):
        return pl.when(step == number)

    @at(0)
    def _():
        greet([{"span": 1 - me}] + [{"seq": lax.rem(s + k, 16)} for k in range(1, 16)])
        down.start(3, 4)
        early_copy(0).start()

    @at(3)
    def _():
        early_copy(0).wait_recv()
        early_sum[...] = pack_rows(payload_ref[...] + early_came[...], 16)
        for k in range(1, 16):
            early_copy(k).start()
        half = pl.ds(pl.multiple_of(me * 48, 16), 48)
        early_all[s, half] = early_sum[half]

    @at(FIRST + 3)
    def _():
        for k in range(1, 16):
            early_copy(k).wait_recv()
        early_copy(16).start()

    @at(2)
    def _():
        out.scatter1()

    @at(4)
    def _():
        out.scatter2()

    @at(FIRST)
    def _():
        up.scatter1()

    @at(FIRST + 1)
    def _():
        out.scatter3()

    @at(FIRST + 2)
    def _():
        up.drain(0)

    @at(3)
    def _():
        down.scatter3()

    @at(FIRST + 4)
    def _():
        rounds[0].scatter1()

    @at(FIRST + 4)
    def _():
        up.scatter3()

    @at(FIRST + 5)
    def _():
        rounds[0].scatter2()
        rounds[1].scatter1()

    def between():
        @at(FIRST + 2)
        def _():
            up.scatter2()

    @at(0)
    def _():
        value = tn(att_ref[...], dattn_ref[...]).astype(BF16)
        out_other[...] = value[:, : D // 2].reshape(out_own.shape)
        out_own[...] = value[:, D // 2 :].reshape(out_own.shape)
        out.scatter0()

    @pl.when(jnp.logical_and(step >= 1, step < FIRST))
    def _():
        value = tn(h_ref[...], dup_ref[...]).astype(BF16)
        value = value.reshape(up_own.shape[:4] + (CHUNK,))
        cols = pl.ds(pl.multiple_of(lax.rem(step - 1, 2) * CHUNK, CHUNK), CHUNK)

        @pl.when(step < 3)
        def _():
            up_other[:, :, :, :, cols] = value

        @pl.when(step >= 3)
        def _():
            up_own[:, :, :, :, cols] = value

    @at(2)
    def _():
        up.scatter0()

    @pl.when(jnp.logical_and(step >= FIRST, step < FIRST + PAIRS))
    def _():
        pair = step - FIRST
        stats = lse[0]
        dq, dk, dv = attend_back_slot(
            ql[...], [ko[...], kx[...]], [vo[...], vx[...]], dol[...], al[...],
            [stats[0:1], stats[1:2]], between,
        )
        dq = turn_back(dq, cos, sin).astype(BF16)
        dq_ref[:rows, :] = dq
        keep_q[lax.rem(pair, 2), :rows, :] = dq
        keep_k[lax.rem(pair, 2)] = dk[0]
        keep_v[lax.rem(pair, 2)] = dv[0]
        leave[pair, :rows, :PAIR] = dk[1].astype(BF16)
        leave[pair, :rows, PAIR:] = dv[1].astype(BF16)
        dq, dk, dv = attend_back_slot(
            qs[...], [ks[...]], [vs[...]], dos[...], as_[...], [stats[2:3], stats[3:4]]
        )
        dq = turn_back(dq, cos, sin).astype(BF16)
        dq_ref[rows:, :] = dq
        keep_q[lax.rem(pair, 2), rows:, :] = dq
        keep_sk[lax.rem(pair, 2)] = dk[0]
        keep_sv[lax.rem(pair, 2)] = dv[0]
        leave[pair, rows:, :PAIR] = dk[0].astype(BF16)
        leave[pair, rows:, PAIR:] = dv[0].astype(BF16)
        kv_copy(pair).start()

    @pl.when(step > FIRST)
    def _():
        pair = step - FIRST - 1
        kv_copy(pair).wait_recv()
        dk = keep_k[lax.rem(pair, 2)] + come[pair, :rows, :PAIR].astype(F32)
        dk_ref[:rows, :] = turn_back(dk, cos, sin).astype(BF16)
        dv = keep_v[lax.rem(pair, 2)] + come[pair, :rows, PAIR:].astype(F32)
        dv_ref[:rows, :] = dv.astype(BF16)
        zero = jnp.zeros((SHORT, PAIR), F32)
        sk = keep_sk[lax.rem(pair, 2)] + come[pair, rows:, :PAIR].astype(F32)
        sk = jnp.where(me == 0, turn_back(sk, cos[:SHORT], sin[:SHORT]), zero)
        sv = keep_sv[lax.rem(pair, 2)] + come[pair, rows:, PAIR:].astype(F32)
        dk_ref[rows : rows + SHORT, :] = sk.astype(BF16)
        dv_ref[rows : rows + SHORT, :] = jnp.where(me == 0, sv, zero).astype(BF16)
        rest = jnp.zeros((rows - SHORT, PAIR), BF16)
        dk_ref[rows + SHORT :, :] = rest
        dv_ref[rows + SHORT :, :] = rest
        later = lax.rem(pair, 2)
        first, second = wide * (1 - me), wide * me
        q_at = first + later * PAIR
        k_at = (first + 2 * PAIR) * (1 - later) + second * later
        v_at = second + PAIR + later * PAIR
        d_round[:, pl.ds(pl.multiple_of(q_at, PAIR), PAIR)] = keep_q[later]
        d_round[:, pl.ds(pl.multiple_of(k_at, PAIR), PAIR)] = dk_ref[...]
        d_round[:, pl.ds(pl.multiple_of(v_at, PAIR), PAIR)] = dv_ref[...]

    for k in range(ROUNDS):
        @at(FIRST + 2 * k + 2)
        def _():
            value = tn(hid1_ref[...], d_round[...]).astype(BF16)
            rounds[k].other[...] = value[:, :wide].reshape(half_shape(part, wide))
            rounds[k].start(0)
            rounds[k].own[...] = value[:, wide:].reshape(half_shape(part, wide))

    @at(FIRST + PAIRS)
    def _():
        out_ref[...] = out.total()
        rounds[0].add2(r_ref)
        rounds[2].arrive(0)
        rounds[2].merge0()
        rounds[1].add1(ra_ref, rb_ref)
        down_ref[...] = down.total()
        up_ref[...] = up.total()
        down.drain(*range(3, 8))
        out.drain(*range(8))
        up.drain(*range(1, 8))
        rounds[0].drain(*range(5))
        rounds[1].drain(0, 1, 2)
        rounds[2].drain(0)
        for pair in range(PAIRS):
            kv_copy(pair).wait_send()
        early_copy(16).wait_recv()
        for k in range(17):
            early_copy(k).wait_send()
        early_ref[...] = early_all[...]


def middle_call(
    att, d_attention, hidden, d_up, hidden1, payload, down_a, down_b, q, kv, d_att, lse, cos, sin, rows,
):
    n = SLOTS * rows
    half = FF // 2
    dr, dc = FF // 16, D // 2
    ur, wr = D // 16, D // 16

    def clamp(s, low, high):
        return jnp.minimum(jnp.maximum(s, low), high)

    def order_of(k):
        return k // 2 + lax.rem(k, 2) * ROUNDS

    def now(s):
        return order_of(clamp(s - FIRST, 0, PAIRS - 1))

    def before(s):
        return order_of(clamp(s - FIRST - 1, 0, PAIRS - 1))

    def long():
        return pl.BlockSpec((rows, PAIR), lambda s: (0, now(s)))

    def second():
        return pl.BlockSpec((rows, PAIR), lambda s: (1, now(s)))

    def short():
        return pl.BlockSpec((SHORT, PAIR), lambda s: (0, now(s)))

    def low(shape):
        return pltpu.VMEM(shape, BF16)

    handed = ((4, ur, WIDE), (2, 2, ur, WIDE), (2, 2, ur, WIDE), half_shape(ur, WIDE))

    return pl.pallas_call(
        middle_kernel,
        name="middle",
        grid=(FIRST + PAIRS + 1,),
        out_shape=(
            jax.ShapeDtypeStruct((n, D), BF16),
            jax.ShapeDtypeStruct((n, D), BF16),
            jax.ShapeDtypeStruct((n, D), BF16),
            jax.ShapeDtypeStruct((dr, dc), F32),
            jax.ShapeDtypeStruct((wr, dc), F32),
            jax.ShapeDtypeStruct((ur, half), F32),
        )
        + tuple(jax.ShapeDtypeStruct(o, BF16) for o in handed + ((16, 96, 128),)),
        in_specs=[
            whole((n, D)),
            whole((n, D)),
            whole((n, D)),
            pl.BlockSpec((n, CHUNK), lambda s: (0, clamp(s - 1, 0, 3))),
            whole((n, D)),
            whole((16, D)),
            whole((2, 2, dr, dc)),
            whole((2, 2, dr, dc)),
            long(), second(), long(), long(), long(), long(), short(), short(), long(), second(),
            long(), second(),
            pl.BlockSpec((1, 4, rows), lambda s: (now(s), 0, 0)),
            whole((LEN, PAIR)),
            whole((LEN, PAIR)),
        ],
        out_specs=(
            pl.BlockSpec((n, PAIR), lambda s: (0, now(s))),
            pl.BlockSpec((n, PAIR), lambda s: (0, before(s))),
            pl.BlockSpec((n, PAIR), lambda s: (0, before(s))),
            whole((dr, dc)),
            whole((wr, dc)),
            whole((ur, half)),
        )
        + tuple(whole(o) for o in handed + ((16, 96, 128),)),
        scratch_shapes=[low((4, dr, dc)), low((3, dr, dc))]
        + [low(half_shape(wr, dc))] * 3
        + [low((2, 2, wr, dc))] * 2
        + [low((4, wr, dc)), low((3, wr, dc))]
        + [low(half_shape(ur, half))] * 3
        + [low((2, 2, ur, half))] * 2
        + [low((4, ur, half)), low((3, ur, half))]
        + [low((ROUNDS,) + half_shape(ur, WIDE))] * 2
        + [low((2, 2, 2, ur, WIDE))] * 2
        + [low((4, ur, WIDE))]
        + [low((n, 2 * WIDE)), low((2, n, PAIR))]
        + [low((PAIRS, rows + SHORT, 2 * PAIR))] * 2
        + [pltpu.VMEM((2, rows, PAIR), F32)] * 2
        + [pltpu.VMEM((2, SHORT, PAIR), F32)] * 2
        + [pltpu.VMEM((16, D), F32), low((96, 128)), low((16, 96, 128))]
        + [DMA((43,)), DMA((43,)), DMA((PAIRS,)), DMA((PAIRS,)), DMA((17,)), DMA((17,))],
        compiler_params=pltpu.CompilerParams(
            collective_id=1, has_side_effects=True, vmem_limit_bytes=BIG
        ),
        cost_estimate=cost(2 * n * D * (FF + 4 * D) + 40 * D * rows * (LEN + SHORT), 50e6),
    )(
        att, d_attention, hidden, d_up, hidden1, payload, down_a, down_b, q, q, *kv, d_att, d_att,
        att, att, lse, cos, sin,
    )


TILES = 4


def end_kernel(
    tok_ref, dmid_ref, dq_ref, dk_ref, dv_ref, mod_ref, gain_ref, weight_ref, lengths,
    r_in, ra, rb, rown,
    grad_ref, gqkv_ref, late_ref,
    r2, r3, last_a, last_b, sums, sums_came, sums_all, late_came,
    send, recv, send_late, recv_late,
):
    step = pl.program_id(0)
    s, me = lax.axis_index("seq"), lax.axis_index("span")
    rounds = [
        Scatter(
            send, recv, 8 * k, own=rown,
            a1=last_a if k == 2 else ra,
            b1=last_b if k == 2 else rb,
            came2=r2.at[k], came3=r3.at[k],
        )
        for k in range(ROUNDS)
    ]

    def late_copy(k):
        if k == 0:
            src, dst, peer = sums, sums_came, {"span": 1 - me}
        else:
            src, dst, peer = sums_all, late_came.at[s], {"seq": lax.rem(s + k, 16)}
        return pltpu.make_async_remote_copy(
            src_ref=src,
            dst_ref=dst,
            send_sem=send_late.at[k],
            recv_sem=recv_late.at[k],
            device_id=peer,
            device_id_type=MESH,
        )

    def at(number):
        return pl.when(step == number)

    @at(0)
    def _():
        r2[0] = r_in[...]
        sums[...] = jnp.zeros_like(sums)
        greet([{"span": 1 - me}] + [{"seq": lax.rem(s + k, 16)} for k in range(1, 16)])
        rounds[2].start(1, 2)
        rounds[1].start(3, 4)
        rounds[0].start(5, 6, 7)

    size = tok_ref.shape[0]
    j = step // 2
    swapped = jnp.full((1, D), jnp.where(lengths[1] > lengths[0], 1.0, 0.0))
    mine = jnp.where(j == 0, swapped, 1.0 - swapped)
    scale = jnp.where(mine == 0.0, mod_ref[0:1, D : 2 * D], mod_ref[1:2, D : 2 * D])
    gain = wide_row(gain_ref)
    d_hidden = (
        nt(dq_ref[...], weight_ref[:, :D])
        + nt(dk_ref[...], weight_ref[:, D : 2 * D])
        + nt(dv_ref[...], weight_ref[:, 2 * D :])
    )
    x = tok_ref[...].astype(F32)
    center = x - row_mean(x)
    r = lax.rsqrt(row_mean(center * center) + EPSILON)
    xhat = center * r
    hx = col_sum(d_hidden * xhat)
    fx = d_hidden * (1.0 + scale) * gain
    grad_ref[...] = dmid_ref[...] + r * (fx - row_mean(fx) - xhat * row_mean(fx * xhat))
    shift = col_sum(d_hidden)
    first, second = mine == 0.0, mine != 0.0
    zero = jnp.zeros((1, D), F32)
    sums[...] += jnp.concatenate(
        [
            jnp.where(first, shift, zero), jnp.where(first, hx * gain, zero),
            jnp.where(second, shift, zero), jnp.where(second, hx * gain, zero),
            hx * (1.0 + scale), jnp.zeros((3, D), F32),
        ],
        axis=0,
    )

    @at(TILES - 1)
    def _():
        late_copy(0).start()
        rounds[2].scatter2()
        rounds[1].scatter3()
        late_copy(0).wait_recv()
        sums_all[...] = pack_rows(sums[...] + sums_came[...], 5)
        for k in range(1, 16):
            late_copy(k).start()
        late_came[s] = sums_all[...]
        rounds[2].scatter3()
        for k in range(ROUNDS):
            total = rounds[k].total()
            for c in range(3):
                cols = slice((c * ROUNDS + k) * PAIR, (c * ROUNDS + k + 1) * PAIR)
                gqkv_ref[:, cols] = total[:, c * PAIR : (c + 1) * PAIR]
        rounds[0].drain(*range(5, 8))
        rounds[1].drain(*range(3, 8))
        rounds[2].drain(*range(1, 8))
        for k in range(16):
            if k > 0:
                late_copy(k).wait_recv()
            late_copy(k).wait_send()
        late_ref[...] = late_came[...]


def end_call(tokens, d_mid, dq, dk, dv, mod, gain, weight, lengths, handed, rows):
    n = SLOTS * rows
    size = n // TILES
    r = D // 16

    def tile():
        return pl.BlockSpec((size, D), lambda s: (s, 0))

    return pl.pallas_call(
        end_kernel,
        name="end",
        grid=(TILES,),
        out_shape=(
            jax.ShapeDtypeStruct((n, D), F32),
            jax.ShapeDtypeStruct((r, 3 * D // 2), F32),
            jax.ShapeDtypeStruct((16, 32, 128), BF16),
        ),
        in_specs=[tile()] * 5
        + [
            whole((8, 6 * D)),
            whole((D,)),
            whole((D, 3 * D)),
            pl.BlockSpec(memory_space=pltpu.SMEM),
        ]
        + [whole(a.shape) for a in handed],
        out_specs=(
            tile(),
            whole((r, 3 * D // 2)),
            whole((16, 32, 128)),
        ),
        scratch_shapes=[
            pltpu.VMEM((ROUNDS, 4, r, WIDE), BF16),
            pltpu.VMEM((ROUNDS, 3, r, WIDE), BF16),
            pltpu.VMEM((2, 2, r, WIDE), BF16),
            pltpu.VMEM((2, 2, r, WIDE), BF16),
            pltpu.VMEM((8, D), F32),
            pltpu.VMEM((8, D), F32),
            pltpu.VMEM((32, 128), BF16),
            pltpu.VMEM((16, 32, 128), BF16),
            DMA((8 * ROUNDS,)),
            DMA((8 * ROUNDS,)),
            DMA((16,)),
            DMA((16,)),
        ],
        compiler_params=pltpu.CompilerParams(
            collective_id=3, has_side_effects=True, vmem_limit_bytes=BIG
        ),
        cost_estimate=cost(2 * n * D * 3 * D, 22e6),
    )(tokens, d_mid, dq, dk, dv, mod, gain, weight, lengths, *handed)


def thirds(value):
    high = value.astype(BF16)
    rest = value - high.astype(F32)
    middle = rest.astype(BF16)
    return [high, middle, (rest - middle.astype(F32)).astype(BF16)]


def condition_kernel(
    lengths, early_ref, late_ref, table_ref, silu_ref, weight_ref,
    qkv_in, out_in, up_in, down_in, sorted_any, result_any,
    ada_ref, bias_ref, gcond_ref, gain1_ref, gain2_ref, bd_ref, bu_ref,
    qkv_ref, out_ref, up_ref, down_ref, natural_any, final_any, stage, stage_out, read, moved,
):
    seq = late_ref.shape[0]
    me, s = lax.axis_index("span"), lax.axis_index("seq")
    half = sorted_any.shape[0] // SLOTS
    reads, moves = [], []
    given = ((sorted_any, stage, natural_any), (result_any, stage_out, final_any))
    for i, (src, held, dst) in enumerate(given):
        for j in range(SLOTS):
            to = pl.ds(pl.multiple_of(slot_of(lengths, j) * half, half), half)
            at = i * SLOTS + j
            reads.append(
                pltpu.make_async_copy(src.at[pl.ds(j * half, half)], held.at[j], read.at[at])
            )
            moves.append(pltpu.make_async_copy(held.at[j], dst.at[to], moved.at[at]))
    for copy in reads:
        copy.start()
    qkv_ref[...] = qkv_in[...]
    out_ref[...] = out_in[...]
    up_ref[...] = up_in[...]
    down_ref[...] = down_in[...]
    for come, go in zip(reads, moves):
        come.wait()
        go.start()
    packed = early_ref[...].astype(F32)
    early = [
        jnp.concatenate([packed[:, 6 * r + c] for c in range(6)], axis=1) for r in range(14)
    ]
    packed = late_ref[...].astype(F32)
    late = [
        jnp.concatenate([packed[:, 6 * r + c] for c in range(6)], axis=1) for r in range(5)
    ]
    mods = []
    for k in range(SLOTS):
        mods.append(
            [late[2 * k], late[2 * k + 1]] + [early[4 * k + b] for b in range(4)]
        )
    gain1_ref[...] = jnp.sum(late[4], axis=0)
    gain2_ref[...] = jnp.sum(early[8], axis=0)
    bd_ref[...] = jnp.sum(early[9], axis=0)
    for f in range(4):
        bu_ref[f * D : (f + 1) * D] = jnp.sum(early[10 + f], axis=0)
    own = []
    asked = [
        jnp.concatenate([table_ref[:, SLOTS + k, :]] * 6, axis=1) for k in range(SLOTS)
    ]
    for b in range(6):
        cols = slice(b * D, (b + 1) * D)
        bias_ref[cols] = jnp.sum(mods[0][b] + mods[1][b], axis=0)
        rows = []
        for r in range(SLOTS):
            wanted = (s * SLOTS + r).astype(F32)
            picked = [jnp.where(asked[k] == wanted, mods[k][b], 0.0) for k in range(SLOTS)]
            rows.append(col_sum(picked[0] + picked[1]))
        own.append(jnp.concatenate(rows + [jnp.zeros((8 - SLOTS, D), F32)], axis=0))
    own = jnp.concatenate(own, axis=1)
    d_silu = nt(jnp.concatenate(thirds(own), axis=0), weight_ref[...])
    d_silu = d_silu[:8] + d_silu[8:16] + d_silu[16:24]
    v = table_ref[s]
    sig = 1.0 / (1.0 + jnp.exp(-v))
    gcond_ref[...] = (d_silu * (sig * (1.0 + v * (1.0 - sig))))[:SLOTS]
    rows = 128 // seq
    pick = lax.broadcasted_iota(jnp.int32, (rows, 128), 1) == (
        s * rows + lax.broadcasted_iota(jnp.int32, (rows, 128), 0)
    )
    pick = jnp.where(pick, 1.0, 0.0)
    silu = [nt(pick.astype(BF16), silu_ref[k].astype(BF16)).astype(BF16) for k in range(SLOTS)]
    silu = jnp.concatenate(silu * 3, axis=1)
    for b in range(3):
        blocks = [jnp.where(me == 0, mods[k][b], mods[k][3 + b]) for k in range(SLOTS)]
        split = [part for part in zip(*(thirds(block) for block in blocks))]
        right = jnp.concatenate([block for part in split for block in part], axis=0)
        ada_ref[:, b * D : (b + 1) * D] = nn(silu, right)
    for move in moves:
        move.wait()


def condition_call(lengths, early, late, table, silu, ada_weight, tiles, grad_in, result):
    seq = late.shape[0]

    def all_of(shape):
        return pl.BlockSpec(shape, lambda i, p: (0,) * len(shape))

    given = (early, late, table, silu, ada_weight) + tiles
    outs = ((128 // seq, 3 * D), (6 * D,), (SLOTS, 128), (D,), (D,), (D,), (FF,))
    outs += tuple(t.shape for t in tiles)
    return pl.pallas_call(
        condition_kernel,
        name="condition",
        out_shape=tuple(jax.ShapeDtypeStruct(o, F32) for o in outs + (grad_in.shape,))
        + (jax.ShapeDtypeStruct(result.shape, BF16),),
        grid_spec=pltpu.PrefetchScalarGridSpec(
            num_scalar_prefetch=1,
            grid=(1,),
            in_specs=[whole(a.shape) for a in given] + [ANY] * 2,
            out_specs=[all_of(o) for o in outs] + [ANY] * 2,
            scratch_shapes=[
                pltpu.VMEM((SLOTS, grad_in.shape[0] // SLOTS, D), F32),
                pltpu.VMEM((SLOTS, grad_in.shape[0] // SLOTS, D), BF16),
                DMA((2 * SLOTS,)),
                DMA((2 * SLOTS,)),
            ],
        ),
        compiler_params=pltpu.CompilerParams(vmem_limit_bytes=BIG),
        cost_estimate=cost(1e7, 12e6),
    )(lengths, *given, grad_in, result)


def from_peers(array, span):
    return [
        lax.ppermute(array, "span", [((i + step) % span, i) for i in range(span)])
        for step in range(1, span)
    ]


def gather_all(flat):
    seq, span = lax.axis_size("seq"), lax.axis_size("span")
    return lax.all_gather(flat, ("seq", "span"), axis=0).reshape(seq, span, flat.shape[0])


def shards(
    tokens, conditions, assignment, lengths, norm1_gain, ada_weight, ada_bias, qkv_weight,
    out_weight, norm2_gain, up_weight, up_bias, down_weight, down_bias, cotangent,
):
    slots, rows, _ = tokens.shape
    seq, span = lax.axis_size("seq"), lax.axis_size("span")
    seq_at, span_at = lax.axis_index("seq"), lax.axis_index("span")
    flat = slots * rows
    place = jnp.concatenate(
        [lengths, jnp.stack([span_at.astype(jnp.int32), seq_at.astype(jnp.int32)])]
    )
    fast = seq == 16 and span == 2
    cos, sin = (jnp.asarray(table) for table in rotary(LEN))
    tokens2 = tokens.reshape(flat, D)
    gain1, gain2 = norm1_gain, norm2_gain
    if fast:
        q, hidden1, kv, mod, table, silu_all, kvx = share_call(
            conditions, assignment, ada_weight, ada_bias, tokens2, gain1, qkv_weight, cos, sin,
            rows,
        )
        att, lse, q, *kv, tokens2, cot, hidden1 = attend_sorted_call(
            lengths, q, kv, kvx, tokens2, cotangent.reshape(flat, D), hidden1, rows
        )
    else:
        mod, table, _ = modulation_call(conditions, assignment, ada_weight, ada_bias, seq)
        q, hidden1, kv_long, kv_tail = project_call(
            place, tokens2, mod, gain1, qkv_weight, cos, sin, rows
        )
        kv_other = jnp.concatenate(from_peers(kv_long, span), axis=0)
        kv_short = kv_tail[:SHORT]
        sent = [lax.ppermute(kv_short, "span", [(0, i)]) for i in range(1, span)]
        kv_short = jnp.where(span_at == 0, kv_short, sum(sent[1:], sent[0]))
        att, lse = attend_call(q, kv_long, kv_other, kv_short, rows)
    if fast:
        out, d_mid, d_att, hidden2, d_up, d_attention, payload, *handed = both_call(
            tokens2, att, cot, mod, gain2, out_weight, up_weight, up_bias, down_weight,
            down_bias, lengths, rows,
        )
        dq, dk, dv, grad_down, grad_out, grad_up, *handed, early = middle_call(
            att, d_attention, hidden2, d_up, hidden1, payload, *handed, q, kv, d_att, lse,
            cos, sin, rows,
        )
        grad_in, grad_qkv, late = end_call(
            tokens2, d_mid, dq, dk, dv, mod, gain1, qkv_weight, lengths, handed, rows
        )
        (
            grad_ada, ada_bias_sum, grad_cond, gain1_sum, gain2_sum, bd_sum, bu_sum,
            grad_qkv, grad_out, grad_up, grad_down, grad_in, out,
        ) = condition_call(
            lengths, early, late, table, silu_all, ada_weight,
            (grad_qkv, grad_out, grad_up, grad_down), grad_in, out,
        )
        return (
            out.reshape(tokens.shape), grad_in.reshape(tokens.shape), grad_cond, gain1_sum,
            grad_ada, ada_bias_sum, grad_qkv, grad_out, gain2_sum, grad_up, bu_sum, grad_down,
            bd_sum,
        )
    (
        out, d_mid, d_att, act, d_low, hidden2, d_up, d_attention, payload, tokens_sorted,
        hidden1_sorted,
    ) = feed_call(
        fast, lengths, tokens2, att, cotangent.reshape(flat, D), hidden1, mod, gain2, out_weight,
        up_weight, up_bias, down_weight, down_bias, rows,
    )
    grad_down = weight_gradient(act, d_low)
    grad_up = weight_gradient(hidden2, d_up)
    grad_out = weight_gradient(att, d_attention)
    early = gather_all(payload[:14].reshape(-1))

    dq, dk, dv, dkx, dvx, dks, dvs = attend_back_call(
        place, q, kv_long, kv_other, kv_short, d_att, att, lse, cos, sin, rows
    )
    ek = ev = None
    for step in range(1, span):
        back = [((i, (i + step) % span)) for i in range(span)]
        cut = slice((step - 1) * rows, step * rows)
        pk, pv = lax.ppermute((dkx[cut], dvx[cut]), "span", back)
        ek = pk if ek is None else (ek.astype(F32) + pk.astype(F32))
        ev = pv if ev is None else (ev.astype(F32) + pv.astype(F32))
    d_short = jnp.concatenate([dks, dvs], axis=1)
    for step in range(1, span):
        d_short = d_short + lax.ppermute(
            jnp.concatenate([dks, dvs], axis=1), "span", [(step, 0)]
        )
    d_qkv = join_call(
        place, dq, dk, dv, ek, ev, d_short[:, :D], d_short[:, D:], cos, sin, rows
    )
    grad_qkv = weight_gradient(hidden1, d_qkv)
    grad_in, d_mod1, d_gain1 = last_call(
        place, tokens2, d_qkv, d_mid, mod, gain1, qkv_weight, rows
    )
    late = gather_all(jnp.concatenate([d_mod1[:, :2].reshape(-1), d_gain1[0]]))

    cut = slots * 4 * D
    mods2 = jnp.sum(early[:, :, :cut], axis=1).reshape(seq * slots, 4 * D)
    sums2 = jnp.sum(early[:, :, cut:], axis=(0, 1))
    cut = slots * 2 * D
    mods1 = jnp.sum(late[:, :, :cut], axis=1).reshape(seq * slots, 2 * D)
    gain1_sum = jnp.sum(late[:, :, cut:], axis=(0, 1))
    d_mods = jnp.concatenate([mods1, mods2], axis=1)
    grad_ada_bias = jnp.sum(d_mods, axis=0)
    cond_all = table[:, :slots].reshape(seq * slots, 128)
    assign_all = table[:, slots : 2 * slots, 0].reshape(seq * slots)
    number = jnp.arange(seq * slots, dtype=jnp.int32).astype(F32)
    picker = (assign_all[:, None] == number[None, :]).astype(F32)
    exact = partial(lax.dot_general, precision=HIGHEST, preferred_element_type=F32)
    cond_rows = exact(picker, cond_all, (((1,), (0,)), ((), ())))
    silu_low = jax.nn.silu(cond_rows).astype(BF16).astype(F32)
    ada_rows, ada_cols = 128 // seq, 6 * D // span
    grad_ada = exact(
        lax.dynamic_slice_in_dim(silu_low, seq_at * ada_rows, ada_rows, 1),
        lax.dynamic_slice_in_dim(d_mods, span_at * ada_cols, ada_cols, 1),
        (((0,), (0,)), ((), ())),
    )
    wanted = lax.dynamic_slice_in_dim(picker, seq_at * slots, slots, 1)
    own_mods = exact(wanted, d_mods, (((0,), (0,)), ((), ())))
    d_silu = exact(own_mods, ada_weight.astype(F32), (((1,), (1,)), ((), ())))
    grad_cond = jax.vjp(jax.nn.silu, conditions.astype(F32))[1](d_silu)[0]
    return (
        out.reshape(tokens.shape),
        grad_in.reshape(tokens.shape),
        grad_cond,
        gain1_sum,
        grad_ada,
        grad_ada_bias,
        grad_qkv,
        grad_out,
        sums2[:D],
        grad_up,
        sums2[2 * D :],
        grad_down,
        sums2[D : 2 * D],
    )


def solution(mesh):
    data, table, one = P("seq", "span", None), P("seq", None), P("seq")
    tile = P("seq", "span")
    in_specs = (data, table, one, one) + (P(),) * 10 + (data,)
    out_specs = (data, data, table, P(), tile, P(), tile, tile, P(), tile, P(), tile, P())
    return jax.shard_map(shards, mesh=mesh, in_specs=in_specs, out_specs=out_specs, check_vma=False)
```

```python
from functools import partial

import jax
import jax.numpy as jnp
import numpy as np
from jax import lax
from jax.experimental import pallas as pl
from jax.experimental.pallas import tpu as pltpu
from jax.sharding import PartitionSpec as P

HEADS = 12
HEAD = 64
D = 768
FF = 3072
PAIR = 128
PAIRS = HEADS // 2
LEN = 1024
SHORT = 128
SLOTS = 2
CHUNK = 768
EPSILON = 1e-5
LOG2E = 1.4426950408889634
GELU_C = 0.7978845608028654
BIG = 62 << 20
MESH = pl.DeviceIdType.MESH
F32 = jnp.float32
BF16 = jnp.bfloat16
HIGHEST = lax.Precision.HIGHEST


def nn(a, b):
    return lax.dot_general(a, b, (((1,), (0,)), ((), ())), preferred_element_type=F32)


def nt(a, b):
    return lax.dot_general(a, b, (((1,), (1,)), ((), ())), preferred_element_type=F32)


def tn(a, b):
    return lax.dot_general(a, b, (((0,), (0,)), ((), ())), preferred_element_type=F32)


def whole(shape, buffers=1):
    return pl.BlockSpec(shape, lambda *_: (0,) * len(shape), pipeline_mode=pl.Buffered(buffers))


def cost(flops, bytes_accessed, transcendentals=0):
    return pl.CostEstimate(
        flops=int(flops), bytes_accessed=int(bytes_accessed), transcendentals=int(transcendentals)
    )


def col_sum(x):
    return jnp.sum(x, axis=0, keepdims=True)


def wide_row(ref):
    return ref[...].astype(F32).reshape(1, ref.shape[0])


def row_mean(x):
    return jnp.mean(x, axis=-1, keepdims=True)


def rotary(length):
    half = HEAD // 2
    freq = np.power(np.float32(10000.0), -np.arange(half, dtype=np.float32) / np.float32(half))
    angles = np.arange(length, dtype=np.float32)[:, None] * freq.astype(np.float32)[None, :]
    cos, sin = np.cos(angles), np.sin(angles)
    return (
        np.concatenate([cos] * 4, axis=1).astype(np.float32),
        np.concatenate([-sin, sin, -sin, sin], axis=1).astype(np.float32),
    )


def swap_halves(x):
    lane = lax.broadcasted_iota(jnp.int32, x.shape, 1)
    first = (lane & 32) == 0
    return jnp.where(first, pltpu.roll(x, x.shape[1] - 32, 1), pltpu.roll(x, 32, 1))


def turn(x, cos, sin):
    return x * cos + swap_halves(x) * sin


def turn_back(x, cos, sin):
    return x * cos - swap_halves(x) * sin


def slot_of(lengths, j):
    long = jnp.where(lengths[1] > lengths[0], 1, 0)
    return j + long - 2 * j * long


def heads_of(x):
    lane = lax.broadcasted_iota(jnp.int32, x.shape, 1)
    zero = jnp.zeros_like(x)
    return jnp.where(lane < HEAD, x, zero), jnp.where(lane < HEAD, zero, x)


def modulation_kernel(
    n, cond_ref, assign_ref, weight_ref, bias_ref, mod_ref, table_ref, silu_ref,
    own_ref, send, recv, local, extra=(), ready=None,
):
    me = lax.axis_index("seq")
    asked = [jnp.full((1, 128), assign_ref[k].astype(F32)) for k in range(SLOTS)]
    own_ref[...] = jnp.concatenate(
        [cond_ref[...].astype(F32)] + asked + [jnp.zeros((8 - 2 * SLOTS, 128), F32)], axis=0
    )
    barrier = pltpu.get_barrier_semaphore()
    for step in range(1, n):
        pl.semaphore_signal(
            barrier, inc=1, device_id={"seq": lax.rem(me + step, n)}, device_id_type=MESH
        )
    for peer in extra:
        pl.semaphore_signal(barrier, inc=1, device_id=peer, device_id_type=MESH)
    mine = pltpu.make_async_copy(own_ref, table_ref.at[me], local)
    mine.start()
    pl.semaphore_wait(barrier, n - 1 + len(extra))
    copies = []
    for step in range(1, n):
        copy = pltpu.make_async_remote_copy(
            src_ref=own_ref,
            dst_ref=table_ref.at[me],
            send_sem=send.at[step],
            recv_sem=recv.at[step],
            device_id={"seq": lax.rem(me + step, n)},
            device_id_type=MESH,
        )
        copy.start()
        copies.append(copy)
    mine.wait()
    for copy in copies:
        copy.wait()
    if ready is not None:
        ready()
    source = lax.broadcasted_iota(jnp.int32, (n, 128), 0).astype(F32) * SLOTS
    rows = []
    for slot in range(SLOTS):
        wanted = own_ref[SLOTS + slot : SLOTS + slot + 1, :]
        row = jnp.zeros((1, 128), F32)
        for k in range(SLOTS):
            row += col_sum(jnp.where(wanted == source + k, table_ref[:, k, :], 0.0))
        rows.append(row)
    cond = jnp.concatenate(rows + [jnp.zeros((8 - SLOTS, 128), F32)], axis=0)
    silu = (cond / (1.0 + jnp.exp(-cond))).astype(BF16)
    mod_ref[...] = nn(silu, weight_ref[...]) + bias_ref[...].astype(F32).reshape(1, 6 * D)
    for slot in range(SLOTS):
        wanted = table_ref[:, SLOTS + slot, :][:, :n]
        lane = lax.broadcasted_iota(jnp.int32, (n, n), 1).astype(F32) * SLOTS
        rows = jnp.zeros((n, 128), F32)
        for k in range(SLOTS):
            chosen = jnp.where(wanted == lane + k, 1.0, 0.0).astype(BF16)
            rows += nn(chosen, table_ref[:, k, :].astype(BF16))
        silu_ref[slot] = (rows / (1.0 + jnp.exp(-rows))).astype(BF16).astype(F32)


def modulation_call(cond, assignment, ada_weight, ada_bias, n):
    vmem = pl.BlockSpec(memory_space=pltpu.VMEM)
    return pl.pallas_call(
        partial(modulation_kernel, n),
        name="modulation",
        out_shape=(
            jax.ShapeDtypeStruct((8, 6 * D), F32),
            jax.ShapeDtypeStruct((n, 8, 128), F32),
            jax.ShapeDtypeStruct((SLOTS, n, 128), F32),
        ),
        in_specs=[vmem, pl.BlockSpec(memory_space=pltpu.SMEM), vmem, vmem],
        out_specs=(vmem, vmem, vmem),
        scratch_shapes=[
            pltpu.VMEM((8, 128), F32),
            pltpu.SemaphoreType.DMA((n,)),
            pltpu.SemaphoreType.DMA((n,)),
            pltpu.SemaphoreType.DMA,
        ],
        compiler_params=pltpu.CompilerParams(
            collective_id=0, has_side_effects=True, vmem_limit_bytes=BIG
        ),
        cost_estimate=cost(1e7, 2e6),
    )(cond, assignment, ada_weight, ada_bias)


def project_kernel(
    order, tok_ref, mod_ref, gain_ref, weight_ref, cos_ref, sin_ref,
    q_ref, h_ref, kvl_ref, kvs_ref,
):
    j = pl.program_id(0)
    row = mod_ref[pl.ds(slot_of(order, j), 1), :]
    shift, scale = row[:, :D], row[:, D : 2 * D]
    x = tok_ref[...].astype(F32)
    center = x - row_mean(x)
    xhat = center * lax.rsqrt(row_mean(center * center) + EPSILON)
    hidden = (xhat * wide_row(gain_ref) * (1.0 + scale) + shift).astype(BF16)
    h_ref[...] = hidden
    cos = jnp.concatenate([cos_ref[...]] * PAIRS, axis=1)
    sin = jnp.concatenate([sin_ref[...]] * PAIRS, axis=1)
    q_ref[...] = turn(nn(hidden, weight_ref[:, :D]), cos, sin).astype(BF16)
    k = turn(nn(hidden, weight_ref[:, D : 2 * D]), cos, sin).astype(BF16)
    v = nn(hidden, weight_ref[:, 2 * D :]).astype(BF16)

    @pl.when(j == 0)
    def _():
        kvl_ref[:, :D] = k
        kvl_ref[:, D:] = v

    @pl.when(j == 1)
    def _():
        kvs_ref[:, :D] = k
        kvs_ref[:, D:] = v


def project_call(place, tokens, mod, gain, weight, cos, sin, rows):
    tile = min(256, rows)
    tiles = rows // tile
    return pl.pallas_call(
        project_kernel,
        name="project",
        out_shape=(
            jax.ShapeDtypeStruct((SLOTS * rows, D), BF16),
            jax.ShapeDtypeStruct((SLOTS * rows, D), BF16),
            jax.ShapeDtypeStruct((rows, 2 * D), BF16),
            jax.ShapeDtypeStruct((rows, 2 * D), BF16),
        ),
        grid_spec=pltpu.PrefetchScalarGridSpec(
            num_scalar_prefetch=1,
            grid=(SLOTS, tiles),
            in_specs=[
                pl.BlockSpec((tile, D), lambda j, t, o: (slot_of(o, j) * tiles + t, 0)),
                whole((8, 6 * D)),
                whole((D,)),
                whole((D, 3 * D)),
                pl.BlockSpec((tile, PAIR), lambda j, t, o: (o[2] * tiles + t, 0)),
                pl.BlockSpec((tile, PAIR), lambda j, t, o: (o[2] * tiles + t, 0)),
            ],
            out_specs=[
                pl.BlockSpec((tile, D), lambda j, t, o: (j * tiles + t, 0)),
                pl.BlockSpec((tile, D), lambda j, t, o: (j * tiles + t, 0)),
                pl.BlockSpec((tile, 2 * D), lambda j, t, o: (t + j * (tiles - 1 - t), 0)),
                pl.BlockSpec((tile, 2 * D), lambda j, t, o: (j * t, 0)),
            ],
        ),
        compiler_params=pltpu.CompilerParams(vmem_limit_bytes=BIG),
        cost_estimate=cost(2 * SLOTS * rows * D * 3 * D, 14e6),
    )(place, tokens, mod, gain, weight, cos, sin)


def attend_slot(q, keys, values):
    outs, stats = [], []
    all_scores = [[nt(k, qh) for k in keys] for qh in heads_of(q)]
    for head, scores in enumerate(all_scores):
        top = jnp.max(scores[0], axis=0, keepdims=True)
        for s in scores[1:]:
            top = jnp.maximum(top, jnp.max(s, axis=0, keepdims=True))
        total, out = None, None
        for s, v in zip(scores, values):
            p = jnp.exp2((s - top) * (0.125 * LOG2E))
            part = col_sum(p)
            o = tn(v, p.astype(BF16))
            total = part if total is None else total + part
            out = o if out is None else out + o
        out = out[head * HEAD : (head + 1) * HEAD] / total
        outs.append(out)
        stats.append(top * (0.125 * LOG2E) + jnp.log2(total))
    return jnp.concatenate(outs, axis=0).T.astype(BF16), stats


def attend_kernel(ql, qs, ko, vo, kx, vx, ks, vs, out_ref, lse_ref):
    rows = ql.shape[0]
    out, stats = attend_slot(ql[...], [ko[...], kx[...]], [vo[...], vx[...]])
    out_ref[:rows, :] = out
    lse_ref[0, 0:1, :] = stats[0]
    lse_ref[0, 1:2, :] = stats[1]
    out, stats = attend_slot(qs[...], [ks[...]], [vs[...]])
    out_ref[rows:, :] = out
    lse_ref[0, 2:3, :] = stats[0]
    lse_ref[0, 3:4, :] = stats[1]


def pair_specs(rows):
    def at(n, block, base):
        return pl.BlockSpec((n, PAIR), lambda h: (block, base + h))

    return [
        at(rows, 0, 0),
        at(rows, 1, 0),
        at(rows, 0, 0),
        at(rows, 0, PAIRS),
        at(LEN - rows, 0, 0),
        at(LEN - rows, 0, PAIRS),
        at(SHORT, 0, 0),
        at(SHORT, 0, PAIRS),
    ]


def attend_call(q, kv_own, kv_other, kv_short, rows):
    return pl.pallas_call(
        attend_kernel,
        name="attend",
        grid=(PAIRS,),
        out_shape=(
            jax.ShapeDtypeStruct((SLOTS * rows, D), BF16),
            jax.ShapeDtypeStruct((PAIRS, 4, rows), F32),
        ),
        in_specs=pair_specs(rows),
        out_specs=(
            pl.BlockSpec((SLOTS * rows, PAIR), lambda h: (0, h)),
            pl.BlockSpec((1, 4, rows), lambda h: (h, 0, 0)),
        ),
        compiler_params=pltpu.CompilerParams(vmem_limit_bytes=BIG),
        cost_estimate=cost(16 * D * rows * (LEN + SHORT), 9e6, HEADS * rows * (LEN + SHORT)),
    )(q, q, kv_own, kv_own, kv_other, kv_other, kv_short, kv_short)


def attend_back_slot(q, keys, values, d_out, out, lse, between=None):
    count = len(keys)
    d_keys, d_values = [None] * count, [None] * count
    d_query = []
    q_heads, d_heads = heads_of(q), heads_of(d_out)
    inner = (d_out.astype(F32) * out.astype(F32)).T
    all_scores = [[nt(k, qh) for k in keys] for qh in q_heads]
    all_d_probs = [[nt(v, dh) for v in values] for dh in d_heads]
    for head in range(2):
        if head == 1 and between is not None:
            between()
        qh, dh = q_heads[head], d_heads[head]
        delta = col_sum(inner[head * HEAD : (head + 1) * HEAD])
        scores, d_probs = all_scores[head], all_d_probs[head]
        dq = None
        for i in range(count):
            probs = jnp.exp2(scores[i] * (0.125 * LOG2E) - lse[head])
            d_scores = (probs * (d_probs[i] - delta)).astype(BF16)
            dv = nn(probs.astype(BF16), dh)
            dk = nn(d_scores, qh)
            part = tn(keys[i], d_scores)
            dq = part if dq is None else dq + part
            d_values[i] = dv if head == 0 else d_values[i] + dv
            d_keys[i] = dk if head == 0 else d_keys[i] + dk
        d_query.append(dq[head * HEAD : (head + 1) * HEAD])
    d_keys = [dk * 0.125 for dk in d_keys]
    return (jnp.concatenate(d_query, axis=0) * 0.125).T, d_keys, d_values


def attend_back_kernel(
    place, ql, qs, ko, vo, kx, vx, ks, vs, dol, dos, al, as_, lse, cos, sin,
    dq_ref, dko, dvo, dkx, dvx, dks, dvs,
):
    rows = ql.shape[0]
    stats = lse[0]
    dq, dk, dv = attend_back_slot(
        ql[...], [ko[...], kx[...]], [vo[...], vx[...]], dol[...], al[...],
        [stats[0:1], stats[1:2]],
    )
    dq_ref[:rows, :] = turn_back(dq, cos[...], sin[...]).astype(BF16)
    dko[...] = dk[0]
    dvo[...] = dv[0]
    dkx[...] = dk[1].astype(BF16)
    dvx[...] = dv[1].astype(BF16)
    dq, dk, dv = attend_back_slot(
        qs[...], [ks[...]], [vs[...]], dos[...], as_[...], [stats[2:3], stats[3:4]]
    )
    dq_ref[rows:, :] = turn_back(dq, cos[...], sin[...]).astype(BF16)
    dks[...] = dk[0]
    dvs[...] = dv[0]


def attend_back_call(place, q, kv_own, kv_other, kv_short, d_att, att, lse, cos, sin, rows):
    specs = [
        pl.BlockSpec(s.block_shape, partial(lambda m, h, o: m(h), s.index_map))
        for s in pair_specs(rows)
    ]
    other = LEN - rows
    return pl.pallas_call(
        attend_back_kernel,
        name="attend_back",
        out_shape=(
            jax.ShapeDtypeStruct((SLOTS * rows, D), BF16),
            jax.ShapeDtypeStruct((rows, D), F32),
            jax.ShapeDtypeStruct((rows, D), F32),
            jax.ShapeDtypeStruct((other, D), BF16),
            jax.ShapeDtypeStruct((other, D), BF16),
            jax.ShapeDtypeStruct((SHORT, D), F32),
            jax.ShapeDtypeStruct((SHORT, D), F32),
        ),
        grid_spec=pltpu.PrefetchScalarGridSpec(
            num_scalar_prefetch=1,
            grid=(PAIRS,),
            in_specs=specs
            + [
                pl.BlockSpec((rows, PAIR), lambda h, o: (0, h)),
                pl.BlockSpec((rows, PAIR), lambda h, o: (1, h)),
                pl.BlockSpec((rows, PAIR), lambda h, o: (0, h)),
                pl.BlockSpec((rows, PAIR), lambda h, o: (1, h)),
                pl.BlockSpec((1, 4, rows), lambda h, o: (h, 0, 0)),
                pl.BlockSpec((rows, PAIR), lambda h, o: (o[2], 0)),
                pl.BlockSpec((rows, PAIR), lambda h, o: (o[2], 0)),
            ],
            out_specs=[
                pl.BlockSpec((SLOTS * rows, PAIR), lambda h, o: (0, h)),
                pl.BlockSpec((rows, PAIR), lambda h, o: (0, h)),
                pl.BlockSpec((rows, PAIR), lambda h, o: (0, h)),
                pl.BlockSpec((other, PAIR), lambda h, o: (0, h)),
                pl.BlockSpec((other, PAIR), lambda h, o: (0, h)),
                pl.BlockSpec((SHORT, PAIR), lambda h, o: (0, h)),
                pl.BlockSpec((SHORT, PAIR), lambda h, o: (0, h)),
            ],
        ),
        compiler_params=pltpu.CompilerParams(vmem_limit_bytes=BIG),
        cost_estimate=cost(40 * D * rows * (LEN + SHORT), 16e6, HEADS * rows * (LEN + SHORT)),
    )(
        place, q, q, kv_own, kv_own, kv_other, kv_other, kv_short, kv_short,
        d_att, d_att, att, att, lse, cos, sin,
    )


def part_of(index, size):
    if isinstance(index, int):
        return pl.ds(index * size, size)
    return pl.ds(pl.multiple_of(index * size, size), size)


def add_to(ref, value, first):
    @pl.when(first)
    def _():
        ref[...] = value

    @pl.when(jnp.logical_not(first))
    def _():
        ref[...] += value


def feed_kernel(
    halves, order, tok_ref, att_ref, cot_ref, hid1_ref, mod_ref, gain_ref, wo_ref, wu_ref, bu_ref, wd_ref, bd_ref,
    out_ref, dmid_ref, datt_ref, act_ref, dlow_ref, h_ref, dup_ref, dattn_ref,
    payload_ref, toks_ref, hid1s_ref,
):
    j, t = pl.program_id(0), pl.program_id(1)
    toks_ref[...] = tok_ref[...]
    hid1s_ref[...] = hid1_ref[...]
    row = mod_ref[pl.ds(slot_of(order, j), 1), :]
    gate1, shift2 = row[:, 2 * D : 3 * D], row[:, 3 * D : 4 * D]
    scale2, gate2 = row[:, 4 * D : 5 * D], row[:, 5 * D :]
    gain, up_bias = wide_row(gain_ref), wide_row(bu_ref)
    attention = nn(att_ref[...], wo_ref[...])
    middle = tok_ref[...].astype(F32) + gate1 * attention
    center = middle - row_mean(middle)
    r = lax.rsqrt(row_mean(center * center) + EPSILON)
    xhat = center * r
    hidden = (xhat * gain * (1.0 + scale2) + shift2).astype(BF16)
    h_ref[...] = hidden
    dy = cot_ref[...].astype(F32)
    d_low = (gate2 * dy).astype(BF16)
    me = lax.axis_index("span")
    at = [h * me + (1 - h) * (1 - me) if halves else h for h in range(2)]
    for h in range(2):
        dlow_ref[:, part_of(at[h], D // 2)] = d_low[:, h * (D // 2) : (h + 1) * (D // 2)]
    lowered, d_hidden = None, None
    sums = []
    for f in range(0, FF, CHUNK):
        cols = slice(f, f + CHUNK)
        up = nn(hidden, wu_ref[:, cols]) + up_bias[:, cols]
        d_act = nt(d_low, wd_ref[cols, :])
        square = up * up
        bend = jnp.tanh(up * (GELU_C + (GELU_C * 0.044715) * square))
        half = 0.5 * (1.0 + bend)
        act = (up * half).astype(BF16)
        slope = half + (0.5 * up) * (1.0 - bend * bend) * (
            GELU_C + (3 * GELU_C * 0.044715) * square
        )
        d_up = (d_act * slope).astype(BF16)
        act_ref[:, cols] = act
        place = at[f // (FF // 2)] * (FF // 2) + f % (FF // 2)
        dup_ref[:, pl.ds(pl.multiple_of(place, CHUNK) if halves else place, CHUNK)] = d_up
        sums.append(col_sum(d_up.astype(F32)))
        low = nn(act, wd_ref[cols, :])
        dh = nt(d_up, wu_ref[:, cols])
        lowered = low if lowered is None else lowered + low
        d_hidden = dh if d_hidden is None else d_hidden + dh
    lowered = lowered + wide_row(bd_ref)
    out_ref[...] = (middle + gate2 * lowered).astype(BF16)
    d_gate2 = col_sum(dy * lowered)
    d_shift2 = col_sum(d_hidden)
    hx = col_sum(d_hidden * xhat)
    e = d_hidden * (1.0 + scale2)
    fx = e * gain
    d_mid = dy + r * (fx - row_mean(fx) - xhat * row_mean(fx * xhat))
    dmid_ref[...] = d_mid
    d_gate1 = col_sum(d_mid * attention)
    d_attention = (gate1 * d_mid).astype(BF16)
    for h in range(2):
        dattn_ref[:, part_of(at[h], D // 2)] = d_attention[:, h * (D // 2) : (h + 1) * (D // 2)]
    datt_ref[...] = nt(d_attention, wo_ref[...]).astype(BF16)
    first = jnp.logical_and(j == 0, t == 0)
    slot = slot_of(order, j)
    four = jnp.concatenate([d_gate1, d_shift2, hx * gain, d_gate2], axis=0)
    none = jnp.zeros((4, D), F32)
    add_to(
        payload_ref,
        jnp.concatenate(
            [
                jnp.where(slot == 0, four, none), jnp.where(slot == 0, none, four),
                hx * (1.0 + scale2), col_sum(d_low.astype(F32)), *sums, jnp.zeros((2, D), F32),
            ],
            axis=0,
        ),
        first,
    )


def feed_call(halves, place, tokens, att, cot, hidden1, mod, gain, wo, wu, bu, wd, bd, rows):
    tile = min(256, rows)
    tiles = rows // tile

    def own(j, t, o):
        return (slot_of(o, j) * tiles + t, 0)

    def sorted_(j, t, o):
        return (j * tiles + t, 0)

    n = SLOTS * rows
    return pl.pallas_call(
        partial(feed_kernel, halves),
        name="feed",
        out_shape=(
            jax.ShapeDtypeStruct((n, D), BF16),
            jax.ShapeDtypeStruct((n, D), F32),
            jax.ShapeDtypeStruct((n, D), BF16),
            jax.ShapeDtypeStruct((n, FF), BF16),
            jax.ShapeDtypeStruct((n, D), BF16),
            jax.ShapeDtypeStruct((n, D), BF16),
            jax.ShapeDtypeStruct((n, FF), BF16),
            jax.ShapeDtypeStruct((n, D), BF16),
            jax.ShapeDtypeStruct((16, D), F32),
            jax.ShapeDtypeStruct((n, D), BF16),
            jax.ShapeDtypeStruct((n, D), BF16),
        ),
        grid_spec=pltpu.PrefetchScalarGridSpec(
            num_scalar_prefetch=1,
            grid=(SLOTS, tiles),
            in_specs=[
                pl.BlockSpec((tile, D), own),
                pl.BlockSpec((tile, D), sorted_),
                pl.BlockSpec((tile, D), own),
                pl.BlockSpec((tile, D), own if halves else sorted_),
                whole((8, 6 * D)),
                whole((D,)),
                whole((D, D)),
                whole((D, FF)),
                whole((FF,)),
                whole((FF, D)),
                whole((D,)),
            ],
            out_specs=[
                pl.BlockSpec((tile, D), own),
                pl.BlockSpec((tile, D), sorted_),
                pl.BlockSpec((tile, D), sorted_),
                pl.BlockSpec((tile, FF), sorted_),
                pl.BlockSpec((tile, D), sorted_),
                pl.BlockSpec((tile, D), sorted_),
                pl.BlockSpec((tile, FF), sorted_),
                pl.BlockSpec((tile, D), sorted_),
                pl.BlockSpec((16, D), lambda j, t, o: (0, 0)),
                pl.BlockSpec((tile, D), sorted_),
                pl.BlockSpec((tile, D), sorted_),
            ],
        ),
        compiler_params=pltpu.CompilerParams(vmem_limit_bytes=BIG),
        cost_estimate=cost(2 * n * D * (4 * FF + 2 * D), 40e6, n * FF),
    )(place, tokens, att, cot, hidden1, mod, gain, wo, wu, bu, wd, bd)


def weight_gradient(left, right):
    seq, span = lax.axis_size("seq"), lax.axis_size("span")
    grad = tn(left, right)
    rows, cols = grad.shape
    shaped = grad.reshape(seq, rows // seq, span, cols // span).transpose(0, 2, 1, 3)
    return lax.psum_scatter(
        shaped.reshape(seq * span, rows // seq, cols // span),
        ("seq", "span"),
        scatter_dimension=0,
        tiled=True,
    )[0]


def join_kernel(place, dq_ref, dk_ref, dv_ref, ek_ref, ev_ref, sk_ref, sv_ref, cos, sin, out_ref):
    j, t = pl.program_id(0), pl.program_id(1)
    out_ref[:, :D] = dq_ref[...]
    wide_cos = jnp.concatenate([cos[...]] * PAIRS, axis=1)
    wide_sin = jnp.concatenate([sin[...]] * PAIRS, axis=1)

    @pl.when(j == 0)
    def _():
        dk = dk_ref[...] + ek_ref[...].astype(F32)
        out_ref[:, D : 2 * D] = turn_back(dk, wide_cos, wide_sin).astype(BF16)
        out_ref[:, 2 * D :] = (dv_ref[...] + ev_ref[...].astype(F32)).astype(BF16)

    @pl.when(j == 1)
    def _():
        out_ref[:, D:] = jnp.zeros((out_ref.shape[0], 2 * D), BF16)

    @pl.when(jnp.logical_and(j == 1, jnp.logical_and(t == 0, place[2] == 0)))
    def _():
        dk = turn_back(sk_ref[...], wide_cos[:SHORT], wide_sin[:SHORT])
        out_ref[:SHORT, D : 2 * D] = dk.astype(BF16)
        out_ref[:SHORT, 2 * D :] = sv_ref[...].astype(BF16)


def join_call(place, dq, dk, dv, ek, ev, sk, sv, cos, sin, rows):
    tile = min(256, rows)
    tiles = rows // tile

    def long(j, t, o):
        return (t + j * (tiles - 1 - t), 0)

    return pl.pallas_call(
        join_kernel,
        name="join",
        out_shape=jax.ShapeDtypeStruct((SLOTS * rows, 3 * D), BF16),
        grid_spec=pltpu.PrefetchScalarGridSpec(
            num_scalar_prefetch=1,
            grid=(SLOTS, tiles),
            in_specs=[pl.BlockSpec((tile, D), lambda j, t, o: (j * tiles + t, 0))]
            + [pl.BlockSpec((tile, D), long)] * 4
            + [whole((SHORT, D))] * 2
            + [pl.BlockSpec((tile, PAIR), lambda j, t, o: (o[2] * tiles + t, 0))] * 2,
            out_specs=pl.BlockSpec((tile, 3 * D), lambda j, t, o: (j * tiles + t, 0)),
        ),
        compiler_params=pltpu.CompilerParams(vmem_limit_bytes=BIG),
        cost_estimate=cost(1e7, 12e6),
    )(place, dq, dk, dv, ek, ev, sk, sv, cos, sin)


def last_kernel(
    order, tok_ref, dqkv_ref, dmid_ref, mod_ref, gain_ref, weight_ref,
    out_ref, dmod_ref, dgain_ref,
):
    j, t = pl.program_id(0), pl.program_id(1)
    scale = mod_ref[pl.ds(slot_of(order, j), 1), :][:, D : 2 * D]
    gain = wide_row(gain_ref)
    d_hidden = nt(dqkv_ref[...], weight_ref[...])
    x = tok_ref[...].astype(F32)
    center = x - row_mean(x)
    r = lax.rsqrt(row_mean(center * center) + EPSILON)
    xhat = center * r
    hx = col_sum(d_hidden * xhat)
    fx = d_hidden * (1.0 + scale) * gain
    out_ref[...] = dmid_ref[...] + r * (fx - row_mean(fx) - xhat * row_mean(fx * xhat))
    first = jnp.logical_and(j == 0, t == 0)
    add_to(
        dmod_ref,
        jnp.concatenate([col_sum(d_hidden), hx * gain, jnp.zeros((6, D), F32)], axis=0)[None],
        t == 0,
    )
    add_to(dgain_ref, hx * (1.0 + scale), first)


def last_call(place, tokens, dqkv, dmid, mod, gain, weight, rows):
    tile = min(256, rows)
    tiles = rows // tile

    def own(j, t, o):
        return (slot_of(o, j) * tiles + t, 0)

    def sorted_(j, t, o):
        return (j * tiles + t, 0)

    n = SLOTS * rows
    return pl.pallas_call(
        last_kernel,
        name="last",
        out_shape=(
            jax.ShapeDtypeStruct((n, D), F32),
            jax.ShapeDtypeStruct((SLOTS, 8, D), F32),
            jax.ShapeDtypeStruct((1, D), F32),
        ),
        grid_spec=pltpu.PrefetchScalarGridSpec(
            num_scalar_prefetch=1,
            grid=(SLOTS, tiles),
            in_specs=[
                pl.BlockSpec((tile, D), own),
                pl.BlockSpec((tile, 3 * D), sorted_),
                pl.BlockSpec((tile, D), sorted_),
                whole((8, 6 * D)),
                whole((D,)),
                whole((D, 3 * D)),
            ],
            out_specs=[
                pl.BlockSpec((tile, D), own),
                pl.BlockSpec((1, 8, D), lambda j, t, o: (slot_of(o, j), 0, 0)),
                pl.BlockSpec((1, D), lambda j, t, o: (0, 0)),
            ],
        ),
        compiler_params=pltpu.CompilerParams(vmem_limit_bytes=BIG),
        cost_estimate=cost(2 * n * D * 3 * D, 18e6),
    )(place, tokens, dqkv, dmid, mod, gain, weight)


def share_kernel(
    cond_ref, assign_ref, ada_any, bias_ref, tok_ref, gain_ref, weight_any, cos_ref, sin_ref,
    q_ref, h_ref, kv_ref, mod_ref, table_out, silu_ref, kvx_any,
    stage, table_ref, ada_ref, weight_ref, send, recv, own_ref, send_cond, recv_cond, local, loaded,
):
    step = pl.program_id(0)
    steps = stage.shape[0]
    tile = tok_ref.shape[0]
    me = lax.axis_index("span")

    def copy(i):
        return pltpu.make_async_remote_copy(
            src_ref=stage.at[i],
            dst_ref=kvx_any.at[pl.ds(pl.multiple_of(i * tile, tile), tile)],
            send_sem=send.at[i],
            recv_sem=recv.at[i],
            device_id={"span": 1 - me},
            device_id_type=MESH,
        )

    @pl.when(step == 0)
    def _():
        loads = [
            pltpu.make_async_copy(ada_any, ada_ref, loaded.at[0]),
            pltpu.make_async_copy(weight_any, weight_ref, loaded.at[1]),
        ]
        for load in loads:
            load.start()
        modulation_kernel(
            table_ref.shape[0], cond_ref, assign_ref, ada_ref, bias_ref, mod_ref, table_ref,
            silu_ref, own_ref, send_cond, recv_cond, local, ({"span": 1 - me},), loads[0].wait,
        )
        loads[1].wait()
        table_out[...] = table_ref[...]

    row = mod_ref[pl.ds(step // (steps // SLOTS), 1), :]
    shift, scale = row[:, :D], row[:, D : 2 * D]
    x = tok_ref[...].astype(F32)
    center = x - row_mean(x)
    xhat = center * lax.rsqrt(row_mean(center * center) + EPSILON)
    hidden = (xhat * wide_row(gain_ref) * (1.0 + scale) + shift).astype(BF16)
    h_ref[...] = hidden
    start = (me * (steps // SLOTS) + lax.rem(step, steps // SLOTS)) * tile
    start = pl.multiple_of(start, tile)
    cos, sin = cos_ref[pl.ds(start, tile), :], sin_ref[pl.ds(start, tile), :]
    k = nn(hidden, weight_ref[:, D : 2 * D])
    k = [turn(k[:, p : p + PAIR], cos, sin).astype(BF16) for p in range(0, D, PAIR)]
    k = jnp.concatenate(k, axis=1)
    v = nn(hidden, weight_ref[:, 2 * D :]).astype(BF16)
    kv_ref[:, :D] = k
    kv_ref[:, D:] = v
    stage[step, :, :D] = k
    stage[step, :, D:] = v

    q = nn(hidden, weight_ref[:, :D])
    for p in range(0, D, PAIR):
        q_ref[:, p : p + PAIR] = turn(q[:, p : p + PAIR], cos, sin).astype(BF16)

    copy(step).start()

    @pl.when(step == steps - 1)
    def _():
        for i in range(steps):
            copy(i).wait()


def share_call(cond, assignment, ada_weight, ada_bias, tokens, gain, weight, cos, sin, rows):
    tile = 256
    n = SLOTS * rows
    steps = n // tile

    def at(width):
        return pl.BlockSpec((tile, width), lambda s: (s, 0))

    return pl.pallas_call(
        share_kernel,
        name="project",
        grid=(steps,),
        out_shape=(
            jax.ShapeDtypeStruct((n, D), BF16),
            jax.ShapeDtypeStruct((n, D), BF16),
            jax.ShapeDtypeStruct((n, 2 * D), BF16),
            jax.ShapeDtypeStruct((8, 6 * D), F32),
            jax.ShapeDtypeStruct((16, 8, 128), F32),
            jax.ShapeDtypeStruct((SLOTS, 16, 128), F32),
            jax.ShapeDtypeStruct((n, 2 * D), BF16),
        ),
        in_specs=[
            whole((SLOTS, 128)),
            pl.BlockSpec(memory_space=pltpu.SMEM),
            pl.BlockSpec(memory_space=pl.ANY),
            whole((6 * D,)),
            at(D),
            whole((D,)),
            pl.BlockSpec(memory_space=pl.ANY),
            whole((LEN, PAIR)),
            whole((LEN, PAIR)),
        ],
        out_specs=(
            at(D), at(D), at(2 * D), whole((8, 6 * D)), whole((16, 8, 128)),
            whole((SLOTS, 16, 128)), pl.BlockSpec(memory_space=pl.ANY),
        ),
        scratch_shapes=[
            pltpu.VMEM((steps, tile, 2 * D), BF16),
            pltpu.VMEM((16, 8, 128), F32),
            pltpu.VMEM((128, 6 * D), BF16),
            pltpu.VMEM((D, 3 * D), BF16),
            pltpu.SemaphoreType.DMA((steps,)),
            pltpu.SemaphoreType.DMA((steps,)),
            pltpu.VMEM((8, 128), F32),
            pltpu.SemaphoreType.DMA((16,)),
            pltpu.SemaphoreType.DMA((16,)),
            pltpu.SemaphoreType.DMA,
            pltpu.SemaphoreType.DMA((2,)),
        ],
        compiler_params=pltpu.CompilerParams(
            collective_id=4, has_side_effects=True, vmem_limit_bytes=BIG
        ),
        cost_estimate=cost(2 * n * D * 3 * D, 14e6),
    )(cond, assignment, ada_weight, ada_bias, tokens, gain, weight, cos, sin)


def attend_sorted_kernel(
    lengths, ql, qs, ko, vo, kx, vx, ks_own, vs_own, ks_other, vs_other,
    tl, ts, cl, cs, hl, hs,
    out_ref, lse_ref, q_ref, ko_ref, vo_ref, kx_ref, vx_ref, ks_ref, vs_ref,
    t_ref, c_ref, h_ref,
):
    rows = ql.shape[0]
    first = lax.axis_index("span") == 0
    ks = jnp.where(first, ks_own[...], ks_other[...])
    vs = jnp.where(first, vs_own[...], vs_other[...])
    for ref, long, short in ((q_ref, ql, qs), (t_ref, tl, ts), (c_ref, cl, cs), (h_ref, hl, hs)):
        ref[:rows, :] = long[...]
        ref[rows:, :] = short[...]
    ks_ref[...] = ks
    vs_ref[...] = vs
    for ref, given in ((ko_ref, ko), (vo_ref, vo), (kx_ref, kx), (vx_ref, vx)):
        ref[...] = given[...]
    out, stats = attend_slot(ql[...], [ko[...], kx[...]], [vo[...], vx[...]])
    out_ref[:rows, :] = out
    lse_ref[0, 0:1, :] = stats[0]
    lse_ref[0, 1:2, :] = stats[1]
    out, stats = attend_slot(qs[...], [ks], [vs])
    out_ref[rows:, :] = out
    lse_ref[0, 2:3, :] = stats[0]
    lse_ref[0, 3:4, :] = stats[1]


def attend_sorted_call(lengths, q, kv, kvx, tokens, cot, hidden, rows):
    n = SLOTS * rows
    per = rows // SHORT

    def long(base):
        return pl.BlockSpec((rows, PAIR), lambda h, o: (slot_of(o, 0), base + h))

    def second():
        return pl.BlockSpec((rows, PAIR), lambda h, o: (slot_of(o, 1), h))

    def short(base):
        return pl.BlockSpec((SHORT, PAIR), lambda h, o: (slot_of(o, 1) * per, base + h))

    def out(size):
        return pl.BlockSpec((size, PAIR), lambda h, o: (0, h))

    return pl.pallas_call(
        attend_sorted_kernel,
        name="attend",
        out_shape=(
            jax.ShapeDtypeStruct((n, D), BF16),
            jax.ShapeDtypeStruct((PAIRS, 4, rows), F32),
            jax.ShapeDtypeStruct((n, D), BF16),
        )
        + (jax.ShapeDtypeStruct((rows, D), BF16),) * 4
        + (jax.ShapeDtypeStruct((SHORT, D), BF16),) * 2
        + (jax.ShapeDtypeStruct((n, D), BF16),) * 3,
        grid_spec=pltpu.PrefetchScalarGridSpec(
            num_scalar_prefetch=1,
            grid=(PAIRS,),
            in_specs=[
                long(0),
                second(),
                long(0), long(PAIRS), long(0), long(PAIRS),
                short(0), short(PAIRS), short(0), short(PAIRS),
            ]
            + [long(0), second()] * 3,
            out_specs=[out(n), pl.BlockSpec((1, 4, rows), lambda h, o: (h, 0, 0)), out(n)]
            + [out(rows)] * 4
            + [out(SHORT)] * 2
            + [out(n)] * 3,
        ),
        compiler_params=pltpu.CompilerParams(vmem_limit_bytes=BIG),
        cost_estimate=cost(16 * D * rows * (LEN + SHORT), 16e6, HEADS * rows * (LEN + SHORT)),
    )(
        lengths, q, q, kv, kv, kvx, kvx, kv, kv, kvx, kvx, tokens, tokens, cot, cot, hidden, hidden
    )


def flip(index, bit):
    return index + bit - 2 * bit * ((index // bit) % 2)


def add_low(a, b):
    return (a.astype(F32) + b.astype(F32)).astype(BF16)


def plane_peers():
    s, c = lax.axis_index("seq"), lax.axis_index("span")
    return [{"span": 1 - c}, {"seq": flip(s, 1)}, {"seq": flip(s, 2)}]


def line_peers():
    s = lax.axis_index("seq")
    return [{"seq": lax.rem(s + 4 * step, 16)} for step in range(1, 4)]


def greet(peers):
    barrier = pltpu.get_barrier_semaphore()
    for peer in peers:
        pl.semaphore_signal(barrier, inc=1, device_id=peer, device_id_type=MESH)
    pl.semaphore_wait(barrier, len(peers))


class Scatter:
    def __init__(self, send, recv, base, other=None, own=None, came0=None, a1=None, b1=None,
                 came2=None, came3=None):
        self.send, self.recv, self.base = send, recv, base
        self.other, self.own, self.came0 = other, own, came0
        self.a1, self.b1, self.came2, self.came3 = a1, b1, came2, came3
        s = lax.axis_index("seq")
        self.x, self.y, self.z = lax.rem(s, 2), lax.rem(s // 2, 2), s // 4
        self.core_peer, self.x_peer, self.y_peer = plane_peers()
        self.z_peers = line_peers()

    def copy(self, i):
        x, y, z = self.x, self.y, self.z
        if i == 0:
            src, dst, peer = self.other, self.came0, self.core_peer
        elif i >= 8:
            src, dst, peer = self.other.at[i - 8], self.came0.at[i - 8], self.core_peer
        elif i == 1:
            src, dst, peer = self.own.at[0:2, :, 1 - x], self.a1, self.x_peer
        elif i == 2:
            src, dst, peer = self.own.at[2:4, 1 - y], self.b1, self.y_peer
        elif i == 3:
            src, dst, peer = self.a1.at[:, 1 - y], self.came2.at[0:2], self.y_peer
        elif i == 4:
            src, dst, peer = self.b1.at[:, 1 - x], self.came2.at[2:4], self.x_peer
        else:
            step = i - 4
            src, dst = self.came2.at[lax.rem(z + step, 4)], self.came3.at[step - 1]
            peer = self.z_peers[step - 1]
        return pltpu.make_async_remote_copy(
            src_ref=src,
            dst_ref=dst,
            send_sem=self.send.at[self.base + i],
            recv_sem=self.recv.at[self.base + i],
            device_id=peer,
            device_id_type=MESH,
        )

    def start(self, *which):
        for i in which:
            self.copy(i).start()

    def arrive(self, *which):
        for i in which:
            self.copy(i).wait_recv()

    def drain(self, *which):
        for i in which:
            self.copy(i).wait_send()

    def merge0(self):
        def body(i, _):
            z, y, x = i // 4, lax.rem(i // 2, 2), lax.rem(i, 2)
            self.own[z, y, x] = add_low(self.own[z, y, x], self.came0[z, y, x])
            return 0

        lax.fori_loop(0, 16, body, 0)

    def add1(self, a_ref, b_ref):
        self.arrive(1, 2)

        def body(i, _):
            z, k = i // 2, lax.rem(i, 2)
            a_ref[z, k] = add_low(self.own[z, k, self.x], self.a1[z, k])
            b_ref[z, k] = add_low(self.own[2 + z, self.y, k], self.b1[z, k])
            return 0

        lax.fori_loop(0, 4, body, 0)

    def add2(self, out_ref):
        self.arrive(3, 4)

        def body(z, _):
            out_ref[z] = add_low(self.a1[z, self.y], self.came2[z])
            out_ref[2 + z] = add_low(self.b1[z, self.x], self.came2[2 + z])
            return 0

        lax.fori_loop(0, 2, body, 0)

    def total(self):
        self.arrive(5, 6, 7)
        total = self.came2[self.z].astype(F32)
        for step in range(3):
            total = total + self.came3[step].astype(F32)
        return total

    def scatter0(self):
        self.start(0)

    def scatter1(self):
        self.arrive(0)
        self.merge0()
        self.start(1, 2)

    def scatter2(self):
        self.add1(self.a1, self.b1)
        self.start(3, 4)

    def scatter3(self):
        self.add2(self.came2)
        self.start(5, 6, 7)


def half_shape(rows, cols):
    return (4, 2, 2, rows, cols)


ANY = pl.BlockSpec(memory_space=pl.ANY)
DMA = pltpu.SemaphoreType.DMA


def both_kernel(
    tok_ref, att_ref, cot_ref, mod_ref, gain_ref, wo_any, wu_any, bu_ref, wd_any, bd_ref, lengths,
    out_ref, dmid_ref, datt_ref, h_ref, dup_ref, dattn_ref, payload_ref, a_ref, b_ref,
    act_all, slope_all, dlow_all, mid_all, attention_all,
    wo_ref, wu_ref, wd_ref, other, own, came0, a1, b1, send, recv, loaded,
):
    step = pl.program_id(0)
    me = lax.axis_index("span")
    down = Scatter(send, recv, 0, other=other, own=own, came0=came0, a1=a1, b1=b1)
    loads = [
        pltpu.make_async_copy(src, dst, loaded.at[k])
        for k, (src, dst) in enumerate([(wo_any, wo_ref), (wu_any, wu_ref), (wd_any, wd_ref)])
    ]
    tiles = act_all.shape[0] // tok_ref.shape[0]
    tile = tok_ref.shape[0]
    t = lax.rem(step, tiles)
    at_rows = pl.ds(pl.multiple_of(t * tile, tile), tile)
    halves = [h * me + (1 - h) * (1 - me) for h in range(2)]
    swapped = jnp.full((1, D), jnp.where(lengths[1] > lengths[0], 1.0, 0.0))
    mine = jnp.where(t // (tiles // SLOTS) == 0, swapped, 1.0 - swapped)

    def modulation(b):
        cols = slice(b * D, (b + 1) * D)
        return jnp.where(mine == 0.0, mod_ref[0:1, cols], mod_ref[1:2, cols])

    @pl.when(step == 0)
    def _():
        loads[0].start()
        loads[1].start()
        greet(plane_peers())
        loads[0].wait()
        loads[1].wait()
        loads[2].start()

    @pl.when(step == 2 * tiles)
    def _():
        loads[2].wait()
        down.arrive(8, 9, 10, 11)
        down.merge0()
        down.start(1, 2)

    @pl.when(step < tiles)
    def _():
        attention = nn(att_ref[...], wo_ref[...])
        middle = tok_ref[...].astype(F32) + modulation(2) * attention
        attention_all[at_rows, :] = attention
        mid_all[at_rows, :] = middle
        center = middle - row_mean(middle)
        xhat = center * lax.rsqrt(row_mean(center * center) + EPSILON)
        hidden = xhat * wide_row(gain_ref) * (1.0 + modulation(4)) + modulation(3)
        hidden = hidden.astype(BF16)
        h_ref[...] = hidden
        d_low = (modulation(5) * cot_ref[...].astype(F32)).astype(BF16)
        for h in range(2):
            half = d_low[:, h * (D // 2) : (h + 1) * (D // 2)]
            dlow_all[at_rows, part_of(halves[h], D // 2)] = half
        up_bias = wide_row(bu_ref)
        for f in range(0, FF, CHUNK):
            cols = slice(f, f + CHUNK)
            up = nn(hidden, wu_ref[:, cols]) + up_bias[:, cols]
            square = up * up
            bend = jnp.tanh(up * (GELU_C + (GELU_C * 0.044715) * square))
            half = 0.5 * (1.0 + bend)
            slope = half + (0.5 * up) * (1.0 - bend * bend) * (
                GELU_C + (3 * GELU_C * 0.044715) * square
            )
            act_all[at_rows, cols] = (up * half).astype(BF16)
            slope_all[at_rows, cols] = slope.astype(BF16)

    @pl.when(jnp.logical_and(step >= tiles, step < 2 * tiles))
    def _():
        cols = pl.ds(pl.multiple_of(t * CHUNK, CHUNK), CHUNK)
        value = tn(act_all[:, cols], dlow_all[...]).astype(BF16)
        shape = own.shape[1:]
        other[t] = value[:, : D // 2].reshape(shape)
        own[t] = value[:, D // 2 :].reshape(shape)

        for m in range(4):
            @pl.when(t == m)
            def _():
                down.start(8 + m)

    @pl.when(step >= 2 * tiles)
    def _():
        middle, attention = mid_all[at_rows, :], attention_all[at_rows, :]
        gain = wide_row(gain_ref)
        gate1, scale2, gate2 = modulation(2), modulation(4), modulation(5)
        dy = cot_ref[...].astype(F32)
        d_low = (gate2 * dy).astype(BF16)
        lowered, d_hidden = None, None
        sums = []
        for f in range(0, FF, CHUNK):
            cols = slice(f, f + CHUNK)
            d_act = nt(d_low, wd_ref[cols, :])
            d_up = (d_act * slope_all[at_rows, cols].astype(F32)).astype(BF16)
            place = halves[f // (FF // 2)] * (FF // 2) + f % (FF // 2)
            dup_ref[:, pl.ds(pl.multiple_of(place, CHUNK), CHUNK)] = d_up
            sums.append(col_sum(d_up.astype(F32)))
            low = nn(act_all[at_rows, cols], wd_ref[cols, :])
            dh = nt(d_up, wu_ref[:, cols])
            lowered = low if lowered is None else lowered + low
            d_hidden = dh if d_hidden is None else d_hidden + dh
        center = middle - row_mean(middle)
        r = lax.rsqrt(row_mean(center * center) + EPSILON)
        xhat = center * r
        lowered = lowered + wide_row(bd_ref)
        out_ref[...] = (middle + gate2 * lowered).astype(BF16)
        hx = col_sum(d_hidden * xhat)
        fx = d_hidden * (1.0 + scale2) * gain
        d_mid = dy + r * (fx - row_mean(fx) - xhat * row_mean(fx * xhat))
        dmid_ref[...] = d_mid
        d_attention = (gate1 * d_mid).astype(BF16)
        for h in range(2):
            half = d_attention[:, h * (D // 2) : (h + 1) * (D // 2)]
            dattn_ref[:, part_of(halves[h], D // 2)] = half
        datt_ref[...] = nt(d_attention, wo_ref[...]).astype(BF16)
        four = jnp.concatenate(
            [
                col_sum(d_mid * attention), col_sum(d_hidden), hx * gain,
                col_sum(dy * lowered),
            ],
            axis=0,
        )
        is_second = jnp.concatenate([mine] * 4, axis=0) != 0.0
        none = jnp.zeros((4, D), F32)
        add_to(
            payload_ref,
            jnp.concatenate(
                [
                    jnp.where(is_second, none, four), jnp.where(is_second, four, none),
                    hx * (1.0 + scale2), col_sum(d_low.astype(F32)), *sums,
                    jnp.zeros((2, D), F32),
                ],
                axis=0,
            ),
            step == 2 * tiles,
        )

    @pl.when(step == 3 * tiles - 1)
    def _():
        down.add1(a_ref, b_ref)
        down.drain(1, 2, 8, 9, 10, 11)


def both_call(tokens, att, cot, mod, gain, wo, wu, bu, wd, bd, lengths, rows):
    n = SLOTS * rows
    tile = 256
    tiles = n // tile
    dr, dc = FF // 16, D // 2

    def first():
        return pl.BlockSpec((tile, D), lambda s: (jnp.minimum(s, tiles - 1), 0))

    def last(width):
        return pl.BlockSpec((tile, width), lambda s: (jnp.maximum(s - 2 * tiles, 0), 0))

    def low(*shape):
        return pltpu.VMEM(shape, BF16)

    return pl.pallas_call(
        both_kernel,
        name="feed",
        grid=(3 * tiles,),
        out_shape=(
            jax.ShapeDtypeStruct((n, D), BF16),
            jax.ShapeDtypeStruct((n, D), F32),
            jax.ShapeDtypeStruct((n, D), BF16),
            jax.ShapeDtypeStruct((n, D), BF16),
            jax.ShapeDtypeStruct((n, FF), BF16),
            jax.ShapeDtypeStruct((n, D), BF16),
            jax.ShapeDtypeStruct((16, D), F32),
            jax.ShapeDtypeStruct((2, 2, dr, dc), BF16),
            jax.ShapeDtypeStruct((2, 2, dr, dc), BF16),
        ),
        in_specs=[
            first(),
            first(),
            pl.BlockSpec((tile, D), lambda s: (lax.rem(s, tiles), 0)),
            whole((8, 6 * D)),
            whole((D,)),
            ANY,
            ANY,
            whole((FF,)),
            ANY,
            whole((D,)),
            pl.BlockSpec(memory_space=pltpu.SMEM),
        ],
        out_specs=(
            last(D), last(D), last(D), first(), last(FF), last(D), whole((16, D)),
            whole((2, 2, dr, dc)),
            whole((2, 2, dr, dc)),
        ),
        scratch_shapes=[
            low(n, FF), low(n, FF), low(n, D),
            pltpu.VMEM((n, D), F32),
            pltpu.VMEM((n, D), F32),
        ]
        + [low(D, D), low(D, FF), low(FF, D)]
        + [low(*half_shape(dr, dc))] * 3
        + [low(2, 2, dr, dc)] * 2
        + [DMA((12,)), DMA((12,)), DMA((3,))],
        compiler_params=pltpu.CompilerParams(
            collective_id=2, has_side_effects=True, vmem_limit_bytes=BIG
        ),
        cost_estimate=cost(2 * n * D * (5 * FF + 2 * D), 40e6, n * FF),
    )(tokens, att, cot, mod, gain, wo, wu, bu, wd, bd, lengths)


def pack_rows(rows, count):
    parts = [rows[r : r + 1, c : c + 128] for r in range(count) for c in range(0, D, 128)]
    rest = -len(parts) % 16
    if rest:
        parts.append(jnp.zeros((rest, 128), F32))
    return jnp.concatenate(parts, axis=0).astype(BF16)


FIRST = 5
ROUNDS = PAIRS // 2
WIDE = 3 * PAIR


def middle_kernel(
    att_ref, dattn_ref, h_any, dup_ref, hid1_any, payload_ref, down_a, down_b,
    ql, qs, ko, vo, kx, vx, ks, vs, dol, dos, al, as_, lse, cos_ref, sin_ref,
    dq_ref, dk_ref, dv_ref, down_ref, out_ref, up_ref, r_ref, ra_ref, rb_ref, rown_ref, early_ref,
    h_ref, hid1_ref, down2, down3,
    out_other, out_own, out_came, out_a, out_b, out2, out3,
    up_other, up_own, up_came, up_a, up_b, up2, up3,
    round_other, round_came, round_a, round_b, round2, d_round, keep_q,
    leave, come, keep_k, keep_v, keep_sk, keep_sv, early_came, early_sum, early_all,
    send, recv, send_kv, recv_kv, send_early, recv_early, loaded,
):
    step = pl.program_id(0)
    s, me = lax.axis_index("seq"), lax.axis_index("span")
    rows = ql.shape[0]
    down = Scatter(send, recv, 0, a1=down_a, b1=down_b, came2=down2, came3=down3)
    out = Scatter(
        send, recv, 12, other=out_other, own=out_own, came0=out_came, a1=out_a, b1=out_b,
        came2=out2, came3=out3,
    )
    up = Scatter(
        send, recv, 20, other=up_other, own=up_own, came0=up_came, a1=up_a, b1=up_b, came2=up2,
        came3=up3,
    )
    part, wide = hid1_ref.shape[1] // 16, WIDE
    rounds = [
        Scatter(
            send, recv, 28 + 5 * k,
            other=round_other.at[k],
            own=(up_other.at[:, :, :, :, :wide], up_other.at[:, :, :, :, wide : 2 * wide], rown_ref)[k],
            came0=round_came.at[k],
            a1=round_a.at[k] if k < 2 else None,
            b1=round_b.at[k] if k < 2 else None,
            came2=round2,
        )
        for k in range(ROUNDS)
    ]
    cos = cos_ref[pl.ds(pl.multiple_of(me * rows, rows), rows), :]
    sin = sin_ref[pl.ds(pl.multiple_of(me * rows, rows), rows), :]

    def kv_copy(pair):
        return pltpu.make_async_remote_copy(
            src_ref=leave.at[pair],
            dst_ref=come.at[pair],
            send_sem=send_kv.at[pair],
            recv_sem=recv_kv.at[pair],
            device_id={"span": 1 - me},
            device_id_type=MESH,
        )

    loads = [
        pltpu.make_async_copy(h_any, h_ref, loaded.at[0]),
        pltpu.make_async_copy(hid1_any, hid1_ref, loaded.at[1]),
    ]

    def early_copy(k):
        half = pl.ds(pl.multiple_of(me * 48, 16), 48)
        if k == 0:
            src, dst, peer = payload_ref, early_came, {"span": 1 - me}
        elif k == 16:
            src, dst, peer = early_all.at[:, half], early_all.at[:, half], {"span": 1 - me}
        else:
            src, dst = early_sum.at[half], early_all.at[s, half]
            peer = {"seq": lax.rem(s + k, 16)}
        return pltpu.make_async_remote_copy(
            src_ref=src,
            dst_ref=dst,
            send_sem=send_early.at[k],
            recv_sem=recv_early.at[k],
            device_id=peer,
            device_id_type=MESH,
        )

    def at(number):
        return pl.when(step == number)

    @at(0)
    def _():
        for load in loads:
            load.start()
        greet([{"span": 1 - me}] + [{"seq": lax.rem(s + k, 16)} for k in range(1, 16)])
        down.start(3, 4)
        early_copy(0).start()

    @at(3)
    def _():
        early_copy(0).wait_recv()
        early_sum[...] = pack_rows(payload_ref[...] + early_came[...], 16)
        for k in range(1, 16):
            early_copy(k).start()
        half = pl.ds(pl.multiple_of(me * 48, 16), 48)
        early_all[s, half] = early_sum[half]

    @at(FIRST + 3)
    def _():
        for k in range(1, 16):
            early_copy(k).wait_recv()
        early_copy(16).start()

    @at(1)
    def _():
        for load in loads:
            load.wait()

    @at(2)
    def _():
        out.scatter1()

    @at(4)
    def _():
        out.scatter2()

    @at(FIRST)
    def _():
        up.scatter1()

    @at(FIRST + 1)
    def _():
        out.scatter3()

    @at(FIRST + 2)
    def _():
        up.drain(0)

    @at(3)
    def _():
        down.scatter3()

    @at(FIRST + 4)
    def _():
        rounds[0].scatter1()

    @at(FIRST + 4)
    def _():
        up.scatter3()

    def between():
        @at(FIRST + 5)
        def _():
            rounds[0].scatter2()
            rounds[1].scatter1()

        @at(FIRST + 2)
        def _():
            up.scatter2()

    @at(0)
    def _():
        value = tn(att_ref[...], dattn_ref[...]).astype(BF16)
        out_other[...] = value[:, : D // 2].reshape(out_own.shape)
        out_own[...] = value[:, D // 2 :].reshape(out_own.shape)
        out.scatter0()

    @pl.when(jnp.logical_and(step >= 1, step < FIRST))
    def _():
        value = tn(h_ref[...], dup_ref[...]).astype(BF16)
        value = value.reshape(up_own.shape[:4] + (CHUNK,))
        cols = pl.ds(pl.multiple_of(lax.rem(step - 1, 2) * CHUNK, CHUNK), CHUNK)

        @pl.when(step < 3)
        def _():
            up_other[:, :, :, :, cols] = value

        @pl.when(step >= 3)
        def _():
            up_own[:, :, :, :, cols] = value

    @at(2)
    def _():
        up.scatter0()

    @pl.when(jnp.logical_and(step >= FIRST, step < FIRST + PAIRS))
    def _():
        pair = step - FIRST
        stats = lse[0]
        dq, dk, dv = attend_back_slot(
            ql[...], [ko[...], kx[...]], [vo[...], vx[...]], dol[...], al[...],
            [stats[0:1], stats[1:2]], between,
        )
        dq = turn_back(dq, cos, sin).astype(BF16)
        dq_ref[:rows, :] = dq
        keep_q[lax.rem(pair, 2), :rows, :] = dq
        keep_k[lax.rem(pair, 2)] = dk[0]
        keep_v[lax.rem(pair, 2)] = dv[0]
        leave[pair, :rows, :PAIR] = dk[1].astype(BF16)
        leave[pair, :rows, PAIR:] = dv[1].astype(BF16)
        dq, dk, dv = attend_back_slot(
            qs[...], [ks[...]], [vs[...]], dos[...], as_[...], [stats[2:3], stats[3:4]]
        )
        dq = turn_back(dq, cos, sin).astype(BF16)
        dq_ref[rows:, :] = dq
        keep_q[lax.rem(pair, 2), rows:, :] = dq
        keep_sk[lax.rem(pair, 2)] = dk[0]
        keep_sv[lax.rem(pair, 2)] = dv[0]
        leave[pair, rows:, :PAIR] = dk[0].astype(BF16)
        leave[pair, rows:, PAIR:] = dv[0].astype(BF16)
        kv_copy(pair).start()

    @pl.when(step > FIRST)
    def _():
        pair = step - FIRST - 1
        kv_copy(pair).wait_recv()
        dk = keep_k[lax.rem(pair, 2)] + come[pair, :rows, :PAIR].astype(F32)
        dk_ref[:rows, :] = turn_back(dk, cos, sin).astype(BF16)
        dv = keep_v[lax.rem(pair, 2)] + come[pair, :rows, PAIR:].astype(F32)
        dv_ref[:rows, :] = dv.astype(BF16)
        zero = jnp.zeros((SHORT, PAIR), F32)
        sk = keep_sk[lax.rem(pair, 2)] + come[pair, rows:, :PAIR].astype(F32)
        sk = jnp.where(me == 0, turn_back(sk, cos[:SHORT], sin[:SHORT]), zero)
        sv = keep_sv[lax.rem(pair, 2)] + come[pair, rows:, PAIR:].astype(F32)
        dk_ref[rows : rows + SHORT, :] = sk.astype(BF16)
        dv_ref[rows : rows + SHORT, :] = jnp.where(me == 0, sv, zero).astype(BF16)
        rest = jnp.zeros((rows - SHORT, PAIR), BF16)
        dk_ref[rows + SHORT :, :] = rest
        dv_ref[rows + SHORT :, :] = rest
        later = lax.rem(pair, 2)
        first, second = wide * (1 - me), wide * me
        q_at = first + later * PAIR
        k_at = (first + 2 * PAIR) * (1 - later) + second * later
        v_at = second + PAIR + later * PAIR
        d_round[:, pl.ds(pl.multiple_of(q_at, PAIR), PAIR)] = keep_q[later]
        d_round[:, pl.ds(pl.multiple_of(k_at, PAIR), PAIR)] = dk_ref[...]
        d_round[:, pl.ds(pl.multiple_of(v_at, PAIR), PAIR)] = dv_ref[...]

    for k in range(ROUNDS):
        @at(FIRST + 2 * k + 2)
        def _():
            value = tn(hid1_ref[...], d_round[...]).astype(BF16)
            rounds[k].other[...] = value[:, :wide].reshape(half_shape(part, wide))
            rounds[k].start(0)
            rounds[k].own[...] = value[:, wide:].reshape(half_shape(part, wide))

    @at(FIRST + PAIRS)
    def _():
        out_ref[...] = out.total()
        rounds[0].add2(r_ref)
        rounds[2].arrive(0)
        rounds[2].merge0()
        rounds[1].add1(ra_ref, rb_ref)
        down_ref[...] = down.total()
        up_ref[...] = up.total()
        down.drain(*range(3, 8))
        out.drain(*range(8))
        up.drain(*range(1, 8))
        rounds[0].drain(*range(5))
        rounds[1].drain(0, 1, 2)
        rounds[2].drain(0)
        for pair in range(PAIRS):
            kv_copy(pair).wait_send()
        early_copy(16).wait_recv()
        for k in range(17):
            early_copy(k).wait_send()
        early_ref[...] = early_all[...]


def middle_call(
    att, d_attention, hidden, d_up, hidden1, payload, down_a, down_b, q, kv, d_att, lse, cos, sin, rows,
):
    n = SLOTS * rows
    half = FF // 2
    dr, dc = FF // 16, D // 2
    ur, wr = D // 16, D // 16

    def clamp(s, low, high):
        return jnp.minimum(jnp.maximum(s, low), high)

    def order_of(k):
        return k // 2 + lax.rem(k, 2) * ROUNDS

    def now(s):
        return order_of(clamp(s - FIRST, 0, PAIRS - 1))

    def before(s):
        return order_of(clamp(s - FIRST - 1, 0, PAIRS - 1))

    def long():
        return pl.BlockSpec((rows, PAIR), lambda s: (0, now(s)))

    def second():
        return pl.BlockSpec((rows, PAIR), lambda s: (1, now(s)))

    def short():
        return pl.BlockSpec((SHORT, PAIR), lambda s: (0, now(s)))

    def low(shape):
        return pltpu.VMEM(shape, BF16)

    handed = ((4, ur, WIDE), (2, 2, ur, WIDE), (2, 2, ur, WIDE), half_shape(ur, WIDE))

    return pl.pallas_call(
        middle_kernel,
        name="middle",
        grid=(FIRST + PAIRS + 1,),
        out_shape=(
            jax.ShapeDtypeStruct((n, D), BF16),
            jax.ShapeDtypeStruct((n, D), BF16),
            jax.ShapeDtypeStruct((n, D), BF16),
            jax.ShapeDtypeStruct((dr, dc), F32),
            jax.ShapeDtypeStruct((wr, dc), F32),
            jax.ShapeDtypeStruct((ur, half), F32),
        )
        + tuple(jax.ShapeDtypeStruct(o, BF16) for o in handed + ((16, 96, 128),)),
        in_specs=[
            whole((n, D)),
            whole((n, D)),
            ANY,
            pl.BlockSpec((n, CHUNK), lambda s: (0, clamp(s - 1, 0, 3))),
            ANY,
            whole((16, D)),
            whole((2, 2, dr, dc)),
            whole((2, 2, dr, dc)),
            long(), second(), long(), long(), long(), long(), short(), short(), long(), second(),
            long(), second(),
            pl.BlockSpec((1, 4, rows), lambda s: (now(s), 0, 0)),
            whole((LEN, PAIR)),
            whole((LEN, PAIR)),
        ],
        out_specs=(
            pl.BlockSpec((n, PAIR), lambda s: (0, now(s))),
            pl.BlockSpec((n, PAIR), lambda s: (0, before(s))),
            pl.BlockSpec((n, PAIR), lambda s: (0, before(s))),
            whole((dr, dc)),
            whole((wr, dc)),
            whole((ur, half)),
        )
        + tuple(whole(o) for o in handed + ((16, 96, 128),)),
        scratch_shapes=[low((n, D)), low((n, D)), low((4, dr, dc)), low((3, dr, dc))]
        + [low(half_shape(wr, dc))] * 3
        + [low((2, 2, wr, dc))] * 2
        + [low((4, wr, dc)), low((3, wr, dc))]
        + [low(half_shape(ur, half))] * 3
        + [low((2, 2, ur, half))] * 2
        + [low((4, ur, half)), low((3, ur, half))]
        + [low((ROUNDS,) + half_shape(ur, WIDE))] * 2
        + [low((2, 2, 2, ur, WIDE))] * 2
        + [low((4, ur, WIDE))]
        + [low((n, 2 * WIDE)), low((2, n, PAIR))]
        + [low((PAIRS, rows + SHORT, 2 * PAIR))] * 2
        + [pltpu.VMEM((2, rows, PAIR), F32)] * 2
        + [pltpu.VMEM((2, SHORT, PAIR), F32)] * 2
        + [pltpu.VMEM((16, D), F32), low((96, 128)), low((16, 96, 128))]
        + [DMA((43,)), DMA((43,)), DMA((PAIRS,)), DMA((PAIRS,)), DMA((17,)), DMA((17,)), DMA((2,))],
        compiler_params=pltpu.CompilerParams(
            collective_id=1, has_side_effects=True, vmem_limit_bytes=BIG
        ),
        cost_estimate=cost(2 * n * D * (FF + 4 * D) + 40 * D * rows * (LEN + SHORT), 50e6),
    )(
        att, d_attention, hidden, d_up, hidden1, payload, down_a, down_b, q, q, *kv, d_att, d_att,
        att, att, lse, cos, sin,
    )


TILES = 4


def end_kernel(
    tok_ref, dmid_ref, dq_ref, dk_ref, dv_ref, mod_ref, gain_ref, weight_any, lengths,
    r_in, ra, rb, rown,
    grad_ref, gqkv_ref, late_ref,
    weight_ref, r2, r3, last_a, last_b, sums, sums_came, sums_all, late_came,
    send, recv, send_late, recv_late, loaded,
):
    step = pl.program_id(0)
    s, me = lax.axis_index("seq"), lax.axis_index("span")
    rounds = [
        Scatter(
            send, recv, 8 * k, own=rown,
            a1=last_a if k == 2 else ra,
            b1=last_b if k == 2 else rb,
            came2=r2.at[k], came3=r3.at[k],
        )
        for k in range(ROUNDS)
    ]

    def late_copy(k):
        if k == 0:
            src, dst, peer = sums, sums_came, {"span": 1 - me}
        else:
            src, dst, peer = sums_all, late_came.at[s], {"seq": lax.rem(s + k, 16)}
        return pltpu.make_async_remote_copy(
            src_ref=src,
            dst_ref=dst,
            send_sem=send_late.at[k],
            recv_sem=recv_late.at[k],
            device_id=peer,
            device_id_type=MESH,
        )

    def at(number):
        return pl.when(step == number)

    @at(0)
    def _():
        load = pltpu.make_async_copy(weight_any, weight_ref, loaded)
        load.start()
        r2[0] = r_in[...]
        sums[...] = jnp.zeros_like(sums)
        greet([{"span": 1 - me}] + [{"seq": lax.rem(s + k, 16)} for k in range(1, 16)])
        rounds[2].start(1, 2)
        rounds[1].start(3, 4)
        rounds[0].start(5, 6, 7)
        load.wait()

    size = tok_ref.shape[0]
    j = step // 2
    swapped = jnp.full((1, D), jnp.where(lengths[1] > lengths[0], 1.0, 0.0))
    mine = jnp.where(j == 0, swapped, 1.0 - swapped)
    scale = jnp.where(mine == 0.0, mod_ref[0:1, D : 2 * D], mod_ref[1:2, D : 2 * D])
    gain = wide_row(gain_ref)
    d_hidden = (
        nt(dq_ref[...], weight_ref[:, :D])
        + nt(dk_ref[...], weight_ref[:, D : 2 * D])
        + nt(dv_ref[...], weight_ref[:, 2 * D :])
    )
    x = tok_ref[...].astype(F32)
    center = x - row_mean(x)
    r = lax.rsqrt(row_mean(center * center) + EPSILON)
    xhat = center * r
    hx = col_sum(d_hidden * xhat)
    fx = d_hidden * (1.0 + scale) * gain
    grad_ref[...] = dmid_ref[...] + r * (fx - row_mean(fx) - xhat * row_mean(fx * xhat))
    shift = col_sum(d_hidden)
    first, second = mine == 0.0, mine != 0.0
    zero = jnp.zeros((1, D), F32)
    sums[...] += jnp.concatenate(
        [
            jnp.where(first, shift, zero), jnp.where(first, hx * gain, zero),
            jnp.where(second, shift, zero), jnp.where(second, hx * gain, zero),
            hx * (1.0 + scale), jnp.zeros((3, D), F32),
        ],
        axis=0,
    )

    @at(TILES - 1)
    def _():
        late_copy(0).start()
        rounds[2].scatter2()
        rounds[1].scatter3()
        late_copy(0).wait_recv()
        sums_all[...] = pack_rows(sums[...] + sums_came[...], 5)
        for k in range(1, 16):
            late_copy(k).start()
        late_came[s] = sums_all[...]
        rounds[2].scatter3()
        for k in range(ROUNDS):
            total = rounds[k].total()
            for c in range(3):
                cols = slice((c * ROUNDS + k) * PAIR, (c * ROUNDS + k + 1) * PAIR)
                gqkv_ref[:, cols] = total[:, c * PAIR : (c + 1) * PAIR]
        rounds[0].drain(*range(5, 8))
        rounds[1].drain(*range(3, 8))
        rounds[2].drain(*range(1, 8))
        for k in range(16):
            if k > 0:
                late_copy(k).wait_recv()
            late_copy(k).wait_send()
        late_ref[...] = late_came[...]


def end_call(tokens, d_mid, dq, dk, dv, mod, gain, weight, lengths, handed, rows):
    n = SLOTS * rows
    size = n // TILES
    r = D // 16

    def tile():
        return pl.BlockSpec((size, D), lambda s: (s, 0))

    return pl.pallas_call(
        end_kernel,
        name="end",
        grid=(TILES,),
        out_shape=(
            jax.ShapeDtypeStruct((n, D), F32),
            jax.ShapeDtypeStruct((r, 3 * D // 2), F32),
            jax.ShapeDtypeStruct((16, 32, 128), BF16),
        ),
        in_specs=[tile()] * 5
        + [
            whole((8, 6 * D)),
            whole((D,)),
            ANY,
            pl.BlockSpec(memory_space=pltpu.SMEM),
        ]
        + [whole(a.shape) for a in handed],
        out_specs=(
            tile(),
            whole((r, 3 * D // 2)),
            whole((16, 32, 128)),
        ),
        scratch_shapes=[
            pltpu.VMEM((D, 3 * D), BF16),
            pltpu.VMEM((ROUNDS, 4, r, WIDE), BF16),
            pltpu.VMEM((ROUNDS, 3, r, WIDE), BF16),
            pltpu.VMEM((2, 2, r, WIDE), BF16),
            pltpu.VMEM((2, 2, r, WIDE), BF16),
            pltpu.VMEM((8, D), F32),
            pltpu.VMEM((8, D), F32),
            pltpu.VMEM((32, 128), BF16),
            pltpu.VMEM((16, 32, 128), BF16),
            DMA((8 * ROUNDS,)),
            DMA((8 * ROUNDS,)),
            DMA((16,)),
            DMA((16,)),
            DMA,
        ],
        compiler_params=pltpu.CompilerParams(
            collective_id=3, has_side_effects=True, vmem_limit_bytes=BIG
        ),
        cost_estimate=cost(2 * n * D * 3 * D, 22e6),
    )(tokens, d_mid, dq, dk, dv, mod, gain, weight, lengths, *handed)


def thirds(value):
    high = value.astype(BF16)
    rest = value - high.astype(F32)
    middle = rest.astype(BF16)
    return [high, middle, (rest - middle.astype(F32)).astype(BF16)]


def condition_kernel(
    lengths, early_ref, late_ref, table_ref, silu_ref, weight_ref,
    qkv_in, out_in, up_in, down_in, sorted_any, result_any,
    ada_ref, bias_ref, gcond_ref, gain1_ref, gain2_ref, bd_ref, bu_ref,
    qkv_ref, out_ref, up_ref, down_ref, natural_any, final_any, stage, stage_out, read, moved,
):
    seq = late_ref.shape[0]
    me, s = lax.axis_index("span"), lax.axis_index("seq")
    half = sorted_any.shape[0] // SLOTS
    reads, moves = [], []
    given = ((sorted_any, stage, natural_any), (result_any, stage_out, final_any))
    for i, (src, held, dst) in enumerate(given):
        for j in range(SLOTS):
            to = pl.ds(pl.multiple_of(slot_of(lengths, j) * half, half), half)
            at = i * SLOTS + j
            reads.append(
                pltpu.make_async_copy(src.at[pl.ds(j * half, half)], held.at[j], read.at[at])
            )
            moves.append(pltpu.make_async_copy(held.at[j], dst.at[to], moved.at[at]))
    for copy in reads:
        copy.start()
    qkv_ref[...] = qkv_in[...]
    out_ref[...] = out_in[...]
    up_ref[...] = up_in[...]
    down_ref[...] = down_in[...]
    for come, go in zip(reads, moves):
        come.wait()
        go.start()
    packed = early_ref[...].astype(F32)
    early = [
        jnp.concatenate([packed[:, 6 * r + c] for c in range(6)], axis=1) for r in range(14)
    ]
    packed = late_ref[...].astype(F32)
    late = [
        jnp.concatenate([packed[:, 6 * r + c] for c in range(6)], axis=1) for r in range(5)
    ]
    mods = []
    for k in range(SLOTS):
        mods.append(
            [late[2 * k], late[2 * k + 1]] + [early[4 * k + b] for b in range(4)]
        )
    gain1_ref[...] = jnp.sum(late[4], axis=0)
    gain2_ref[...] = jnp.sum(early[8], axis=0)
    bd_ref[...] = jnp.sum(early[9], axis=0)
    for f in range(4):
        bu_ref[f * D : (f + 1) * D] = jnp.sum(early[10 + f], axis=0)
    own = []
    asked = [
        jnp.concatenate([table_ref[:, SLOTS + k, :]] * 6, axis=1) for k in range(SLOTS)
    ]
    for b in range(6):
        cols = slice(b * D, (b + 1) * D)
        bias_ref[cols] = jnp.sum(mods[0][b] + mods[1][b], axis=0)
        rows = []
        for r in range(SLOTS):
            wanted = (s * SLOTS + r).astype(F32)
            picked = [jnp.where(asked[k] == wanted, mods[k][b], 0.0) for k in range(SLOTS)]
            rows.append(col_sum(picked[0] + picked[1]))
        own.append(jnp.concatenate(rows + [jnp.zeros((8 - SLOTS, D), F32)], axis=0))
    own = jnp.concatenate(own, axis=1)
    d_silu = nt(jnp.concatenate(thirds(own), axis=0), weight_ref[...])
    d_silu = d_silu[:8] + d_silu[8:16] + d_silu[16:24]
    v = table_ref[s]
    sig = 1.0 / (1.0 + jnp.exp(-v))
    gcond_ref[...] = (d_silu * (sig * (1.0 + v * (1.0 - sig))))[:SLOTS]
    rows = 128 // seq
    pick = lax.broadcasted_iota(jnp.int32, (rows, 128), 1) == (
        s * rows + lax.broadcasted_iota(jnp.int32, (rows, 128), 0)
    )
    pick = jnp.where(pick, 1.0, 0.0)
    silu = [nt(pick.astype(BF16), silu_ref[k].astype(BF16)).astype(BF16) for k in range(SLOTS)]
    silu = jnp.concatenate(silu * 3, axis=1)
    for b in range(3):
        blocks = [jnp.where(me == 0, mods[k][b], mods[k][3 + b]) for k in range(SLOTS)]
        split = [part for part in zip(*(thirds(block) for block in blocks))]
        right = jnp.concatenate([block for part in split for block in part], axis=0)
        ada_ref[:, b * D : (b + 1) * D] = nn(silu, right)
    for move in moves:
        move.wait()


def condition_call(lengths, early, late, table, silu, ada_weight, tiles, grad_in, result):
    seq = late.shape[0]

    def all_of(shape):
        return pl.BlockSpec(shape, lambda i, p: (0,) * len(shape))

    given = (early, late, table, silu, ada_weight) + tiles
    outs = ((128 // seq, 3 * D), (6 * D,), (SLOTS, 128), (D,), (D,), (D,), (FF,))
    outs += tuple(t.shape for t in tiles)
    return pl.pallas_call(
        condition_kernel,
        name="condition",
        out_shape=tuple(jax.ShapeDtypeStruct(o, F32) for o in outs + (grad_in.shape,))
        + (jax.ShapeDtypeStruct(result.shape, BF16),),
        grid_spec=pltpu.PrefetchScalarGridSpec(
            num_scalar_prefetch=1,
            grid=(1,),
            in_specs=[whole(a.shape) for a in given] + [ANY] * 2,
            out_specs=[all_of(o) for o in outs] + [ANY] * 2,
            scratch_shapes=[
                pltpu.VMEM((SLOTS, grad_in.shape[0] // SLOTS, D), F32),
                pltpu.VMEM((SLOTS, grad_in.shape[0] // SLOTS, D), BF16),
                DMA((2 * SLOTS,)),
                DMA((2 * SLOTS,)),
            ],
        ),
        compiler_params=pltpu.CompilerParams(vmem_limit_bytes=BIG),
        cost_estimate=cost(1e7, 12e6),
    )(lengths, *given, grad_in, result)


def from_peers(array, span):
    return [
        lax.ppermute(array, "span", [((i + step) % span, i) for i in range(span)])
        for step in range(1, span)
    ]


def gather_all(flat):
    seq, span = lax.axis_size("seq"), lax.axis_size("span")
    return lax.all_gather(flat, ("seq", "span"), axis=0).reshape(seq, span, flat.shape[0])


def shards(
    tokens, conditions, assignment, lengths, norm1_gain, ada_weight, ada_bias, qkv_weight,
    out_weight, norm2_gain, up_weight, up_bias, down_weight, down_bias, cotangent,
):
    slots, rows, _ = tokens.shape
    seq, span = lax.axis_size("seq"), lax.axis_size("span")
    seq_at, span_at = lax.axis_index("seq"), lax.axis_index("span")
    flat = slots * rows
    place = jnp.concatenate(
        [lengths, jnp.stack([span_at.astype(jnp.int32), seq_at.astype(jnp.int32)])]
    )
    fast = seq == 16 and span == 2
    cos, sin = (jnp.asarray(table) for table in rotary(LEN))
    tokens2 = tokens.reshape(flat, D)
    gain1, gain2 = norm1_gain, norm2_gain
    if fast:
        q, hidden1, kv, mod, table, silu_all, kvx = share_call(
            conditions, assignment, ada_weight, ada_bias, tokens2, gain1, qkv_weight, cos, sin,
            rows,
        )
        att, lse, q, *kv, tokens2, cot, hidden1 = attend_sorted_call(
            lengths, q, kv, kvx, tokens2, cotangent.reshape(flat, D), hidden1, rows
        )
    else:
        mod, table, _ = modulation_call(conditions, assignment, ada_weight, ada_bias, seq)
        q, hidden1, kv_long, kv_tail = project_call(
            place, tokens2, mod, gain1, qkv_weight, cos, sin, rows
        )
        kv_other = jnp.concatenate(from_peers(kv_long, span), axis=0)
        kv_short = kv_tail[:SHORT]
        sent = [lax.ppermute(kv_short, "span", [(0, i)]) for i in range(1, span)]
        kv_short = jnp.where(span_at == 0, kv_short, sum(sent[1:], sent[0]))
        att, lse = attend_call(q, kv_long, kv_other, kv_short, rows)
    if fast:
        out, d_mid, d_att, hidden2, d_up, d_attention, payload, *handed = both_call(
            tokens2, att, cot, mod, gain2, out_weight, up_weight, up_bias, down_weight,
            down_bias, lengths, rows,
        )
        dq, dk, dv, grad_down, grad_out, grad_up, *handed, early = middle_call(
            att, d_attention, hidden2, d_up, hidden1, payload, *handed, q, kv, d_att, lse,
            cos, sin, rows,
        )
        grad_in, grad_qkv, late = end_call(
            tokens2, d_mid, dq, dk, dv, mod, gain1, qkv_weight, lengths, handed, rows
        )
        (
            grad_ada, ada_bias_sum, grad_cond, gain1_sum, gain2_sum, bd_sum, bu_sum,
            grad_qkv, grad_out, grad_up, grad_down, grad_in, out,
        ) = condition_call(
            lengths, early, late, table, silu_all, ada_weight,
            (grad_qkv, grad_out, grad_up, grad_down), grad_in, out,
        )
        return (
            out.reshape(tokens.shape), grad_in.reshape(tokens.shape), grad_cond, gain1_sum,
            grad_ada, ada_bias_sum, grad_qkv, grad_out, gain2_sum, grad_up, bu_sum, grad_down,
            bd_sum,
        )
    (
        out, d_mid, d_att, act, d_low, hidden2, d_up, d_attention, payload, tokens_sorted,
        hidden1_sorted,
    ) = feed_call(
        fast, lengths, tokens2, att, cotangent.reshape(flat, D), hidden1, mod, gain2, out_weight,
        up_weight, up_bias, down_weight, down_bias, rows,
    )
    grad_down = weight_gradient(act, d_low)
    grad_up = weight_gradient(hidden2, d_up)
    grad_out = weight_gradient(att, d_attention)
    early = gather_all(payload[:14].reshape(-1))

    dq, dk, dv, dkx, dvx, dks, dvs = attend_back_call(
        place, q, kv_long, kv_other, kv_short, d_att, att, lse, cos, sin, rows
    )
    ek = ev = None
    for step in range(1, span):
        back = [((i, (i + step) % span)) for i in range(span)]
        cut = slice((step - 1) * rows, step * rows)
        pk, pv = lax.ppermute((dkx[cut], dvx[cut]), "span", back)
        ek = pk if ek is None else (ek.astype(F32) + pk.astype(F32))
        ev = pv if ev is None else (ev.astype(F32) + pv.astype(F32))
    d_short = jnp.concatenate([dks, dvs], axis=1)
    for step in range(1, span):
        d_short = d_short + lax.ppermute(
            jnp.concatenate([dks, dvs], axis=1), "span", [(step, 0)]
        )
    d_qkv = join_call(
        place, dq, dk, dv, ek, ev, d_short[:, :D], d_short[:, D:], cos, sin, rows
    )
    grad_qkv = weight_gradient(hidden1, d_qkv)
    grad_in, d_mod1, d_gain1 = last_call(
        place, tokens2, d_qkv, d_mid, mod, gain1, qkv_weight, rows
    )
    late = gather_all(jnp.concatenate([d_mod1[:, :2].reshape(-1), d_gain1[0]]))

    cut = slots * 4 * D
    mods2 = jnp.sum(early[:, :, :cut], axis=1).reshape(seq * slots, 4 * D)
    sums2 = jnp.sum(early[:, :, cut:], axis=(0, 1))
    cut = slots * 2 * D
    mods1 = jnp.sum(late[:, :, :cut], axis=1).reshape(seq * slots, 2 * D)
    gain1_sum = jnp.sum(late[:, :, cut:], axis=(0, 1))
    d_mods = jnp.concatenate([mods1, mods2], axis=1)
    grad_ada_bias = jnp.sum(d_mods, axis=0)
    cond_all = table[:, :slots].reshape(seq * slots, 128)
    assign_all = table[:, slots : 2 * slots, 0].reshape(seq * slots)
    number = jnp.arange(seq * slots, dtype=jnp.int32).astype(F32)
    picker = (assign_all[:, None] == number[None, :]).astype(F32)
    exact = partial(lax.dot_general, precision=HIGHEST, preferred_element_type=F32)
    cond_rows = exact(picker, cond_all, (((1,), (0,)), ((), ())))
    silu_low = jax.nn.silu(cond_rows).astype(BF16).astype(F32)
    ada_rows, ada_cols = 128 // seq, 6 * D // span
    grad_ada = exact(
        lax.dynamic_slice_in_dim(silu_low, seq_at * ada_rows, ada_rows, 1),
        lax.dynamic_slice_in_dim(d_mods, span_at * ada_cols, ada_cols, 1),
        (((0,), (0,)), ((), ())),
    )
    wanted = lax.dynamic_slice_in_dim(picker, seq_at * slots, slots, 1)
    own_mods = exact(wanted, d_mods, (((0,), (0,)), ((), ())))
    d_silu = exact(own_mods, ada_weight.astype(F32), (((1,), (1,)), ((), ())))
    grad_cond = jax.vjp(jax.nn.silu, conditions.astype(F32))[1](d_silu)[0]
    return (
        out.reshape(tokens.shape),
        grad_in.reshape(tokens.shape),
        grad_cond,
        gain1_sum,
        grad_ada,
        grad_ada_bias,
        grad_qkv,
        grad_out,
        sums2[:D],
        grad_up,
        sums2[2 * D :],
        grad_down,
        sums2[D : 2 * D],
    )


def solution(mesh):
    data, table, one = P("seq", "span", None), P("seq", None), P("seq")
    tile = P("seq", "span")
    in_specs = (data, table, one, one) + (P(),) * 10 + (data,)
    out_specs = (data, data, table, P(), tile, P(), tile, tile, P(), tile, P(), tile, P())
    return jax.shard_map(shards, mesh=mesh, in_specs=in_specs, out_specs=out_specs, check_vma=False)
```

```python
from functools import partial

import jax
import jax.numpy as jnp
import numpy as np
from jax import lax
from jax.experimental import pallas as pl
from jax.experimental.pallas import tpu as pltpu
from jax.sharding import PartitionSpec as P

HEADS = 12
HEAD = 64
D = 768
FF = 3072
PAIR = 128
PAIRS = HEADS // 2
LEN = 1024
SHORT = 128
SLOTS = 2
CHUNK = 768
STRIP = 1536
EPSILON = 1e-5
LOG2E = 1.4426950408889634
GELU_C = 0.7978845608028654
BIG = 62 << 20
MESH = pl.DeviceIdType.MESH
F32 = jnp.float32
BF16 = jnp.bfloat16
HIGHEST = lax.Precision.HIGHEST


def nn(a, b):
    return lax.dot_general(a, b, (((1,), (0,)), ((), ())), preferred_element_type=F32)


def nt(a, b):
    return lax.dot_general(a, b, (((1,), (1,)), ((), ())), preferred_element_type=F32)


def tn(a, b):
    return lax.dot_general(a, b, (((0,), (0,)), ((), ())), preferred_element_type=F32)


def whole(shape, buffers=1):
    return pl.BlockSpec(shape, lambda *_: (0,) * len(shape), pipeline_mode=pl.Buffered(buffers))


def cost(flops, bytes_accessed, transcendentals=0):
    return pl.CostEstimate(
        flops=int(flops), bytes_accessed=int(bytes_accessed), transcendentals=int(transcendentals)
    )


def col_sum(x):
    return jnp.sum(x, axis=0, keepdims=True)


def wide_row(ref):
    return ref[...].astype(F32).reshape(1, ref.shape[0])


def row_mean(x):
    return jnp.mean(x, axis=-1, keepdims=True)


def rotary(length):
    half = HEAD // 2
    freq = np.power(np.float32(10000.0), -np.arange(half, dtype=np.float32) / np.float32(half))
    angles = np.arange(length, dtype=np.float32)[:, None] * freq.astype(np.float32)[None, :]
    cos, sin = np.cos(angles), np.sin(angles)
    return (
        np.concatenate([cos] * 4, axis=1).astype(np.float32),
        np.concatenate([-sin, sin, -sin, sin], axis=1).astype(np.float32),
    )


def swap_halves(x):
    lane = lax.broadcasted_iota(jnp.int32, x.shape, 1)
    first = (lane & 32) == 0
    return jnp.where(first, pltpu.roll(x, x.shape[1] - 32, 1), pltpu.roll(x, 32, 1))


def turn(x, cos, sin):
    return x * cos + swap_halves(x) * sin


def turn_back(x, cos, sin):
    return x * cos - swap_halves(x) * sin


def slot_of(lengths, j):
    long = jnp.where(lengths[1] > lengths[0], 1, 0)
    return j + long - 2 * j * long


def heads_of(x):
    lane = lax.broadcasted_iota(jnp.int32, x.shape, 1)
    zero = jnp.zeros_like(x)
    return jnp.where(lane < HEAD, x, zero), jnp.where(lane < HEAD, zero, x)


def modulation_kernel(
    n, cond_ref, assign_ref, weight_ref, bias_ref, mod_ref, table_ref, silu_ref,
    own_ref, send, recv, local, extra=(), ready=None,
):
    me = lax.axis_index("seq")
    asked = [jnp.full((1, 128), assign_ref[k].astype(F32)) for k in range(SLOTS)]
    own_ref[...] = jnp.concatenate(
        [cond_ref[...].astype(F32)] + asked + [jnp.zeros((8 - 2 * SLOTS, 128), F32)], axis=0
    )
    barrier = pltpu.get_barrier_semaphore()
    for step in range(1, n):
        pl.semaphore_signal(
            barrier, inc=1, device_id={"seq": lax.rem(me + step, n)}, device_id_type=MESH
        )
    for peer in extra:
        pl.semaphore_signal(barrier, inc=1, device_id=peer, device_id_type=MESH)
    mine = pltpu.make_async_copy(own_ref, table_ref.at[me], local)
    mine.start()
    pl.semaphore_wait(barrier, n - 1 + len(extra))
    copies = []
    for step in range(1, n):
        copy = pltpu.make_async_remote_copy(
            src_ref=own_ref,
            dst_ref=table_ref.at[me],
            send_sem=send.at[step],
            recv_sem=recv.at[step],
            device_id={"seq": lax.rem(me + step, n)},
            device_id_type=MESH,
        )
        copy.start()
        copies.append(copy)
    mine.wait()
    for copy in copies:
        copy.wait()
    if ready is not None:
        ready()
    source = lax.broadcasted_iota(jnp.int32, (n, 128), 0).astype(F32) * SLOTS
    rows = []
    for slot in range(SLOTS):
        wanted = own_ref[SLOTS + slot : SLOTS + slot + 1, :]
        row = jnp.zeros((1, 128), F32)
        for k in range(SLOTS):
            row += col_sum(jnp.where(wanted == source + k, table_ref[:, k, :], 0.0))
        rows.append(row)
    cond = jnp.concatenate(rows + [jnp.zeros((8 - SLOTS, 128), F32)], axis=0)
    silu = (cond / (1.0 + jnp.exp(-cond))).astype(BF16)
    mod_ref[...] = nn(silu, weight_ref[...]) + bias_ref[...].astype(F32).reshape(1, 6 * D)
    for slot in range(SLOTS):
        wanted = table_ref[:, SLOTS + slot, :][:, :n]
        lane = lax.broadcasted_iota(jnp.int32, (n, n), 1).astype(F32) * SLOTS
        rows = jnp.zeros((n, 128), F32)
        for k in range(SLOTS):
            chosen = jnp.where(wanted == lane + k, 1.0, 0.0).astype(BF16)
            rows += nn(chosen, table_ref[:, k, :].astype(BF16))
        silu_ref[slot] = (rows / (1.0 + jnp.exp(-rows))).astype(BF16).astype(F32)


def modulation_call(cond, assignment, ada_weight, ada_bias, n):
    vmem = pl.BlockSpec(memory_space=pltpu.VMEM)
    return pl.pallas_call(
        partial(modulation_kernel, n),
        name="modulation",
        out_shape=(
            jax.ShapeDtypeStruct((8, 6 * D), F32),
            jax.ShapeDtypeStruct((n, 8, 128), F32),
            jax.ShapeDtypeStruct((SLOTS, n, 128), F32),
        ),
        in_specs=[vmem, pl.BlockSpec(memory_space=pltpu.SMEM), vmem, vmem],
        out_specs=(vmem, vmem, vmem),
        scratch_shapes=[
            pltpu.VMEM((8, 128), F32),
            pltpu.SemaphoreType.DMA((n,)),
            pltpu.SemaphoreType.DMA((n,)),
            pltpu.SemaphoreType.DMA,
        ],
        compiler_params=pltpu.CompilerParams(
            collective_id=0, has_side_effects=True, vmem_limit_bytes=BIG
        ),
        cost_estimate=cost(1e7, 2e6),
    )(cond, assignment, ada_weight, ada_bias)


def project_kernel(
    order, tok_ref, mod_ref, gain_ref, weight_ref, cos_ref, sin_ref,
    q_ref, h_ref, kvl_ref, kvs_ref,
):
    j = pl.program_id(0)
    row = mod_ref[pl.ds(slot_of(order, j), 1), :]
    shift, scale = row[:, :D], row[:, D : 2 * D]
    x = tok_ref[...].astype(F32)
    center = x - row_mean(x)
    xhat = center * lax.rsqrt(row_mean(center * center) + EPSILON)
    hidden = (xhat * wide_row(gain_ref) * (1.0 + scale) + shift).astype(BF16)
    h_ref[...] = hidden
    cos = jnp.concatenate([cos_ref[...]] * PAIRS, axis=1)
    sin = jnp.concatenate([sin_ref[...]] * PAIRS, axis=1)
    q_ref[...] = turn(nn(hidden, weight_ref[:, :D]), cos, sin).astype(BF16)
    k = turn(nn(hidden, weight_ref[:, D : 2 * D]), cos, sin).astype(BF16)
    v = nn(hidden, weight_ref[:, 2 * D :]).astype(BF16)

    @pl.when(j == 0)
    def _():
        kvl_ref[:, :D] = k
        kvl_ref[:, D:] = v

    @pl.when(j == 1)
    def _():
        kvs_ref[:, :D] = k
        kvs_ref[:, D:] = v


def project_call(place, tokens, mod, gain, weight, cos, sin, rows):
    tile = min(256, rows)
    tiles = rows // tile
    return pl.pallas_call(
        project_kernel,
        name="project",
        out_shape=(
            jax.ShapeDtypeStruct((SLOTS * rows, D), BF16),
            jax.ShapeDtypeStruct((SLOTS * rows, D), BF16),
            jax.ShapeDtypeStruct((rows, 2 * D), BF16),
            jax.ShapeDtypeStruct((rows, 2 * D), BF16),
        ),
        grid_spec=pltpu.PrefetchScalarGridSpec(
            num_scalar_prefetch=1,
            grid=(SLOTS, tiles),
            in_specs=[
                pl.BlockSpec((tile, D), lambda j, t, o: (slot_of(o, j) * tiles + t, 0)),
                whole((8, 6 * D)),
                whole((D,)),
                whole((D, 3 * D)),
                pl.BlockSpec((tile, PAIR), lambda j, t, o: (o[2] * tiles + t, 0)),
                pl.BlockSpec((tile, PAIR), lambda j, t, o: (o[2] * tiles + t, 0)),
            ],
            out_specs=[
                pl.BlockSpec((tile, D), lambda j, t, o: (j * tiles + t, 0)),
                pl.BlockSpec((tile, D), lambda j, t, o: (j * tiles + t, 0)),
                pl.BlockSpec((tile, 2 * D), lambda j, t, o: (t + j * (tiles - 1 - t), 0)),
                pl.BlockSpec((tile, 2 * D), lambda j, t, o: (j * t, 0)),
            ],
        ),
        compiler_params=pltpu.CompilerParams(vmem_limit_bytes=BIG),
        cost_estimate=cost(2 * SLOTS * rows * D * 3 * D, 14e6),
    )(place, tokens, mod, gain, weight, cos, sin)


def attend_slot(q, keys, values):
    outs, stats = [], []
    all_scores = [[nt(k, qh) for k in keys] for qh in heads_of(q)]
    for head, scores in enumerate(all_scores):
        top = jnp.max(scores[0], axis=0, keepdims=True)
        for s in scores[1:]:
            top = jnp.maximum(top, jnp.max(s, axis=0, keepdims=True))
        total, out = None, None
        for s, v in zip(scores, values):
            p = jnp.exp2((s - top) * (0.125 * LOG2E))
            part = col_sum(p)
            o = tn(v, p.astype(BF16))
            total = part if total is None else total + part
            out = o if out is None else out + o
        out = out[head * HEAD : (head + 1) * HEAD] / total
        outs.append(out)
        stats.append(top * (0.125 * LOG2E) + jnp.log2(total))
    return jnp.concatenate(outs, axis=0).T.astype(BF16), stats


def attend_kernel(ql, qs, ko, vo, kx, vx, ks, vs, out_ref, lse_ref):
    rows = ql.shape[0]
    out, stats = attend_slot(ql[...], [ko[...], kx[...]], [vo[...], vx[...]])
    out_ref[:rows, :] = out
    lse_ref[0, 0:1, :] = stats[0]
    lse_ref[0, 1:2, :] = stats[1]
    out, stats = attend_slot(qs[...], [ks[...]], [vs[...]])
    out_ref[rows:, :] = out
    lse_ref[0, 2:3, :] = stats[0]
    lse_ref[0, 3:4, :] = stats[1]


def pair_specs(rows):
    def at(n, block, base):
        return pl.BlockSpec((n, PAIR), lambda h: (block, base + h))

    return [
        at(rows, 0, 0),
        at(rows, 1, 0),
        at(rows, 0, 0),
        at(rows, 0, PAIRS),
        at(LEN - rows, 0, 0),
        at(LEN - rows, 0, PAIRS),
        at(SHORT, 0, 0),
        at(SHORT, 0, PAIRS),
    ]


def attend_call(q, kv_own, kv_other, kv_short, rows):
    return pl.pallas_call(
        attend_kernel,
        name="attend",
        grid=(PAIRS,),
        out_shape=(
            jax.ShapeDtypeStruct((SLOTS * rows, D), BF16),
            jax.ShapeDtypeStruct((PAIRS, 4, rows), F32),
        ),
        in_specs=pair_specs(rows),
        out_specs=(
            pl.BlockSpec((SLOTS * rows, PAIR), lambda h: (0, h)),
            pl.BlockSpec((1, 4, rows), lambda h: (h, 0, 0)),
        ),
        compiler_params=pltpu.CompilerParams(vmem_limit_bytes=BIG),
        cost_estimate=cost(16 * D * rows * (LEN + SHORT), 9e6, HEADS * rows * (LEN + SHORT)),
    )(q, q, kv_own, kv_own, kv_other, kv_other, kv_short, kv_short)


def attend_back_slot(q, keys, values, d_out, out, lse, between=None):
    count = len(keys)
    d_keys, d_values = [None] * count, [None] * count
    d_query = []
    q_heads, d_heads = heads_of(q), heads_of(d_out)
    inner = (d_out.astype(F32) * out.astype(F32)).T
    all_scores = [[nt(k, qh) for k in keys] for qh in q_heads]
    all_d_probs = [[nt(v, dh) for v in values] for dh in d_heads]
    for head in range(2):
        if head == 1 and between is not None:
            between()
        qh, dh = q_heads[head], d_heads[head]
        delta = col_sum(inner[head * HEAD : (head + 1) * HEAD])
        scores, d_probs = all_scores[head], all_d_probs[head]
        dq = None
        for i in range(count):
            probs = jnp.exp2(scores[i] * (0.125 * LOG2E) - lse[head])
            d_scores = (probs * (d_probs[i] - delta)).astype(BF16)
            dv = nn(probs.astype(BF16), dh)
            dk = nn(d_scores, qh)
            part = tn(keys[i], d_scores)
            dq = part if dq is None else dq + part
            d_values[i] = dv if head == 0 else d_values[i] + dv
            d_keys[i] = dk if head == 0 else d_keys[i] + dk
        d_query.append(dq[head * HEAD : (head + 1) * HEAD])
    d_keys = [dk * 0.125 for dk in d_keys]
    return (jnp.concatenate(d_query, axis=0) * 0.125).T, d_keys, d_values


def attend_back_kernel(
    place, ql, qs, ko, vo, kx, vx, ks, vs, dol, dos, al, as_, lse, cos, sin,
    dq_ref, dko, dvo, dkx, dvx, dks, dvs,
):
    rows = ql.shape[0]
    stats = lse[0]
    dq, dk, dv = attend_back_slot(
        ql[...], [ko[...], kx[...]], [vo[...], vx[...]], dol[...], al[...],
        [stats[0:1], stats[1:2]],
    )
    dq_ref[:rows, :] = turn_back(dq, cos[...], sin[...]).astype(BF16)
    dko[...] = dk[0]
    dvo[...] = dv[0]
    dkx[...] = dk[1].astype(BF16)
    dvx[...] = dv[1].astype(BF16)
    dq, dk, dv = attend_back_slot(
        qs[...], [ks[...]], [vs[...]], dos[...], as_[...], [stats[2:3], stats[3:4]]
    )
    dq_ref[rows:, :] = turn_back(dq, cos[...], sin[...]).astype(BF16)
    dks[...] = dk[0]
    dvs[...] = dv[0]


def attend_back_call(place, q, kv_own, kv_other, kv_short, d_att, att, lse, cos, sin, rows):
    specs = [
        pl.BlockSpec(s.block_shape, partial(lambda m, h, o: m(h), s.index_map))
        for s in pair_specs(rows)
    ]
    other = LEN - rows
    return pl.pallas_call(
        attend_back_kernel,
        name="attend_back",
        out_shape=(
            jax.ShapeDtypeStruct((SLOTS * rows, D), BF16),
            jax.ShapeDtypeStruct((rows, D), F32),
            jax.ShapeDtypeStruct((rows, D), F32),
            jax.ShapeDtypeStruct((other, D), BF16),
            jax.ShapeDtypeStruct((other, D), BF16),
            jax.ShapeDtypeStruct((SHORT, D), F32),
            jax.ShapeDtypeStruct((SHORT, D), F32),
        ),
        grid_spec=pltpu.PrefetchScalarGridSpec(
            num_scalar_prefetch=1,
            grid=(PAIRS,),
            in_specs=specs
            + [
                pl.BlockSpec((rows, PAIR), lambda h, o: (0, h)),
                pl.BlockSpec((rows, PAIR), lambda h, o: (1, h)),
                pl.BlockSpec((rows, PAIR), lambda h, o: (0, h)),
                pl.BlockSpec((rows, PAIR), lambda h, o: (1, h)),
                pl.BlockSpec((1, 4, rows), lambda h, o: (h, 0, 0)),
                pl.BlockSpec((rows, PAIR), lambda h, o: (o[2], 0)),
                pl.BlockSpec((rows, PAIR), lambda h, o: (o[2], 0)),
            ],
            out_specs=[
                pl.BlockSpec((SLOTS * rows, PAIR), lambda h, o: (0, h)),
                pl.BlockSpec((rows, PAIR), lambda h, o: (0, h)),
                pl.BlockSpec((rows, PAIR), lambda h, o: (0, h)),
                pl.BlockSpec((other, PAIR), lambda h, o: (0, h)),
                pl.BlockSpec((other, PAIR), lambda h, o: (0, h)),
                pl.BlockSpec((SHORT, PAIR), lambda h, o: (0, h)),
                pl.BlockSpec((SHORT, PAIR), lambda h, o: (0, h)),
            ],
        ),
        compiler_params=pltpu.CompilerParams(vmem_limit_bytes=BIG),
        cost_estimate=cost(40 * D * rows * (LEN + SHORT), 16e6, HEADS * rows * (LEN + SHORT)),
    )(
        place, q, q, kv_own, kv_own, kv_other, kv_other, kv_short, kv_short,
        d_att, d_att, att, att, lse, cos, sin,
    )


def part_of(index, size):
    if isinstance(index, int):
        return pl.ds(index * size, size)
    return pl.ds(pl.multiple_of(index * size, size), size)


def add_to(ref, value, first):
    @pl.when(first)
    def _():
        ref[...] = value

    @pl.when(jnp.logical_not(first))
    def _():
        ref[...] += value


def feed_kernel(
    halves, order, tok_ref, att_ref, cot_ref, hid1_ref, mod_ref, gain_ref, wo_ref, wu_ref, bu_ref, wd_ref, bd_ref,
    out_ref, dmid_ref, datt_ref, act_ref, dlow_ref, h_ref, dup_ref, dattn_ref,
    payload_ref, toks_ref, hid1s_ref,
):
    j, t = pl.program_id(0), pl.program_id(1)
    toks_ref[...] = tok_ref[...]
    hid1s_ref[...] = hid1_ref[...]
    row = mod_ref[pl.ds(slot_of(order, j), 1), :]
    gate1, shift2 = row[:, 2 * D : 3 * D], row[:, 3 * D : 4 * D]
    scale2, gate2 = row[:, 4 * D : 5 * D], row[:, 5 * D :]
    gain, up_bias = wide_row(gain_ref), wide_row(bu_ref)
    attention = nn(att_ref[...], wo_ref[...])
    middle = tok_ref[...].astype(F32) + gate1 * attention
    center = middle - row_mean(middle)
    r = lax.rsqrt(row_mean(center * center) + EPSILON)
    xhat = center * r
    hidden = (xhat * gain * (1.0 + scale2) + shift2).astype(BF16)
    h_ref[...] = hidden
    dy = cot_ref[...].astype(F32)
    d_low = (gate2 * dy).astype(BF16)
    me = lax.axis_index("span")
    at = [h * me + (1 - h) * (1 - me) if halves else h for h in range(2)]
    for h in range(2):
        dlow_ref[:, part_of(at[h], D // 2)] = d_low[:, h * (D // 2) : (h + 1) * (D // 2)]
    lowered, d_hidden = None, None
    sums = []
    for f in range(0, FF, CHUNK):
        cols = slice(f, f + CHUNK)
        up = nn(hidden, wu_ref[:, cols]) + up_bias[:, cols]
        d_act = nt(d_low, wd_ref[cols, :])
        square = up * up
        bend = jnp.tanh(up * (GELU_C + (GELU_C * 0.044715) * square))
        half = 0.5 * (1.0 + bend)
        act = (up * half).astype(BF16)
        slope = half + (0.5 * up) * (1.0 - bend * bend) * (
            GELU_C + (3 * GELU_C * 0.044715) * square
        )
        d_up = (d_act * slope).astype(BF16)
        act_ref[:, cols] = act
        place = at[f // (FF // 2)] * (FF // 2) + f % (FF // 2)
        dup_ref[:, pl.ds(pl.multiple_of(place, CHUNK) if halves else place, CHUNK)] = d_up
        sums.append(col_sum(d_up.astype(F32)))
        low = nn(act, wd_ref[cols, :])
        dh = nt(d_up, wu_ref[:, cols])
        lowered = low if lowered is None else lowered + low
        d_hidden = dh if d_hidden is None else d_hidden + dh
    lowered = lowered + wide_row(bd_ref)
    out_ref[...] = (middle + gate2 * lowered).astype(BF16)
    d_gate2 = col_sum(dy * lowered)
    d_shift2 = col_sum(d_hidden)
    hx = col_sum(d_hidden * xhat)
    e = d_hidden * (1.0 + scale2)
    fx = e * gain
    d_mid = dy + r * (fx - row_mean(fx) - xhat * row_mean(fx * xhat))
    dmid_ref[...] = d_mid
    d_gate1 = col_sum(d_mid * attention)
    d_attention = (gate1 * d_mid).astype(BF16)
    for h in range(2):
        dattn_ref[:, part_of(at[h], D // 2)] = d_attention[:, h * (D // 2) : (h + 1) * (D // 2)]
    datt_ref[...] = nt(d_attention, wo_ref[...]).astype(BF16)
    first = jnp.logical_and(j == 0, t == 0)
    slot = slot_of(order, j)
    four = jnp.concatenate([d_gate1, d_shift2, hx * gain, d_gate2], axis=0)
    none = jnp.zeros((4, D), F32)
    add_to(
        payload_ref,
        jnp.concatenate(
            [
                jnp.where(slot == 0, four, none), jnp.where(slot == 0, none, four),
                hx * (1.0 + scale2), col_sum(d_low.astype(F32)), *sums, jnp.zeros((2, D), F32),
            ],
            axis=0,
        ),
        first,
    )


def feed_call(halves, place, tokens, att, cot, hidden1, mod, gain, wo, wu, bu, wd, bd, rows):
    tile = min(256, rows)
    tiles = rows // tile

    def own(j, t, o):
        return (slot_of(o, j) * tiles + t, 0)

    def sorted_(j, t, o):
        return (j * tiles + t, 0)

    n = SLOTS * rows
    return pl.pallas_call(
        partial(feed_kernel, halves),
        name="feed",
        out_shape=(
            jax.ShapeDtypeStruct((n, D), BF16),
            jax.ShapeDtypeStruct((n, D), F32),
            jax.ShapeDtypeStruct((n, D), BF16),
            jax.ShapeDtypeStruct((n, FF), BF16),
            jax.ShapeDtypeStruct((n, D), BF16),
            jax.ShapeDtypeStruct((n, D), BF16),
            jax.ShapeDtypeStruct((n, FF), BF16),
            jax.ShapeDtypeStruct((n, D), BF16),
            jax.ShapeDtypeStruct((16, D), F32),
            jax.ShapeDtypeStruct((n, D), BF16),
            jax.ShapeDtypeStruct((n, D), BF16),
        ),
        grid_spec=pltpu.PrefetchScalarGridSpec(
            num_scalar_prefetch=1,
            grid=(SLOTS, tiles),
            in_specs=[
                pl.BlockSpec((tile, D), own),
                pl.BlockSpec((tile, D), sorted_),
                pl.BlockSpec((tile, D), own),
                pl.BlockSpec((tile, D), own if halves else sorted_),
                whole((8, 6 * D)),
                whole((D,)),
                whole((D, D)),
                whole((D, FF)),
                whole((FF,)),
                whole((FF, D)),
                whole((D,)),
            ],
            out_specs=[
                pl.BlockSpec((tile, D), own),
                pl.BlockSpec((tile, D), sorted_),
                pl.BlockSpec((tile, D), sorted_),
                pl.BlockSpec((tile, FF), sorted_),
                pl.BlockSpec((tile, D), sorted_),
                pl.BlockSpec((tile, D), sorted_),
                pl.BlockSpec((tile, FF), sorted_),
                pl.BlockSpec((tile, D), sorted_),
                pl.BlockSpec((16, D), lambda j, t, o: (0, 0)),
                pl.BlockSpec((tile, D), sorted_),
                pl.BlockSpec((tile, D), sorted_),
            ],
        ),
        compiler_params=pltpu.CompilerParams(vmem_limit_bytes=BIG),
        cost_estimate=cost(2 * n * D * (4 * FF + 2 * D), 40e6, n * FF),
    )(place, tokens, att, cot, hidden1, mod, gain, wo, wu, bu, wd, bd)


def weight_gradient(left, right):
    seq, span = lax.axis_size("seq"), lax.axis_size("span")
    grad = tn(left, right)
    rows, cols = grad.shape
    shaped = grad.reshape(seq, rows // seq, span, cols // span).transpose(0, 2, 1, 3)
    return lax.psum_scatter(
        shaped.reshape(seq * span, rows // seq, cols // span),
        ("seq", "span"),
        scatter_dimension=0,
        tiled=True,
    )[0]


def join_kernel(place, dq_ref, dk_ref, dv_ref, ek_ref, ev_ref, sk_ref, sv_ref, cos, sin, out_ref):
    j, t = pl.program_id(0), pl.program_id(1)
    out_ref[:, :D] = dq_ref[...]
    wide_cos = jnp.concatenate([cos[...]] * PAIRS, axis=1)
    wide_sin = jnp.concatenate([sin[...]] * PAIRS, axis=1)

    @pl.when(j == 0)
    def _():
        dk = dk_ref[...] + ek_ref[...].astype(F32)
        out_ref[:, D : 2 * D] = turn_back(dk, wide_cos, wide_sin).astype(BF16)
        out_ref[:, 2 * D :] = (dv_ref[...] + ev_ref[...].astype(F32)).astype(BF16)

    @pl.when(j == 1)
    def _():
        out_ref[:, D:] = jnp.zeros((out_ref.shape[0], 2 * D), BF16)

    @pl.when(jnp.logical_and(j == 1, jnp.logical_and(t == 0, place[2] == 0)))
    def _():
        dk = turn_back(sk_ref[...], wide_cos[:SHORT], wide_sin[:SHORT])
        out_ref[:SHORT, D : 2 * D] = dk.astype(BF16)
        out_ref[:SHORT, 2 * D :] = sv_ref[...].astype(BF16)


def join_call(place, dq, dk, dv, ek, ev, sk, sv, cos, sin, rows):
    tile = min(256, rows)
    tiles = rows // tile

    def long(j, t, o):
        return (t + j * (tiles - 1 - t), 0)

    return pl.pallas_call(
        join_kernel,
        name="join",
        out_shape=jax.ShapeDtypeStruct((SLOTS * rows, 3 * D), BF16),
        grid_spec=pltpu.PrefetchScalarGridSpec(
            num_scalar_prefetch=1,
            grid=(SLOTS, tiles),
            in_specs=[pl.BlockSpec((tile, D), lambda j, t, o: (j * tiles + t, 0))]
            + [pl.BlockSpec((tile, D), long)] * 4
            + [whole((SHORT, D))] * 2
            + [pl.BlockSpec((tile, PAIR), lambda j, t, o: (o[2] * tiles + t, 0))] * 2,
            out_specs=pl.BlockSpec((tile, 3 * D), lambda j, t, o: (j * tiles + t, 0)),
        ),
        compiler_params=pltpu.CompilerParams(vmem_limit_bytes=BIG),
        cost_estimate=cost(1e7, 12e6),
    )(place, dq, dk, dv, ek, ev, sk, sv, cos, sin)


def last_kernel(
    order, tok_ref, dqkv_ref, dmid_ref, mod_ref, gain_ref, weight_ref,
    out_ref, dmod_ref, dgain_ref,
):
    j, t = pl.program_id(0), pl.program_id(1)
    scale = mod_ref[pl.ds(slot_of(order, j), 1), :][:, D : 2 * D]
    gain = wide_row(gain_ref)
    d_hidden = nt(dqkv_ref[...], weight_ref[...])
    x = tok_ref[...].astype(F32)
    center = x - row_mean(x)
    r = lax.rsqrt(row_mean(center * center) + EPSILON)
    xhat = center * r
    hx = col_sum(d_hidden * xhat)
    fx = d_hidden * (1.0 + scale) * gain
    out_ref[...] = dmid_ref[...] + r * (fx - row_mean(fx) - xhat * row_mean(fx * xhat))
    first = jnp.logical_and(j == 0, t == 0)
    add_to(
        dmod_ref,
        jnp.concatenate([col_sum(d_hidden), hx * gain, jnp.zeros((6, D), F32)], axis=0)[None],
        t == 0,
    )
    add_to(dgain_ref, hx * (1.0 + scale), first)


def last_call(place, tokens, dqkv, dmid, mod, gain, weight, rows):
    tile = min(256, rows)
    tiles = rows // tile

    def own(j, t, o):
        return (slot_of(o, j) * tiles + t, 0)

    def sorted_(j, t, o):
        return (j * tiles + t, 0)

    n = SLOTS * rows
    return pl.pallas_call(
        last_kernel,
        name="last",
        out_shape=(
            jax.ShapeDtypeStruct((n, D), F32),
            jax.ShapeDtypeStruct((SLOTS, 8, D), F32),
            jax.ShapeDtypeStruct((1, D), F32),
        ),
        grid_spec=pltpu.PrefetchScalarGridSpec(
            num_scalar_prefetch=1,
            grid=(SLOTS, tiles),
            in_specs=[
                pl.BlockSpec((tile, D), own),
                pl.BlockSpec((tile, 3 * D), sorted_),
                pl.BlockSpec((tile, D), sorted_),
                whole((8, 6 * D)),
                whole((D,)),
                whole((D, 3 * D)),
            ],
            out_specs=[
                pl.BlockSpec((tile, D), own),
                pl.BlockSpec((1, 8, D), lambda j, t, o: (slot_of(o, j), 0, 0)),
                pl.BlockSpec((1, D), lambda j, t, o: (0, 0)),
            ],
        ),
        compiler_params=pltpu.CompilerParams(vmem_limit_bytes=BIG),
        cost_estimate=cost(2 * n * D * 3 * D, 18e6),
    )(place, tokens, dqkv, dmid, mod, gain, weight)


def share_kernel(
    cond_ref, assign_ref, ada_any, bias_ref, tok_ref, gain_ref, weight_any, cos_ref, sin_ref,
    q_ref, h_ref, kv_ref, mod_ref, table_out, silu_ref, kvx_any,
    stage, table_ref, ada_ref, weight_ref, send, recv, own_ref, send_cond, recv_cond, local, loaded,
):
    step = pl.program_id(0)
    steps = stage.shape[0]
    tile = tok_ref.shape[0]
    me = lax.axis_index("span")

    def copy(i):
        return pltpu.make_async_remote_copy(
            src_ref=stage.at[i],
            dst_ref=kvx_any.at[pl.ds(pl.multiple_of(i * tile, tile), tile)],
            send_sem=send.at[i],
            recv_sem=recv.at[i],
            device_id={"span": 1 - me},
            device_id_type=MESH,
        )

    @pl.when(step == 0)
    def _():
        loads = [
            pltpu.make_async_copy(ada_any, ada_ref, loaded.at[0]),
            pltpu.make_async_copy(weight_any, weight_ref, loaded.at[1]),
        ]
        for load in loads:
            load.start()
        modulation_kernel(
            table_ref.shape[0], cond_ref, assign_ref, ada_ref, bias_ref, mod_ref, table_ref,
            silu_ref, own_ref, send_cond, recv_cond, local, ({"span": 1 - me},), loads[0].wait,
        )
        loads[1].wait()
        table_out[...] = table_ref[...]

    row = mod_ref[pl.ds(step // (steps // SLOTS), 1), :]
    shift, scale = row[:, :D], row[:, D : 2 * D]
    x = tok_ref[...].astype(F32)
    center = x - row_mean(x)
    xhat = center * lax.rsqrt(row_mean(center * center) + EPSILON)
    hidden = (xhat * wide_row(gain_ref) * (1.0 + scale) + shift).astype(BF16)
    h_ref[...] = hidden
    start = (me * (steps // SLOTS) + lax.rem(step, steps // SLOTS)) * tile
    start = pl.multiple_of(start, tile)
    cos, sin = cos_ref[pl.ds(start, tile), :], sin_ref[pl.ds(start, tile), :]
    k = nn(hidden, weight_ref[:, D : 2 * D])
    k = [turn(k[:, p : p + PAIR], cos, sin).astype(BF16) for p in range(0, D, PAIR)]
    k = jnp.concatenate(k, axis=1)
    v = nn(hidden, weight_ref[:, 2 * D :]).astype(BF16)
    kv_ref[:, :D] = k
    kv_ref[:, D:] = v
    stage[step, :, :D] = k
    stage[step, :, D:] = v

    q = nn(hidden, weight_ref[:, :D])
    for p in range(0, D, PAIR):
        q_ref[:, p : p + PAIR] = turn(q[:, p : p + PAIR], cos, sin).astype(BF16)

    copy(step).start()

    @pl.when(step == steps - 1)
    def _():
        for i in range(steps):
            copy(i).wait()


def share_call(cond, assignment, ada_weight, ada_bias, tokens, gain, weight, cos, sin, rows):
    tile = 256
    n = SLOTS * rows
    steps = n // tile

    def at(width):
        return pl.BlockSpec((tile, width), lambda s: (s, 0))

    return pl.pallas_call(
        share_kernel,
        name="project",
        grid=(steps,),
        out_shape=(
            jax.ShapeDtypeStruct((n, D), BF16),
            jax.ShapeDtypeStruct((n, D), BF16),
            jax.ShapeDtypeStruct((n, 2 * D), BF16),
            jax.ShapeDtypeStruct((8, 6 * D), F32),
            jax.ShapeDtypeStruct((16, 8, 128), F32),
            jax.ShapeDtypeStruct((SLOTS, 16, 128), F32),
            jax.ShapeDtypeStruct((n, 2 * D), BF16),
        ),
        in_specs=[
            whole((SLOTS, 128)),
            pl.BlockSpec(memory_space=pltpu.SMEM),
            pl.BlockSpec(memory_space=pl.ANY),
            whole((6 * D,)),
            at(D),
            whole((D,)),
            pl.BlockSpec(memory_space=pl.ANY),
            whole((LEN, PAIR)),
            whole((LEN, PAIR)),
        ],
        out_specs=(
            at(D), at(D), at(2 * D), whole((8, 6 * D)), whole((16, 8, 128)),
            whole((SLOTS, 16, 128)), pl.BlockSpec(memory_space=pl.ANY),
        ),
        scratch_shapes=[
            pltpu.VMEM((steps, tile, 2 * D), BF16),
            pltpu.VMEM((16, 8, 128), F32),
            pltpu.VMEM((128, 6 * D), BF16),
            pltpu.VMEM((D, 3 * D), BF16),
            pltpu.SemaphoreType.DMA((steps,)),
            pltpu.SemaphoreType.DMA((steps,)),
            pltpu.VMEM((8, 128), F32),
            pltpu.SemaphoreType.DMA((16,)),
            pltpu.SemaphoreType.DMA((16,)),
            pltpu.SemaphoreType.DMA,
            pltpu.SemaphoreType.DMA((2,)),
        ],
        compiler_params=pltpu.CompilerParams(
            collective_id=4, has_side_effects=True, vmem_limit_bytes=BIG
        ),
        cost_estimate=cost(2 * n * D * 3 * D, 14e6),
    )(cond, assignment, ada_weight, ada_bias, tokens, gain, weight, cos, sin)


def attend_sorted_kernel(
    lengths, ql, qs, ko, vo, kx, vx, ks_own, vs_own, ks_other, vs_other,
    tl, ts, cl, cs, hl, hs,
    out_ref, lse_ref, q_ref, ko_ref, vo_ref, kx_ref, vx_ref, ks_ref, vs_ref,
    t_ref, c_ref, h_ref,
):
    rows = ql.shape[0]
    first = lax.axis_index("span") == 0
    ks = jnp.where(first, ks_own[...], ks_other[...])
    vs = jnp.where(first, vs_own[...], vs_other[...])
    for ref, long, short in ((q_ref, ql, qs), (t_ref, tl, ts), (c_ref, cl, cs), (h_ref, hl, hs)):
        ref[:rows, :] = long[...]
        ref[rows:, :] = short[...]
    ks_ref[...] = ks
    vs_ref[...] = vs
    for ref, given in ((ko_ref, ko), (vo_ref, vo), (kx_ref, kx), (vx_ref, vx)):
        ref[...] = given[...]
    out, stats = attend_slot(qs[...], [ks], [vs])
    out_ref[rows:, :] = out
    lse_ref[0, 2:3, :] = stats[0]
    lse_ref[0, 3:4, :] = stats[1]
    out, stats = attend_slot(ql[...], [ko[...], kx[...]], [vo[...], vx[...]])
    out_ref[:rows, :] = out
    lse_ref[0, 0:1, :] = stats[0]
    lse_ref[0, 1:2, :] = stats[1]


def attend_sorted_call(lengths, q, kv, kvx, tokens, cot, hidden, rows):
    n = SLOTS * rows
    per = rows // SHORT

    def long(base):
        return pl.BlockSpec((rows, PAIR), lambda h, o: (slot_of(o, 0), base + h))

    def second():
        return pl.BlockSpec((rows, PAIR), lambda h, o: (slot_of(o, 1), h))

    def short(base):
        return pl.BlockSpec((SHORT, PAIR), lambda h, o: (slot_of(o, 1) * per, base + h))

    def out(size):
        return pl.BlockSpec((size, PAIR), lambda h, o: (0, h))

    return pl.pallas_call(
        attend_sorted_kernel,
        name="attend",
        out_shape=(
            jax.ShapeDtypeStruct((n, D), BF16),
            jax.ShapeDtypeStruct((PAIRS, 4, rows), F32),
            jax.ShapeDtypeStruct((n, D), BF16),
        )
        + (jax.ShapeDtypeStruct((rows, D), BF16),) * 4
        + (jax.ShapeDtypeStruct((SHORT, D), BF16),) * 2
        + (jax.ShapeDtypeStruct((n, D), BF16),) * 3,
        grid_spec=pltpu.PrefetchScalarGridSpec(
            num_scalar_prefetch=1,
            grid=(PAIRS,),
            in_specs=[
                long(0),
                second(),
                long(0), long(PAIRS), long(0), long(PAIRS),
                short(0), short(PAIRS), short(0), short(PAIRS),
            ]
            + [long(0), second()] * 3,
            out_specs=[out(n), pl.BlockSpec((1, 4, rows), lambda h, o: (h, 0, 0)), out(n)]
            + [out(rows)] * 4
            + [out(SHORT)] * 2
            + [out(n)] * 3,
        ),
        compiler_params=pltpu.CompilerParams(vmem_limit_bytes=BIG),
        cost_estimate=cost(16 * D * rows * (LEN + SHORT), 16e6, HEADS * rows * (LEN + SHORT)),
    )(
        lengths, q, q, kv, kv, kvx, kvx, kv, kv, kvx, kvx, tokens, tokens, cot, cot, hidden, hidden
    )


def flip(index, bit):
    return index + bit - 2 * bit * ((index // bit) % 2)


def add_low(a, b):
    return (a.astype(F32) + b.astype(F32)).astype(BF16)


def plane_peers():
    s, c = lax.axis_index("seq"), lax.axis_index("span")
    return [{"span": 1 - c}, {"seq": flip(s, 1)}, {"seq": flip(s, 2)}]


def line_peers():
    s = lax.axis_index("seq")
    return [{"seq": lax.rem(s + 4 * step, 16)} for step in range(1, 4)]


def greet(peers):
    barrier = pltpu.get_barrier_semaphore()
    for peer in peers:
        pl.semaphore_signal(barrier, inc=1, device_id=peer, device_id_type=MESH)
    pl.semaphore_wait(barrier, len(peers))


class Scatter:
    def __init__(self, send, recv, base, other=None, own=None, came0=None, a1=None, b1=None,
                 came2=None, came3=None):
        self.send, self.recv, self.base = send, recv, base
        self.other, self.own, self.came0 = other, own, came0
        self.a1, self.b1, self.came2, self.came3 = a1, b1, came2, came3
        s = lax.axis_index("seq")
        self.x, self.y, self.z = lax.rem(s, 2), lax.rem(s // 2, 2), s // 4
        self.core_peer, self.x_peer, self.y_peer = plane_peers()
        self.z_peers = line_peers()

    def copy(self, i):
        x, y, z = self.x, self.y, self.z
        if i == 0:
            src, dst, peer = self.other, self.came0, self.core_peer
        elif i >= 8:
            src, dst, peer = self.other.at[i - 8], self.came0.at[i - 8], self.core_peer
        elif i == 1:
            src, dst, peer = self.own.at[0:2, :, 1 - x], self.a1, self.x_peer
        elif i == 2:
            src, dst, peer = self.own.at[2:4, 1 - y], self.b1, self.y_peer
        elif i == 3:
            src, dst, peer = self.a1.at[:, 1 - y], self.came2.at[0:2], self.y_peer
        elif i == 4:
            src, dst, peer = self.b1.at[:, 1 - x], self.came2.at[2:4], self.x_peer
        else:
            step = i - 4
            src, dst = self.came2.at[lax.rem(z + step, 4)], self.came3.at[step - 1]
            peer = self.z_peers[step - 1]
        return pltpu.make_async_remote_copy(
            src_ref=src,
            dst_ref=dst,
            send_sem=self.send.at[self.base + i],
            recv_sem=self.recv.at[self.base + i],
            device_id=peer,
            device_id_type=MESH,
        )

    def start(self, *which):
        for i in which:
            self.copy(i).start()

    def arrive(self, *which):
        for i in which:
            self.copy(i).wait_recv()

    def drain(self, *which):
        for i in which:
            self.copy(i).wait_send()

    def merge0(self):
        def body(i, _):
            z, y, x = i // 4, lax.rem(i // 2, 2), lax.rem(i, 2)
            self.own[z, y, x] = add_low(self.own[z, y, x], self.came0[z, y, x])
            return 0

        lax.fori_loop(0, 16, body, 0)

    def add1(self, a_ref, b_ref):
        self.arrive(1, 2)

        def body(i, _):
            z, k = i // 2, lax.rem(i, 2)
            a_ref[z, k] = add_low(self.own[z, k, self.x], self.a1[z, k])
            b_ref[z, k] = add_low(self.own[2 + z, self.y, k], self.b1[z, k])
            return 0

        lax.fori_loop(0, 4, body, 0)

    def add2(self, out_ref):
        self.arrive(3, 4)

        def body(z, _):
            out_ref[z] = add_low(self.a1[z, self.y], self.came2[z])
            out_ref[2 + z] = add_low(self.b1[z, self.x], self.came2[2 + z])
            return 0

        lax.fori_loop(0, 2, body, 0)

    def total(self):
        self.arrive(5, 6, 7)
        total = self.came2[self.z].astype(F32)
        for step in range(3):
            total = total + self.came3[step].astype(F32)
        return total

    def scatter0(self):
        self.start(0)

    def scatter1(self):
        self.arrive(0)
        self.merge0()
        self.start(1, 2)

    def scatter2(self):
        self.add1(self.a1, self.b1)
        self.start(3, 4)

    def scatter3(self):
        self.add2(self.came2)
        self.start(5, 6, 7)


def half_shape(rows, cols):
    return (4, 2, 2, rows, cols)


ANY = pl.BlockSpec(memory_space=pl.ANY)
DMA = pltpu.SemaphoreType.DMA


def both_kernel(
    tok_ref, att_ref, cot_ref, mod_ref, gain_ref, wo_any, wu_any, bu_ref, wd_any, bd_ref, lengths,
    out_ref, dmid_ref, datt_ref, h_ref, dup_ref, dattn_ref, payload_ref, a_ref, b_ref,
    act_all, slope_all, dlow_all, mid_all, attention_all,
    wo_ref, wu_ref, wd_ref, other, own, came0, a1, b1, send, recv, loaded,
):
    step = pl.program_id(0)
    me = lax.axis_index("span")
    down = Scatter(send, recv, 0, other=other, own=own, came0=came0, a1=a1, b1=b1)
    loads = [
        pltpu.make_async_copy(src, dst, loaded.at[k])
        for k, (src, dst) in enumerate([(wo_any, wo_ref), (wu_any, wu_ref), (wd_any, wd_ref)])
    ]
    tiles = act_all.shape[0] // tok_ref.shape[0]
    tile = tok_ref.shape[0]
    t = lax.rem(step, tiles)
    at_rows = pl.ds(pl.multiple_of(t * tile, tile), tile)
    halves = [h * me + (1 - h) * (1 - me) for h in range(2)]
    swapped = jnp.full((1, D), jnp.where(lengths[1] > lengths[0], 1.0, 0.0))
    mine = jnp.where(t // (tiles // SLOTS) == 0, swapped, 1.0 - swapped)

    def modulation(b):
        cols = slice(b * D, (b + 1) * D)
        return jnp.where(mine == 0.0, mod_ref[0:1, cols], mod_ref[1:2, cols])

    @pl.when(step == 0)
    def _():
        loads[0].start()
        loads[1].start()
        greet(plane_peers())
        loads[0].wait()
        loads[1].wait()
        loads[2].start()

    @pl.when(step == 2 * tiles)
    def _():
        loads[2].wait()
        down.arrive(8, 9, 10, 11)
        down.merge0()
        down.start(1, 2)

    @pl.when(step < tiles)
    def _():
        attention = nn(att_ref[...], wo_ref[...])
        middle = tok_ref[...].astype(F32) + modulation(2) * attention
        attention_all[at_rows, :] = attention
        mid_all[at_rows, :] = middle
        center = middle - row_mean(middle)
        xhat = center * lax.rsqrt(row_mean(center * center) + EPSILON)
        hidden = xhat * wide_row(gain_ref) * (1.0 + modulation(4)) + modulation(3)
        hidden = hidden.astype(BF16)
        h_ref[...] = hidden
        d_low = (modulation(5) * cot_ref[...].astype(F32)).astype(BF16)
        for h in range(2):
            half = d_low[:, h * (D // 2) : (h + 1) * (D // 2)]
            dlow_all[at_rows, part_of(halves[h], D // 2)] = half
        up_bias = wide_row(bu_ref)
        for f in range(0, FF, STRIP):
            cols = slice(f, f + STRIP)
            up = nn(hidden, wu_ref[:, cols]) + up_bias[:, cols]
            square = up * up
            bend = jnp.tanh(up * (GELU_C + (GELU_C * 0.044715) * square))
            half = 0.5 * (1.0 + bend)
            slope = half + (0.5 * up) * (1.0 - bend * bend) * (
                GELU_C + (3 * GELU_C * 0.044715) * square
            )
            act_all[at_rows, cols] = (up * half).astype(BF16)
            slope_all[at_rows, cols] = slope.astype(BF16)

    @pl.when(jnp.logical_and(step >= tiles, step < 2 * tiles))
    def _():
        cols = pl.ds(pl.multiple_of(t * CHUNK, CHUNK), CHUNK)
        value = tn(act_all[:, cols], dlow_all[...]).astype(BF16)
        shape = own.shape[1:]
        other[t] = value[:, : D // 2].reshape(shape)
        own[t] = value[:, D // 2 :].reshape(shape)

        for m in range(4):
            @pl.when(t == m)
            def _():
                down.start(8 + m)

    @pl.when(step >= 2 * tiles)
    def _():
        middle, attention = mid_all[at_rows, :], attention_all[at_rows, :]
        gain = wide_row(gain_ref)
        gate1, scale2, gate2 = modulation(2), modulation(4), modulation(5)
        dy = cot_ref[...].astype(F32)
        d_low = (gate2 * dy).astype(BF16)
        lowered, d_hidden = None, None
        sums = []
        for f in range(0, FF, STRIP):
            cols = slice(f, f + STRIP)
            d_act = nt(d_low, wd_ref[cols, :])
            d_up = (d_act * slope_all[at_rows, cols].astype(F32)).astype(BF16)
            place = halves[f // (FF // 2)] * (FF // 2) + f % (FF // 2)
            dup_ref[:, pl.ds(pl.multiple_of(place, STRIP), STRIP)] = d_up
            sums.append(col_sum(d_up.astype(F32)))
            low = nn(act_all[at_rows, cols], wd_ref[cols, :])
            dh = nt(d_up, wu_ref[:, cols])
            lowered = low if lowered is None else lowered + low
            d_hidden = dh if d_hidden is None else d_hidden + dh
        center = middle - row_mean(middle)
        r = lax.rsqrt(row_mean(center * center) + EPSILON)
        xhat = center * r
        lowered = lowered + wide_row(bd_ref)
        out_ref[...] = (middle + gate2 * lowered).astype(BF16)
        hx = col_sum(d_hidden * xhat)
        fx = d_hidden * (1.0 + scale2) * gain
        d_mid = dy + r * (fx - row_mean(fx) - xhat * row_mean(fx * xhat))
        dmid_ref[...] = d_mid
        d_attention = (gate1 * d_mid).astype(BF16)
        for h in range(2):
            half = d_attention[:, h * (D // 2) : (h + 1) * (D // 2)]
            dattn_ref[:, part_of(halves[h], D // 2)] = half
        datt_ref[...] = nt(d_attention, wo_ref[...]).astype(BF16)
        total = jnp.concatenate(sums, axis=1)
        sums = [total[:, f : f + D] for f in range(0, FF, D)]
        four = jnp.concatenate(
            [
                col_sum(d_mid * attention), col_sum(d_hidden), hx * gain,
                col_sum(dy * lowered),
            ],
            axis=0,
        )
        is_second = jnp.concatenate([mine] * 4, axis=0) != 0.0
        none = jnp.zeros((4, D), F32)
        add_to(
            payload_ref,
            jnp.concatenate(
                [
                    jnp.where(is_second, none, four), jnp.where(is_second, four, none),
                    hx * (1.0 + scale2), col_sum(d_low.astype(F32)), *sums,
                    jnp.zeros((2, D), F32),
                ],
                axis=0,
            ),
            step == 2 * tiles,
        )

    @pl.when(step == 3 * tiles - 1)
    def _():
        down.add1(a_ref, b_ref)
        down.drain(1, 2, 8, 9, 10, 11)


def both_call(tokens, att, cot, mod, gain, wo, wu, bu, wd, bd, lengths, rows):
    n = SLOTS * rows
    tile = 256
    tiles = n // tile
    dr, dc = FF // 16, D // 2

    def first():
        return pl.BlockSpec((tile, D), lambda s: (jnp.minimum(s, tiles - 1), 0))

    def last(width):
        return pl.BlockSpec((tile, width), lambda s: (jnp.maximum(s - 2 * tiles, 0), 0))

    def low(*shape):
        return pltpu.VMEM(shape, BF16)

    return pl.pallas_call(
        both_kernel,
        name="feed",
        grid=(3 * tiles,),
        out_shape=(
            jax.ShapeDtypeStruct((n, D), BF16),
            jax.ShapeDtypeStruct((n, D), F32),
            jax.ShapeDtypeStruct((n, D), BF16),
            jax.ShapeDtypeStruct((n, D), BF16),
            jax.ShapeDtypeStruct((n, FF), BF16),
            jax.ShapeDtypeStruct((n, D), BF16),
            jax.ShapeDtypeStruct((16, D), F32),
            jax.ShapeDtypeStruct((2, 2, dr, dc), BF16),
            jax.ShapeDtypeStruct((2, 2, dr, dc), BF16),
        ),
        in_specs=[
            first(),
            first(),
            pl.BlockSpec((tile, D), lambda s: (lax.rem(s, tiles), 0)),
            whole((8, 6 * D)),
            whole((D,)),
            ANY,
            ANY,
            whole((FF,)),
            ANY,
            whole((D,)),
            pl.BlockSpec(memory_space=pltpu.SMEM),
        ],
        out_specs=(
            last(D), last(D), last(D), first(), last(FF), last(D), whole((16, D)),
            whole((2, 2, dr, dc)),
            whole((2, 2, dr, dc)),
        ),
        scratch_shapes=[
            low(n, FF), low(n, FF), low(n, D),
            pltpu.VMEM((n, D), F32),
            pltpu.VMEM((n, D), F32),
        ]
        + [low(D, D), low(D, FF), low(FF, D)]
        + [low(*half_shape(dr, dc))] * 3
        + [low(2, 2, dr, dc)] * 2
        + [DMA((12,)), DMA((12,)), DMA((3,))],
        compiler_params=pltpu.CompilerParams(
            collective_id=2, has_side_effects=True, vmem_limit_bytes=BIG
        ),
        cost_estimate=cost(2 * n * D * (5 * FF + 2 * D), 40e6, n * FF),
    )(tokens, att, cot, mod, gain, wo, wu, bu, wd, bd, lengths)


def pack_rows(rows, count):
    parts = [rows[r : r + 1, c : c + 128] for r in range(count) for c in range(0, D, 128)]
    rest = -len(parts) % 16
    if rest:
        parts.append(jnp.zeros((rest, 128), F32))
    return jnp.concatenate(parts, axis=0).astype(BF16)


FIRST = 5
ROUNDS = PAIRS // 2
WIDE = 3 * PAIR


def middle_kernel(
    att_ref, dattn_ref, h_any, dup_ref, hid1_any, payload_ref, down_a, down_b,
    ql, qs, ko, vo, kx, vx, ks, vs, dol, dos, al, as_, lse, cos_ref, sin_ref,
    dq_ref, dk_ref, dv_ref, down_ref, out_ref, up_ref, r_ref, ra_ref, rb_ref, rown_ref, early_ref,
    h_ref, hid1_ref, down2, down3,
    out_other, out_own, out_came, out_a, out_b, out2, out3,
    up_other, up_own, up_came, up_a, up_b, up2, up3,
    round_other, round_came, round_a, round_b, round2, d_round, keep_q,
    leave, come, keep_k, keep_v, keep_sk, keep_sv, early_came, early_sum, early_all,
    send, recv, send_kv, recv_kv, send_early, recv_early, loaded,
):
    step = pl.program_id(0)
    s, me = lax.axis_index("seq"), lax.axis_index("span")
    rows = ql.shape[0]
    down = Scatter(send, recv, 0, a1=down_a, b1=down_b, came2=down2, came3=down3)
    out = Scatter(
        send, recv, 12, other=out_other, own=out_own, came0=out_came, a1=out_a, b1=out_b,
        came2=out2, came3=out3,
    )
    up = Scatter(
        send, recv, 20, other=up_other, own=up_own, came0=up_came, a1=up_a, b1=up_b, came2=up2,
        came3=up3,
    )
    part, wide = hid1_ref.shape[1] // 16, WIDE
    rounds = [
        Scatter(
            send, recv, 28 + 5 * k,
            other=round_other.at[k],
            own=(up_other.at[:, :, :, :, :wide], up_other.at[:, :, :, :, wide : 2 * wide], rown_ref)[k],
            came0=round_came.at[k],
            a1=round_a.at[k] if k < 2 else None,
            b1=round_b.at[k] if k < 2 else None,
            came2=round2,
        )
        for k in range(ROUNDS)
    ]
    cos = cos_ref[pl.ds(pl.multiple_of(me * rows, rows), rows), :]
    sin = sin_ref[pl.ds(pl.multiple_of(me * rows, rows), rows), :]

    def kv_copy(pair):
        return pltpu.make_async_remote_copy(
            src_ref=leave.at[pair],
            dst_ref=come.at[pair],
            send_sem=send_kv.at[pair],
            recv_sem=recv_kv.at[pair],
            device_id={"span": 1 - me},
            device_id_type=MESH,
        )

    loads = [
        pltpu.make_async_copy(h_any, h_ref, loaded.at[0]),
        pltpu.make_async_copy(hid1_any, hid1_ref, loaded.at[1]),
    ]

    def early_copy(k):
        half = pl.ds(pl.multiple_of(me * 48, 16), 48)
        if k == 0:
            src, dst, peer = payload_ref, early_came, {"span": 1 - me}
        elif k == 16:
            src, dst, peer = early_all.at[:, half], early_all.at[:, half], {"span": 1 - me}
        else:
            src, dst = early_sum.at[half], early_all.at[s, half]
            peer = {"seq": lax.rem(s + k, 16)}
        return pltpu.make_async_remote_copy(
            src_ref=src,
            dst_ref=dst,
            send_sem=send_early.at[k],
            recv_sem=recv_early.at[k],
            device_id=peer,
            device_id_type=MESH,
        )

    def at(number):
        return pl.when(step == number)

    @at(0)
    def _():
        for load in loads:
            load.start()
        greet([{"span": 1 - me}] + [{"seq": lax.rem(s + k, 16)} for k in range(1, 16)])
        down.start(3, 4)
        early_copy(0).start()

    @at(3)
    def _():
        early_copy(0).wait_recv()
        early_sum[...] = pack_rows(payload_ref[...] + early_came[...], 16)
        for k in range(1, 16):
            early_copy(k).start()
        half = pl.ds(pl.multiple_of(me * 48, 16), 48)
        early_all[s, half] = early_sum[half]

    @at(FIRST + 3)
    def _():
        for k in range(1, 16):
            early_copy(k).wait_recv()
        early_copy(16).start()

    @at(1)
    def _():
        for load in loads:
            load.wait()

    @at(2)
    def _():
        out.scatter1()

    @at(4)
    def _():
        out.scatter2()

    @at(FIRST)
    def _():
        up.scatter1()

    @at(FIRST + 1)
    def _():
        out.scatter3()

    @at(FIRST + 2)
    def _():
        up.drain(0)

    @at(3)
    def _():
        down.scatter3()

    @at(FIRST + 4)
    def _():
        rounds[0].scatter1()

    @at(FIRST + 4)
    def _():
        up.scatter3()

    def between():
        @at(FIRST + 5)
        def _():
            rounds[0].scatter2()
            rounds[1].scatter1()

        @at(FIRST + 2)
        def _():
            up.scatter2()

    @at(0)
    def _():
        value = tn(att_ref[...], dattn_ref[...]).astype(BF16)
        out_other[...] = value[:, : D // 2].reshape(out_own.shape)
        out_own[...] = value[:, D // 2 :].reshape(out_own.shape)
        out.scatter0()

    @pl.when(jnp.logical_and(step >= 1, step < FIRST))
    def _():
        value = tn(h_ref[...], dup_ref[...]).astype(BF16)
        value = value.reshape(up_own.shape[:4] + (CHUNK,))
        cols = pl.ds(pl.multiple_of(lax.rem(step - 1, 2) * CHUNK, CHUNK), CHUNK)

        @pl.when(step < 3)
        def _():
            up_other[:, :, :, :, cols] = value

        @pl.when(step >= 3)
        def _():
            up_own[:, :, :, :, cols] = value

    @at(2)
    def _():
        up.scatter0()

    @pl.when(jnp.logical_and(step >= FIRST, step < FIRST + PAIRS))
    def _():
        pair = step - FIRST
        stats = lse[0]
        dq, dk, dv = attend_back_slot(
            ql[...], [ko[...], kx[...]], [vo[...], vx[...]], dol[...], al[...],
            [stats[0:1], stats[1:2]], between,
        )
        dq = turn_back(dq, cos, sin).astype(BF16)
        dq_ref[:rows, :] = dq
        keep_q[lax.rem(pair, 2), :rows, :] = dq
        keep_k[lax.rem(pair, 2)] = dk[0]
        keep_v[lax.rem(pair, 2)] = dv[0]
        leave[pair, :rows, :PAIR] = dk[1].astype(BF16)
        leave[pair, :rows, PAIR:] = dv[1].astype(BF16)
        dq, dk, dv = attend_back_slot(
            qs[...], [ks[...]], [vs[...]], dos[...], as_[...], [stats[2:3], stats[3:4]]
        )
        dq = turn_back(dq, cos, sin).astype(BF16)
        dq_ref[rows:, :] = dq
        keep_q[lax.rem(pair, 2), rows:, :] = dq
        keep_sk[lax.rem(pair, 2)] = dk[0]
        keep_sv[lax.rem(pair, 2)] = dv[0]
        leave[pair, rows:, :PAIR] = dk[0].astype(BF16)
        leave[pair, rows:, PAIR:] = dv[0].astype(BF16)
        kv_copy(pair).start()

    @pl.when(step > FIRST)
    def _():
        pair = step - FIRST - 1
        kv_copy(pair).wait_recv()
        dk = keep_k[lax.rem(pair, 2)] + come[pair, :rows, :PAIR].astype(F32)
        dk_ref[:rows, :] = turn_back(dk, cos, sin).astype(BF16)
        dv = keep_v[lax.rem(pair, 2)] + come[pair, :rows, PAIR:].astype(F32)
        dv_ref[:rows, :] = dv.astype(BF16)
        zero = jnp.zeros((SHORT, PAIR), F32)
        sk = keep_sk[lax.rem(pair, 2)] + come[pair, rows:, :PAIR].astype(F32)
        sk = jnp.where(me == 0, turn_back(sk, cos[:SHORT], sin[:SHORT]), zero)
        sv = keep_sv[lax.rem(pair, 2)] + come[pair, rows:, PAIR:].astype(F32)
        dk_ref[rows : rows + SHORT, :] = sk.astype(BF16)
        dv_ref[rows : rows + SHORT, :] = jnp.where(me == 0, sv, zero).astype(BF16)
        rest = jnp.zeros((rows - SHORT, PAIR), BF16)
        dk_ref[rows + SHORT :, :] = rest
        dv_ref[rows + SHORT :, :] = rest
        later = lax.rem(pair, 2)
        first, second = wide * (1 - me), wide * me
        q_at = first + later * PAIR
        k_at = (first + 2 * PAIR) * (1 - later) + second * later
        v_at = second + PAIR + later * PAIR
        d_round[:, pl.ds(pl.multiple_of(q_at, PAIR), PAIR)] = keep_q[later]
        d_round[:, pl.ds(pl.multiple_of(k_at, PAIR), PAIR)] = dk_ref[...]
        d_round[:, pl.ds(pl.multiple_of(v_at, PAIR), PAIR)] = dv_ref[...]

    for k in range(ROUNDS):
        @at(FIRST + 2 * k + 2)
        def _():
            value = tn(hid1_ref[...], d_round[...]).astype(BF16)
            rounds[k].other[...] = value[:, :wide].reshape(half_shape(part, wide))
            rounds[k].start(0)
            rounds[k].own[...] = value[:, wide:].reshape(half_shape(part, wide))

    @at(FIRST + PAIRS)
    def _():
        out_ref[...] = out.total()
        rounds[0].add2(r_ref)
        rounds[2].arrive(0)
        rounds[2].merge0()
        rounds[1].add1(ra_ref, rb_ref)
        down_ref[...] = down.total()
        up_ref[...] = up.total()
        down.drain(*range(3, 8))
        out.drain(*range(8))
        up.drain(*range(1, 8))
        rounds[0].drain(*range(5))
        rounds[1].drain(0, 1, 2)
        rounds[2].drain(0)
        for pair in range(PAIRS):
            kv_copy(pair).wait_send()
        early_copy(16).wait_recv()
        for k in range(17):
            early_copy(k).wait_send()
        early_ref[...] = early_all[...]


def middle_call(
    att, d_attention, hidden, d_up, hidden1, payload, down_a, down_b, q, kv, d_att, lse, cos, sin, rows,
):
    n = SLOTS * rows
    half = FF // 2
    dr, dc = FF // 16, D // 2
    ur, wr = D // 16, D // 16

    def clamp(s, low, high):
        return jnp.minimum(jnp.maximum(s, low), high)

    def order_of(k):
        return k // 2 + lax.rem(k, 2) * ROUNDS

    def now(s):
        return order_of(clamp(s - FIRST, 0, PAIRS - 1))

    def before(s):
        return order_of(clamp(s - FIRST - 1, 0, PAIRS - 1))

    def long():
        return pl.BlockSpec((rows, PAIR), lambda s: (0, now(s)))

    def second():
        return pl.BlockSpec((rows, PAIR), lambda s: (1, now(s)))

    def short():
        return pl.BlockSpec((SHORT, PAIR), lambda s: (0, now(s)))

    def low(shape):
        return pltpu.VMEM(shape, BF16)

    handed = ((4, ur, WIDE), (2, 2, ur, WIDE), (2, 2, ur, WIDE), half_shape(ur, WIDE))

    return pl.pallas_call(
        middle_kernel,
        name="middle",
        grid=(FIRST + PAIRS + 1,),
        out_shape=(
            jax.ShapeDtypeStruct((n, D), BF16),
            jax.ShapeDtypeStruct((n, D), BF16),
            jax.ShapeDtypeStruct((n, D), BF16),
            jax.ShapeDtypeStruct((dr, dc), F32),
            jax.ShapeDtypeStruct((wr, dc), F32),
            jax.ShapeDtypeStruct((ur, half), F32),
        )
        + tuple(jax.ShapeDtypeStruct(o, BF16) for o in handed + ((16, 96, 128),)),
        in_specs=[
            whole((n, D)),
            whole((n, D)),
            ANY,
            pl.BlockSpec((n, CHUNK), lambda s: (0, clamp(s - 1, 0, 3))),
            ANY,
            whole((16, D)),
            whole((2, 2, dr, dc)),
            whole((2, 2, dr, dc)),
            long(), second(), long(), long(), long(), long(), short(), short(), long(), second(),
            long(), second(),
            pl.BlockSpec((1, 4, rows), lambda s: (now(s), 0, 0)),
            whole((LEN, PAIR)),
            whole((LEN, PAIR)),
        ],
        out_specs=(
            pl.BlockSpec((n, PAIR), lambda s: (0, now(s))),
            pl.BlockSpec((n, PAIR), lambda s: (0, before(s))),
            pl.BlockSpec((n, PAIR), lambda s: (0, before(s))),
            whole((dr, dc)),
            whole((wr, dc)),
            whole((ur, half)),
        )
        + tuple(whole(o) for o in handed + ((16, 96, 128),)),
        scratch_shapes=[low((n, D)), low((n, D)), low((4, dr, dc)), low((3, dr, dc))]
        + [low(half_shape(wr, dc))] * 3
        + [low((2, 2, wr, dc))] * 2
        + [low((4, wr, dc)), low((3, wr, dc))]
        + [low(half_shape(ur, half))] * 3
        + [low((2, 2, ur, half))] * 2
        + [low((4, ur, half)), low((3, ur, half))]
        + [low((ROUNDS,) + half_shape(ur, WIDE))] * 2
        + [low((2, 2, 2, ur, WIDE))] * 2
        + [low((4, ur, WIDE))]
        + [low((n, 2 * WIDE)), low((2, n, PAIR))]
        + [low((PAIRS, rows + SHORT, 2 * PAIR))] * 2
        + [pltpu.VMEM((2, rows, PAIR), F32)] * 2
        + [pltpu.VMEM((2, SHORT, PAIR), F32)] * 2
        + [pltpu.VMEM((16, D), F32), low((96, 128)), low((16, 96, 128))]
        + [DMA((43,)), DMA((43,)), DMA((PAIRS,)), DMA((PAIRS,)), DMA((17,)), DMA((17,)), DMA((2,))],
        compiler_params=pltpu.CompilerParams(
            collective_id=1, has_side_effects=True, vmem_limit_bytes=BIG
        ),
        cost_estimate=cost(2 * n * D * (FF + 4 * D) + 40 * D * rows * (LEN + SHORT), 50e6),
    )(
        att, d_attention, hidden, d_up, hidden1, payload, down_a, down_b, q, q, *kv, d_att, d_att,
        att, att, lse, cos, sin,
    )


TILES = 4


def end_kernel(
    tok_ref, dmid_ref, dq_ref, dk_ref, dv_ref, mod_ref, gain_ref, weight_any, lengths,
    r_in, ra, rb, rown,
    grad_ref, gqkv_ref, late_ref,
    weight_ref, r2, r3, last_a, last_b, sums, sums_came, sums_all, late_came,
    send, recv, send_late, recv_late, loaded,
):
    step = pl.program_id(0)
    s, me = lax.axis_index("seq"), lax.axis_index("span")
    rounds = [
        Scatter(
            send, recv, 8 * k, own=rown,
            a1=last_a if k == 2 else ra,
            b1=last_b if k == 2 else rb,
            came2=r2.at[k], came3=r3.at[k],
        )
        for k in range(ROUNDS)
    ]

    def late_copy(k):
        if k == 0:
            src, dst, peer = sums, sums_came, {"span": 1 - me}
        else:
            src, dst, peer = sums_all, late_came.at[s], {"seq": lax.rem(s + k, 16)}
        return pltpu.make_async_remote_copy(
            src_ref=src,
            dst_ref=dst,
            send_sem=send_late.at[k],
            recv_sem=recv_late.at[k],
            device_id=peer,
            device_id_type=MESH,
        )

    def at(number):
        return pl.when(step == number)

    @at(0)
    def _():
        load = pltpu.make_async_copy(weight_any, weight_ref, loaded)
        load.start()
        r2[0] = r_in[...]
        sums[...] = jnp.zeros_like(sums)
        greet([{"span": 1 - me}] + [{"seq": lax.rem(s + k, 16)} for k in range(1, 16)])
        rounds[2].start(1, 2)
        rounds[1].start(3, 4)
        rounds[0].start(5, 6, 7)
        load.wait()

    size = tok_ref.shape[0]
    j = step // 2
    swapped = jnp.full((1, D), jnp.where(lengths[1] > lengths[0], 1.0, 0.0))
    mine = jnp.where(j == 0, swapped, 1.0 - swapped)
    scale = jnp.where(mine == 0.0, mod_ref[0:1, D : 2 * D], mod_ref[1:2, D : 2 * D])
    gain = wide_row(gain_ref)
    d_hidden = (
        nt(dq_ref[...], weight_ref[:, :D])
        + nt(dk_ref[...], weight_ref[:, D : 2 * D])
        + nt(dv_ref[...], weight_ref[:, 2 * D :])
    )
    x = tok_ref[...].astype(F32)
    center = x - row_mean(x)
    r = lax.rsqrt(row_mean(center * center) + EPSILON)
    xhat = center * r
    hx = col_sum(d_hidden * xhat)
    fx = d_hidden * (1.0 + scale) * gain
    grad_ref[...] = dmid_ref[...] + r * (fx - row_mean(fx) - xhat * row_mean(fx * xhat))
    shift = col_sum(d_hidden)
    first, second = mine == 0.0, mine != 0.0
    zero = jnp.zeros((1, D), F32)
    sums[...] += jnp.concatenate(
        [
            jnp.where(first, shift, zero), jnp.where(first, hx * gain, zero),
            jnp.where(second, shift, zero), jnp.where(second, hx * gain, zero),
            hx * (1.0 + scale), jnp.zeros((3, D), F32),
        ],
        axis=0,
    )

    @at(TILES - 1)
    def _():
        late_copy(0).start()
        rounds[2].scatter2()
        rounds[1].scatter3()
        late_copy(0).wait_recv()
        sums_all[...] = pack_rows(sums[...] + sums_came[...], 5)
        for k in range(1, 16):
            late_copy(k).start()
        late_came[s] = sums_all[...]
        rounds[2].scatter3()
        for k in range(ROUNDS):
            total = rounds[k].total()
            for c in range(3):
                cols = slice((c * ROUNDS + k) * PAIR, (c * ROUNDS + k + 1) * PAIR)
                gqkv_ref[:, cols] = total[:, c * PAIR : (c + 1) * PAIR]
        rounds[0].drain(*range(5, 8))
        rounds[1].drain(*range(3, 8))
        rounds[2].drain(*range(1, 8))
        for k in range(16):
            if k > 0:
                late_copy(k).wait_recv()
            late_copy(k).wait_send()
        late_ref[...] = late_came[...]


def end_call(tokens, d_mid, dq, dk, dv, mod, gain, weight, lengths, handed, rows):
    n = SLOTS * rows
    size = n // TILES
    r = D // 16

    def tile():
        return pl.BlockSpec((size, D), lambda s: (s, 0))

    return pl.pallas_call(
        end_kernel,
        name="end",
        grid=(TILES,),
        out_shape=(
            jax.ShapeDtypeStruct((n, D), F32),
            jax.ShapeDtypeStruct((r, 3 * D // 2), F32),
            jax.ShapeDtypeStruct((16, 32, 128), BF16),
        ),
        in_specs=[tile()] * 5
        + [
            whole((8, 6 * D)),
            whole((D,)),
            ANY,
            pl.BlockSpec(memory_space=pltpu.SMEM),
        ]
        + [whole(a.shape) for a in handed],
        out_specs=(
            tile(),
            whole((r, 3 * D // 2)),
            whole((16, 32, 128)),
        ),
        scratch_shapes=[
            pltpu.VMEM((D, 3 * D), BF16),
            pltpu.VMEM((ROUNDS, 4, r, WIDE), BF16),
            pltpu.VMEM((ROUNDS, 3, r, WIDE), BF16),
            pltpu.VMEM((2, 2, r, WIDE), BF16),
            pltpu.VMEM((2, 2, r, WIDE), BF16),
            pltpu.VMEM((8, D), F32),
            pltpu.VMEM((8, D), F32),
            pltpu.VMEM((32, 128), BF16),
            pltpu.VMEM((16, 32, 128), BF16),
            DMA((8 * ROUNDS,)),
            DMA((8 * ROUNDS,)),
            DMA((16,)),
            DMA((16,)),
            DMA,
        ],
        compiler_params=pltpu.CompilerParams(
            collective_id=3, has_side_effects=True, vmem_limit_bytes=BIG
        ),
        cost_estimate=cost(2 * n * D * 3 * D, 22e6),
    )(tokens, d_mid, dq, dk, dv, mod, gain, weight, lengths, *handed)


def thirds(value):
    high = value.astype(BF16)
    rest = value - high.astype(F32)
    middle = rest.astype(BF16)
    return [high, middle, (rest - middle.astype(F32)).astype(BF16)]


def condition_kernel(
    lengths, early_ref, late_ref, table_ref, silu_ref, weight_ref,
    qkv_in, out_in, up_in, down_in, sorted_any, result_any,
    ada_ref, bias_ref, gcond_ref, gain1_ref, gain2_ref, bd_ref, bu_ref,
    qkv_ref, out_ref, up_ref, down_ref, natural_any, final_any, stage, stage_out, read, moved,
):
    seq = late_ref.shape[0]
    me, s = lax.axis_index("span"), lax.axis_index("seq")
    half = sorted_any.shape[0] // SLOTS
    reads, moves = [], []
    given = ((sorted_any, stage, natural_any), (result_any, stage_out, final_any))
    for i, (src, held, dst) in enumerate(given):
        for j in range(SLOTS):
            to = pl.ds(pl.multiple_of(slot_of(lengths, j) * half, half), half)
            at = i * SLOTS + j
            reads.append(
                pltpu.make_async_copy(src.at[pl.ds(j * half, half)], held.at[j], read.at[at])
            )
            moves.append(pltpu.make_async_copy(held.at[j], dst.at[to], moved.at[at]))
    for copy in reads:
        copy.start()
    qkv_ref[...] = qkv_in[...]
    out_ref[...] = out_in[...]
    up_ref[...] = up_in[...]
    down_ref[...] = down_in[...]
    packed = early_ref[...].astype(F32)
    early = [
        jnp.concatenate([packed[:, 6 * r + c] for c in range(6)], axis=1) for r in range(14)
    ]
    packed = late_ref[...].astype(F32)
    late = [
        jnp.concatenate([packed[:, 6 * r + c] for c in range(6)], axis=1) for r in range(5)
    ]
    mods = []
    for k in range(SLOTS):
        mods.append(
            [late[2 * k], late[2 * k + 1]] + [early[4 * k + b] for b in range(4)]
        )
    gain1_ref[...] = jnp.sum(late[4], axis=0)
    gain2_ref[...] = jnp.sum(early[8], axis=0)
    bd_ref[...] = jnp.sum(early[9], axis=0)
    for f in range(4):
        bu_ref[f * D : (f + 1) * D] = jnp.sum(early[10 + f], axis=0)
    own = []
    asked = [
        jnp.concatenate([table_ref[:, SLOTS + k, :]] * 6, axis=1) for k in range(SLOTS)
    ]
    for b in range(6):
        cols = slice(b * D, (b + 1) * D)
        bias_ref[cols] = jnp.sum(mods[0][b] + mods[1][b], axis=0)
        rows = []
        for r in range(SLOTS):
            wanted = (s * SLOTS + r).astype(F32)
            picked = [jnp.where(asked[k] == wanted, mods[k][b], 0.0) for k in range(SLOTS)]
            rows.append(col_sum(picked[0] + picked[1]))
        own.append(jnp.concatenate(rows + [jnp.zeros((8 - SLOTS, D), F32)], axis=0))
    own = jnp.concatenate(own, axis=1)
    d_silu = nt(jnp.concatenate(thirds(own), axis=0), weight_ref[...])
    d_silu = d_silu[:8] + d_silu[8:16] + d_silu[16:24]
    for come, go in zip(reads, moves):
        come.wait()
        go.start()
    v = table_ref[s]
    sig = 1.0 / (1.0 + jnp.exp(-v))
    gcond_ref[...] = (d_silu * (sig * (1.0 + v * (1.0 - sig))))[:SLOTS]
    rows = 128 // seq
    pick = lax.broadcasted_iota(jnp.int32, (rows, 128), 1) == (
        s * rows + lax.broadcasted_iota(jnp.int32, (rows, 128), 0)
    )
    pick = jnp.where(pick, 1.0, 0.0)
    silu = [nt(pick.astype(BF16), silu_ref[k].astype(BF16)).astype(BF16) for k in range(SLOTS)]
    silu = jnp.concatenate(silu * 3, axis=1)
    for b in range(3):
        blocks = [jnp.where(me == 0, mods[k][b], mods[k][3 + b]) for k in range(SLOTS)]
        split = [part for part in zip(*(thirds(block) for block in blocks))]
        right = jnp.concatenate([block for part in split for block in part], axis=0)
        ada_ref[:, b * D : (b + 1) * D] = nn(silu, right)
    for move in moves:
        move.wait()


def condition_call(lengths, early, late, table, silu, ada_weight, tiles, grad_in, result):
    seq = late.shape[0]

    def all_of(shape):
        return pl.BlockSpec(shape, lambda i, p: (0,) * len(shape))

    given = (early, late, table, silu, ada_weight) + tiles
    outs = ((128 // seq, 3 * D), (6 * D,), (SLOTS, 128), (D,), (D,), (D,), (FF,))
    outs += tuple(t.shape for t in tiles)
    return pl.pallas_call(
        condition_kernel,
        name="condition",
        out_shape=tuple(jax.ShapeDtypeStruct(o, F32) for o in outs + (grad_in.shape,))
        + (jax.ShapeDtypeStruct(result.shape, BF16),),
        grid_spec=pltpu.PrefetchScalarGridSpec(
            num_scalar_prefetch=1,
            grid=(1,),
            in_specs=[whole(a.shape) for a in given] + [ANY] * 2,
            out_specs=[all_of(o) for o in outs] + [ANY] * 2,
            scratch_shapes=[
                pltpu.VMEM((SLOTS, grad_in.shape[0] // SLOTS, D), F32),
                pltpu.VMEM((SLOTS, grad_in.shape[0] // SLOTS, D), BF16),
                DMA((2 * SLOTS,)),
                DMA((2 * SLOTS,)),
            ],
        ),
        compiler_params=pltpu.CompilerParams(vmem_limit_bytes=BIG),
        cost_estimate=cost(1e7, 12e6),
    )(lengths, *given, grad_in, result)


def from_peers(array, span):
    return [
        lax.ppermute(array, "span", [((i + step) % span, i) for i in range(span)])
        for step in range(1, span)
    ]


def gather_all(flat):
    seq, span = lax.axis_size("seq"), lax.axis_size("span")
    return lax.all_gather(flat, ("seq", "span"), axis=0).reshape(seq, span, flat.shape[0])


def shards(
    tokens, conditions, assignment, lengths, norm1_gain, ada_weight, ada_bias, qkv_weight,
    out_weight, norm2_gain, up_weight, up_bias, down_weight, down_bias, cotangent,
):
    slots, rows, _ = tokens.shape
    seq, span = lax.axis_size("seq"), lax.axis_size("span")
    seq_at, span_at = lax.axis_index("seq"), lax.axis_index("span")
    flat = slots * rows
    place = jnp.concatenate(
        [lengths, jnp.stack([span_at.astype(jnp.int32), seq_at.astype(jnp.int32)])]
    )
    fast = seq == 16 and span == 2
    cos, sin = (jnp.asarray(table) for table in rotary(LEN))
    tokens2 = tokens.reshape(flat, D)
    gain1, gain2 = norm1_gain, norm2_gain
    if fast:
        q, hidden1, kv, mod, table, silu_all, kvx = share_call(
            conditions, assignment, ada_weight, ada_bias, tokens2, gain1, qkv_weight, cos, sin,
            rows,
        )
        att, lse, q, *kv, tokens2, cot, hidden1 = attend_sorted_call(
            lengths, q, kv, kvx, tokens2, cotangent.reshape(flat, D), hidden1, rows
        )
    else:
        mod, table, _ = modulation_call(conditions, assignment, ada_weight, ada_bias, seq)
        q, hidden1, kv_long, kv_tail = project_call(
            place, tokens2, mod, gain1, qkv_weight, cos, sin, rows
        )
        kv_other = jnp.concatenate(from_peers(kv_long, span), axis=0)
        kv_short = kv_tail[:SHORT]
        sent = [lax.ppermute(kv_short, "span", [(0, i)]) for i in range(1, span)]
        kv_short = jnp.where(span_at == 0, kv_short, sum(sent[1:], sent[0]))
        att, lse = attend_call(q, kv_long, kv_other, kv_short, rows)
    if fast:
        out, d_mid, d_att, hidden2, d_up, d_attention, payload, *handed = both_call(
            tokens2, att, cot, mod, gain2, out_weight, up_weight, up_bias, down_weight,
            down_bias, lengths, rows,
        )
        dq, dk, dv, grad_down, grad_out, grad_up, *handed, early = middle_call(
            att, d_attention, hidden2, d_up, hidden1, payload, *handed, q, kv, d_att, lse,
            cos, sin, rows,
        )
        grad_in, grad_qkv, late = end_call(
            tokens2, d_mid, dq, dk, dv, mod, gain1, qkv_weight, lengths, handed, rows
        )
        (
            grad_ada, ada_bias_sum, grad_cond, gain1_sum, gain2_sum, bd_sum, bu_sum,
            grad_qkv, grad_out, grad_up, grad_down, grad_in, out,
        ) = condition_call(
            lengths, early, late, table, silu_all, ada_weight,
            (grad_qkv, grad_out, grad_up, grad_down), grad_in, out,
        )
        return (
            out.reshape(tokens.shape), grad_in.reshape(tokens.shape), grad_cond, gain1_sum,
            grad_ada, ada_bias_sum, grad_qkv, grad_out, gain2_sum, grad_up, bu_sum, grad_down,
            bd_sum,
        )
    (
        out, d_mid, d_att, act, d_low, hidden2, d_up, d_attention, payload, tokens_sorted,
        hidden1_sorted,
    ) = feed_call(
        fast, lengths, tokens2, att, cotangent.reshape(flat, D), hidden1, mod, gain2, out_weight,
        up_weight, up_bias, down_weight, down_bias, rows,
    )
    grad_down = weight_gradient(act, d_low)
    grad_up = weight_gradient(hidden2, d_up)
    grad_out = weight_gradient(att, d_attention)
    early = gather_all(payload[:14].reshape(-1))

    dq, dk, dv, dkx, dvx, dks, dvs = attend_back_call(
        place, q, kv_long, kv_other, kv_short, d_att, att, lse, cos, sin, rows
    )
    ek = ev = None
    for step in range(1, span):
        back = [((i, (i + step) % span)) for i in range(span)]
        cut = slice((step - 1) * rows, step * rows)
        pk, pv = lax.ppermute((dkx[cut], dvx[cut]), "span", back)
        ek = pk if ek is None else (ek.astype(F32) + pk.astype(F32))
        ev = pv if ev is None else (ev.astype(F32) + pv.astype(F32))
    d_short = jnp.concatenate([dks, dvs], axis=1)
    for step in range(1, span):
        d_short = d_short + lax.ppermute(
            jnp.concatenate([dks, dvs], axis=1), "span", [(step, 0)]
        )
    d_qkv = join_call(
        place, dq, dk, dv, ek, ev, d_short[:, :D], d_short[:, D:], cos, sin, rows
    )
    grad_qkv = weight_gradient(hidden1, d_qkv)
    grad_in, d_mod1, d_gain1 = last_call(
        place, tokens2, d_qkv, d_mid, mod, gain1, qkv_weight, rows
    )
    late = gather_all(jnp.concatenate([d_mod1[:, :2].reshape(-1), d_gain1[0]]))

    cut = slots * 4 * D
    mods2 = jnp.sum(early[:, :, :cut], axis=1).reshape(seq * slots, 4 * D)
    sums2 = jnp.sum(early[:, :, cut:], axis=(0, 1))
    cut = slots * 2 * D
    mods1 = jnp.sum(late[:, :, :cut], axis=1).reshape(seq * slots, 2 * D)
    gain1_sum = jnp.sum(late[:, :, cut:], axis=(0, 1))
    d_mods = jnp.concatenate([mods1, mods2], axis=1)
    grad_ada_bias = jnp.sum(d_mods, axis=0)
    cond_all = table[:, :slots].reshape(seq * slots, 128)
    assign_all = table[:, slots : 2 * slots, 0].reshape(seq * slots)
    number = jnp.arange(seq * slots, dtype=jnp.int32).astype(F32)
    picker = (assign_all[:, None] == number[None, :]).astype(F32)
    exact = partial(lax.dot_general, precision=HIGHEST, preferred_element_type=F32)
    cond_rows = exact(picker, cond_all, (((1,), (0,)), ((), ())))
    silu_low = jax.nn.silu(cond_rows).astype(BF16).astype(F32)
    ada_rows, ada_cols = 128 // seq, 6 * D // span
    grad_ada = exact(
        lax.dynamic_slice_in_dim(silu_low, seq_at * ada_rows, ada_rows, 1),
        lax.dynamic_slice_in_dim(d_mods, span_at * ada_cols, ada_cols, 1),
        (((0,), (0,)), ((), ())),
    )
    wanted = lax.dynamic_slice_in_dim(picker, seq_at * slots, slots, 1)
    own_mods = exact(wanted, d_mods, (((0,), (0,)), ((), ())))
    d_silu = exact(own_mods, ada_weight.astype(F32), (((1,), (1,)), ((), ())))
    grad_cond = jax.vjp(jax.nn.silu, conditions.astype(F32))[1](d_silu)[0]
    return (
        out.reshape(tokens.shape),
        grad_in.reshape(tokens.shape),
        grad_cond,
        gain1_sum,
        grad_ada,
        grad_ada_bias,
        grad_qkv,
        grad_out,
        sums2[:D],
        grad_up,
        sums2[2 * D :],
        grad_down,
        sums2[D : 2 * D],
    )


def solution(mesh):
    data, table, one = P("seq", "span", None), P("seq", None), P("seq")
    tile = P("seq", "span")
    in_specs = (data, table, one, one) + (P(),) * 10 + (data,)
    out_specs = (data, data, table, P(), tile, P(), tile, tile, P(), tile, P(), tile, P())
    return jax.shard_map(shards, mesh=mesh, in_specs=in_specs, out_specs=out_specs, check_vma=False)
```
